32 devices in a mesh: req: 8 (over z, x), tp: 4 (over y, core).
Axes of the slice: x: 2, y: 2, z: 4, core: 2. Of those that a mesh axis runs over, the one named last changes fastest.
Arguments:
- hidden_in: bfloat16 [1024, 2048], P('req', 'tp'), may hold values from -48 to 48
- norm_in_gain: float32 [2048], replicated, may hold values from 0.1 to 1.9
- q_weight: bfloat16 [2048, 2048], P(None, 'tp'), may hold values from -0.125 to 0.125
- k_weight: bfloat16 [2048, 512], P(None, 'tp'), may hold values from -0.125 to 0.125
- v_weight: bfloat16 [2048, 512], P(None, 'tp'), may hold values from -0.125 to 0.125
- q_gain: float32 [128], replicated, may hold values from 0.1 to 1.9
- k_gain: float32 [128], replicated, may hold values from 0.1 to 1.9
- o_weight: bfloat16 [2048, 2048], P('tp'), may hold values from -0.125 to 0.125
- key_pages: bfloat16 [4, 384, 128, 128], P('tp', 'req'), may hold values from -256 to 256
- value_pages: bfloat16 [4, 384, 128, 128], P('tp', 'req'), may hold values from -6 to 6
- page_table: int32 [72, 32], P('req'), may hold values from 0 to 47, as said below
- cache_len: int32 [72], P('req'), may hold values from 1 to 4096, as said below
- norm_post_gain: float32 [2048], replicated, may hold values from 0.1 to 1.9
- expert_ids: int32 [1024, 8], P('req'), may hold values from 0 to 15, all different within a row; in each aligned block of 128 rows (0 to 127, 128 to 255, ...) at most 96 rows name the same one
- route_weights: float32 [1024, 8], P('req'), may hold values from 0.02 to 0.25
- gate_weight: bfloat16 [16, 2048, 768], P('req', None, 'tp'), may hold values from -0.125 to 0.125
- up_weight: bfloat16 [16, 2048, 768], P('req', None, 'tp'), may hold values from -0.125 to 0.125
- down_weight: bfloat16 [16, 768, 2048], P('req', 'tp'), may hold values from -0.21875 to 0.21875
Outputs:
- layer_out: bfloat16 [1024, 2048], P('req', 'tp')
The draws below stay inside these ranges and needn't reach their ends.
Inputs may be any that keep to these rules, and one draw needn't show every extreme that they name: `cache_len`: in each group of 9 consecutive requests one request holds 4096 cached tokens and another exactly 256; the others hold at most 256. `page_table`: for request r of group g = r // 9, entry j with j * 128 below cache_len[r] names the page, among group g's 48 pages of the caches, that holds the request's cached tokens j * 128 to j * 128 + 127; these pages are distinct within a group. Other entries name arbitrary pages of the group and are not read; pages that no read entry names hold unused data. `expert_ids`: among the 128 rows of one group no expert is named more than 96 times.
All inputs are finite; a program needn't handle non-finite values.
Results may differ from the reference program's by a relative error of at most 0.006.
Values may be sent and summed in bfloat16 or wider, within the bound.
No kernel may reach another device: no remote copies, remote signals or barrier semaphores. Data moves between devices by JAX's collectives and lax.ppermute only.
A program may use at most 128 MiB of HBM per device.

```python
import math
import jax
import jax.numpy as jnp
import numpy as np
from jax import lax

D = 2048
HD = 128
HQ = 16
KVH = 4
FF = 768
TOP = 8
PAGE = 128
MAXPG = 32
SHORT_PG = 2
PRE = 120
TOK_DEV = 128
REQS_DEV = 9
POOL = 48
TOKENS = 1024
REQS = 72
PAGES = 384
EXPERTS = 16
CAP = 96
N_REQ = 8
N_TP = 4


def draw_hidden_in(key, part):
    key_base, key_col, key_row = jax.random.split(jax.random.fold_in(key, 202), 3)
    column = jnp.arange(D, dtype=jnp.float32) / D
    col_scale = 0.3 * jnp.power(10.0, 0.5 * column + 0.5 * jax.random.uniform(key_col, (D,)))
    row_scale = jnp.power(10.0, jax.random.uniform(key_row, (TOKENS, 1), minval=-0.5, maxval=0.5))
    base_draw = jnp.clip(jax.random.normal(key_base, (TOKENS, D)), -5.0, 5.0)
    return (base_draw * row_scale * col_scale[None, :]).astype(jnp.bfloat16)


def draw_key_pages(key, part):
    key_one = jax.random.fold_in(jax.random.fold_in(key, 303), 0)
    values = 2.5 * jnp.clip(jax.random.normal(key_one, (KVH, PAGES, PAGE, HD)), -6.0, 6.0)
    return values.astype(jnp.bfloat16)


def request_layout(key):
    base_key = jax.random.fold_in(key, 101)
    key_long, key_next, key_exp, key_len, key_perm, key_spare = jax.random.split(base_key, 6)
    groups = REQS // REQS_DEV
    short_cap = SHORT_PG * PAGE
    top_exp = short_cap.bit_length() - 1
    long_pick = jax.random.randint(key_long, (groups, 1), 0, REQS_DEV)
    full_pick = (long_pick + 1 + jax.random.randint(key_next, (groups, 1), 0, REQS_DEV - 1)) % REQS_DEV
    exponent = jax.random.randint(key_exp, (groups, REQS_DEV), 0, top_exp + 1)
    low_len = jnp.left_shift(jnp.ones((groups, REQS_DEV), jnp.int32), exponent)
    extra_len = jax.random.randint(key_len, (groups, REQS_DEV), 0, 1 << 30) % low_len
    short_len = jnp.minimum(low_len + extra_len, short_cap)
    member = jnp.arange(REQS_DEV, dtype=jnp.int32)[None, :]
    lengths = jnp.where(member == long_pick, MAXPG * PAGE, jnp.where(member == full_pick, short_cap, short_len)).astype(jnp.int32)
    pages_used = (lengths + PAGE - 1) // PAGE
    page_begin = jnp.cumsum(pages_used, axis=1) - pages_used
    order_keys = jax.random.randint(key_perm, (groups, POOL), 0, 1 << 20) * POOL + jnp.arange(POOL, dtype=jnp.int32)[None, :]
    pool_order = jnp.argsort(order_keys, axis=1).astype(jnp.int32)
    entry_idx = jnp.arange(MAXPG, dtype=jnp.int32)[None, None, :]
    pool_spot = jnp.minimum(page_begin[:, :, None] + entry_idx, POOL - 1).reshape(groups, REQS_DEV * MAXPG)
    pool_taken = jnp.take_along_axis(pool_order, pool_spot, axis=1).reshape(groups, REQS_DEV, MAXPG)
    spare_page = jax.random.randint(key_spare, (groups, REQS_DEV, MAXPG), 0, POOL)
    table = jnp.where(entry_idx < pages_used[:, :, None], pool_taken, spare_page).astype(jnp.int32)
    return (lengths.reshape(REQS), table.reshape(REQS, MAXPG))


def draw_cache_len(key, part):
    return request_layout(key)[0]


def draw_page_table(key, part):
    return request_layout(key)[1]


def block_levels(own_key, shape, shards, smallest, largest):
    def one(position, parts):
        steps = jax.random.uniform(jax.random.fold_in(jax.random.fold_in(own_key, 6), position), (parts,), jnp.float32, smallest / len(shards), largest / len(shards))
        return jnp.repeat(jnp.exp(steps), shape[position] // parts).reshape((-1,) + (1,) * (len(shape) - position - 1))

    gain = one(*shards[0])
    for cut in shards[1:]:
        gain = gain * one(*cut)
    return gain


def assign_block(own_key, own, number, rows, amount, top, reach, lean):
    order = jax.random.permutation(own_key, amount)
    packed, usual = portions_of(amount, rows * top, reach, lean, True), portions_of(amount, rows * top, reach, lean, False)
    places = jnp.arange(amount)

    def named(sizes, rotation):
        used = int((sizes > 0).sum())
        fixed = max(1, used // 4)
        passed = fixed + (places - fixed + rotation * (used - fixed)) % max(1, amount - fixed)
        return jnp.zeros((amount,), jnp.int32).at[order[jnp.where(places < fixed, places, passed)]].set(jnp.asarray(sizes, jnp.int32))

    sizes = jnp.where(number % 4 == 0, named(packed, number // 4), named(usual, number - number // 4 - 1))
    mixed = jax.random.permutation(jax.random.fold_in(own, 3), amount)
    giver, taker = mixed[0:amount // 2 * 2:2], mixed[1:amount // 2 * 2:2]
    margin = jnp.minimum(sizes[giver] - 1, reach - sizes[taker]) // 2
    margin = jnp.where((giver == order[0]) | (taker == order[0]) | (sizes[taker] == 0), 0, jnp.maximum(margin, 0))
    passed = jax.random.randint(jax.random.fold_in(own, 4), (amount // 2,), 0, 1 << 20) % (margin + 1)
    sizes = sizes.at[giver].add(-passed).at[taker].add(passed)
    members = jnp.searchsorted(jnp.cumsum(sizes), jnp.arange(rows * top), side="right").astype(jnp.int32)
    table = members.reshape(top, rows).T
    table = table[jax.random.permutation(jax.random.fold_in(own, 1), rows)]
    rotation = jax.random.randint(jax.random.fold_in(own, 2), (rows, 1), 0, top)
    return jnp.take_along_axis(table, (jnp.arange(top)[None, :] + rotation) % top, axis=1)


def portions_of(amount, total, bound, slope, full):
    portions = [(1 << 20) // math.isqrt(standing ** slope) + 1 for standing in range(1, amount + 1)]
    largest = bound if full else min(bound, max(-(-total // amount), total * portions[0] // sum(portions)))
    least = 1 if total - largest >= amount - 1 else 0
    counts, spare = [largest] + [least] * (amount - 1), total - largest - least * (amount - 1)
    while spare > 0:
        movable = [i for i in range(1, amount) if counts[i] < largest] or [i for i in range(1, amount) if counts[i] < bound]
        whole, left = sum([portions[i] for i in movable]), spare
        for i in movable:
            more = min(bound - counts[i], max(1, left * portions[i] // whole), spare)
            counts[i] = counts[i] + more
            spare = spare - more
    return np.array(counts)


def normal_values(own_key, shape, deviation, bound, pieces=(), kind=jnp.bfloat16):
    loudness = block_levels(own_key, shape, pieces, -0.22, 0.18) if pieces else 1.0
    result = jax.random.normal(own_key, shape, jnp.float32) * deviation * loudness
    return jnp.minimum(jnp.maximum(result, -bound), bound).astype(kind)


def setup_inputs(seed: int = 0) -> dict:
    splits = jax.random.split(jax.random.key(seed), 19)
    hidden_in = draw_hidden_in(jax.random.fold_in(splits[18], 71), 0)
    norm_in_gain = jnp.clip(1.0 + 0.18 * jax.random.normal(splits[1], (D,), jnp.float32), 0.1, 1.9)
    q_weight = normal_values(splits[2], (D, HQ * HD), D ** -0.5, 0.125, ((1, 4),))
    k_weight = normal_values(splits[3], (D, KVH * HD), D ** -0.5, 0.125, ((1, 4),))
    v_weight = normal_values(splits[4], (D, KVH * HD), D ** -0.5, 0.125, ((1, 4),))
    q_gain = jnp.clip(1.0 + 0.18 * jax.random.normal(splits[5], (HD,), jnp.float32), 0.1, 1.9)
    k_gain = jnp.clip(1.0 + 0.18 * jax.random.normal(splits[6], (HD,), jnp.float32), 0.1, 1.9)
    o_weight = normal_values(splits[7], (HQ * HD, D), (HQ * HD) ** -0.5, 0.125, ((0, 4),))
    key_pages = draw_key_pages(jax.random.fold_in(splits[18], 71), 0)
    value_pages = normal_values(splits[9], (KVH, PAGES, PAGE, HD), 1.0, 6.0, ((0, 4), (1, 8)))
    page_table = draw_page_table(jax.random.fold_in(splits[18], 71), 0)
    cache_len = draw_cache_len(jax.random.fold_in(splits[18], 71), 0)
    norm_post_gain = jnp.clip(1.0 + 0.18 * jax.random.normal(splits[12], (D,), jnp.float32), 0.1, 1.9)
    expert_ids_keys = jax.random.split(jax.random.fold_in(splits[13], 1), TOKENS // TOK_DEV)
    expert_ids_turns = jax.random.permutation(jax.random.fold_in(splits[13], 3), TOKENS // TOK_DEV)
    expert_ids = jax.vmap(lambda own, number: assign_block(jax.random.fold_in(splits[13], 2), own, number, TOK_DEV, EXPERTS, TOP, CAP, 2))(expert_ids_keys, expert_ids_turns).reshape((TOKENS, TOP))
    route_weights = jnp.clip(0.02 + 0.23 * jax.random.uniform(splits[14], (TOKENS, TOP), jnp.float32) ** block_levels(splits[14], (TOKENS, TOP), ((0, 8),), -0.2, 0.2), 0.02, 0.25)
    gate_weight = normal_values(splits[15], (EXPERTS, D, FF), D ** -0.5, 0.125, ((0, 8), (2, 4)))
    up_weight = normal_values(splits[16], (EXPERTS, D, FF), D ** -0.5, 0.125, ((0, 8), (2, 4)))
    down_weight = normal_values(splits[17], (EXPERTS, FF, D), FF ** -0.5, 0.21875, ((0, 8), (1, 4)))
    return dict(hidden_in=hidden_in, norm_in_gain=norm_in_gain, q_weight=q_weight, k_weight=k_weight, v_weight=v_weight, q_gain=q_gain, k_gain=k_gain, o_weight=o_weight, key_pages=key_pages, value_pages=value_pages, page_table=page_table, cache_len=cache_len, norm_post_gain=norm_post_gain, expert_ids=expert_ids, route_weights=route_weights, gate_weight=gate_weight, up_weight=up_weight, down_weight=down_weight)


NORM_EPS = 1e-06
ROPE_BASE = 1000000.0

def rms_scale(values, gain_vec):
    mean_square = lax.optimization_barrier(jnp.mean(values * values, axis=-1, keepdims=True))
    return values * lax.rsqrt(mean_square + NORM_EPS) * gain_vec

def rotate(values, positions):
    half_dim = values.shape[-1] // 2
    exponent = jnp.arange(half_dim, dtype=jnp.float32) * (2.0 / values.shape[-1])
    frequency = jnp.power(jnp.float32(ROPE_BASE), -exponent)
    angles = positions.astype(jnp.float32)[:, None] * frequency[None, :]
    cosine = jnp.cos(angles)[:, None, :]
    sine_val = jnp.sin(angles)[:, None, :]
    front_half = values[..., :half_dim]
    back_half = values[..., half_dim:]
    return jnp.concatenate([front_half * cosine - back_half * sine_val, back_half * cosine + front_half * sine_val], axis=-1)

def token_layout(lengths):
    local_idx = jnp.arange(TOK_DEV, dtype=jnp.int32)
    requests = jnp.where(local_idx < PRE, 0, local_idx - PRE + 1).astype(jnp.int32)
    offsets = jnp.where(local_idx < PRE, local_idx, 0).astype(jnp.int32)
    request_hot = (requests[:, None] == jnp.arange(REQS_DEV, dtype=jnp.int32)[None, :]).astype(jnp.int32)
    positions = lax.optimization_barrier(jnp.sum(request_hot * lengths[None, :], axis=1)) + offsets
    return (requests, positions)

def page_slots(table, lengths):
    pages_used = (lengths + PAGE - 1) // PAGE
    entry_live = jnp.arange(MAXPG, dtype=jnp.int32)[None, :] < pages_used[:, None]
    page_match = ((table[:, :, None] == jnp.arange(POOL, dtype=jnp.int32)[None, None, :]) & entry_live[:, :, None]).astype(jnp.int32)
    page_owner = lax.optimization_barrier(jnp.sum(page_match * jnp.arange(REQS_DEV, dtype=jnp.int32)[:, None, None], axis=(0, 1)))
    page_start = lax.optimization_barrier(jnp.sum(page_match * (jnp.arange(MAXPG, dtype=jnp.int32) * PAGE)[None, :, None], axis=(0, 1)))
    page_used = lax.optimization_barrier(jnp.sum(page_match, axis=(0, 1))) > 0
    owner_length = lax.optimization_barrier(jnp.sum(page_match * lengths[:, None, None], axis=(0, 1)))
    slot_pos = page_start[:, None] + jnp.arange(PAGE, dtype=jnp.int32)[None, :]
    slot_live = page_used[:, None] & (slot_pos < owner_length[:, None])
    slot_owner = jnp.where(slot_live, page_owner[:, None], -1).astype(jnp.int32)
    return slot_owner.reshape(POOL * PAGE)

def attend(queries, keys_new, values_new, keys_cache, values_cache, requests, positions, slot_owner):
    inv_root = 1.0 / math.sqrt(queries.shape[-1])
    cache_mask = slot_owner[None, :] == requests[:, None]
    new_mask = (requests[None, :] == requests[:, None]) & (positions[None, :] <= positions[:, None])
    score_cache = jnp.einsum('tkgh,knh->kgtn', queries.astype(jnp.float32), keys_cache.astype(jnp.float32)) * inv_root
    score_new = jnp.einsum('tkgh,skh->kgts', queries.astype(jnp.float32), keys_new.astype(jnp.float32)) * inv_root
    score_cache = jnp.where(cache_mask[None, None], score_cache, -1e+30)
    score_new = jnp.where(new_mask[None, None], score_new, -1e+30)
    row_max = jnp.maximum(lax.optimization_barrier(jnp.max(score_cache, axis=-1, keepdims=True)), lax.optimization_barrier(jnp.max(score_new, axis=-1, keepdims=True)))
    exp_cache = jnp.where(cache_mask[None, None], jnp.exp(score_cache - row_max), 0.0)
    exp_new = jnp.where(new_mask[None, None], jnp.exp(score_new - row_max), 0.0)
    total = lax.optimization_barrier(jnp.sum(exp_cache, axis=-1, keepdims=True)) + lax.optimization_barrier(jnp.sum(exp_new, axis=-1, keepdims=True))
    prob_cache = (exp_cache / total).astype(jnp.bfloat16)
    prob_new = (exp_new / total).astype(jnp.bfloat16)
    mixed = jnp.einsum('kgtn,knh->tkgh', prob_cache.astype(jnp.float32), values_cache.astype(jnp.float32))
    mixed = mixed + jnp.einsum('kgts,skh->tkgh', prob_new.astype(jnp.float32), values_new.astype(jnp.float32))
    return mixed.astype(jnp.bfloat16).reshape(queries.shape[0], -1)

def reference(hidden_in, norm_in_gain, q_weight, k_weight, v_weight, q_gain, k_gain, o_weight, key_pages, value_pages, page_table, cache_len, norm_post_gain, expert_ids, route_weights, gate_weight, up_weight, down_weight):
    group_size = HQ // KVH
    x_float = hidden_in.astype(jnp.float32)
    normed_in = rms_scale(x_float, norm_in_gain).astype(jnp.bfloat16)
    query_lin = jnp.dot(normed_in, q_weight, preferred_element_type=jnp.float32).reshape(TOKENS, HQ, HD)
    key_lin = jnp.dot(normed_in, k_weight, preferred_element_type=jnp.float32).reshape(TOKENS, KVH, HD)
    values_new = jnp.dot(normed_in, v_weight, preferred_element_type=jnp.float32).astype(jnp.bfloat16).reshape(TOKENS, KVH, HD)
    lengths_grp = cache_len.reshape(N_REQ, REQS_DEV)
    table_grp = page_table.reshape(N_REQ, REQS_DEV, MAXPG)

    def group_positions(group_len):
        return token_layout(group_len)[1]
    positions = jax.vmap(group_positions)(lengths_grp).reshape(TOKENS)
    queries = rotate(rms_scale(query_lin, q_gain), positions).astype(jnp.bfloat16)
    keys_new = rotate(rms_scale(key_lin, k_gain), positions).astype(jnp.bfloat16)
    queries_grp = queries.reshape(N_REQ, TOK_DEV, KVH, group_size, HD)
    keys_grp = keys_new.reshape(N_REQ, TOK_DEV, KVH, HD)
    values_grp = values_new.reshape(N_REQ, TOK_DEV, KVH, HD)

    def one_group(inputs):
        group_idx, group_q, group_k, group_v, group_table, group_len = inputs
        requests, group_pos = token_layout(group_len)
        slot_owner = page_slots(group_table, group_len)
        start_page = (group_idx * POOL).astype(jnp.int32)
        keys_cache = lax.dynamic_slice_in_dim(key_pages, start_page, POOL, 1).reshape(KVH, POOL * PAGE, HD)
        values_cache = lax.dynamic_slice_in_dim(value_pages, start_page, POOL, 1).reshape(KVH, POOL * PAGE, HD)
        return attend(group_q, group_k, group_v, keys_cache, values_cache, requests, group_pos, slot_owner)
    attended = lax.map(one_group, (jnp.arange(N_REQ, dtype=jnp.int32), queries_grp, keys_grp, values_grp, table_grp, lengths_grp))
    attended = attended.reshape(TOKENS, HQ * HD)
    residual = x_float + jnp.dot(attended, o_weight, preferred_element_type=jnp.float32)
    normed_post = rms_scale(residual, norm_post_gain).astype(jnp.bfloat16)
    flat_expert = expert_ids.reshape(N_REQ, TOK_DEV * TOP)
    one_hot = (flat_expert[:, :, None] == jnp.arange(EXPERTS, dtype=jnp.int32)[None, None, :]).astype(jnp.int32)
    slot_rank = lax.optimization_barrier(jnp.sum((jnp.cumsum(one_hot, axis=1) - one_hot) * one_hot, axis=2))
    slot_index = flat_expert * (N_REQ * CAP) + jnp.arange(N_REQ, dtype=jnp.int32)[:, None] * CAP + slot_rank
    slot_index = slot_index.reshape(TOKENS * TOP).astype(jnp.int32)
    token_of = jnp.arange(TOKENS * TOP, dtype=jnp.int32) // TOP
    slot_token = jnp.full((EXPERTS * N_REQ * CAP,), TOKENS, jnp.int32).at[slot_index].set(token_of)
    slot_weight = jnp.zeros((EXPERTS * N_REQ * CAP,), jnp.float32).at[slot_index].set(route_weights.reshape(TOKENS * TOP))
    normed_pad = jnp.concatenate([normed_post, jnp.zeros((1, D), jnp.bfloat16)], axis=0)

    def one_expert(carry_sum, inputs):
        token_ids, weights, w_gate, w_up, w_down = inputs
        token_rows = normed_pad[token_ids]
        gate_acts = jnp.dot(token_rows, w_gate, preferred_element_type=jnp.float32)
        up_acts = jnp.dot(token_rows, w_up, preferred_element_type=jnp.float32)
        hidden_act = (jax.nn.silu(gate_acts) * up_acts).astype(jnp.bfloat16)
        part_sums = jnp.einsum('rgf,gfd->rgd', hidden_act.reshape(-1, N_TP, FF // N_TP).astype(jnp.float32), w_down.reshape(N_TP, FF // N_TP, D).astype(jnp.float32)).astype(jnp.bfloat16)
        contrib = lax.optimization_barrier(jnp.sum(part_sums.astype(jnp.float32), axis=1)) * weights[:, None]
        return (carry_sum.at[token_ids].add(contrib), None)
    start_sum = jnp.zeros((TOKENS + 1, D), jnp.float32)
    moe, _ = lax.scan(one_expert, start_sum, (slot_token.reshape(EXPERTS, N_REQ * CAP), slot_weight.reshape(EXPERTS, N_REQ * CAP), gate_weight, up_weight, down_weight))
    return (residual + moe[:TOKENS]).astype(jnp.bfloat16)
```

```python
import math

import jax
import jax.numpy as jnp
from jax import lax
from jax.sharding import PartitionSpec as P

PAGE = 128
MAXPG = 32
PRE = 120
TOK_DEV = 128
REQS_DEV = 9
POOL = 48


NORM_EPS = 1e-06
ROPE_BASE = 1000000.0


def rms_scale(values, gain_vec):
    mean_square = jnp.mean(values * values, axis=-1, keepdims=True)
    return values * lax.rsqrt(mean_square + NORM_EPS) * gain_vec


def rotate(values, positions):
    half_dim = values.shape[-1] // 2
    exponent = jnp.arange(half_dim, dtype=jnp.float32) * (2.0 / values.shape[-1])
    frequency = jnp.power(jnp.float32(ROPE_BASE), -exponent)
    angles = positions.astype(jnp.float32)[:, None] * frequency[None, :]
    cosine = jnp.cos(angles)[:, None, :]
    sine_val = jnp.sin(angles)[:, None, :]
    front_half = values[..., :half_dim]
    back_half = values[..., half_dim:]
    return jnp.concatenate(
        [front_half * cosine - back_half * sine_val, back_half * cosine + front_half * sine_val],
        axis=-1,
    )


def token_layout(lengths):
    local_idx = jnp.arange(TOK_DEV, dtype=jnp.int32)
    requests = jnp.where(local_idx < PRE, 0, local_idx - PRE + 1)
    offsets = jnp.where(local_idx < PRE, local_idx, 0)
    request_hot = (requests[:, None] == jnp.arange(REQS_DEV, dtype=jnp.int32)[None, :]).astype(
        jnp.int32
    )
    positions = jnp.sum(request_hot * lengths[None, :], axis=1) + offsets
    return (requests, positions)


def page_slots(table, lengths):
    pages_used = (lengths + PAGE - 1) // PAGE
    entry_live = jnp.arange(MAXPG, dtype=jnp.int32)[None, :] < pages_used[:, None]
    page_match = (
        (table[:, :, None] == jnp.arange(POOL, dtype=jnp.int32)[None, None, :])
        & entry_live[:, :, None]
    ).astype(jnp.int32)
    page_owner = jnp.sum(
        page_match * jnp.arange(REQS_DEV, dtype=jnp.int32)[:, None, None], axis=(0, 1)
    )
    page_start = jnp.sum(
        page_match * (jnp.arange(MAXPG, dtype=jnp.int32) * PAGE)[None, :, None], axis=(0, 1)
    )
    page_used = jnp.sum(page_match, axis=(0, 1)) > 0
    owner_length = jnp.sum(page_match * lengths[:, None, None], axis=(0, 1))
    slot_pos = page_start[:, None] + jnp.arange(PAGE, dtype=jnp.int32)[None, :]
    slot_live = page_used[:, None] & (slot_pos < owner_length[:, None])
    slot_owner = jnp.where(slot_live, page_owner[:, None], -1)
    return slot_owner.reshape(POOL * PAGE)


def attend(
    queries, keys_new, values_new, keys_cache, values_cache, requests, positions, slot_owner
):
    inv_root = 1.0 / math.sqrt(queries.shape[-1])
    cache_mask = slot_owner[None, :] == requests[:, None]
    new_mask = (requests[None, :] == requests[:, None]) & (positions[None, :] <= positions[:, None])
    score_cache = (
        jnp.einsum("tkgh,knh->kgtn", queries, keys_cache, preferred_element_type=jnp.float32)
        * inv_root
    )
    score_new = (
        jnp.einsum("tkgh,skh->kgts", queries, keys_new, preferred_element_type=jnp.float32)
        * inv_root
    )
    score_cache = jnp.where(cache_mask[None, None], score_cache, -1e30)
    score_new = jnp.where(new_mask[None, None], score_new, -1e30)
    row_max = jnp.maximum(
        jnp.max(score_cache, axis=-1, keepdims=True), jnp.max(score_new, axis=-1, keepdims=True)
    )
    exp_cache = jnp.where(cache_mask[None, None], jnp.exp(score_cache - row_max), 0.0)
    exp_new = jnp.where(new_mask[None, None], jnp.exp(score_new - row_max), 0.0)
    total = jnp.sum(exp_cache, axis=-1, keepdims=True) + jnp.sum(exp_new, axis=-1, keepdims=True)
    prob_cache = (exp_cache / total).astype(jnp.bfloat16)
    prob_new = (exp_new / total).astype(jnp.bfloat16)
    mixed = jnp.einsum(
        "kgtn,knh->tkgh", prob_cache, values_cache, preferred_element_type=jnp.float32
    )
    mixed = mixed + jnp.einsum(
        "kgts,skh->tkgh", prob_new, values_new, preferred_element_type=jnp.float32
    )
    return mixed.astype(jnp.bfloat16).reshape(queries.shape[0], -1)


def expert_apply(blocks, gate_weight, up_weight, down_weight):
    local_experts = gate_weight.shape[0]
    sources = blocks.shape[0] // local_experts
    slot_count = blocks.shape[1]
    grouped = blocks.reshape(sources, local_experts, slot_count, blocks.shape[2])
    gate_acts = jnp.einsum(
        "sekd,edf->sekf", grouped, gate_weight, preferred_element_type=jnp.float32
    )
    up_acts = jnp.einsum("sekd,edf->sekf", grouped, up_weight, preferred_element_type=jnp.float32)
    hidden_act = (jax.nn.silu(gate_acts) * up_acts).astype(jnp.bfloat16)
    part_sums = jnp.einsum(
        "sekf,efd->sekd", hidden_act, down_weight, preferred_element_type=jnp.float32
    ).astype(jnp.bfloat16)
    return part_sums.reshape(sources * local_experts, slot_count, part_sums.shape[3])


def build_buffer(normed, slot_index, top_count, expert_count, capacity):
    picked = jnp.repeat(normed, top_count, axis=0)
    buffer_rows = (
        jnp.zeros((expert_count * capacity, normed.shape[1]), normed.dtype)
        .at[slot_index]
        .set(picked)
    )
    return buffer_rows.reshape(expert_count, capacity, normed.shape[1])


def weigh_back(returned, slot_index, route_weights, token_count, top_count):
    row_width = returned.shape[2]
    back_rows = returned.reshape(returned.shape[0] * returned.shape[1], row_width)[slot_index]
    weighted = (
        back_rows.astype(jnp.float32) * route_weights.reshape(token_count * top_count)[:, None]
    )
    return jnp.sum(weighted.reshape(token_count, top_count, row_width), axis=1)


def experts_dense(rows, routes, gate_weight, up_weight, down_weight):
    gate_acts = jnp.einsum("td,edf->tef", rows, gate_weight, preferred_element_type=jnp.float32)
    up_acts = jnp.einsum("td,edf->tef", rows, up_weight, preferred_element_type=jnp.float32)
    hidden_act = (jax.nn.silu(gate_acts) * up_acts * routes[:, :, None]).astype(jnp.bfloat16)
    return jnp.einsum("tef,efd->td", hidden_act, down_weight, preferred_element_type=jnp.float32)


def moe_dense(
    x_float,
    head_part,
    norm_post_gain,
    expert_ids,
    route_weights,
    gate_weight,
    up_weight,
    down_weight,
):
    req_count = lax.axis_size("req")
    tp_index = lax.axis_index("tp")
    token_count = x_float.shape[0]
    tp_count = lax.axis_size("tp")
    share_width = x_float.shape[1] // tp_count
    expert_local = gate_weight.shape[0]
    expert_count = expert_local * req_count
    share_rows = token_count // tp_count
    named = expert_ids[:, :, None] == jnp.arange(expert_count, dtype=jnp.int32)[None, None, :]
    group_routes = jnp.sum(jnp.where(named, route_weights[:, :, None], 0.0), axis=1)
    routes = lax.all_gather(group_routes, "req", axis=0, tiled=True)
    routes = lax.dynamic_slice_in_dim(
        routes, lax.axis_index("req") * expert_local, expert_local, 1
    )
    head_sum = lax.psum_scatter(
        head_part.astype(jnp.bfloat16), "tp", scatter_dimension=0, tiled=True
    ).astype(jnp.float32)
    residual = lax.dynamic_slice_in_dim(x_float, tp_index * share_rows, share_rows, 0) + head_sum
    normed_post = rms_scale(residual, norm_post_gain).astype(jnp.bfloat16)
    rows = lax.all_gather(normed_post, ("req", "tp"), axis=0, tiled=True)
    part_sums = experts_dense(rows, routes, gate_weight, up_weight, down_weight)
    own_rows = (lax.axis_index("req") * tp_count + tp_index) * share_rows
    own = lax.dynamic_slice_in_dim(part_sums, own_rows, share_rows, 0)
    part_sums = lax.dynamic_update_slice_in_dim(part_sums, own + residual, own_rows, 0)
    blocks = part_sums.astype(jnp.bfloat16).reshape(req_count, token_count, tp_count, share_width)
    blocks = blocks.transpose(0, 2, 1, 3).reshape(
        req_count * tp_count * token_count, share_width
    )
    return lax.psum_scatter(blocks, ("req", "tp"), scatter_dimension=0, tiled=True)


def moe_routed(
    x_float,
    head_part,
    norm_post_gain,
    expert_ids,
    route_weights,
    gate_weight,
    up_weight,
    down_weight,
):
    req_count = lax.axis_size("req")
    tp_index = lax.axis_index("tp")
    token_count = x_float.shape[0]
    share_width = x_float.shape[1] // lax.axis_size("tp")
    top_count = expert_ids.shape[1]
    expert_count = gate_weight.shape[0] * req_count
    capacity = max(2, 3 * token_count * top_count // (2 * expert_count))
    flat_expert = expert_ids.reshape(token_count * top_count)
    one_hot = (flat_expert[:, None] == jnp.arange(expert_count, dtype=jnp.int32)[None, :]).astype(
        jnp.int32
    )
    slot_rank = jnp.sum((jnp.cumsum(one_hot, axis=0) - one_hot) * one_hot, axis=1)
    slot_index = flat_expert * capacity + slot_rank
    head_sum = lax.psum(head_part.astype(jnp.bfloat16), "tp").astype(jnp.float32)
    residual_full = x_float + head_sum
    normed_post = rms_scale(residual_full, norm_post_gain).astype(jnp.bfloat16)
    residual = lax.dynamic_slice_in_dim(residual_full, tp_index * share_width, share_width, 1)
    send_buffer = build_buffer(normed_post, slot_index, top_count, expert_count, capacity)
    part_sums = expert_apply(
        lax.all_to_all(send_buffer, "req", split_axis=0, concat_axis=0, tiled=True),
        gate_weight,
        up_weight,
        down_weight,
    )
    returned = lax.all_to_all(part_sums, "req", split_axis=0, concat_axis=0, tiled=True)
    moe_term = weigh_back(returned, slot_index, route_weights, token_count, top_count)
    moe_share = lax.psum_scatter(
        moe_term.astype(jnp.bfloat16), "tp", scatter_dimension=1, tiled=True
    ).astype(jnp.float32)
    return (residual + moe_share).astype(jnp.bfloat16)


def body(
    hidden_in,
    norm_in_gain,
    q_weight,
    k_weight,
    v_weight,
    q_gain,
    k_gain,
    o_weight,
    key_pages,
    value_pages,
    page_table,
    cache_len,
    norm_post_gain,
    expert_ids,
    route_weights,
    gate_weight,
    up_weight,
    down_weight,
):
    req_count = lax.axis_size("req")
    head_dim = q_gain.shape[0]
    kv_local = key_pages.shape[0]
    group_size = q_weight.shape[1] // head_dim // kv_local
    token_count = hidden_in.shape[0]
    x_full = lax.all_gather(hidden_in, "tp", axis=1, tiled=True)
    x_float = x_full.astype(jnp.float32)
    normed_in = rms_scale(x_float, norm_in_gain).astype(jnp.bfloat16)
    query_lin = jnp.dot(normed_in, q_weight, preferred_element_type=jnp.float32).reshape(
        token_count, kv_local * group_size, head_dim
    )
    key_lin = jnp.dot(normed_in, k_weight, preferred_element_type=jnp.float32).reshape(
        token_count, kv_local, head_dim
    )
    values_new = (
        jnp.dot(normed_in, v_weight, preferred_element_type=jnp.float32)
        .astype(jnp.bfloat16)
        .reshape(token_count, kv_local, head_dim)
    )
    requests, positions = token_layout(cache_len)
    queries = (
        rotate(rms_scale(query_lin, q_gain), positions)
        .astype(jnp.bfloat16)
        .reshape(token_count, kv_local, group_size, head_dim)
    )
    keys_new = rotate(rms_scale(key_lin, k_gain), positions).astype(jnp.bfloat16)
    slot_owner = page_slots(page_table, cache_len)
    cache_slots = key_pages.shape[1] * key_pages.shape[2]
    keys_cache = key_pages.reshape(kv_local, cache_slots, head_dim)
    values_cache = value_pages.reshape(kv_local, cache_slots, head_dim)
    attended = attend(
        queries, keys_new, values_new, keys_cache, values_cache, requests, positions, slot_owner
    )
    head_part = jnp.dot(attended, o_weight, preferred_element_type=jnp.float32)
    expert_count = gate_weight.shape[0] * req_count
    moe_layer = moe_dense if expert_count <= 2 * expert_ids.shape[1] else moe_routed
    return moe_layer(
        x_float,
        head_part,
        norm_post_gain,
        expert_ids,
        route_weights,
        gate_weight,
        up_weight,
        down_weight,
    )


def solution(mesh):
    return jax.shard_map(
        body,
        mesh=mesh,
        in_specs=(
            P("req", "tp"),
            P(),
            P(None, "tp"),
            P(None, "tp"),
            P(None, "tp"),
            P(),
            P(),
            P("tp", None),
            P("tp", "req", None, None),
            P("tp", "req", None, None),
            P("req", None),
            P("req"),
            P(),
            P("req", None),
            P("req", None),
            P("req", None, "tp"),
            P("req", None, "tp"),
            P("req", "tp", None),
        ),
        out_specs=P("req", "tp"),
        check_vma=False,
    )
```

```python
import math

import jax
import jax.numpy as jnp
from jax import lax
from jax.experimental import pallas as pl
from jax.experimental.pallas import tpu as pltpu
from jax.sharding import PartitionSpec as P

PAGE = 128
MAXPG = 32
PRE = 120
TOK_DEV = 128
REQS_DEV = 9
POOL = 48


NORM_EPS = 1e-06
ROPE_BASE = 1000000.0


def rms_scale(values, gain_vec):
    mean_square = jnp.mean(values * values, axis=-1, keepdims=True)
    return values * lax.rsqrt(mean_square + NORM_EPS) * gain_vec


def rotate(values, positions):
    half_dim = values.shape[-1] // 2
    exponent = jnp.arange(half_dim, dtype=jnp.float32) * (2.0 / values.shape[-1])
    frequency = jnp.power(jnp.float32(ROPE_BASE), -exponent)
    angles = positions.astype(jnp.float32)[:, None] * frequency[None, :]
    cosine = jnp.cos(angles)[:, None, :]
    sine_val = jnp.sin(angles)[:, None, :]
    front_half = values[..., :half_dim]
    back_half = values[..., half_dim:]
    return jnp.concatenate(
        [front_half * cosine - back_half * sine_val, back_half * cosine + front_half * sine_val],
        axis=-1,
    )


def token_layout(lengths):
    local_idx = jnp.arange(TOK_DEV, dtype=jnp.int32)
    requests = jnp.where(local_idx < PRE, 0, local_idx - PRE + 1)
    offsets = jnp.where(local_idx < PRE, local_idx, 0)
    request_hot = (requests[:, None] == jnp.arange(REQS_DEV, dtype=jnp.int32)[None, :]).astype(
        jnp.int32
    )
    positions = jnp.sum(request_hot * lengths[None, :], axis=1) + offsets
    return (requests, positions)


def page_slots(table, lengths):
    pages_used = (lengths + PAGE - 1) // PAGE
    entry_live = jnp.arange(MAXPG, dtype=jnp.int32)[None, :] < pages_used[:, None]
    page_match = (
        (table[:, :, None] == jnp.arange(POOL, dtype=jnp.int32)[None, None, :])
        & entry_live[:, :, None]
    ).astype(jnp.int32)
    page_owner = jnp.sum(
        page_match * jnp.arange(REQS_DEV, dtype=jnp.int32)[:, None, None], axis=(0, 1)
    )
    page_start = jnp.sum(
        page_match * (jnp.arange(MAXPG, dtype=jnp.int32) * PAGE)[None, :, None], axis=(0, 1)
    )
    page_used = jnp.sum(page_match, axis=(0, 1)) > 0
    owner_length = jnp.sum(page_match * lengths[:, None, None], axis=(0, 1))
    slot_pos = page_start[:, None] + jnp.arange(PAGE, dtype=jnp.int32)[None, :]
    slot_live = page_used[:, None] & (slot_pos < owner_length[:, None])
    slot_owner = jnp.where(slot_live, page_owner[:, None], -1)
    return slot_owner.reshape(POOL * PAGE)


def attend(
    queries, keys_new, values_new, keys_cache, values_cache, requests, positions, slot_owner
):
    inv_root = 1.0 / math.sqrt(queries.shape[-1])
    cache_mask = slot_owner[None, :] == requests[:, None]
    new_mask = (requests[None, :] == requests[:, None]) & (positions[None, :] <= positions[:, None])
    score_cache = (
        jnp.einsum("tkgh,knh->kgtn", queries, keys_cache, preferred_element_type=jnp.float32)
        * inv_root
    )
    score_new = (
        jnp.einsum("tkgh,skh->kgts", queries, keys_new, preferred_element_type=jnp.float32)
        * inv_root
    )
    score_cache = jnp.where(cache_mask[None, None], score_cache, -1e30)
    score_new = jnp.where(new_mask[None, None], score_new, -1e30)
    row_max = jnp.maximum(
        jnp.max(score_cache, axis=-1, keepdims=True), jnp.max(score_new, axis=-1, keepdims=True)
    )
    exp_cache = jnp.where(cache_mask[None, None], jnp.exp(score_cache - row_max), 0.0)
    exp_new = jnp.where(new_mask[None, None], jnp.exp(score_new - row_max), 0.0)
    total = jnp.sum(exp_cache, axis=-1, keepdims=True) + jnp.sum(exp_new, axis=-1, keepdims=True)
    prob_cache = (exp_cache / total).astype(jnp.bfloat16)
    prob_new = (exp_new / total).astype(jnp.bfloat16)
    mixed = jnp.einsum(
        "kgtn,knh->tkgh", prob_cache, values_cache, preferred_element_type=jnp.float32
    )
    mixed = mixed + jnp.einsum(
        "kgts,skh->tkgh", prob_new, values_new, preferred_element_type=jnp.float32
    )
    return mixed.astype(jnp.bfloat16).reshape(queries.shape[0], -1)


def expert_apply(blocks, gate_weight, up_weight, down_weight):
    local_experts = gate_weight.shape[0]
    sources = blocks.shape[0] // local_experts
    slot_count = blocks.shape[1]
    grouped = blocks.reshape(sources, local_experts, slot_count, blocks.shape[2])
    gate_acts = jnp.einsum(
        "sekd,edf->sekf", grouped, gate_weight, preferred_element_type=jnp.float32
    )
    up_acts = jnp.einsum("sekd,edf->sekf", grouped, up_weight, preferred_element_type=jnp.float32)
    hidden_act = (jax.nn.silu(gate_acts) * up_acts).astype(jnp.bfloat16)
    part_sums = jnp.einsum(
        "sekf,efd->sekd", hidden_act, down_weight, preferred_element_type=jnp.float32
    ).astype(jnp.bfloat16)
    return part_sums.reshape(sources * local_experts, slot_count, part_sums.shape[3])


def build_buffer(normed, slot_index, top_count, expert_count, capacity):
    picked = jnp.repeat(normed, top_count, axis=0)
    buffer_rows = (
        jnp.zeros((expert_count * capacity, normed.shape[1]), normed.dtype)
        .at[slot_index]
        .set(picked)
    )
    return buffer_rows.reshape(expert_count, capacity, normed.shape[1])


def weigh_back(returned, slot_index, route_weights, token_count, top_count):
    row_width = returned.shape[2]
    back_rows = returned.reshape(returned.shape[0] * returned.shape[1], row_width)[slot_index]
    weighted = (
        back_rows.astype(jnp.float32) * route_weights.reshape(token_count * top_count)[:, None]
    )
    return jnp.sum(weighted.reshape(token_count, top_count, row_width), axis=1)


LANES = 128
VMEM = pl.BlockSpec(memory_space=pltpu.VMEM)
SMEM = pl.BlockSpec(memory_space=pltpu.SMEM)
VMEM_LIMIT = 48 * 1024 * 1024


def flip(value, axis, bits):
    return lax.ppermute(value, axis, [(i, i ^ bits) for i in range(lax.axis_size(axis))])


def pack_kernel(
    place_ref, own_ref, near_ref, far_ref, cross_ref, x_ref, gain_ref, ids_ref, routes_ref,
    rows_ref, keep_ref, near_out, far_out, cross_out, residual_ref,
):
    tp_index = place_ref[1]
    share_rows, width = own_ref.shape
    share_width = keep_ref.shape[1]
    mine = pl.ds(pl.multiple_of(tp_index * share_rows, share_rows), share_rows)
    head_sum = (own_ref[...] + near_ref[...].astype(jnp.float32)) + (
        far_ref[...].astype(jnp.float32) + cross_ref[...].astype(jnp.float32)
    )
    residual = x_ref[mine, :].astype(jnp.float32) + head_sum
    residual_ref[...] = residual
    rows_ref[:, :width] = rms_scale(residual, gain_ref[...]).astype(jnp.bfloat16)
    ids = ids_ref[mine, :]
    weights = routes_ref[mine, :]
    lane = lax.broadcasted_iota(jnp.int32, (share_rows, LANES), 1)
    spread = jnp.zeros((share_rows, LANES), jnp.float32)
    for k in range(ids.shape[1]):
        spread = spread + jnp.where(lane % (LANES // 2) == ids[:, k : k + 1], weights[:, k : k + 1], 0.0)
    high = spread.astype(jnp.bfloat16).astype(jnp.float32)
    rows_ref[:, width:] = jnp.where(lane < LANES // 2, high, spread - high).astype(jnp.bfloat16)
    for step, out_ref in enumerate((keep_ref, near_out, far_out, cross_out)):
        column = pl.multiple_of((tp_index ^ step) * share_width, share_width)
        out_ref[...] = residual_ref[:, pl.ds(column, share_width)]


def experts_kernel(place_ref, rows_ref, gate_up_ref, down_ref, send_ref, keep_ref):
    req_index, tp_index = place_ref[0], place_ref[1]
    width, doubled = gate_up_ref.shape
    units = doubled // 2
    half_rows, share_width = keep_ref.shape[3], keep_ref.shape[4]
    acts = jnp.dot(rows_ref[:, :width], gate_up_ref[...], preferred_element_type=jnp.float32)
    gate_acts, up_acts = acts[:, :units], acts[:, units:]
    spread = rows_ref[:, width:].astype(jnp.float32)
    lane = lax.broadcasted_iota(jnp.int32, spread.shape, 1) % (LANES // 2)
    weights = [
        jnp.sum(jnp.where(lane == 2 * req_index + e, spread, 0.0), axis=1, keepdims=True)
        for e in range(2)
    ]
    unit = lax.broadcasted_iota(jnp.int32, gate_acts.shape, 1)
    weight = jnp.where(unit < units // 2, weights[0], weights[1])
    hidden_act = (gate_acts / (1.0 + jnp.exp(-gate_acts)) * up_acts * weight).astype(jnp.bfloat16)
    for step in range(4):
        column = pl.multiple_of((tp_index ^ step) * share_width, share_width)
        part = jnp.dot(
            hidden_act, down_ref[:, pl.ds(column, share_width)], preferred_element_type=jnp.float32
        )
        target = send_ref if step % 2 else keep_ref
        for x in range(2):
            target[step // 2, (req_index % 2) ^ x, 0] = part[
                x * half_rows : (x + 1) * half_rows
            ].astype(target.dtype)


def finish_kernel(place_ref, total_ref, keep_ref, near_ref, far_ref, cross_ref, out_ref):
    tp_index = place_ref[1]
    share_rows = keep_ref.shape[0]
    for step, part_ref in enumerate((keep_ref, near_ref, far_ref, cross_ref)):
        rows = pl.ds(pl.multiple_of((tp_index ^ step) * share_rows, share_rows), share_rows)
        out_ref[rows, :] = (total_ref[rows, :] + part_ref[...]).astype(jnp.bfloat16)


def moe_dense(
    x_full,
    head_part,
    norm_post_gain,
    expert_ids,
    route_weights,
    gate_weight,
    up_weight,
    down_weight,
):
    req_index, tp_index = lax.axis_index("req"), lax.axis_index("tp")
    token_count, width = x_full.shape
    share_rows, share_width = token_count // 4, width // 4
    units = 2 * gate_weight.shape[2]
    place = jnp.stack([req_index, tp_index]).astype(jnp.int32)

    def head_rows(bits):
        return lax.dynamic_slice_in_dim(head_part, (tp_index ^ bits) * share_rows, share_rows, 0)

    received = [flip(head_rows(bits).astype(jnp.bfloat16), "tp", bits) for bits in (1, 2, 3)]
    share_f32 = jax.ShapeDtypeStruct((share_rows, share_width), jnp.float32)
    rows, *residuals = pl.pallas_call(
        pack_kernel,
        out_shape=[jax.ShapeDtypeStruct((share_rows, width + LANES), jnp.bfloat16)] + [share_f32] * 4,
        in_specs=[SMEM] + [VMEM] * 8,
        out_specs=[VMEM] * 5,
        scratch_shapes=[pltpu.VMEM((share_rows, width), jnp.float32)],
        name="pack_rows",
    )(place, head_rows(0), *received, x_full, norm_post_gain[None, :], expert_ids, route_weights)
    residuals = residuals[:1] + [flip(residuals[bits], "tp", bits) for bits in (1, 2, 3)]
    all_rows = lax.all_gather(rows, ("req", "tp"), axis=0, tiled=True)
    gate_up = jnp.concatenate([gate_weight[0], gate_weight[1], up_weight[0], up_weight[1]], axis=1)
    block = (2, 2, 1, token_count, share_width)
    parts = (2, 2, 4, token_count, share_width)
    out_spec = pl.BlockSpec(block, lambda z: (0, 0, z, 0, 0))
    send, keep = pl.pallas_call(
        experts_kernel,
        grid=(4,),
        out_shape=[
            jax.ShapeDtypeStruct(parts, jnp.bfloat16),
            jax.ShapeDtypeStruct(parts, jnp.float32),
        ],
        in_specs=[
            SMEM,
            pl.BlockSpec((2 * token_count, width + LANES), lambda z: (z, 0)),
            pl.BlockSpec((width, 2 * units), lambda z: (0, 0)),
            pl.BlockSpec((units, width), lambda z: (0, 0)),
        ],
        out_specs=[out_spec, out_spec],
        compiler_params=pltpu.CompilerParams(vmem_limit_bytes=VMEM_LIMIT),
        name="experts",
    )(place, all_rows, gate_up, down_weight.reshape(units, width))
    half = token_count // 2
    got = flip(send, "tp", 1)
    low = keep[..., :half, :] + got[..., :half, :].astype(jnp.float32)
    high = keep[..., half:, :] + got[..., half:, :].astype(jnp.float32)
    got_low = flip(low[1].astype(jnp.bfloat16), "tp", 2)
    got_high = flip(high[:, 1].astype(jnp.bfloat16), "req", 1)
    low = low[0] + got_low.astype(jnp.float32)
    high = high[:, 0] + got_high.astype(jnp.float32)
    got_low = flip(low[1].astype(jnp.bfloat16), "req", 1)
    got_high = flip(high[1].astype(jnp.bfloat16), "tp", 2)
    low = low[0] + got_low.astype(jnp.float32)
    high = high[0] + got_high.astype(jnp.float32)
    both = jnp.concatenate([low, high], axis=1)

    def level(bits):
        return lax.dynamic_index_in_dim(both, (req_index // 2) ^ bits, 0, keepdims=False)

    total = level(0)
    for bits in (1, 2, 3):
        total = total + flip(level(bits).astype(jnp.bfloat16), "req", 2 * bits).astype(jnp.float32)
    return pl.pallas_call(
        finish_kernel,
        out_shape=jax.ShapeDtypeStruct((token_count, share_width), jnp.bfloat16),
        in_specs=[SMEM] + [VMEM] * 5,
        out_specs=VMEM,
        name="finish",
    )(place, total, *residuals)


def moe_routed(
    x_full,
    head_part,
    norm_post_gain,
    expert_ids,
    route_weights,
    gate_weight,
    up_weight,
    down_weight,
):
    req_count = lax.axis_size("req")
    tp_index = lax.axis_index("tp")
    x_float = x_full.astype(jnp.float32)
    token_count = x_float.shape[0]
    share_width = x_float.shape[1] // lax.axis_size("tp")
    top_count = expert_ids.shape[1]
    expert_count = gate_weight.shape[0] * req_count
    capacity = max(2, 3 * token_count * top_count // (2 * expert_count))
    flat_expert = expert_ids.reshape(token_count * top_count)
    one_hot = (flat_expert[:, None] == jnp.arange(expert_count, dtype=jnp.int32)[None, :]).astype(
        jnp.int32
    )
    slot_rank = jnp.sum((jnp.cumsum(one_hot, axis=0) - one_hot) * one_hot, axis=1)
    slot_index = flat_expert * capacity + slot_rank
    head_sum = lax.psum(head_part.astype(jnp.bfloat16), "tp").astype(jnp.float32)
    residual_full = x_float + head_sum
    normed_post = rms_scale(residual_full, norm_post_gain).astype(jnp.bfloat16)
    residual = lax.dynamic_slice_in_dim(residual_full, tp_index * share_width, share_width, 1)
    send_buffer = build_buffer(normed_post, slot_index, top_count, expert_count, capacity)
    part_sums = expert_apply(
        lax.all_to_all(send_buffer, "req", split_axis=0, concat_axis=0, tiled=True),
        gate_weight,
        up_weight,
        down_weight,
    )
    returned = lax.all_to_all(part_sums, "req", split_axis=0, concat_axis=0, tiled=True)
    moe_term = weigh_back(returned, slot_index, route_weights, token_count, top_count)
    moe_share = lax.psum_scatter(
        moe_term.astype(jnp.bfloat16), "tp", scatter_dimension=1, tiled=True
    ).astype(jnp.float32)
    return (residual + moe_share).astype(jnp.bfloat16)


def body(
    hidden_in,
    norm_in_gain,
    q_weight,
    k_weight,
    v_weight,
    q_gain,
    k_gain,
    o_weight,
    key_pages,
    value_pages,
    page_table,
    cache_len,
    norm_post_gain,
    expert_ids,
    route_weights,
    gate_weight,
    up_weight,
    down_weight,
):
    req_count = lax.axis_size("req")
    head_dim = q_gain.shape[0]
    kv_local = key_pages.shape[0]
    group_size = q_weight.shape[1] // head_dim // kv_local
    token_count = hidden_in.shape[0]
    x_full = lax.all_gather(hidden_in, "tp", axis=1, tiled=True)
    x_float = x_full.astype(jnp.float32)
    normed_in = rms_scale(x_float, norm_in_gain).astype(jnp.bfloat16)
    query_lin = jnp.dot(normed_in, q_weight, preferred_element_type=jnp.float32).reshape(
        token_count, kv_local * group_size, head_dim
    )
    key_lin = jnp.dot(normed_in, k_weight, preferred_element_type=jnp.float32).reshape(
        token_count, kv_local, head_dim
    )
    values_new = (
        jnp.dot(normed_in, v_weight, preferred_element_type=jnp.float32)
        .astype(jnp.bfloat16)
        .reshape(token_count, kv_local, head_dim)
    )
    requests, positions = token_layout(cache_len)
    queries = (
        rotate(rms_scale(query_lin, q_gain), positions)
        .astype(jnp.bfloat16)
        .reshape(token_count, kv_local, group_size, head_dim)
    )
    keys_new = rotate(rms_scale(key_lin, k_gain), positions).astype(jnp.bfloat16)
    slot_owner = page_slots(page_table, cache_len)
    cache_slots = key_pages.shape[1] * key_pages.shape[2]
    keys_cache = key_pages.reshape(kv_local, cache_slots, head_dim)
    values_cache = value_pages.reshape(kv_local, cache_slots, head_dim)
    attended = attend(
        queries, keys_new, values_new, keys_cache, values_cache, requests, positions, slot_owner
    )
    head_part = jnp.dot(attended, o_weight, preferred_element_type=jnp.float32)
    expert_count = gate_weight.shape[0] * req_count
    staged = (req_count, lax.axis_size("tp"), gate_weight.shape[0]) == (8, 4, 2)
    moe_layer = moe_dense if staged and expert_count <= LANES // 2 else moe_routed
    return moe_layer(
        x_full,
        head_part,
        norm_post_gain,
        expert_ids,
        route_weights,
        gate_weight,
        up_weight,
        down_weight,
    )


def solution(mesh):
    return jax.shard_map(
        body,
        mesh=mesh,
        in_specs=(
            P("req", "tp"),
            P(),
            P(None, "tp"),
            P(None, "tp"),
            P(None, "tp"),
            P(),
            P(),
            P("tp", None),
            P("tp", "req", None, None),
            P("tp", "req", None, None),
            P("req", None),
            P("req"),
            P(),
            P("req", None),
            P("req", None),
            P("req", None, "tp"),
            P("req", None, "tp"),
            P("req", "tp", None),
        ),
        out_specs=P("req", "tp"),
        check_vma=False,
    )
```

```python
import functools
import math

import jax
import jax.numpy as jnp
from jax import lax
from jax.experimental import pallas as pl
from jax.experimental.pallas import tpu as pltpu
from jax.sharding import PartitionSpec as P

PAGE = 128
MAXPG = 32
PRE = 120
TOK_DEV = 128
REQS_DEV = 9
POOL = 48


NORM_EPS = 1e-06
ROPE_BASE = 1000000.0


def rms_scale(values, gain_vec):
    mean_square = jnp.mean(values * values, axis=-1, keepdims=True)
    return values * lax.rsqrt(mean_square + NORM_EPS) * gain_vec


def rotate(values, positions):
    half_dim = values.shape[-1] // 2
    exponent = jnp.arange(half_dim, dtype=jnp.float32) * (2.0 / values.shape[-1])
    frequency = jnp.power(jnp.float32(ROPE_BASE), -exponent)
    angles = positions.astype(jnp.float32)[:, None] * frequency[None, :]
    cosine = jnp.cos(angles)[:, None, :]
    sine_val = jnp.sin(angles)[:, None, :]
    front_half = values[..., :half_dim]
    back_half = values[..., half_dim:]
    return jnp.concatenate(
        [front_half * cosine - back_half * sine_val, back_half * cosine + front_half * sine_val],
        axis=-1,
    )


def token_layout(lengths):
    local_idx = jnp.arange(TOK_DEV, dtype=jnp.int32)
    requests = jnp.where(local_idx < PRE, 0, local_idx - PRE + 1)
    offsets = jnp.where(local_idx < PRE, local_idx, 0)
    request_hot = (requests[:, None] == jnp.arange(REQS_DEV, dtype=jnp.int32)[None, :]).astype(
        jnp.int32
    )
    positions = jnp.sum(request_hot * lengths[None, :], axis=1) + offsets
    return (requests, positions)


def page_slots(table, lengths):
    pages_used = (lengths + PAGE - 1) // PAGE
    entry_live = jnp.arange(MAXPG, dtype=jnp.int32)[None, :] < pages_used[:, None]
    page_match = (
        (table[:, :, None] == jnp.arange(POOL, dtype=jnp.int32)[None, None, :])
        & entry_live[:, :, None]
    ).astype(jnp.int32)
    page_owner = jnp.sum(
        page_match * jnp.arange(REQS_DEV, dtype=jnp.int32)[:, None, None], axis=(0, 1)
    )
    page_start = jnp.sum(
        page_match * (jnp.arange(MAXPG, dtype=jnp.int32) * PAGE)[None, :, None], axis=(0, 1)
    )
    page_used = jnp.sum(page_match, axis=(0, 1)) > 0
    owner_length = jnp.sum(page_match * lengths[:, None, None], axis=(0, 1))
    slot_pos = page_start[:, None] + jnp.arange(PAGE, dtype=jnp.int32)[None, :]
    slot_live = page_used[:, None] & (slot_pos < owner_length[:, None])
    slot_owner = jnp.where(slot_live, page_owner[:, None], -1)
    return slot_owner.reshape(POOL * PAGE)


def attend(
    queries, keys_new, values_new, keys_cache, values_cache, requests, positions, slot_owner
):
    inv_root = 1.0 / math.sqrt(queries.shape[-1])
    cache_mask = slot_owner[None, :] == requests[:, None]
    new_mask = (requests[None, :] == requests[:, None]) & (positions[None, :] <= positions[:, None])
    score_cache = (
        jnp.einsum("tkgh,knh->kgtn", queries, keys_cache, preferred_element_type=jnp.float32)
        * inv_root
    )
    score_new = (
        jnp.einsum("tkgh,skh->kgts", queries, keys_new, preferred_element_type=jnp.float32)
        * inv_root
    )
    score_cache = jnp.where(cache_mask[None, None], score_cache, -1e30)
    score_new = jnp.where(new_mask[None, None], score_new, -1e30)
    row_max = jnp.maximum(
        jnp.max(score_cache, axis=-1, keepdims=True), jnp.max(score_new, axis=-1, keepdims=True)
    )
    exp_cache = jnp.where(cache_mask[None, None], jnp.exp(score_cache - row_max), 0.0)
    exp_new = jnp.where(new_mask[None, None], jnp.exp(score_new - row_max), 0.0)
    total = jnp.sum(exp_cache, axis=-1, keepdims=True) + jnp.sum(exp_new, axis=-1, keepdims=True)
    prob_cache = (exp_cache / total).astype(jnp.bfloat16)
    prob_new = (exp_new / total).astype(jnp.bfloat16)
    mixed = jnp.einsum(
        "kgtn,knh->tkgh", prob_cache, values_cache, preferred_element_type=jnp.float32
    )
    mixed = mixed + jnp.einsum(
        "kgts,skh->tkgh", prob_new, values_new, preferred_element_type=jnp.float32
    )
    return mixed.astype(jnp.bfloat16).reshape(queries.shape[0], -1)


def expert_apply(blocks, gate_weight, up_weight, down_weight):
    local_experts = gate_weight.shape[0]
    sources = blocks.shape[0] // local_experts
    slot_count = blocks.shape[1]
    grouped = blocks.reshape(sources, local_experts, slot_count, blocks.shape[2])
    gate_acts = jnp.einsum(
        "sekd,edf->sekf", grouped, gate_weight, preferred_element_type=jnp.float32
    )
    up_acts = jnp.einsum("sekd,edf->sekf", grouped, up_weight, preferred_element_type=jnp.float32)
    hidden_act = (jax.nn.silu(gate_acts) * up_acts).astype(jnp.bfloat16)
    part_sums = jnp.einsum(
        "sekf,efd->sekd", hidden_act, down_weight, preferred_element_type=jnp.float32
    ).astype(jnp.bfloat16)
    return part_sums.reshape(sources * local_experts, slot_count, part_sums.shape[3])


def build_buffer(normed, slot_index, top_count, expert_count, capacity):
    picked = jnp.repeat(normed, top_count, axis=0)
    buffer_rows = (
        jnp.zeros((expert_count * capacity, normed.shape[1]), normed.dtype)
        .at[slot_index]
        .set(picked)
    )
    return buffer_rows.reshape(expert_count, capacity, normed.shape[1])


def weigh_back(returned, slot_index, route_weights, token_count, top_count):
    row_width = returned.shape[2]
    back_rows = returned.reshape(returned.shape[0] * returned.shape[1], row_width)[slot_index]
    weighted = (
        back_rows.astype(jnp.float32) * route_weights.reshape(token_count * top_count)[:, None]
    )
    return jnp.sum(weighted.reshape(token_count, top_count, row_width), axis=1)


LANES = 128
VMEM = pl.BlockSpec(memory_space=pltpu.VMEM)
SMEM = pl.BlockSpec(memory_space=pltpu.SMEM)
VMEM_LIMIT = 48 * 1024 * 1024


def flip(value, axis, bits):
    return lax.ppermute(value, axis, [(i, i ^ bits) for i in range(lax.axis_size(axis))])


def pack_kernel(
    place_ref, own_ref, near_ref, far_ref, cross_ref, x_ref, gain_ref, ids_ref, routes_ref,
    rows_ref, keep_ref, near_out, far_out, cross_out, residual_ref, spread_ref,
):
    tp_index = place_ref[1]
    share_rows, width = own_ref.shape
    share_width = keep_ref.shape[1]
    mine = pl.ds(pl.multiple_of(tp_index * share_rows, share_rows), share_rows)
    head_sum = (own_ref[...] + near_ref[...].astype(jnp.float32)) + (
        far_ref[...].astype(jnp.float32) + cross_ref[...].astype(jnp.float32)
    )
    residual = x_ref[mine, :].astype(jnp.float32) + head_sum
    residual_ref[...] = residual
    rows_ref[:, :width] = rms_scale(residual, gain_ref[...]).astype(jnp.bfloat16)
    expert = lax.broadcasted_iota(jnp.int32, (LANES, spread_ref.shape[0]), 0) % (LANES // 2)
    spread = jnp.zeros(expert.shape, jnp.float32)
    for k in range(ids_ref.shape[0]):
        spread = spread + jnp.where(expert == ids_ref[k : k + 1, :], routes_ref[k : k + 1, :], 0.0)
    spread_ref[...] = spread.T
    spread = spread_ref[mine, :]
    lane = lax.broadcasted_iota(jnp.int32, spread.shape, 1)
    high = spread.astype(jnp.bfloat16).astype(jnp.float32)
    rows_ref[:, width:] = jnp.where(lane < LANES // 2, high, spread - high).astype(jnp.bfloat16)
    for step, out_ref in enumerate((keep_ref, near_out, far_out, cross_out)):
        column = pl.multiple_of((tp_index ^ step) * share_width, share_width)
        out_ref[...] = residual_ref[:, pl.ds(column, share_width)]


def experts_kernel(far_parts, place_ref, *refs):
    near_ref, core_ref = refs[:2]
    far_refs, far_core_refs = refs[2 : 2 + far_parts], refs[2 + far_parts : 2 + 2 * far_parts]
    gate_ref, up_ref, down_ref = refs[2 + 2 * far_parts : 5 + 2 * far_parts]
    out_refs, rows_ref = refs[5 + 2 * far_parts : -1], refs[-1]
    req_index, tp_index = place_ref[0], place_ref[1]
    levels, share_rows, _ = near_ref.shape
    units = gate_ref.shape[2]
    width = gate_ref.shape[1]
    share_width = width // 4

    def pick(parts):
        if len(parts) == 1:
            return parts[0][...]
        return jnp.where(pl.program_id(0) == 0, parts[0][...], parts[1][...])

    for step, value in enumerate((near_ref[...], core_ref[...], pick(far_refs), pick(far_core_refs))):
        for level in range(levels):
            start = (4 * level + (tp_index ^ step)) * share_rows
            rows_ref[pl.ds(pl.multiple_of(start, share_rows), share_rows), :] = value[level]
    spread = rows_ref[:, width:].astype(jnp.float32)
    lane = lax.broadcasted_iota(jnp.int32, spread.shape, 1) % (LANES // 2)
    acts = []
    for e in range(2):
        weight = jnp.sum(jnp.where(lane == 2 * req_index + e, spread, 0.0), axis=1, keepdims=True)
        gate = jnp.dot(rows_ref[:, :width], gate_ref[e], preferred_element_type=jnp.float32)
        up = jnp.dot(rows_ref[:, :width], up_ref[e], preferred_element_type=jnp.float32)
        acts.append((gate / (1.0 + jnp.exp(-gate)) * up * weight).astype(jnp.bfloat16))
    for step in range(4):
        column = pl.multiple_of((tp_index ^ step) * share_width, share_width)
        part = jnp.dot(
            acts[0], down_ref[0, :, pl.ds(column, share_width)], preferred_element_type=jnp.float32
        ) + jnp.dot(
            acts[1], down_ref[1, :, pl.ds(column, share_width)], preferred_element_type=jnp.float32
        )
        target = out_refs[step]
        target[...] = part.reshape(target.shape).astype(target.dtype)


def run_experts(place, near, core, far, far_core, gate_weight, up_weight, down_weight):
    levels, share_rows, packed = near.shape
    share_width = down_weight.shape[2] // 4
    block = pl.BlockSpec((2, share_rows, packed), lambda z: (z, 0, 0))
    fixed = pl.BlockSpec((2, share_rows, packed), lambda z: (0, 0, 0))
    far_spec = block if len(far) == 1 else fixed
    weight_specs = [
        pl.BlockSpec(w.shape, lambda z: (0, 0, 0), pipeline_mode=pl.Buffered(1))
        for w in (gate_weight, up_weight, down_weight)
    ]
    out_shape = (levels, 4 * share_rows, share_width)
    return pl.pallas_call(
        functools.partial(experts_kernel, len(far)),
        grid=(levels // 2,),
        out_shape=[
            jax.ShapeDtypeStruct(out_shape, jnp.bfloat16 if step % 2 else jnp.float32)
            for step in range(4)
        ],
        in_specs=[SMEM, block, block] + [far_spec] * (2 * len(far)) + weight_specs,
        out_specs=[pl.BlockSpec((2,) + out_shape[1:], lambda z: (z, 0, 0))] * 4,
        scratch_shapes=[pltpu.VMEM((8 * share_rows, packed), jnp.bfloat16)],
        compiler_params=pltpu.CompilerParams(vmem_limit_bytes=VMEM_LIMIT),
        name="experts",
    )(place, near, core, *far, *far_core, gate_weight, up_weight, down_weight)


def finish_kernel(
    place_ref, own_ref, x_ref, y_ref, z1_ref, z2_ref, z3_ref, keep_ref, near_ref, far_ref, cross_ref, out_ref
):
    tp_index = place_ref[1]
    share_rows = keep_ref.shape[0]
    for step, part_ref in enumerate((keep_ref, near_ref, far_ref, cross_ref)):
        rows = pl.ds(pl.multiple_of((tp_index ^ step) * share_rows, share_rows), share_rows)
        total = own_ref[0, rows, :] + part_ref[...]
        for extra_ref in (x_ref, y_ref):
            total = total + extra_ref[0, rows, :].astype(jnp.float32)
        for extra_ref in (z1_ref, z2_ref, z3_ref):
            total = total + extra_ref[rows, :].astype(jnp.float32)
        out_ref[rows, :] = total.astype(jnp.bfloat16)


def moe_dense(
    x_full,
    head_part,
    norm_post_gain,
    expert_ids,
    route_weights,
    gate_weight,
    up_weight,
    down_weight,
):
    req_index, tp_index = lax.axis_index("req"), lax.axis_index("tp")
    token_count, width = x_full.shape
    share_rows, share_width = token_count // 4, width // 4
    place = jnp.stack([req_index, tp_index]).astype(jnp.int32)

    def head_rows(bits):
        return lax.dynamic_slice_in_dim(head_part, (tp_index ^ bits) * share_rows, share_rows, 0)

    received = [flip(head_rows(bits).astype(jnp.bfloat16), "tp", bits) for bits in (1, 2, 3)]
    share_f32 = jax.ShapeDtypeStruct((share_rows, share_width), jnp.float32)
    rows, *residuals = pl.pallas_call(
        pack_kernel,
        out_shape=[jax.ShapeDtypeStruct((share_rows, width + LANES), jnp.bfloat16)] + [share_f32] * 4,
        in_specs=[SMEM] + [VMEM] * 8,
        out_specs=[VMEM] * 5,
        scratch_shapes=[
            pltpu.VMEM((share_rows, width), jnp.float32),
            pltpu.VMEM((token_count, LANES), jnp.float32),
        ],
        name="pack_rows",
    )(place, head_rows(0), *received, x_full, norm_post_gain[None, :], expert_ids.T, route_weights.T)
    residuals = residuals[:1] + [flip(residuals[bits], "tp", bits) for bits in (1, 2, 3)]
    line = jnp.stack([rows] + [flip(rows, "req", 2 * bits) for bits in (1, 2, 3)])
    line_x, line_y = flip(line, "req", 1), flip(line, "tp", 2)
    across = (flip(line_x[:2], "tp", 2), flip(line_y[2:], "req", 1))
    line_core, line_x_core, line_y_core = (flip(part, "tp", 1) for part in (line, line_x, line_y))
    across_core = tuple(flip(part, "tp", 1) for part in across)
    weights = (gate_weight, up_weight, down_weight)
    near = run_experts(place, line, line_core, (line_y,), (line_y_core,), *weights)
    side = run_experts(place, line_x, line_x_core, across, across_core, *weights)
    keep_00, keep_01, keep_10, keep_11 = (
        (part[2 * y], flip(part[2 * y + 1], "tp", 1)) for part in (near, side) for y in range(2)
    )

    def both(pair, levels):
        return pair[0][levels] + pair[1][levels].astype(jnp.float32)

    low, high = slice(0, 2), slice(2, 4)
    by_x = flip(both(keep_11, low).astype(jnp.bfloat16), "req", 1).astype(jnp.float32)
    by_y = flip(both(keep_11, high).astype(jnp.bfloat16), "tp", 2).astype(jnp.float32)
    from_y = [
        flip((both(keep_01, low) + by_x).astype(jnp.bfloat16), "tp", 2),
        flip(both(keep_01, high).astype(jnp.bfloat16), "tp", 2),
    ]
    from_x = [
        flip(both(keep_10, low).astype(jnp.bfloat16), "req", 1),
        flip((both(keep_10, high) + by_y).astype(jnp.bfloat16), "req", 1),
    ]

    def level(z):
        part = from_x[z // 2][z % 2].astype(jnp.float32) + from_y[z // 2][z % 2].astype(jnp.float32)
        return (both(keep_00, z) + part).astype(jnp.bfloat16)

    from_z = [flip(level(z), "req", 2 * z) for z in (1, 2, 3)]
    return pl.pallas_call(
        finish_kernel,
        out_shape=jax.ShapeDtypeStruct((token_count, share_width), jnp.bfloat16),
        in_specs=[SMEM] + [VMEM] * 10,
        out_specs=VMEM,
        name="finish",
    )(place, both(keep_00, low), from_x[0], from_y[0], *from_z, *residuals)


def moe_routed(
    x_full,
    head_part,
    norm_post_gain,
    expert_ids,
    route_weights,
    gate_weight,
    up_weight,
    down_weight,
):
    req_count = lax.axis_size("req")
    tp_index = lax.axis_index("tp")
    x_float = x_full.astype(jnp.float32)
    token_count = x_float.shape[0]
    share_width = x_float.shape[1] // lax.axis_size("tp")
    top_count = expert_ids.shape[1]
    expert_count = gate_weight.shape[0] * req_count
    capacity = max(2, 3 * token_count * top_count // (2 * expert_count))
    flat_expert = expert_ids.reshape(token_count * top_count)
    one_hot = (flat_expert[:, None] == jnp.arange(expert_count, dtype=jnp.int32)[None, :]).astype(
        jnp.int32
    )
    slot_rank = jnp.sum((jnp.cumsum(one_hot, axis=0) - one_hot) * one_hot, axis=1)
    slot_index = flat_expert * capacity + slot_rank
    head_sum = lax.psum(head_part.astype(jnp.bfloat16), "tp").astype(jnp.float32)
    residual_full = x_float + head_sum
    normed_post = rms_scale(residual_full, norm_post_gain).astype(jnp.bfloat16)
    residual = lax.dynamic_slice_in_dim(residual_full, tp_index * share_width, share_width, 1)
    send_buffer = build_buffer(normed_post, slot_index, top_count, expert_count, capacity)
    part_sums = expert_apply(
        lax.all_to_all(send_buffer, "req", split_axis=0, concat_axis=0, tiled=True),
        gate_weight,
        up_weight,
        down_weight,
    )
    returned = lax.all_to_all(part_sums, "req", split_axis=0, concat_axis=0, tiled=True)
    moe_term = weigh_back(returned, slot_index, route_weights, token_count, top_count)
    moe_share = lax.psum_scatter(
        moe_term.astype(jnp.bfloat16), "tp", scatter_dimension=1, tiled=True
    ).astype(jnp.float32)
    return (residual + moe_share).astype(jnp.bfloat16)


def body(
    hidden_in,
    norm_in_gain,
    q_weight,
    k_weight,
    v_weight,
    q_gain,
    k_gain,
    o_weight,
    key_pages,
    value_pages,
    page_table,
    cache_len,
    norm_post_gain,
    expert_ids,
    route_weights,
    gate_weight,
    up_weight,
    down_weight,
):
    req_count = lax.axis_size("req")
    head_dim = q_gain.shape[0]
    kv_local = key_pages.shape[0]
    group_size = q_weight.shape[1] // head_dim // kv_local
    token_count = hidden_in.shape[0]
    x_full = lax.all_gather(hidden_in, "tp", axis=1, tiled=True)
    x_float = x_full.astype(jnp.float32)
    normed_in = rms_scale(x_float, norm_in_gain).astype(jnp.bfloat16)
    query_lin = jnp.dot(normed_in, q_weight, preferred_element_type=jnp.float32).reshape(
        token_count, kv_local * group_size, head_dim
    )
    key_lin = jnp.dot(normed_in, k_weight, preferred_element_type=jnp.float32).reshape(
        token_count, kv_local, head_dim
    )
    values_new = (
        jnp.dot(normed_in, v_weight, preferred_element_type=jnp.float32)
        .astype(jnp.bfloat16)
        .reshape(token_count, kv_local, head_dim)
    )
    requests, positions = token_layout(cache_len)
    queries = (
        rotate(rms_scale(query_lin, q_gain), positions)
        .astype(jnp.bfloat16)
        .reshape(token_count, kv_local, group_size, head_dim)
    )
    keys_new = rotate(rms_scale(key_lin, k_gain), positions).astype(jnp.bfloat16)
    slot_owner = page_slots(page_table, cache_len)
    cache_slots = key_pages.shape[1] * key_pages.shape[2]
    keys_cache = key_pages.reshape(kv_local, cache_slots, head_dim)
    values_cache = value_pages.reshape(kv_local, cache_slots, head_dim)
    attended = attend(
        queries, keys_new, values_new, keys_cache, values_cache, requests, positions, slot_owner
    )
    head_part = jnp.dot(attended, o_weight, preferred_element_type=jnp.float32)
    expert_count = gate_weight.shape[0] * req_count
    staged = (req_count, lax.axis_size("tp"), gate_weight.shape[0]) == (8, 4, 2)
    moe_layer = moe_dense if staged and expert_count <= LANES // 2 else moe_routed
    return moe_layer(
        x_full,
        head_part,
        norm_post_gain,
        expert_ids,
        route_weights,
        gate_weight,
        up_weight,
        down_weight,
    )


def solution(mesh):
    return jax.shard_map(
        body,
        mesh=mesh,
        in_specs=(
            P("req", "tp"),
            P(),
            P(None, "tp"),
            P(None, "tp"),
            P(None, "tp"),
            P(),
            P(),
            P("tp", None),
            P("tp", "req", None, None),
            P("tp", "req", None, None),
            P("req", None),
            P("req"),
            P(),
            P("req", None),
            P("req", None),
            P("req", None, "tp"),
            P("req", None, "tp"),
            P("req", "tp", None),
        ),
        out_specs=P("req", "tp"),
        check_vma=False,
    )
```

```python
import functools
import math

import jax
import jax.numpy as jnp
import numpy as np
from jax import lax
from jax.experimental import pallas as pl
from jax.experimental.pallas import tpu as pltpu
from jax.sharding import PartitionSpec as P

PAGE = 128
MAXPG = 32
PRE = 120
TOK_DEV = 128
REQS_DEV = 9
POOL = 48


NORM_EPS = 1e-06
ROPE_BASE = 1000000.0


def rms_scale(values, gain_vec):
    mean_square = jnp.mean(values * values, axis=-1, keepdims=True)
    return values * lax.rsqrt(mean_square + NORM_EPS) * gain_vec


def rotate(values, positions):
    half_dim = values.shape[-1] // 2
    exponent = jnp.arange(half_dim, dtype=jnp.float32) * (2.0 / values.shape[-1])
    frequency = jnp.power(jnp.float32(ROPE_BASE), -exponent)
    angles = positions.astype(jnp.float32)[:, None] * frequency[None, :]
    cosine = jnp.cos(angles)[:, None, :]
    sine_val = jnp.sin(angles)[:, None, :]
    front_half = values[..., :half_dim]
    back_half = values[..., half_dim:]
    return jnp.concatenate(
        [front_half * cosine - back_half * sine_val, back_half * cosine + front_half * sine_val],
        axis=-1,
    )


def token_layout(lengths):
    local_idx = jnp.arange(TOK_DEV, dtype=jnp.int32)
    requests = jnp.where(local_idx < PRE, 0, local_idx - PRE + 1)
    offsets = jnp.where(local_idx < PRE, local_idx, 0)
    request_hot = (requests[:, None] == jnp.arange(REQS_DEV, dtype=jnp.int32)[None, :]).astype(
        jnp.int32
    )
    positions = jnp.sum(request_hot * lengths[None, :], axis=1) + offsets
    return (requests, positions)


def page_slots(table, lengths):
    pages_used = (lengths + PAGE - 1) // PAGE
    entry_live = jnp.arange(MAXPG, dtype=jnp.int32)[None, :] < pages_used[:, None]
    page_match = (
        (table[:, :, None] == jnp.arange(POOL, dtype=jnp.int32)[None, None, :])
        & entry_live[:, :, None]
    ).astype(jnp.int32)
    page_owner = jnp.sum(
        page_match * jnp.arange(REQS_DEV, dtype=jnp.int32)[:, None, None], axis=(0, 1)
    )
    page_start = jnp.sum(
        page_match * (jnp.arange(MAXPG, dtype=jnp.int32) * PAGE)[None, :, None], axis=(0, 1)
    )
    page_used = jnp.sum(page_match, axis=(0, 1)) > 0
    owner_length = jnp.sum(page_match * lengths[:, None, None], axis=(0, 1))
    slot_pos = page_start[:, None] + jnp.arange(PAGE, dtype=jnp.int32)[None, :]
    slot_live = page_used[:, None] & (slot_pos < owner_length[:, None])
    slot_owner = jnp.where(slot_live, page_owner[:, None], -1)
    return slot_owner.reshape(POOL * PAGE)


def attend(
    queries, keys_new, values_new, keys_cache, values_cache, requests, positions, slot_owner
):
    inv_root = 1.0 / math.sqrt(queries.shape[-1])
    cache_mask = slot_owner[None, :] == requests[:, None]
    new_mask = (requests[None, :] == requests[:, None]) & (positions[None, :] <= positions[:, None])
    score_cache = (
        jnp.einsum("tkgh,knh->kgtn", queries, keys_cache, preferred_element_type=jnp.float32)
        * inv_root
    )
    score_new = (
        jnp.einsum("tkgh,skh->kgts", queries, keys_new, preferred_element_type=jnp.float32)
        * inv_root
    )
    score_cache = jnp.where(cache_mask[None, None], score_cache, -1e30)
    score_new = jnp.where(new_mask[None, None], score_new, -1e30)
    row_max = jnp.maximum(
        jnp.max(score_cache, axis=-1, keepdims=True), jnp.max(score_new, axis=-1, keepdims=True)
    )
    exp_cache = jnp.where(cache_mask[None, None], jnp.exp(score_cache - row_max), 0.0)
    exp_new = jnp.where(new_mask[None, None], jnp.exp(score_new - row_max), 0.0)
    total = jnp.sum(exp_cache, axis=-1, keepdims=True) + jnp.sum(exp_new, axis=-1, keepdims=True)
    prob_cache = (exp_cache / total).astype(jnp.bfloat16)
    prob_new = (exp_new / total).astype(jnp.bfloat16)
    mixed = jnp.einsum(
        "kgtn,knh->tkgh", prob_cache, values_cache, preferred_element_type=jnp.float32
    )
    mixed = mixed + jnp.einsum(
        "kgts,skh->tkgh", prob_new, values_new, preferred_element_type=jnp.float32
    )
    return mixed.astype(jnp.bfloat16).reshape(queries.shape[0], -1)


def expert_apply(blocks, gate_weight, up_weight, down_weight):
    local_experts = gate_weight.shape[0]
    sources = blocks.shape[0] // local_experts
    slot_count = blocks.shape[1]
    grouped = blocks.reshape(sources, local_experts, slot_count, blocks.shape[2])
    gate_acts = jnp.einsum(
        "sekd,edf->sekf", grouped, gate_weight, preferred_element_type=jnp.float32
    )
    up_acts = jnp.einsum("sekd,edf->sekf", grouped, up_weight, preferred_element_type=jnp.float32)
    hidden_act = (jax.nn.silu(gate_acts) * up_acts).astype(jnp.bfloat16)
    part_sums = jnp.einsum(
        "sekf,efd->sekd", hidden_act, down_weight, preferred_element_type=jnp.float32
    ).astype(jnp.bfloat16)
    return part_sums.reshape(sources * local_experts, slot_count, part_sums.shape[3])


def build_buffer(normed, slot_index, top_count, expert_count, capacity):
    picked = jnp.repeat(normed, top_count, axis=0)
    buffer_rows = (
        jnp.zeros((expert_count * capacity, normed.shape[1]), normed.dtype)
        .at[slot_index]
        .set(picked)
    )
    return buffer_rows.reshape(expert_count, capacity, normed.shape[1])


def weigh_back(returned, slot_index, route_weights, token_count, top_count):
    row_width = returned.shape[2]
    back_rows = returned.reshape(returned.shape[0] * returned.shape[1], row_width)[slot_index]
    weighted = (
        back_rows.astype(jnp.float32) * route_weights.reshape(token_count * top_count)[:, None]
    )
    return jnp.sum(weighted.reshape(token_count, top_count, row_width), axis=1)


LANES = 128
VMEM = pl.BlockSpec(memory_space=pltpu.VMEM)
SMEM = pl.BlockSpec(memory_space=pltpu.SMEM)
VMEM_LIMIT = 24 * 1024 * 1024


def flip(value, axis, bits):
    return lax.ppermute(value, axis, [(i, i ^ bits) for i in range(lax.axis_size(axis))])


def attention_kernel(
    length_ref, table_ref, x_ref, gain_ref, frequency_ref, q_gain_ref, k_gain_ref,
    q_hbm, k_hbm, v_hbm, key_hbm, value_hbm, o_hbm,
    keep_out, near_out, far_out, cross_out,
    q_ref, k_ref, v_ref, key_ref, value_ref, o_ref, query_ref, run_max, run_sum, run_mix,
    mixed_ref, part_ref, owner_ref, slots_ref, page_owner, page_live, sems,
):
    sources = (q_hbm, k_hbm, v_hbm, key_hbm, value_hbm, o_hbm)
    targets = (q_ref, k_ref, v_ref, key_ref, value_ref, o_ref)
    copies = [
        pltpu.make_async_copy(source, target, sems.at[i])
        for i, (source, target) in enumerate(zip(sources, targets))
    ]
    for copy in copies:
        copy.start()
    tokens, head_dim = x_ref.shape[0], k_gain_ref.shape[1]
    heads = q_ref.shape[1] // head_dim
    decodes = tokens - PRE
    for page in range(POOL):
        page_owner[page] = -1
        page_live[page] = 0
    for request in range(1, REQS_DEV):

        def name_page(entry, carry):
            page = table_ref[request, entry]
            page_owner[page] = request
            page_live[page] = jnp.minimum(length_ref[request] - entry * PAGE, PAGE)
            return carry

        lax.fori_loop(0, (length_ref[request] + PAGE - 1) // PAGE, name_page, 0)
    slot = lax.broadcasted_iota(jnp.int32, (1, PAGE), 1)
    for page in range(POOL):
        owner_ref[:, page * PAGE : (page + 1) * PAGE] = jnp.where(
            slot < page_live[page], page_owner[page], -1
        )
    token = lax.broadcasted_iota(jnp.int32, (tokens, head_dim), 0)
    lane = lax.broadcasted_iota(jnp.int32, (tokens, head_dim), 1)
    position = length_ref[0] + token
    for i in range(decodes):
        position = jnp.where(token == PRE + i, length_ref[i + 1], position)
    angle = position.astype(jnp.float32) * frequency_ref[...]
    cosine = jnp.cos(angle)
    sine = jnp.where(lane < head_dim // 2, -jnp.sin(angle), jnp.sin(angle))

    def turned(values, gain):
        values = rms_scale(values, gain)
        return values * cosine + pltpu.roll(values, head_dim // 2, 1) * sine

    normed = rms_scale(x_ref[...].astype(jnp.float32), gain_ref[...]).astype(jnp.bfloat16)
    contract = (((1,), (1,)), ((), ()))
    copies[0].wait()
    query_lin = jnp.dot(normed, q_ref[...], preferred_element_type=jnp.float32)
    copies[1].wait()
    key_lin = jnp.dot(normed, k_ref[...], preferred_element_type=jnp.float32)
    copies[2].wait()
    values_new = jnp.dot(normed, v_ref[...], preferred_element_type=jnp.float32).astype(jnp.bfloat16)
    keys_new = turned(key_lin, k_gain_ref[...]).astype(jnp.bfloat16)
    to_log2 = math.log2(math.e) / math.sqrt(head_dim)
    own_mask = (lane == token) | ((lane < token) & (token < PRE))
    decode_q, decode_max, decode_sum, decode_mix = [], [], [], []
    for head in range(heads):
        span = slice(head * tokens, (head + 1) * tokens)
        query = turned(query_lin[:, head * head_dim : (head + 1) * head_dim], q_gain_ref[...]) * to_log2
        rounded = query.astype(jnp.bfloat16)
        query_ref[span, :] = rounded
        scores = lax.dot_general(rounded, keys_new, contract, preferred_element_type=jnp.float32)
        scores = jnp.where(own_mask, scores, -1e30)
        top = jnp.max(scores, axis=1, keepdims=True)
        weights = jnp.exp2(scores - top)
        total = jnp.sum(weights, axis=1, keepdims=True)
        mix = jnp.dot(weights.astype(jnp.bfloat16), values_new, preferred_element_type=jnp.float32)
        run_max[span, :] = jnp.broadcast_to(top, mix.shape)
        run_sum[span, :] = jnp.broadcast_to(total, mix.shape)
        run_mix[span, :] = mix
        decode_q.append(query[PRE:])
        decode_max.append(top[PRE:])
        decode_sum.append(total[PRE:])
        decode_mix.append(mix[PRE:])
    copies[3].wait()
    copies[4].wait()
    decode_q = jnp.concatenate(decode_q, axis=0).astype(jnp.bfloat16)
    decode_max, decode_sum, decode_mix = (
        jnp.concatenate(part, axis=0) for part in (decode_max, decode_sum, decode_mix)
    )
    row_request = 1 + lax.broadcasted_iota(jnp.int32, (heads * decodes, 1), 0) % decodes
    top = decode_max
    width = 8 * PAGE
    for start in range(0, POOL * PAGE, width):
        keys = key_ref[start // PAGE : (start + width) // PAGE].reshape(width, head_dim)
        scores = lax.dot_general(decode_q, keys, contract, preferred_element_type=jnp.float32)
        scores = jnp.where(owner_ref[:, start : start + width] == row_request, scores, -1e30)
        slots_ref[:, start : start + width] = scores
        top = jnp.maximum(top, jnp.max(scores, axis=1, keepdims=True))
    scale = jnp.exp2(decode_max - top)
    total = decode_sum * scale
    mix = decode_mix * scale
    for start in range(0, POOL * PAGE, width):
        weights = jnp.exp2(slots_ref[:, start : start + width] - top)
        total = total + jnp.sum(weights, axis=1, keepdims=True)
        values = value_ref[start // PAGE : (start + width) // PAGE].reshape(width, head_dim)
        mix = mix + jnp.dot(weights.astype(jnp.bfloat16), values, preferred_element_type=jnp.float32)
    decoded = mix / total
    pages = 4
    width = pages * PAGE
    length = length_ref[0]
    column = lax.broadcasted_iota(jnp.int32, (1, width), 1)

    def prefill(step, carry):
        names = [table_ref[0, jnp.minimum(step * pages + i, MAXPG - 1)] for i in range(pages)]
        keys = jnp.concatenate([key_ref[name] for name in names], axis=0)
        values = jnp.concatenate([value_ref[name] for name in names], axis=0)
        live = column + step * width < length
        for head in range(heads):
            span = slice(head * tokens, (head + 1) * tokens)
            scores = lax.dot_general(
                query_ref[span, :], keys, contract, preferred_element_type=jnp.float32
            )
            scores = jnp.where(live, scores, -1e30)
            before = run_max[span, :1]
            top = jnp.maximum(before, jnp.max(scores, axis=1, keepdims=True))
            scale = jnp.exp2(before - top)
            weights = jnp.exp2(scores - top)
            total = run_sum[span, :1] * scale + jnp.sum(weights, axis=1, keepdims=True)
            mix = run_mix[span, :] * scale + jnp.dot(
                weights.astype(jnp.bfloat16), values, preferred_element_type=jnp.float32
            )
            run_max[span, :] = jnp.broadcast_to(top, mix.shape)
            run_sum[span, :] = jnp.broadcast_to(total, mix.shape)
            run_mix[span, :] = mix
        return carry

    lax.fori_loop(0, (length + width - 1) // width, prefill, 0)
    for head in range(heads):
        span = slice(head * tokens, (head + 1) * tokens)
        columns = slice(head * head_dim, (head + 1) * head_dim)
        mixed_ref[:, columns] = run_mix[span, :] / run_sum[span, :]
        mixed_ref[PRE:, columns] = decoded[head * decodes : (head + 1) * decodes]
    copies[5].wait()
    part_ref[...] = jnp.dot(
        mixed_ref[...].astype(jnp.bfloat16), o_ref[...], preferred_element_type=jnp.float32
    )
    tp_index = lax.axis_index("tp")
    share_rows = keep_out.shape[0]
    for step, out_ref in enumerate((keep_out, near_out, far_out, cross_out)):
        start = pl.multiple_of((tp_index ^ step) * share_rows, share_rows)
        out_ref[...] = part_ref[pl.ds(start, share_rows), :].astype(out_ref.dtype)


def attention_shares(
    x_full, norm_in_gain, q_weight, k_weight, v_weight, q_gain, k_gain, o_weight,
    key_pages, value_pages, page_table, cache_len,
):
    tokens, width = x_full.shape
    head_dim = q_gain.shape[0]
    rows = q_weight.shape[1] // head_dim * tokens
    decode_rows = rows // tokens * (tokens - PRE)
    half = ROPE_BASE ** (-np.arange(head_dim // 2) / (head_dim // 2))
    frequency = jnp.asarray(np.concatenate([half, half])[None, :], jnp.float32)
    large = (q_weight, k_weight, v_weight, key_pages[0], value_pages[0], o_weight)
    share = (tokens // 4, width)
    return pl.pallas_call(
        attention_kernel,
        out_shape=[jax.ShapeDtypeStruct(share, jnp.float32)]
        + [jax.ShapeDtypeStruct(share, jnp.bfloat16)] * 3,
        in_specs=[SMEM] * 2 + [VMEM] * 5 + [pl.BlockSpec(memory_space=pl.ANY)] * 6,
        out_specs=[VMEM] * 4,
        scratch_shapes=[pltpu.VMEM(array.shape, array.dtype) for array in large]
        + [
            pltpu.VMEM((rows, head_dim), jnp.bfloat16),
            pltpu.VMEM((rows, head_dim), jnp.float32),
            pltpu.VMEM((rows, head_dim), jnp.float32),
            pltpu.VMEM((rows, head_dim), jnp.float32),
            pltpu.VMEM((tokens, q_weight.shape[1]), jnp.float32),
            pltpu.VMEM((tokens, width), jnp.float32),
            pltpu.VMEM((1, POOL * PAGE), jnp.int32),
            pltpu.VMEM((decode_rows, POOL * PAGE), jnp.float32),
            pltpu.SMEM((POOL,), jnp.int32),
            pltpu.SMEM((POOL,), jnp.int32),
            pltpu.SemaphoreType.DMA((6,)),
        ],
        compiler_params=pltpu.CompilerParams(vmem_limit_bytes=24 * 1024 * 1024),
        name="attention",
    )(
        cache_len, page_table, x_full, norm_in_gain[None, :], frequency, q_gain[None, :],
        k_gain[None, :], *large,
    )


def pack_kernel(
    own_ref, near_ref, far_ref, cross_ref, x_ref, gain_ref, ids_ref, routes_ref,
    rows_ref, keep_ref, near_out, far_out, cross_out, residual_ref, spread_ref,
):
    tp_index = lax.axis_index("tp")
    share_rows, width = own_ref.shape
    share_width = keep_ref.shape[1]
    mine = pl.ds(pl.multiple_of(tp_index * share_rows, share_rows), share_rows)
    head_sum = (own_ref[...] + near_ref[...].astype(jnp.float32)) + (
        far_ref[...].astype(jnp.float32) + cross_ref[...].astype(jnp.float32)
    )
    residual = x_ref[mine, :].astype(jnp.float32) + head_sum
    residual_ref[...] = residual
    rows_ref[:, :width] = rms_scale(residual, gain_ref[...]).astype(jnp.bfloat16)
    expert = lax.broadcasted_iota(jnp.int32, (LANES, spread_ref.shape[0]), 0) % (LANES // 2)
    spread = jnp.zeros(expert.shape, jnp.float32)
    for k in range(ids_ref.shape[0]):
        spread = spread + jnp.where(expert == ids_ref[k : k + 1, :], routes_ref[k : k + 1, :], 0.0)
    spread_ref[...] = spread.T
    spread = spread_ref[mine, :]
    lane = lax.broadcasted_iota(jnp.int32, spread.shape, 1)
    high = spread.astype(jnp.bfloat16).astype(jnp.float32)
    rows_ref[:, width:] = jnp.where(lane < LANES // 2, high, spread - high).astype(jnp.bfloat16)
    for step, out_ref in enumerate((keep_ref, near_out, far_out, cross_out)):
        column = pl.multiple_of((tp_index ^ step) * share_width, share_width)
        out_ref[...] = residual_ref[:, pl.ds(column, share_width)]


def experts_kernel(far_parts, *refs):
    near_ref, core_ref = refs[:2]
    far_refs, far_core_refs = refs[2 : 2 + far_parts], refs[2 + far_parts : 2 + 2 * far_parts]
    gate_ref, up_ref, down_ref = refs[2 + 2 * far_parts : 5 + 2 * far_parts]
    out_refs, rows_ref = refs[5 + 2 * far_parts : -1], refs[-1]
    req_index, tp_index = lax.axis_index("req"), lax.axis_index("tp")
    levels, share_rows, _ = near_ref.shape
    width = gate_ref.shape[1]
    units = gate_ref.shape[0] // 2
    share_width = width // 4

    def pick(parts):
        if len(parts) == 1:
            return parts[0][...]
        return jnp.where(pl.program_id(0) == 0, parts[0][...], parts[1][...])

    for step, value in enumerate((near_ref[...], core_ref[...], pick(far_refs), pick(far_core_refs))):
        for level in range(levels):
            start = (4 * level + (tp_index ^ step)) * share_rows
            rows_ref[pl.ds(pl.multiple_of(start, share_rows), share_rows), :] = value[level]
    spread = rows_ref[:, width:].astype(jnp.float32)
    lane = lax.broadcasted_iota(jnp.int32, spread.shape, 1) % (LANES // 2)
    weights = [
        jnp.sum(jnp.where(lane == 2 * req_index + e, spread, 0.0), axis=1, keepdims=True)
        for e in range(2)
    ]
    contract = (((1,), (1,)), ((), ()))
    rows = rows_ref[:, :width]
    gate = lax.dot_general(rows, gate_ref[...], contract, preferred_element_type=jnp.float32)
    up = lax.dot_general(rows, up_ref[...], contract, preferred_element_type=jnp.float32)
    unit = lax.broadcasted_iota(jnp.int32, gate.shape, 1)
    weight = jnp.where(unit < units, weights[0], weights[1])
    acts = (gate / (1.0 + jnp.exp(-gate)) * up * weight).astype(jnp.bfloat16)
    for step in range(4):
        column = pl.multiple_of((tp_index ^ step) * share_width, share_width)
        part = jnp.dot(
            acts, down_ref[:, pl.ds(column, share_width)], preferred_element_type=jnp.float32
        )
        target = out_refs[step]
        target[...] = part.reshape(target.shape).astype(target.dtype)


def run_experts(near, core, far, far_core, gate_weight, up_weight, down_weight):
    levels, share_rows, packed = near.shape
    share_width = down_weight.shape[1] // 4
    block = pl.BlockSpec((2, share_rows, packed), lambda z: (z, 0, 0))
    fixed = pl.BlockSpec((2, share_rows, packed), lambda z: (0, 0, 0))
    far_spec = block if len(far) == 1 else fixed
    weight_specs = [
        pl.BlockSpec(w.shape, lambda z: (0, 0), pipeline_mode=pl.Buffered(1))
        for w in (gate_weight, up_weight, down_weight)
    ]
    out_shape = (levels, 4 * share_rows, share_width)
    return pl.pallas_call(
        functools.partial(experts_kernel, len(far)),
        grid=(levels // 2,),
        out_shape=[
            jax.ShapeDtypeStruct(out_shape, jnp.bfloat16 if step % 2 else jnp.float32)
            for step in range(4)
        ],
        in_specs=[block, block] + [far_spec] * (2 * len(far)) + weight_specs,
        out_specs=[pl.BlockSpec((2,) + out_shape[1:], lambda z: (z, 0, 0))] * 4,
        scratch_shapes=[pltpu.VMEM((8 * share_rows, packed), jnp.bfloat16)],
        compiler_params=pltpu.CompilerParams(vmem_limit_bytes=VMEM_LIMIT),
        name="experts",
    )(near, core, *far, *far_core, gate_weight, up_weight, down_weight)


def finish_kernel(
    own_ref, x_ref, y_ref, z1_ref, z2_ref, z3_ref, keep_ref, near_ref, far_ref, cross_ref, out_ref
):
    tp_index = lax.axis_index("tp")
    share_rows = keep_ref.shape[0]
    for step, part_ref in enumerate((keep_ref, near_ref, far_ref, cross_ref)):
        rows = pl.ds(pl.multiple_of((tp_index ^ step) * share_rows, share_rows), share_rows)
        total = own_ref[0, rows, :] + part_ref[...]
        for extra_ref in (x_ref, y_ref):
            total = total + extra_ref[0, rows, :].astype(jnp.float32)
        for extra_ref in (z1_ref, z2_ref, z3_ref):
            total = total + extra_ref[rows, :].astype(jnp.float32)
        out_ref[rows, :] = total.astype(jnp.bfloat16)


def moe_dense(
    x_full,
    kept,
    sent,
    norm_post_gain,
    expert_ids,
    route_weights,
    gate_weight,
    up_weight,
    down_weight,
):
    token_count, width = x_full.shape
    share_rows, share_width = token_count // 4, width // 4

    received = [flip(part, "tp", bits) for bits, part in enumerate(sent, 1)]
    share_f32 = jax.ShapeDtypeStruct((share_rows, share_width), jnp.float32)
    rows, *residuals = pl.pallas_call(
        pack_kernel,
        out_shape=[jax.ShapeDtypeStruct((share_rows, width + LANES), jnp.bfloat16)] + [share_f32] * 4,
        in_specs=[VMEM] * 8,
        out_specs=[VMEM] * 5,
        scratch_shapes=[
            pltpu.VMEM((share_rows, width), jnp.float32),
            pltpu.VMEM((token_count, LANES), jnp.float32),
        ],
        compiler_params=pltpu.CompilerParams(vmem_limit_bytes=8 * 1024 * 1024),
        name="pack_rows",
    )(kept, *received, x_full, norm_post_gain[None, :], expert_ids.T, route_weights.T)
    residuals = residuals[:1] + [flip(residuals[bits], "tp", bits) for bits in (1, 2, 3)]
    line = jnp.stack([rows] + [flip(rows, "req", 2 * bits) for bits in (1, 2, 3)])
    line_x, line_y = flip(line, "req", 1), flip(line, "tp", 2)
    across = (flip(line_x[:2], "tp", 2), flip(line_y[2:], "req", 1))
    line_core, line_x_core, line_y_core = (flip(part, "tp", 1) for part in (line, line_x, line_y))
    across_core = tuple(flip(part, "tp", 1) for part in across)
    gate_up = [w.transpose(0, 2, 1).reshape(-1, width) for w in (gate_weight, up_weight)]
    weights = (*gate_up, down_weight.reshape(-1, width))
    near = run_experts(line, line_core, (line_y,), (line_y_core,), *weights)
    side = run_experts(line_x, line_x_core, across, across_core, *weights)
    keep_00, keep_01, keep_10, keep_11 = (
        (part[2 * y], flip(part[2 * y + 1], "tp", 1)) for part in (near, side) for y in range(2)
    )

    def both(pair, levels):
        return pair[0][levels] + pair[1][levels].astype(jnp.float32)

    low, high = slice(0, 2), slice(2, 4)
    by_x = flip(both(keep_11, low).astype(jnp.bfloat16), "req", 1).astype(jnp.float32)
    by_y = flip(both(keep_11, high).astype(jnp.bfloat16), "tp", 2).astype(jnp.float32)
    from_y = [
        flip((both(keep_01, low) + by_x).astype(jnp.bfloat16), "tp", 2),
        flip(both(keep_01, high).astype(jnp.bfloat16), "tp", 2),
    ]
    from_x = [
        flip(both(keep_10, low).astype(jnp.bfloat16), "req", 1),
        flip((both(keep_10, high) + by_y).astype(jnp.bfloat16), "req", 1),
    ]

    def level(z):
        part = from_x[z // 2][z % 2].astype(jnp.float32) + from_y[z // 2][z % 2].astype(jnp.float32)
        return (both(keep_00, z) + part).astype(jnp.bfloat16)

    from_z = [flip(level(z), "req", 2 * z) for z in (1, 2, 3)]
    return pl.pallas_call(
        finish_kernel,
        out_shape=jax.ShapeDtypeStruct((token_count, share_width), jnp.bfloat16),
        in_specs=[VMEM] * 10,
        out_specs=VMEM,
        compiler_params=pltpu.CompilerParams(vmem_limit_bytes=8 * 1024 * 1024),
        name="finish",
    )(both(keep_00, low), from_x[0], from_y[0], *from_z, *residuals)


def moe_routed(
    x_full,
    head_part,
    norm_post_gain,
    expert_ids,
    route_weights,
    gate_weight,
    up_weight,
    down_weight,
):
    req_count = lax.axis_size("req")
    tp_index = lax.axis_index("tp")
    x_float = x_full.astype(jnp.float32)
    token_count = x_float.shape[0]
    share_width = x_float.shape[1] // lax.axis_size("tp")
    top_count = expert_ids.shape[1]
    expert_count = gate_weight.shape[0] * req_count
    capacity = max(2, 3 * token_count * top_count // (2 * expert_count))
    flat_expert = expert_ids.reshape(token_count * top_count)
    one_hot = (flat_expert[:, None] == jnp.arange(expert_count, dtype=jnp.int32)[None, :]).astype(
        jnp.int32
    )
    slot_rank = jnp.sum((jnp.cumsum(one_hot, axis=0) - one_hot) * one_hot, axis=1)
    slot_index = flat_expert * capacity + slot_rank
    head_sum = lax.psum(head_part.astype(jnp.bfloat16), "tp").astype(jnp.float32)
    residual_full = x_float + head_sum
    normed_post = rms_scale(residual_full, norm_post_gain).astype(jnp.bfloat16)
    residual = lax.dynamic_slice_in_dim(residual_full, tp_index * share_width, share_width, 1)
    send_buffer = build_buffer(normed_post, slot_index, top_count, expert_count, capacity)
    part_sums = expert_apply(
        lax.all_to_all(send_buffer, "req", split_axis=0, concat_axis=0, tiled=True),
        gate_weight,
        up_weight,
        down_weight,
    )
    returned = lax.all_to_all(part_sums, "req", split_axis=0, concat_axis=0, tiled=True)
    moe_term = weigh_back(returned, slot_index, route_weights, token_count, top_count)
    moe_share = lax.psum_scatter(
        moe_term.astype(jnp.bfloat16), "tp", scatter_dimension=1, tiled=True
    ).astype(jnp.float32)
    return (residual + moe_share).astype(jnp.bfloat16)


def attention_part(
    x_full,
    norm_in_gain,
    q_weight,
    k_weight,
    v_weight,
    q_gain,
    k_gain,
    o_weight,
    key_pages,
    value_pages,
    page_table,
    cache_len,
):
    head_dim = q_gain.shape[0]
    kv_local = key_pages.shape[0]
    group_size = q_weight.shape[1] // head_dim // kv_local
    token_count = x_full.shape[0]
    x_float = x_full.astype(jnp.float32)
    normed_in = rms_scale(x_float, norm_in_gain).astype(jnp.bfloat16)
    query_lin = jnp.dot(normed_in, q_weight, preferred_element_type=jnp.float32).reshape(
        token_count, kv_local * group_size, head_dim
    )
    key_lin = jnp.dot(normed_in, k_weight, preferred_element_type=jnp.float32).reshape(
        token_count, kv_local, head_dim
    )
    values_new = (
        jnp.dot(normed_in, v_weight, preferred_element_type=jnp.float32)
        .astype(jnp.bfloat16)
        .reshape(token_count, kv_local, head_dim)
    )
    requests, positions = token_layout(cache_len)
    queries = (
        rotate(rms_scale(query_lin, q_gain), positions)
        .astype(jnp.bfloat16)
        .reshape(token_count, kv_local, group_size, head_dim)
    )
    keys_new = rotate(rms_scale(key_lin, k_gain), positions).astype(jnp.bfloat16)
    slot_owner = page_slots(page_table, cache_len)
    cache_slots = key_pages.shape[1] * key_pages.shape[2]
    keys_cache = key_pages.reshape(kv_local, cache_slots, head_dim)
    values_cache = value_pages.reshape(kv_local, cache_slots, head_dim)
    attended = attend(
        queries, keys_new, values_new, keys_cache, values_cache, requests, positions, slot_owner
    )
    return jnp.dot(attended, o_weight, preferred_element_type=jnp.float32)


def body(
    hidden_in,
    norm_in_gain,
    q_weight,
    k_weight,
    v_weight,
    q_gain,
    k_gain,
    o_weight,
    key_pages,
    value_pages,
    page_table,
    cache_len,
    norm_post_gain,
    expert_ids,
    route_weights,
    gate_weight,
    up_weight,
    down_weight,
):
    req_count = lax.axis_size("req")
    x_full = lax.all_gather(hidden_in, "tp", axis=1, tiled=True)
    attention = (
        x_full,
        norm_in_gain,
        q_weight,
        k_weight,
        v_weight,
        q_gain,
        k_gain,
        o_weight,
        key_pages,
        value_pages,
        page_table,
        cache_len,
    )
    experts = (norm_post_gain, expert_ids, route_weights, gate_weight, up_weight, down_weight)
    expert_count = gate_weight.shape[0] * req_count
    staged = (req_count, lax.axis_size("tp"), gate_weight.shape[0]) == (8, 4, 2)
    if staged and expert_count <= LANES // 2:
        kept, *sent = attention_shares(*attention)
        return moe_dense(x_full, kept, sent, *experts)
    return moe_routed(x_full, attention_part(*attention), *experts)


def solution(mesh):
    return jax.shard_map(
        body,
        mesh=mesh,
        in_specs=(
            P("req", "tp"),
            P(),
            P(None, "tp"),
            P(None, "tp"),
            P(None, "tp"),
            P(),
            P(),
            P("tp", None),
            P("tp", "req", None, None),
            P("tp", "req", None, None),
            P("req", None),
            P("req"),
            P(),
            P("req", None),
            P("req", None),
            P("req", None, "tp"),
            P("req", None, "tp"),
            P("req", "tp", None),
        ),
        out_specs=P("req", "tp"),
        check_vma=False,
    )
```

```python
import functools
import math

import jax
import jax.numpy as jnp
import numpy as np
from jax import lax
from jax.experimental import pallas as pl
from jax.experimental.pallas import tpu as pltpu
from jax.sharding import PartitionSpec as P

PAGE = 128
MAXPG = 32
PRE = 120
TOK_DEV = 128
REQS_DEV = 9
POOL = 48


NORM_EPS = 1e-06
ROPE_BASE = 1000000.0


def rms_scale(values, gain_vec):
    mean_square = jnp.mean(values * values, axis=-1, keepdims=True)
    return values * lax.rsqrt(mean_square + NORM_EPS) * gain_vec


def rotate(values, positions):
    half_dim = values.shape[-1] // 2
    exponent = jnp.arange(half_dim, dtype=jnp.float32) * (2.0 / values.shape[-1])
    frequency = jnp.power(jnp.float32(ROPE_BASE), -exponent)
    angles = positions.astype(jnp.float32)[:, None] * frequency[None, :]
    cosine = jnp.cos(angles)[:, None, :]
    sine_val = jnp.sin(angles)[:, None, :]
    front_half = values[..., :half_dim]
    back_half = values[..., half_dim:]
    return jnp.concatenate(
        [front_half * cosine - back_half * sine_val, back_half * cosine + front_half * sine_val],
        axis=-1,
    )


def token_layout(lengths):
    local_idx = jnp.arange(TOK_DEV, dtype=jnp.int32)
    requests = jnp.where(local_idx < PRE, 0, local_idx - PRE + 1)
    offsets = jnp.where(local_idx < PRE, local_idx, 0)
    request_hot = (requests[:, None] == jnp.arange(REQS_DEV, dtype=jnp.int32)[None, :]).astype(
        jnp.int32
    )
    positions = jnp.sum(request_hot * lengths[None, :], axis=1) + offsets
    return (requests, positions)


def page_slots(table, lengths):
    pages_used = (lengths + PAGE - 1) // PAGE
    entry_live = jnp.arange(MAXPG, dtype=jnp.int32)[None, :] < pages_used[:, None]
    page_match = (
        (table[:, :, None] == jnp.arange(POOL, dtype=jnp.int32)[None, None, :])
        & entry_live[:, :, None]
    ).astype(jnp.int32)
    page_owner = jnp.sum(
        page_match * jnp.arange(REQS_DEV, dtype=jnp.int32)[:, None, None], axis=(0, 1)
    )
    page_start = jnp.sum(
        page_match * (jnp.arange(MAXPG, dtype=jnp.int32) * PAGE)[None, :, None], axis=(0, 1)
    )
    page_used = jnp.sum(page_match, axis=(0, 1)) > 0
    owner_length = jnp.sum(page_match * lengths[:, None, None], axis=(0, 1))
    slot_pos = page_start[:, None] + jnp.arange(PAGE, dtype=jnp.int32)[None, :]
    slot_live = page_used[:, None] & (slot_pos < owner_length[:, None])
    slot_owner = jnp.where(slot_live, page_owner[:, None], -1)
    return slot_owner.reshape(POOL * PAGE)


def attend(
    queries, keys_new, values_new, keys_cache, values_cache, requests, positions, slot_owner
):
    inv_root = 1.0 / math.sqrt(queries.shape[-1])
    cache_mask = slot_owner[None, :] == requests[:, None]
    new_mask = (requests[None, :] == requests[:, None]) & (positions[None, :] <= positions[:, None])
    score_cache = (
        jnp.einsum("tkgh,knh->kgtn", queries, keys_cache, preferred_element_type=jnp.float32)
        * inv_root
    )
    score_new = (
        jnp.einsum("tkgh,skh->kgts", queries, keys_new, preferred_element_type=jnp.float32)
        * inv_root
    )
    score_cache = jnp.where(cache_mask[None, None], score_cache, -1e30)
    score_new = jnp.where(new_mask[None, None], score_new, -1e30)
    row_max = jnp.maximum(
        jnp.max(score_cache, axis=-1, keepdims=True), jnp.max(score_new, axis=-1, keepdims=True)
    )
    exp_cache = jnp.where(cache_mask[None, None], jnp.exp(score_cache - row_max), 0.0)
    exp_new = jnp.where(new_mask[None, None], jnp.exp(score_new - row_max), 0.0)
    total = jnp.sum(exp_cache, axis=-1, keepdims=True) + jnp.sum(exp_new, axis=-1, keepdims=True)
    prob_cache = (exp_cache / total).astype(jnp.bfloat16)
    prob_new = (exp_new / total).astype(jnp.bfloat16)
    mixed = jnp.einsum(
        "kgtn,knh->tkgh", prob_cache, values_cache, preferred_element_type=jnp.float32
    )
    mixed = mixed + jnp.einsum(
        "kgts,skh->tkgh", prob_new, values_new, preferred_element_type=jnp.float32
    )
    return mixed.astype(jnp.bfloat16).reshape(queries.shape[0], -1)


def expert_apply(blocks, gate_weight, up_weight, down_weight):
    local_experts = gate_weight.shape[0]
    sources = blocks.shape[0] // local_experts
    slot_count = blocks.shape[1]
    grouped = blocks.reshape(sources, local_experts, slot_count, blocks.shape[2])
    gate_acts = jnp.einsum(
        "sekd,edf->sekf", grouped, gate_weight, preferred_element_type=jnp.float32
    )
    up_acts = jnp.einsum("sekd,edf->sekf", grouped, up_weight, preferred_element_type=jnp.float32)
    hidden_act = (jax.nn.silu(gate_acts) * up_acts).astype(jnp.bfloat16)
    part_sums = jnp.einsum(
        "sekf,efd->sekd", hidden_act, down_weight, preferred_element_type=jnp.float32
    ).astype(jnp.bfloat16)
    return part_sums.reshape(sources * local_experts, slot_count, part_sums.shape[3])


def build_buffer(normed, slot_index, top_count, expert_count, capacity):
    picked = jnp.repeat(normed, top_count, axis=0)
    buffer_rows = (
        jnp.zeros((expert_count * capacity, normed.shape[1]), normed.dtype)
        .at[slot_index]
        .set(picked)
    )
    return buffer_rows.reshape(expert_count, capacity, normed.shape[1])


def weigh_back(returned, slot_index, route_weights, token_count, top_count):
    row_width = returned.shape[2]
    back_rows = returned.reshape(returned.shape[0] * returned.shape[1], row_width)[slot_index]
    weighted = (
        back_rows.astype(jnp.float32) * route_weights.reshape(token_count * top_count)[:, None]
    )
    return jnp.sum(weighted.reshape(token_count, top_count, row_width), axis=1)


LANES = 128
VMEM = pl.BlockSpec(memory_space=pltpu.VMEM)
SMEM = pl.BlockSpec(memory_space=pltpu.SMEM)
VMEM_LIMIT = 24 * 1024 * 1024


def flip(value, axis, bits):
    return lax.ppermute(value, axis, [(i, i ^ bits) for i in range(lax.axis_size(axis))])


def attention_kernel(*refs):
    pieces, hbm_refs, (keep_out, near_out, far_out, cross_out) = refs[:4], refs[4:16], refs[16:20]
    local_refs, value_hbm = refs[20:31], hbm_refs[11]
    (length_ref, table_ref, gain_ref, frequency_ref, q_gain_ref, k_gain_ref) = local_refs[:6]
    (q_ref, k_ref, v_ref, key_ref, o_ref) = local_refs[6:]
    (
        value_ref, x_ref, query_ref, own_scores, top_ref, scores_ref, mix_ref, mixed_ref, part_ref,
        owner_ref, slots_ref, page_owner, page_live, sems,
    ) = refs[31:]
    tokens, head_dim = x_ref.shape[0], k_gain_ref.shape[1]
    targets = (*local_refs, value_ref.at[:, :, :head_dim])
    copies = [
        pltpu.make_async_copy(source, target, sems.at[i])
        for i, (source, target) in enumerate(zip(hbm_refs, targets))
    ]
    for copy in copies:
        copy.start()
    tp_index = lax.axis_index("tp")
    heads = q_ref.shape[1] // head_dim
    decodes = tokens - PRE
    rows = heads * tokens
    value_ref[:, :, head_dim:] = jnp.ones((POOL, PAGE, head_dim), jnp.bfloat16)
    for step, piece in enumerate(pieces):
        width = piece.shape[1]
        start = pl.multiple_of((tp_index ^ step) * width, width)
        x_ref[:, pl.ds(start, width)] = piece[...]
    for copy in copies[:6]:
        copy.wait()
    token = lax.broadcasted_iota(jnp.int32, (tokens, head_dim), 0)
    lane = lax.broadcasted_iota(jnp.int32, (tokens, head_dim), 1)
    position = length_ref[0] + token
    for i in range(decodes):
        position = jnp.where(token == PRE + i, length_ref[i + 1], position)
    angle = position.astype(jnp.float32) * frequency_ref[...]
    cosine, sine = jnp.cos(angle), jnp.sin(angle)
    sine = jnp.where(lane < head_dim // 2, -sine, sine)

    def turned(values, gain):
        values = rms_scale(values, gain)
        return values * cosine + pltpu.roll(values, head_dim // 2, 1) * sine

    normed = rms_scale(x_ref[...].astype(jnp.float32), gain_ref[...]).astype(jnp.bfloat16)
    contract = (((1,), (1,)), ((), ()))
    for copy in copies[6:9]:
        copy.wait()
    key_lin = jnp.dot(normed, k_ref[...], preferred_element_type=jnp.float32)
    values_new = jnp.dot(normed, v_ref[...], preferred_element_type=jnp.float32).astype(jnp.bfloat16)
    query_lin = jnp.dot(normed, q_ref[...], preferred_element_type=jnp.float32)
    keys_new = turned(key_lin, k_gain_ref[...]).astype(jnp.bfloat16)
    values_new = jnp.concatenate([values_new, jnp.ones_like(values_new)], axis=1)
    to_log2 = math.log2(math.e) / math.sqrt(head_dim)
    own_mask = (lane == token) | ((lane < token) & (token < PRE))
    decode_query, decode_own = [], []
    for head in range(heads):
        span = slice(head * tokens, (head + 1) * tokens)
        query = turned(query_lin[:, head * head_dim : (head + 1) * head_dim], q_gain_ref[...]) * to_log2
        rounded = query.astype(jnp.bfloat16)
        query_ref[span, :] = rounded
        scores = lax.dot_general(rounded, keys_new, contract, preferred_element_type=jnp.float32)
        scores = jnp.where(own_mask, scores, -1e30)
        own_scores[span, :] = scores
        top_ref[span, :] = scores
        decode_query.append(query[PRE:])
        decode_own.append(scores[PRE:])
    decode_query = jnp.concatenate(decode_query, axis=0).astype(jnp.bfloat16)
    decode_own = jnp.concatenate(decode_own, axis=0)
    for page in range(POOL):
        page_owner[page] = -1
        page_live[page] = 0
    for request in range(1, REQS_DEV):

        def name_page(entry, carry):
            page = table_ref[request, entry]
            page_owner[page] = request
            page_live[page] = jnp.minimum(length_ref[request] - entry * PAGE, PAGE)
            return carry

        lax.fori_loop(0, (length_ref[request] + PAGE - 1) // PAGE, name_page, 0)
    slot = lax.broadcasted_iota(jnp.int32, (1, PAGE), 1)
    for page in range(POOL):
        owner_ref[:, page * PAGE : (page + 1) * PAGE] = jnp.where(
            slot < page_live[page], page_owner[page], -1
        )
    copies[9].wait()
    pages = scores_ref.shape[2] // PAGE
    width = pages * PAGE
    length = length_ref[0]
    steps = (length + width - 1) // width
    column = lax.broadcasted_iota(jnp.int32, (1, width), 1)

    def named(ref, step):
        names = [table_ref[0, jnp.minimum(step * pages + i, MAXPG - 1)] for i in range(pages)]
        return jnp.concatenate([ref[name] for name in names], axis=0)

    def score(step, carry):
        scores = lax.dot_general(
            query_ref[...], named(key_ref, step), contract, preferred_element_type=jnp.float32
        )
        scores = jnp.where(column + step * width < length, scores, -1e30)
        scores_ref[step] = scores
        top = top_ref[...]
        for page in range(pages):
            top = jnp.maximum(top, scores[:, page * PAGE : (page + 1) * PAGE])
        top_ref[...] = top
        return carry

    lax.fori_loop(0, steps, score, 0)
    row_request = 1 + lax.broadcasted_iota(jnp.int32, (heads * decodes, 1), 0) % decodes
    top = decode_own
    span = 8 * PAGE
    for start in range(0, POOL * PAGE, span):
        keys = key_ref[start // PAGE : (start + span) // PAGE].reshape(span, head_dim)
        scores = lax.dot_general(decode_query, keys, contract, preferred_element_type=jnp.float32)
        scores = jnp.where(owner_ref[:, start : start + span] == row_request, scores, -1e30)
        slots_ref[:, start : start + span] = scores
        for page in range(8):
            top = jnp.maximum(top, scores[:, page * PAGE : (page + 1) * PAGE])
    top = jnp.max(top, axis=1, keepdims=True)
    copies[11].wait()
    decode_mix = jnp.dot(
        jnp.exp2(decode_own - top).astype(jnp.bfloat16), values_new, preferred_element_type=jnp.float32
    )
    for start in range(0, POOL * PAGE, span):
        weights = jnp.exp2(slots_ref[:, start : start + span] - top).astype(jnp.bfloat16)
        values = value_ref[start // PAGE : (start + span) // PAGE].reshape(span, 2 * head_dim)
        decode_mix = decode_mix + jnp.dot(weights, values, preferred_element_type=jnp.float32)
    decoded = decode_mix[:, :head_dim] / decode_mix[:, head_dim:]
    top = jnp.max(top_ref[...], axis=1, keepdims=True)
    top_ref[...] = jnp.broadcast_to(top, top_ref.shape)
    mix_ref[...] = jnp.dot(
        jnp.exp2(own_scores[...] - top).astype(jnp.bfloat16), values_new, preferred_element_type=jnp.float32
    )

    def mix(step, carry):
        weights = jnp.exp2(scores_ref[step] - top_ref[:, :1]).astype(jnp.bfloat16)
        mix_ref[...] += jnp.dot(weights, named(value_ref, step), preferred_element_type=jnp.float32)
        return carry

    lax.fori_loop(0, steps, mix, 0)
    for head in range(heads):
        part = mix_ref[head * tokens : (head + 1) * tokens, :]
        columns = slice(head * head_dim, (head + 1) * head_dim)
        mixed_ref[:, columns] = part[:, :head_dim] / part[:, head_dim:]
        mixed_ref[PRE:, columns] = decoded[head * decodes : (head + 1) * decodes]
    copies[10].wait()
    part_ref[...] = jnp.dot(
        mixed_ref[...].astype(jnp.bfloat16), o_ref[...], preferred_element_type=jnp.float32
    )
    share_rows = keep_out.shape[0]
    for step, out_ref in enumerate((keep_out, near_out, far_out, cross_out)):
        mine = pl.ds(pl.multiple_of((tp_index ^ step) * share_rows, share_rows), share_rows)
        part = part_ref[mine, :]
        if step == 0:
            part = part + x_ref[mine, :].astype(jnp.float32)
        out_ref[...] = part.astype(out_ref.dtype)


def attention_shares(
    hidden_in, norm_in_gain, q_weight, k_weight, v_weight, q_gain, k_gain, o_weight,
    key_pages, value_pages, page_table, cache_len,
):
    far = flip(hidden_in, "tp", 2)
    pieces = (hidden_in, flip(hidden_in, "tp", 1), far, flip(far, "tp", 1))
    tokens, width = hidden_in.shape[0], 4 * hidden_in.shape[1]
    head_dim = q_gain.shape[0]
    rows = q_weight.shape[1] // head_dim * tokens
    decode_rows = rows // tokens * (tokens - PRE)
    half = ROPE_BASE ** (-np.arange(head_dim // 2) / (head_dim // 2))
    frequency = jnp.asarray(np.concatenate([half, half])[None, :], jnp.float32)
    scalars = (cache_len, page_table)
    arrays = (
        norm_in_gain[None, :], frequency, q_gain[None, :], k_gain[None, :],
        q_weight, k_weight, v_weight, key_pages[0], o_weight,
    )
    share = (tokens // 4, width)
    score_pages = 4
    return pl.pallas_call(
        attention_kernel,
        out_shape=[jax.ShapeDtypeStruct(share, jnp.float32)]
        + [jax.ShapeDtypeStruct(share, jnp.bfloat16)] * 3,
        in_specs=[VMEM] * 4 + [pl.BlockSpec(memory_space=pltpu.HBM)] * 12,
        out_specs=[VMEM] * 4,
        scratch_shapes=[pltpu.SMEM(array.shape, array.dtype) for array in scalars]
        + [pltpu.VMEM(array.shape, array.dtype) for array in arrays]
        + [
            pltpu.VMEM((POOL, PAGE, 2 * head_dim), jnp.bfloat16),
            pltpu.VMEM((tokens, width), jnp.bfloat16),
            pltpu.VMEM((rows, head_dim), jnp.bfloat16),
            pltpu.VMEM((rows, tokens), jnp.float32),
            pltpu.VMEM((rows, head_dim), jnp.float32),
            pltpu.VMEM((MAXPG // score_pages, rows, score_pages * PAGE), jnp.float32),
            pltpu.VMEM((rows, 2 * head_dim), jnp.float32),
            pltpu.VMEM((tokens, q_weight.shape[1]), jnp.float32),
            pltpu.VMEM((tokens, width), jnp.float32),
            pltpu.VMEM((1, POOL * PAGE), jnp.int32),
            pltpu.VMEM((decode_rows, POOL * PAGE), jnp.float32),
            pltpu.SMEM((POOL,), jnp.int32),
            pltpu.SMEM((POOL,), jnp.int32),
            pltpu.SemaphoreType.DMA((12,)),
        ],
        compiler_params=pltpu.CompilerParams(vmem_limit_bytes=56 * 1024 * 1024),
        name="attention",
    )(*pieces, *scalars, *arrays, value_pages[0])


def pack_kernel(
    own_ref, near_ref, far_ref, cross_ref, gain_ref, ids_ref, routes_ref,
    rows_ref, keep_ref, near_out, far_out, cross_out, residual_ref, spread_ref,
):
    tp_index = lax.axis_index("tp")
    share_rows, width = own_ref.shape
    share_width = keep_ref.shape[1]
    mine = pl.ds(pl.multiple_of(tp_index * share_rows, share_rows), share_rows)
    residual = (own_ref[...] + near_ref[...].astype(jnp.float32)) + (
        far_ref[...].astype(jnp.float32) + cross_ref[...].astype(jnp.float32)
    )
    residual_ref[...] = residual
    rows_ref[:, :width] = rms_scale(residual, gain_ref[...]).astype(jnp.bfloat16)
    expert = lax.broadcasted_iota(jnp.int32, (LANES, spread_ref.shape[0]), 0) % (LANES // 2)
    spread = jnp.zeros(expert.shape, jnp.float32)
    for k in range(ids_ref.shape[0]):
        spread = spread + jnp.where(expert == ids_ref[k : k + 1, :], routes_ref[k : k + 1, :], 0.0)
    spread_ref[...] = spread.T
    spread = spread_ref[mine, :]
    lane = lax.broadcasted_iota(jnp.int32, spread.shape, 1)
    high = spread.astype(jnp.bfloat16).astype(jnp.float32)
    rows_ref[:, width:] = jnp.where(lane < LANES // 2, high, spread - high).astype(jnp.bfloat16)
    for step, out_ref in enumerate((keep_ref, near_out, far_out, cross_out)):
        column = pl.multiple_of((tp_index ^ step) * share_width, share_width)
        out_ref[...] = residual_ref[:, pl.ds(column, share_width)]


def experts_kernel(far_parts, *refs):
    near_ref, core_ref = refs[:2]
    far_refs, far_core_refs = refs[2 : 2 + far_parts], refs[2 + far_parts : 2 + 2 * far_parts]
    gate_ref, up_ref, down_ref = refs[2 + 2 * far_parts : 5 + 2 * far_parts]
    out_refs, rows_ref = refs[5 + 2 * far_parts : -1], refs[-1]
    req_index, tp_index = lax.axis_index("req"), lax.axis_index("tp")
    levels, share_rows, _ = near_ref.shape
    width = gate_ref.shape[1]
    units = gate_ref.shape[0] // 2
    share_width = width // 4

    def pick(parts):
        if len(parts) == 1:
            return parts[0][...]
        return jnp.where(pl.program_id(0) == 0, parts[0][...], parts[1][...])

    for step, value in enumerate((near_ref[...], core_ref[...], pick(far_refs), pick(far_core_refs))):
        for level in range(levels):
            start = (4 * level + (tp_index ^ step)) * share_rows
            rows_ref[pl.ds(pl.multiple_of(start, share_rows), share_rows), :] = value[level]
    spread = rows_ref[:, width:].astype(jnp.float32)
    lane = lax.broadcasted_iota(jnp.int32, spread.shape, 1) % (LANES // 2)
    weights = [
        jnp.sum(jnp.where(lane == 2 * req_index + e, spread, 0.0), axis=1, keepdims=True)
        for e in range(2)
    ]
    contract = (((1,), (1,)), ((), ()))
    rows = rows_ref[:, :width]
    gate = lax.dot_general(rows, gate_ref[...], contract, preferred_element_type=jnp.float32)
    up = lax.dot_general(rows, up_ref[...], contract, preferred_element_type=jnp.float32)
    unit = lax.broadcasted_iota(jnp.int32, gate.shape, 1)
    weight = jnp.where(unit < units, weights[0], weights[1])
    acts = (gate / (1.0 + jnp.exp(-gate)) * up * weight).astype(jnp.bfloat16)
    for step in range(4):
        column = pl.multiple_of((tp_index ^ step) * share_width, share_width)
        part = jnp.dot(
            acts, down_ref[:, pl.ds(column, share_width)], preferred_element_type=jnp.float32
        )
        target = out_refs[step]
        target[...] = part.reshape(target.shape).astype(target.dtype)


def run_experts(near, core, far, far_core, gate_weight, up_weight, down_weight):
    levels, share_rows, packed = near.shape
    share_width = down_weight.shape[1] // 4
    block = pl.BlockSpec((2, share_rows, packed), lambda z: (z, 0, 0))
    fixed = pl.BlockSpec((2, share_rows, packed), lambda z: (0, 0, 0))
    far_spec = block if len(far) == 1 else fixed
    weight_specs = [
        pl.BlockSpec(w.shape, lambda z: (0, 0), pipeline_mode=pl.Buffered(1))
        for w in (gate_weight, up_weight, down_weight)
    ]
    out_shape = (levels, 4 * share_rows, share_width)
    return pl.pallas_call(
        functools.partial(experts_kernel, len(far)),
        grid=(levels // 2,),
        out_shape=[
            jax.ShapeDtypeStruct(out_shape, jnp.bfloat16 if step % 2 else jnp.float32)
            for step in range(4)
        ],
        in_specs=[block, block] + [far_spec] * (2 * len(far)) + weight_specs,
        out_specs=[pl.BlockSpec((2,) + out_shape[1:], lambda z: (z, 0, 0))] * 4,
        scratch_shapes=[pltpu.VMEM((8 * share_rows, packed), jnp.bfloat16)],
        compiler_params=pltpu.CompilerParams(vmem_limit_bytes=VMEM_LIMIT),
        name="experts",
    )(near, core, *far, *far_core, gate_weight, up_weight, down_weight)


def finish_kernel(
    own_ref, x_ref, y_ref, z1_ref, z2_ref, z3_ref, keep_ref, near_ref, far_ref, cross_ref, out_ref
):
    tp_index = lax.axis_index("tp")
    share_rows = keep_ref.shape[0]
    for step, part_ref in enumerate((keep_ref, near_ref, far_ref, cross_ref)):
        rows = pl.ds(pl.multiple_of((tp_index ^ step) * share_rows, share_rows), share_rows)
        total = own_ref[0, rows, :] + part_ref[...]
        for extra_ref in (x_ref, y_ref):
            total = total + extra_ref[0, rows, :].astype(jnp.float32)
        for extra_ref in (z1_ref, z2_ref, z3_ref):
            total = total + extra_ref[rows, :].astype(jnp.float32)
        out_ref[rows, :] = total.astype(jnp.bfloat16)


def moe_dense(
    kept,
    sent,
    norm_post_gain,
    expert_ids,
    route_weights,
    gate_weight,
    up_weight,
    down_weight,
):
    share_rows, width = kept.shape
    token_count, share_width = 4 * share_rows, width // 4
    received = [flip(part, "tp", bits) for bits, part in enumerate(sent, 1)]
    share_f32 = jax.ShapeDtypeStruct((share_rows, share_width), jnp.float32)
    rows, *residuals = pl.pallas_call(
        pack_kernel,
        out_shape=[jax.ShapeDtypeStruct((share_rows, width + LANES), jnp.bfloat16)] + [share_f32] * 4,
        in_specs=[VMEM] * 7,
        out_specs=[VMEM] * 5,
        scratch_shapes=[
            pltpu.VMEM((share_rows, width), jnp.float32),
            pltpu.VMEM((token_count, LANES), jnp.float32),
        ],
        compiler_params=pltpu.CompilerParams(vmem_limit_bytes=8 * 1024 * 1024),
        name="pack_rows",
    )(kept, *received, norm_post_gain[None, :], expert_ids.T, route_weights.T)
    residuals = residuals[:1] + [flip(residuals[bits], "tp", bits) for bits in (1, 2, 3)]
    line = jnp.stack([rows] + [flip(rows, "req", 2 * bits) for bits in (1, 2, 3)])
    gate_up = [w.transpose(0, 2, 1).reshape(-1, width) for w in (gate_weight, up_weight)]
    weights = (*gate_up, down_weight.reshape(-1, width))
    line_x, line_y, line_core = lax.optimization_barrier(
        (flip(line, "req", 1), flip(line, "tp", 2), flip(line, "tp", 1))
    )
    across = (flip(line_x[:2], "tp", 2), flip(line_y[2:], "req", 1))
    line_y_core, line_x_core = flip(line_y, "tp", 1), flip(line_x, "tp", 1)
    near = run_experts(line, line_core, (line_y,), (line_y_core,), *weights)
    near, across, line_x_core, residuals = lax.optimization_barrier(
        (near, across, line_x_core, residuals)
    )
    across_core = tuple(flip(part, "tp", 1) for part in across)
    side = run_experts(line_x, line_x_core, across, across_core, *weights)
    keep_00, keep_01, keep_10, keep_11 = (
        (part[2 * y], flip(part[2 * y + 1], "tp", 1)) for part in (near, side) for y in range(2)
    )

    def both(pair, levels):
        return pair[0][levels] + pair[1][levels].astype(jnp.float32)

    low, high = slice(0, 2), slice(2, 4)
    by_x = flip(both(keep_11, low).astype(jnp.bfloat16), "req", 1).astype(jnp.float32)
    by_y = flip(both(keep_11, high).astype(jnp.bfloat16), "tp", 2).astype(jnp.float32)
    from_y = [
        flip((both(keep_01, low) + by_x).astype(jnp.bfloat16), "tp", 2),
        flip(both(keep_01, high).astype(jnp.bfloat16), "tp", 2),
    ]
    from_x = [
        flip(both(keep_10, low).astype(jnp.bfloat16), "req", 1),
        flip((both(keep_10, high) + by_y).astype(jnp.bfloat16), "req", 1),
    ]

    def level(z):
        part = from_x[z // 2][z % 2].astype(jnp.float32) + from_y[z // 2][z % 2].astype(jnp.float32)
        return (both(keep_00, z) + part).astype(jnp.bfloat16)

    from_z = [flip(level(z), "req", 2 * z) for z in (1, 2, 3)]
    return pl.pallas_call(
        finish_kernel,
        out_shape=jax.ShapeDtypeStruct((token_count, share_width), jnp.bfloat16),
        in_specs=[VMEM] * 10,
        out_specs=VMEM,
        compiler_params=pltpu.CompilerParams(vmem_limit_bytes=8 * 1024 * 1024),
        name="finish",
    )(both(keep_00, low), from_x[0], from_y[0], *from_z, *residuals)


def moe_routed(
    x_full,
    head_part,
    norm_post_gain,
    expert_ids,
    route_weights,
    gate_weight,
    up_weight,
    down_weight,
):
    req_count = lax.axis_size("req")
    tp_index = lax.axis_index("tp")
    x_float = x_full.astype(jnp.float32)
    token_count = x_float.shape[0]
    share_width = x_float.shape[1] // lax.axis_size("tp")
    top_count = expert_ids.shape[1]
    expert_count = gate_weight.shape[0] * req_count
    capacity = max(2, 3 * token_count * top_count // (2 * expert_count))
    flat_expert = expert_ids.reshape(token_count * top_count)
    one_hot = (flat_expert[:, None] == jnp.arange(expert_count, dtype=jnp.int32)[None, :]).astype(
        jnp.int32
    )
    slot_rank = jnp.sum((jnp.cumsum(one_hot, axis=0) - one_hot) * one_hot, axis=1)
    slot_index = flat_expert * capacity + slot_rank
    head_sum = lax.psum(head_part.astype(jnp.bfloat16), "tp").astype(jnp.float32)
    residual_full = x_float + head_sum
    normed_post = rms_scale(residual_full, norm_post_gain).astype(jnp.bfloat16)
    residual = lax.dynamic_slice_in_dim(residual_full, tp_index * share_width, share_width, 1)
    send_buffer = build_buffer(normed_post, slot_index, top_count, expert_count, capacity)
    part_sums = expert_apply(
        lax.all_to_all(send_buffer, "req", split_axis=0, concat_axis=0, tiled=True),
        gate_weight,
        up_weight,
        down_weight,
    )
    returned = lax.all_to_all(part_sums, "req", split_axis=0, concat_axis=0, tiled=True)
    moe_term = weigh_back(returned, slot_index, route_weights, token_count, top_count)
    moe_share = lax.psum_scatter(
        moe_term.astype(jnp.bfloat16), "tp", scatter_dimension=1, tiled=True
    ).astype(jnp.float32)
    return (residual + moe_share).astype(jnp.bfloat16)


def attention_part(
    x_full,
    norm_in_gain,
    q_weight,
    k_weight,
    v_weight,
    q_gain,
    k_gain,
    o_weight,
    key_pages,
    value_pages,
    page_table,
    cache_len,
):
    head_dim = q_gain.shape[0]
    kv_local = key_pages.shape[0]
    group_size = q_weight.shape[1] // head_dim // kv_local
    token_count = x_full.shape[0]
    x_float = x_full.astype(jnp.float32)
    normed_in = rms_scale(x_float, norm_in_gain).astype(jnp.bfloat16)
    query_lin = jnp.dot(normed_in, q_weight, preferred_element_type=jnp.float32).reshape(
        token_count, kv_local * group_size, head_dim
    )
    key_lin = jnp.dot(normed_in, k_weight, preferred_element_type=jnp.float32).reshape(
        token_count, kv_local, head_dim
    )
    values_new = (
        jnp.dot(normed_in, v_weight, preferred_element_type=jnp.float32)
        .astype(jnp.bfloat16)
        .reshape(token_count, kv_local, head_dim)
    )
    requests, positions = token_layout(cache_len)
    queries = (
        rotate(rms_scale(query_lin, q_gain), positions)
        .astype(jnp.bfloat16)
        .reshape(token_count, kv_local, group_size, head_dim)
    )
    keys_new = rotate(rms_scale(key_lin, k_gain), positions).astype(jnp.bfloat16)
    slot_owner = page_slots(page_table, cache_len)
    cache_slots = key_pages.shape[1] * key_pages.shape[2]
    keys_cache = key_pages.reshape(kv_local, cache_slots, head_dim)
    values_cache = value_pages.reshape(kv_local, cache_slots, head_dim)
    attended = attend(
        queries, keys_new, values_new, keys_cache, values_cache, requests, positions, slot_owner
    )
    return jnp.dot(attended, o_weight, preferred_element_type=jnp.float32)


def body(
    hidden_in,
    norm_in_gain,
    q_weight,
    k_weight,
    v_weight,
    q_gain,
    k_gain,
    o_weight,
    key_pages,
    value_pages,
    page_table,
    cache_len,
    norm_post_gain,
    expert_ids,
    route_weights,
    gate_weight,
    up_weight,
    down_weight,
):
    req_count = lax.axis_size("req")
    attention = (
        norm_in_gain,
        q_weight,
        k_weight,
        v_weight,
        q_gain,
        k_gain,
        o_weight,
        key_pages,
        value_pages,
        page_table,
        cache_len,
    )
    experts = (norm_post_gain, expert_ids, route_weights, gate_weight, up_weight, down_weight)
    expert_count = gate_weight.shape[0] * req_count
    staged = (req_count, lax.axis_size("tp"), gate_weight.shape[0]) == (8, 4, 2)
    if staged and expert_count <= LANES // 2:
        kept, *sent = attention_shares(hidden_in, *attention)
        return moe_dense(kept, sent, *experts)
    x_full = lax.all_gather(hidden_in, "tp", axis=1, tiled=True)
    return moe_routed(x_full, attention_part(x_full, *attention), *experts)


def solution(mesh):
    return jax.shard_map(
        body,
        mesh=mesh,
        in_specs=(
            P("req", "tp"),
            P(),
            P(None, "tp"),
            P(None, "tp"),
            P(None, "tp"),
            P(),
            P(),
            P("tp", None),
            P("tp", "req", None, None),
            P("tp", "req", None, None),
            P("req", None),
            P("req"),
            P(),
            P("req", None),
            P("req", None),
            P("req", None, "tp"),
            P("req", None, "tp"),
            P("req", "tp", None),
        ),
        out_specs=P("req", "tp"),
        check_vma=False,
    )
```

```python
import functools
import math

import jax
import jax.numpy as jnp
import numpy as np
from jax import lax
from jax.experimental import pallas as pl
from jax.experimental.pallas import tpu as pltpu
from jax.sharding import PartitionSpec as P

PAGE = 128
MAXPG = 32
PRE = 120
TOK_DEV = 128
REQS_DEV = 9
POOL = 48


NORM_EPS = 1e-06
ROPE_BASE = 1000000.0


def rms_scale(values, gain_vec):
    mean_square = jnp.mean(values * values, axis=-1, keepdims=True)
    return values * lax.rsqrt(mean_square + NORM_EPS) * gain_vec


def rotate(values, positions):
    half_dim = values.shape[-1] // 2
    exponent = jnp.arange(half_dim, dtype=jnp.float32) * (2.0 / values.shape[-1])
    frequency = jnp.power(jnp.float32(ROPE_BASE), -exponent)
    angles = positions.astype(jnp.float32)[:, None] * frequency[None, :]
    cosine = jnp.cos(angles)[:, None, :]
    sine_val = jnp.sin(angles)[:, None, :]
    front_half = values[..., :half_dim]
    back_half = values[..., half_dim:]
    return jnp.concatenate(
        [front_half * cosine - back_half * sine_val, back_half * cosine + front_half * sine_val],
        axis=-1,
    )


def token_layout(lengths):
    local_idx = jnp.arange(TOK_DEV, dtype=jnp.int32)
    requests = jnp.where(local_idx < PRE, 0, local_idx - PRE + 1)
    offsets = jnp.where(local_idx < PRE, local_idx, 0)
    request_hot = (requests[:, None] == jnp.arange(REQS_DEV, dtype=jnp.int32)[None, :]).astype(
        jnp.int32
    )
    positions = jnp.sum(request_hot * lengths[None, :], axis=1) + offsets
    return (requests, positions)


def page_slots(table, lengths):
    pages_used = (lengths + PAGE - 1) // PAGE
    entry_live = jnp.arange(MAXPG, dtype=jnp.int32)[None, :] < pages_used[:, None]
    page_match = (
        (table[:, :, None] == jnp.arange(POOL, dtype=jnp.int32)[None, None, :])
        & entry_live[:, :, None]
    ).astype(jnp.int32)
    page_owner = jnp.sum(
        page_match * jnp.arange(REQS_DEV, dtype=jnp.int32)[:, None, None], axis=(0, 1)
    )
    page_start = jnp.sum(
        page_match * (jnp.arange(MAXPG, dtype=jnp.int32) * PAGE)[None, :, None], axis=(0, 1)
    )
    page_used = jnp.sum(page_match, axis=(0, 1)) > 0
    owner_length = jnp.sum(page_match * lengths[:, None, None], axis=(0, 1))
    slot_pos = page_start[:, None] + jnp.arange(PAGE, dtype=jnp.int32)[None, :]
    slot_live = page_used[:, None] & (slot_pos < owner_length[:, None])
    slot_owner = jnp.where(slot_live, page_owner[:, None], -1)
    return slot_owner.reshape(POOL * PAGE)


def attend(
    queries, keys_new, values_new, keys_cache, values_cache, requests, positions, slot_owner
):
    inv_root = 1.0 / math.sqrt(queries.shape[-1])
    cache_mask = slot_owner[None, :] == requests[:, None]
    new_mask = (requests[None, :] == requests[:, None]) & (positions[None, :] <= positions[:, None])
    score_cache = (
        jnp.einsum("tkgh,knh->kgtn", queries, keys_cache, preferred_element_type=jnp.float32)
        * inv_root
    )
    score_new = (
        jnp.einsum("tkgh,skh->kgts", queries, keys_new, preferred_element_type=jnp.float32)
        * inv_root
    )
    score_cache = jnp.where(cache_mask[None, None], score_cache, -1e30)
    score_new = jnp.where(new_mask[None, None], score_new, -1e30)
    row_max = jnp.maximum(
        jnp.max(score_cache, axis=-1, keepdims=True), jnp.max(score_new, axis=-1, keepdims=True)
    )
    exp_cache = jnp.where(cache_mask[None, None], jnp.exp(score_cache - row_max), 0.0)
    exp_new = jnp.where(new_mask[None, None], jnp.exp(score_new - row_max), 0.0)
    total = jnp.sum(exp_cache, axis=-1, keepdims=True) + jnp.sum(exp_new, axis=-1, keepdims=True)
    prob_cache = (exp_cache / total).astype(jnp.bfloat16)
    prob_new = (exp_new / total).astype(jnp.bfloat16)
    mixed = jnp.einsum(
        "kgtn,knh->tkgh", prob_cache, values_cache, preferred_element_type=jnp.float32
    )
    mixed = mixed + jnp.einsum(
        "kgts,skh->tkgh", prob_new, values_new, preferred_element_type=jnp.float32
    )
    return mixed.astype(jnp.bfloat16).reshape(queries.shape[0], -1)


def expert_apply(blocks, gate_weight, up_weight, down_weight):
    local_experts = gate_weight.shape[0]
    sources = blocks.shape[0] // local_experts
    slot_count = blocks.shape[1]
    grouped = blocks.reshape(sources, local_experts, slot_count, blocks.shape[2])
    gate_acts = jnp.einsum(
        "sekd,edf->sekf", grouped, gate_weight, preferred_element_type=jnp.float32
    )
    up_acts = jnp.einsum("sekd,edf->sekf", grouped, up_weight, preferred_element_type=jnp.float32)
    hidden_act = (jax.nn.silu(gate_acts) * up_acts).astype(jnp.bfloat16)
    part_sums = jnp.einsum(
        "sekf,efd->sekd", hidden_act, down_weight, preferred_element_type=jnp.float32
    ).astype(jnp.bfloat16)
    return part_sums.reshape(sources * local_experts, slot_count, part_sums.shape[3])


def build_buffer(normed, slot_index, top_count, expert_count, capacity):
    picked = jnp.repeat(normed, top_count, axis=0)
    buffer_rows = (
        jnp.zeros((expert_count * capacity, normed.shape[1]), normed.dtype)
        .at[slot_index]
        .set(picked)
    )
    return buffer_rows.reshape(expert_count, capacity, normed.shape[1])


def weigh_back(returned, slot_index, route_weights, token_count, top_count):
    row_width = returned.shape[2]
    back_rows = returned.reshape(returned.shape[0] * returned.shape[1], row_width)[slot_index]
    weighted = (
        back_rows.astype(jnp.float32) * route_weights.reshape(token_count * top_count)[:, None]
    )
    return jnp.sum(weighted.reshape(token_count, top_count, row_width), axis=1)


LANES = 128
VMEM = pl.BlockSpec(memory_space=pltpu.VMEM)
SMEM = pl.BlockSpec(memory_space=pltpu.SMEM)
VMEM_LIMIT = 24 * 1024 * 1024


def flip(value, axis, bits):
    return lax.ppermute(value, axis, [(i, i ^ bits) for i in range(lax.axis_size(axis))])


def attention_kernel(*refs):
    pieces, hbm_refs, (keep_out, near_out, far_out, cross_out) = refs[:4], refs[4:16], refs[16:20]
    local_refs, value_hbm = refs[20:31], hbm_refs[11]
    (length_ref, table_ref, gain_ref, frequency_ref, q_gain_ref, k_gain_ref) = local_refs[:6]
    (q_ref, k_ref, v_ref, key_ref, o_ref) = local_refs[6:]
    (
        value_ref, x_ref, query_ref, own_scores, top_ref, scores_ref, mix_ref, mixed_ref, part_ref,
        owner_ref, slots_ref, page_owner, page_live, sems,
    ) = refs[31:]
    tokens, head_dim = x_ref.shape[0], k_gain_ref.shape[1]
    targets = (*local_refs, value_ref.at[:, :, :head_dim])
    copies = [
        pltpu.make_async_copy(source, target, sems.at[i])
        for i, (source, target) in enumerate(zip(hbm_refs, targets))
    ]
    for copy in copies:
        copy.start()
    tp_index = lax.axis_index("tp")
    heads = q_ref.shape[1] // head_dim
    decodes = tokens - PRE
    rows = heads * tokens
    value_ref[:, :, head_dim:] = jnp.ones((POOL, PAGE, head_dim), jnp.bfloat16)
    for step, piece in enumerate(pieces):
        width = piece.shape[1]
        start = pl.multiple_of((tp_index ^ step) * width, width)
        x_ref[:, pl.ds(start, width)] = piece[...]
    for copy in copies[:6]:
        copy.wait()
    token = lax.broadcasted_iota(jnp.int32, (tokens, head_dim), 0)
    lane = lax.broadcasted_iota(jnp.int32, (tokens, head_dim), 1)
    position = length_ref[0] + token
    for i in range(decodes):
        position = jnp.where(token == PRE + i, length_ref[i + 1], position)
    angle = position.astype(jnp.float32) * frequency_ref[...]
    cosine, sine = jnp.cos(angle), jnp.sin(angle)
    sine = jnp.where(lane < head_dim // 2, -sine, sine)

    def turned(values, gain):
        values = rms_scale(values, gain)
        return values * cosine + pltpu.roll(values, head_dim // 2, 1) * sine

    normed = rms_scale(x_ref[...].astype(jnp.float32), gain_ref[...]).astype(jnp.bfloat16)
    contract = (((1,), (1,)), ((), ()))
    for copy in copies[6:9]:
        copy.wait()
    key_lin = jnp.dot(normed, k_ref[...], preferred_element_type=jnp.float32)
    values_new = jnp.dot(normed, v_ref[...], preferred_element_type=jnp.float32).astype(jnp.bfloat16)
    query_lin = jnp.dot(normed, q_ref[...], preferred_element_type=jnp.float32)
    keys_new = turned(key_lin, k_gain_ref[...]).astype(jnp.bfloat16)
    values_new = jnp.concatenate([values_new, jnp.ones_like(values_new)], axis=1)
    to_log2 = math.log2(math.e) / math.sqrt(head_dim)
    own_mask = (lane == token) | ((lane < token) & (token < PRE))
    decode_query, decode_own = [], []
    for head in range(heads):
        span = slice(head * tokens, (head + 1) * tokens)
        query = turned(query_lin[:, head * head_dim : (head + 1) * head_dim], q_gain_ref[...]) * to_log2
        rounded = query.astype(jnp.bfloat16)
        query_ref[span, :] = rounded
        scores = lax.dot_general(rounded, keys_new, contract, preferred_element_type=jnp.float32)
        scores = jnp.where(own_mask, scores, -1e30)
        own_scores[span, :] = scores
        top_ref[span, :] = scores
        decode_query.append(query[PRE:])
        decode_own.append(scores[PRE:])
    decode_query = jnp.concatenate(decode_query, axis=0).astype(jnp.bfloat16)
    decode_own = jnp.concatenate(decode_own, axis=0)
    for page in range(POOL):
        page_owner[page] = -1
        page_live[page] = 0
    for request in range(1, REQS_DEV):

        def name_page(entry, carry):
            page = table_ref[request, entry]
            page_owner[page] = request
            page_live[page] = jnp.minimum(length_ref[request] - entry * PAGE, PAGE)
            return carry

        lax.fori_loop(0, (length_ref[request] + PAGE - 1) // PAGE, name_page, 0)
    slot = lax.broadcasted_iota(jnp.int32, (1, PAGE), 1)
    for page in range(POOL):
        owner_ref[:, page * PAGE : (page + 1) * PAGE] = jnp.where(
            slot < page_live[page], page_owner[page], -1
        )
    copies[9].wait()
    pages = scores_ref.shape[2] // PAGE
    width = pages * PAGE
    length = length_ref[0]
    steps = (length + width - 1) // width
    column = lax.broadcasted_iota(jnp.int32, (1, width), 1)

    def named(ref, step):
        names = [table_ref[0, jnp.minimum(step * pages + i, MAXPG - 1)] for i in range(pages)]
        return jnp.concatenate([ref[name] for name in names], axis=0)

    def score(step, carry):
        scores = lax.dot_general(
            query_ref[...], named(key_ref, step), contract, preferred_element_type=jnp.float32
        )
        scores = jnp.where(column + step * width < length, scores, -1e30)
        scores_ref[step] = scores
        top = top_ref[...]
        for page in range(pages):
            top = jnp.maximum(top, scores[:, page * PAGE : (page + 1) * PAGE])
        top_ref[...] = top
        return carry

    lax.fori_loop(0, steps, score, 0)
    row_request = 1 + lax.broadcasted_iota(jnp.int32, (heads * decodes, 1), 0) % decodes
    top = decode_own
    span = 8 * PAGE
    for start in range(0, POOL * PAGE, span):
        keys = key_ref[start // PAGE : (start + span) // PAGE].reshape(span, head_dim)
        scores = lax.dot_general(decode_query, keys, contract, preferred_element_type=jnp.float32)
        scores = jnp.where(owner_ref[:, start : start + span] == row_request, scores, -1e30)
        slots_ref[:, start : start + span] = scores
        for page in range(8):
            top = jnp.maximum(top, scores[:, page * PAGE : (page + 1) * PAGE])
    top = jnp.max(top, axis=1, keepdims=True)
    copies[11].wait()
    decode_mix = jnp.dot(
        jnp.exp2(decode_own - top).astype(jnp.bfloat16), values_new, preferred_element_type=jnp.float32
    )
    for start in range(0, POOL * PAGE, span):
        weights = jnp.exp2(slots_ref[:, start : start + span] - top).astype(jnp.bfloat16)
        values = value_ref[start // PAGE : (start + span) // PAGE].reshape(span, 2 * head_dim)
        decode_mix = decode_mix + jnp.dot(weights, values, preferred_element_type=jnp.float32)
    decoded = decode_mix[:, :head_dim] / decode_mix[:, head_dim:]
    top = jnp.max(top_ref[...], axis=1, keepdims=True)
    top_ref[...] = jnp.broadcast_to(top, top_ref.shape)
    mix_ref[...] = jnp.dot(
        jnp.exp2(own_scores[...] - top).astype(jnp.bfloat16), values_new, preferred_element_type=jnp.float32
    )

    def mix(step, carry):
        weights = jnp.exp2(scores_ref[step] - top_ref[:, :1]).astype(jnp.bfloat16)
        mix_ref[...] += jnp.dot(weights, named(value_ref, step), preferred_element_type=jnp.float32)
        return carry

    lax.fori_loop(0, steps, mix, 0)
    for head in range(heads):
        part = mix_ref[head * tokens : (head + 1) * tokens, :]
        columns = slice(head * head_dim, (head + 1) * head_dim)
        mixed_ref[:, columns] = part[:, :head_dim] / part[:, head_dim:]
        mixed_ref[PRE:, columns] = decoded[head * decodes : (head + 1) * decodes]
    copies[10].wait()
    part_ref[...] = jnp.dot(
        mixed_ref[...].astype(jnp.bfloat16), o_ref[...], preferred_element_type=jnp.float32
    )
    share_rows = keep_out.shape[0]
    for step, out_ref in enumerate((keep_out, near_out, far_out, cross_out)):
        mine = pl.ds(pl.multiple_of((tp_index ^ step) * share_rows, share_rows), share_rows)
        part = part_ref[mine, :]
        if step == 0:
            part = part + x_ref[mine, :].astype(jnp.float32)
        out_ref[...] = part.astype(out_ref.dtype)


def attention_shares(
    hidden_in, norm_in_gain, q_weight, k_weight, v_weight, q_gain, k_gain, o_weight,
    key_pages, value_pages, page_table, cache_len,
):
    far = flip(hidden_in, "tp", 2)
    pieces = (hidden_in, flip(hidden_in, "tp", 1), far, flip(far, "tp", 1))
    tokens, width = hidden_in.shape[0], 4 * hidden_in.shape[1]
    head_dim = q_gain.shape[0]
    rows = q_weight.shape[1] // head_dim * tokens
    decode_rows = rows // tokens * (tokens - PRE)
    half = ROPE_BASE ** (-np.arange(head_dim // 2) / (head_dim // 2))
    frequency = jnp.asarray(np.concatenate([half, half])[None, :], jnp.float32)
    scalars = (cache_len, page_table)
    arrays = (
        norm_in_gain[None, :], frequency, q_gain[None, :], k_gain[None, :],
        q_weight, k_weight, v_weight, key_pages[0], o_weight,
    )
    share = (tokens // 4, width)
    score_pages = 4
    return pl.pallas_call(
        attention_kernel,
        out_shape=[jax.ShapeDtypeStruct(share, jnp.float32)]
        + [jax.ShapeDtypeStruct(share, jnp.bfloat16)] * 3,
        in_specs=[VMEM] * 4 + [pl.BlockSpec(memory_space=pltpu.HBM)] * 12,
        out_specs=[VMEM] * 4,
        scratch_shapes=[pltpu.SMEM(array.shape, array.dtype) for array in scalars]
        + [pltpu.VMEM(array.shape, array.dtype) for array in arrays]
        + [
            pltpu.VMEM((POOL, PAGE, 2 * head_dim), jnp.bfloat16),
            pltpu.VMEM((tokens, width), jnp.bfloat16),
            pltpu.VMEM((rows, head_dim), jnp.bfloat16),
            pltpu.VMEM((rows, tokens), jnp.float32),
            pltpu.VMEM((rows, head_dim), jnp.float32),
            pltpu.VMEM((MAXPG // score_pages, rows, score_pages * PAGE), jnp.float32),
            pltpu.VMEM((rows, 2 * head_dim), jnp.float32),
            pltpu.VMEM((tokens, q_weight.shape[1]), jnp.float32),
            pltpu.VMEM((tokens, width), jnp.float32),
            pltpu.VMEM((1, POOL * PAGE), jnp.int32),
            pltpu.VMEM((decode_rows, POOL * PAGE), jnp.float32),
            pltpu.SMEM((POOL,), jnp.int32),
            pltpu.SMEM((POOL,), jnp.int32),
            pltpu.SemaphoreType.DMA((12,)),
        ],
        compiler_params=pltpu.CompilerParams(vmem_limit_bytes=56 * 1024 * 1024),
        name="attention",
    )(*pieces, *scalars, *arrays, value_pages[0])


def pack_kernel(
    own_ref, near_ref, far_ref, cross_ref, gain_ref, ids_ref, routes_ref,
    low_ref, high_ref, keep_ref, near_out, far_out, cross_out, residual_ref, spread_ref, rows_ref,
):
    tp_index = lax.axis_index("tp")
    share_rows, width = own_ref.shape
    share_width = keep_ref.shape[1]
    mine = pl.ds(pl.multiple_of(tp_index * share_rows, share_rows), share_rows)
    residual = (own_ref[...] + near_ref[...].astype(jnp.float32)) + (
        far_ref[...].astype(jnp.float32) + cross_ref[...].astype(jnp.float32)
    )
    residual_ref[...] = residual
    rows_ref[:, :width] = rms_scale(residual, gain_ref[...]).astype(jnp.bfloat16)
    expert = lax.broadcasted_iota(jnp.int32, (LANES, spread_ref.shape[0]), 0) % (LANES // 2)
    spread = jnp.zeros(expert.shape, jnp.float32)
    for k in range(ids_ref.shape[0]):
        spread = spread + jnp.where(expert == ids_ref[k : k + 1, :], routes_ref[k : k + 1, :], 0.0)
    spread_ref[...] = spread.T
    spread = spread_ref[mine, :]
    lane = lax.broadcasted_iota(jnp.int32, spread.shape, 1)
    high = spread.astype(jnp.bfloat16).astype(jnp.float32)
    rows_ref[:, width:] = jnp.where(lane < LANES // 2, high, spread - high).astype(jnp.bfloat16)
    low_ref[...] = rows_ref[: share_rows // 2, :]
    high_ref[...] = rows_ref[share_rows // 2 :, :]
    for step, out_ref in enumerate((keep_ref, near_out, far_out, cross_out)):
        column = pl.multiple_of((tp_index ^ step) * share_width, share_width)
        out_ref[...] = residual_ref[:, pl.ds(column, share_width)]


def experts_kernel(far_parts, *refs):
    near_ref, core_ref = refs[:2]
    far_refs, far_core_refs = refs[2 : 2 + far_parts], refs[2 + far_parts : 2 + 2 * far_parts]
    gate_ref, up_ref, down_ref, keep_ref, send_ref, rows_ref = refs[2 + 2 * far_parts :]
    req_index, tp_index = lax.axis_index("req"), lax.axis_index("tp")
    width = gate_ref.shape[1]
    units = gate_ref.shape[0] // 2
    share_width = width // 4
    for step, parts in enumerate(((near_ref,), (core_ref,), far_refs, far_core_refs)):
        level = 0
        for part in parts:
            levels, share_rows, _ = part.shape
            for i in range(levels):
                start = (4 * level + (tp_index ^ step)) * share_rows
                rows_ref[pl.ds(pl.multiple_of(start, share_rows), share_rows), :] = part[i]
                level += 1
    spread = rows_ref[:, width:].astype(jnp.float32)
    lane = lax.broadcasted_iota(jnp.int32, spread.shape, 1) % (LANES // 2)
    weights = [
        jnp.sum(jnp.where(lane == 2 * req_index + e, spread, 0.0), axis=1, keepdims=True)
        for e in range(2)
    ]
    contract = (((1,), (1,)), ((), ()))
    rows = rows_ref[:, :width]
    gate = lax.dot_general(rows, gate_ref[...], contract, preferred_element_type=jnp.float32)
    up = lax.dot_general(rows, up_ref[...], contract, preferred_element_type=jnp.float32)
    unit = lax.broadcasted_iota(jnp.int32, gate.shape, 1)
    weight = jnp.where(unit < units, weights[0], weights[1])
    acts = (gate / (1.0 + jnp.exp(-gate)) * up * weight).astype(jnp.bfloat16)
    for step in range(4):
        column = pl.multiple_of((tp_index ^ step) * share_width, share_width)
        part = jnp.dot(
            acts, down_ref[:, pl.ds(column, share_width)], preferred_element_type=jnp.float32
        )
        target = send_ref if step % 2 else keep_ref
        target[step // 2] = part.reshape(target.shape[1:]).astype(target.dtype)


def run_experts(near, core, far, far_core, weights):
    levels, share_rows, packed = near.shape
    units, width = weights[2].shape
    rows = 4 * levels * share_rows
    out_shape = (2, levels, 4 * share_rows, width // 4)
    return pl.pallas_call(
        functools.partial(experts_kernel, len(far)),
        out_shape=[
            jax.ShapeDtypeStruct(out_shape, jnp.float32),
            jax.ShapeDtypeStruct(out_shape, jnp.bfloat16),
        ],
        in_specs=[VMEM] * (5 + 2 * len(far)),
        out_specs=[VMEM] * 2,
        scratch_shapes=[pltpu.VMEM((rows, packed), jnp.bfloat16)],
        compiler_params=pltpu.CompilerParams(vmem_limit_bytes=VMEM_LIMIT),
        cost_estimate=pl.CostEstimate(
            flops=6 * rows * width * units,
            bytes_accessed=6 * width * units + 5 * rows * width,
            transcendentals=rows * units,
        ),
        name="experts",
    )(near, core, *far, *far_core, *weights)


def finish_kernel(*refs):
    tp_index = lax.axis_index("tp")
    halves, residual_refs, out_ref = (refs[:6], refs[6:12]), refs[12:16], refs[16]
    count = refs[0].shape[1] // 4
    for half, (own_ref, x_ref, y_ref, *z_refs) in enumerate(halves):
        for step, residual_ref in enumerate(residual_refs):
            index = tp_index ^ step
            rows = pl.ds(pl.multiple_of(index * count, count), count)
            total = own_ref[0, rows, :] + residual_ref[half * count : (half + 1) * count, :]
            for extra_ref in (x_ref, y_ref):
                total = total + extra_ref[0, rows, :].astype(jnp.float32)
            for extra_ref in z_refs:
                total = total + extra_ref[rows, :].astype(jnp.float32)
            target = pl.ds(pl.multiple_of((2 * index + half) * count, count), count)
            out_ref[target, :] = total.astype(jnp.bfloat16)


def ordered(*values):
    return lax.optimization_barrier(values)


def z_line(rows):
    return [rows] + [flip(rows, "req", 2 * bits) for bits in (1, 2, 3)]


def across_parts(line_x, line_y):
    return flip(line_x[:2], "tp", 2), flip(line_y[2:], "req", 1)


def other_core(parts):
    return tuple(flip(part, "tp", 1) for part in parts)


def with_core(pair):
    return pair[0], flip(pair[1], "tp", 1)


def joined(pair, y):
    return pair[0][y] + pair[1][y].astype(jnp.float32)


def relayed(side):
    part = joined(side, 1).astype(jnp.bfloat16)
    return flip(part[:2], "req", 1), flip(part[2:], "tp", 2)


def neighbours(near, side, by_x, by_y):
    to_y, to_x = joined(near, 1), joined(side, 0)
    to_y = jnp.concatenate([to_y[:2] + by_x.astype(jnp.float32), to_y[2:]])
    to_x = jnp.concatenate([to_x[:2], to_x[2:] + by_y.astype(jnp.float32)])
    return flip(to_x.astype(jnp.bfloat16), "req", 1), flip(to_y.astype(jnp.bfloat16), "tp", 2)


def z_share(near, from_x, from_y):
    total = joined(near, 0)
    sent = (total + from_x.astype(jnp.float32) + from_y.astype(jnp.float32)).astype(jnp.bfloat16)
    return [total, from_x, from_y] + [flip(sent[bits], "req", 2 * bits) for bits in (1, 2, 3)]


def moe_dense(
    kept,
    sent,
    norm_post_gain,
    expert_ids,
    route_weights,
    gate_weight,
    up_weight,
    down_weight,
):
    share_rows, width = kept.shape
    token_count, share_width = 4 * share_rows, width // 4
    received = [flip(part, "tp", bits) for bits, part in enumerate(sent, 1)]
    share_f32 = jax.ShapeDtypeStruct((share_rows, share_width), jnp.float32)
    half_rows = jax.ShapeDtypeStruct((share_rows // 2, width + LANES), jnp.bfloat16)
    rows_a, rows_b, *residuals = pl.pallas_call(
        pack_kernel,
        out_shape=[half_rows] * 2 + [share_f32] * 4,
        in_specs=[VMEM] * 7,
        out_specs=[VMEM] * 6,
        scratch_shapes=[
            pltpu.VMEM((share_rows, width), jnp.float32),
            pltpu.VMEM((token_count, LANES), jnp.float32),
            pltpu.VMEM((share_rows, width + LANES), jnp.bfloat16),
        ],
        compiler_params=pltpu.CompilerParams(vmem_limit_bytes=8 * 1024 * 1024),
        name="pack_rows",
    )(kept, *received, norm_post_gain[None, :], expert_ids.T, route_weights.T)
    gate_up = [w.transpose(0, 2, 1).reshape(-1, width) for w in (gate_weight, up_weight)]
    weights = (*gate_up, down_weight.reshape(-1, width))
    residuals = residuals[:1] + [flip(residuals[bits], "tp", bits) for bits in (1, 2, 3)]
    line_a, residuals, rows_b = ordered(z_line(rows_a), residuals, rows_b)
    line_a = jnp.stack(line_a)
    x_a, y_a, core_a, line_b = ordered(
        flip(line_a, "req", 1), flip(line_a, "tp", 2), flip(line_a, "tp", 1), z_line(rows_b)
    )
    line_b = jnp.stack(line_b)
    across_a = across_parts(x_a, y_a)
    x_b, y_b = flip(line_b, "req", 1), flip(line_b, "tp", 2)
    y_core_a = flip(y_a, "tp", 1)
    near_a = run_experts(line_a, core_a, (y_a,), (y_core_a,), weights)
    near_a, across_a, x_b, y_b = ordered(near_a, across_a, x_b, y_b)
    across_b = across_parts(x_b, y_b)
    side_a = run_experts(x_a, flip(x_a, "tp", 1), across_a, other_core(across_a), weights)
    across_b, side_a, near_a, line_b, x_b, y_b = ordered(
        across_b, side_a, near_a, line_b, x_b, y_b
    )
    side_a = with_core(side_a)
    side_b = run_experts(x_b, flip(x_b, "tp", 1), across_b, other_core(across_b), weights)
    side_a, side_b, near_a, line_b, y_b = ordered(side_a, side_b, near_a, line_b, y_b)
    relay_a = relayed(side_a)
    near_a, side_b = with_core(near_a), with_core(side_b)
    core_b, y_core_b = other_core((line_b, y_b))
    near_b = run_experts(line_b, core_b, (y_b,), (y_core_b,), weights)
    sides_a = neighbours(near_a, side_a, *relay_a)
    relay_b = relayed(side_b)
    near_b = with_core(near_b)
    sides_a, relay_b, near_b = ordered(sides_a, relay_b, near_b)
    sides_b = neighbours(near_b, side_b, *relay_b)
    parts_a = z_share(near_a, *sides_a)
    sides_b, parts_a = ordered(sides_b, parts_a)
    parts_b = z_share(near_b, *sides_b)
    return pl.pallas_call(
        finish_kernel,
        out_shape=jax.ShapeDtypeStruct((token_count, share_width), jnp.bfloat16),
        in_specs=[VMEM] * 16,
        out_specs=VMEM,
        compiler_params=pltpu.CompilerParams(vmem_limit_bytes=8 * 1024 * 1024),
        name="finish",
    )(*parts_a, *parts_b, *residuals)


def moe_routed(
    x_full,
    head_part,
    norm_post_gain,
    expert_ids,
    route_weights,
    gate_weight,
    up_weight,
    down_weight,
):
    req_count = lax.axis_size("req")
    tp_index = lax.axis_index("tp")
    x_float = x_full.astype(jnp.float32)
    token_count = x_float.shape[0]
    share_width = x_float.shape[1] // lax.axis_size("tp")
    top_count = expert_ids.shape[1]
    expert_count = gate_weight.shape[0] * req_count
    capacity = max(2, 3 * token_count * top_count // (2 * expert_count))
    flat_expert = expert_ids.reshape(token_count * top_count)
    one_hot = (flat_expert[:, None] == jnp.arange(expert_count, dtype=jnp.int32)[None, :]).astype(
        jnp.int32
    )
    slot_rank = jnp.sum((jnp.cumsum(one_hot, axis=0) - one_hot) * one_hot, axis=1)
    slot_index = flat_expert * capacity + slot_rank
    head_sum = lax.psum(head_part.astype(jnp.bfloat16), "tp").astype(jnp.float32)
    residual_full = x_float + head_sum
    normed_post = rms_scale(residual_full, norm_post_gain).astype(jnp.bfloat16)
    residual = lax.dynamic_slice_in_dim(residual_full, tp_index * share_width, share_width, 1)
    send_buffer = build_buffer(normed_post, slot_index, top_count, expert_count, capacity)
    part_sums = expert_apply(
        lax.all_to_all(send_buffer, "req", split_axis=0, concat_axis=0, tiled=True),
        gate_weight,
        up_weight,
        down_weight,
    )
    returned = lax.all_to_all(part_sums, "req", split_axis=0, concat_axis=0, tiled=True)
    moe_term = weigh_back(returned, slot_index, route_weights, token_count, top_count)
    moe_share = lax.psum_scatter(
        moe_term.astype(jnp.bfloat16), "tp", scatter_dimension=1, tiled=True
    ).astype(jnp.float32)
    return (residual + moe_share).astype(jnp.bfloat16)


def attention_part(
    x_full,
    norm_in_gain,
    q_weight,
    k_weight,
    v_weight,
    q_gain,
    k_gain,
    o_weight,
    key_pages,
    value_pages,
    page_table,
    cache_len,
):
    head_dim = q_gain.shape[0]
    kv_local = key_pages.shape[0]
    group_size = q_weight.shape[1] // head_dim // kv_local
    token_count = x_full.shape[0]
    x_float = x_full.astype(jnp.float32)
    normed_in = rms_scale(x_float, norm_in_gain).astype(jnp.bfloat16)
    query_lin = jnp.dot(normed_in, q_weight, preferred_element_type=jnp.float32).reshape(
        token_count, kv_local * group_size, head_dim
    )
    key_lin = jnp.dot(normed_in, k_weight, preferred_element_type=jnp.float32).reshape(
        token_count, kv_local, head_dim
    )
    values_new = (
        jnp.dot(normed_in, v_weight, preferred_element_type=jnp.float32)
        .astype(jnp.bfloat16)
        .reshape(token_count, kv_local, head_dim)
    )
    requests, positions = token_layout(cache_len)
    queries = (
        rotate(rms_scale(query_lin, q_gain), positions)
        .astype(jnp.bfloat16)
        .reshape(token_count, kv_local, group_size, head_dim)
    )
    keys_new = rotate(rms_scale(key_lin, k_gain), positions).astype(jnp.bfloat16)
    slot_owner = page_slots(page_table, cache_len)
    cache_slots = key_pages.shape[1] * key_pages.shape[2]
    keys_cache = key_pages.reshape(kv_local, cache_slots, head_dim)
    values_cache = value_pages.reshape(kv_local, cache_slots, head_dim)
    attended = attend(
        queries, keys_new, values_new, keys_cache, values_cache, requests, positions, slot_owner
    )
    return jnp.dot(attended, o_weight, preferred_element_type=jnp.float32)


def body(
    hidden_in,
    norm_in_gain,
    q_weight,
    k_weight,
    v_weight,
    q_gain,
    k_gain,
    o_weight,
    key_pages,
    value_pages,
    page_table,
    cache_len,
    norm_post_gain,
    expert_ids,
    route_weights,
    gate_weight,
    up_weight,
    down_weight,
):
    req_count = lax.axis_size("req")
    attention = (
        norm_in_gain,
        q_weight,
        k_weight,
        v_weight,
        q_gain,
        k_gain,
        o_weight,
        key_pages,
        value_pages,
        page_table,
        cache_len,
    )
    experts = (norm_post_gain, expert_ids, route_weights, gate_weight, up_weight, down_weight)
    expert_count = gate_weight.shape[0] * req_count
    staged = (req_count, lax.axis_size("tp"), gate_weight.shape[0]) == (8, 4, 2)
    if staged and expert_count <= LANES // 2:
        kept, *sent = attention_shares(hidden_in, *attention)
        return moe_dense(kept, sent, *experts)
    x_full = lax.all_gather(hidden_in, "tp", axis=1, tiled=True)
    return moe_routed(x_full, attention_part(x_full, *attention), *experts)


def solution(mesh):
    return jax.shard_map(
        body,
        mesh=mesh,
        in_specs=(
            P("req", "tp"),
            P(),
            P(None, "tp"),
            P(None, "tp"),
            P(None, "tp"),
            P(),
            P(),
            P("tp", None),
            P("tp", "req", None, None),
            P("tp", "req", None, None),
            P("req", None),
            P("req"),
            P(),
            P("req", None),
            P("req", None),
            P("req", None, "tp"),
            P("req", None, "tp"),
            P("req", "tp", None),
        ),
        out_specs=P("req", "tp"),
        check_vma=False,
    )
```

```python
import functools
import math

import jax
import jax.numpy as jnp
import numpy as np
from jax import lax
from jax.experimental import pallas as pl
from jax.experimental.pallas import tpu as pltpu
from jax.sharding import PartitionSpec as P

PAGE = 128
MAXPG = 32
PRE = 120
TOK_DEV = 128
REQS_DEV = 9
POOL = 48


NORM_EPS = 1e-06
ROPE_BASE = 1000000.0


def rms_scale(values, gain_vec):
    mean_square = jnp.mean(values * values, axis=-1, keepdims=True)
    return values * lax.rsqrt(mean_square + NORM_EPS) * gain_vec


def rotate(values, positions):
    half_dim = values.shape[-1] // 2
    exponent = jnp.arange(half_dim, dtype=jnp.float32) * (2.0 / values.shape[-1])
    frequency = jnp.power(jnp.float32(ROPE_BASE), -exponent)
    angles = positions.astype(jnp.float32)[:, None] * frequency[None, :]
    cosine = jnp.cos(angles)[:, None, :]
    sine_val = jnp.sin(angles)[:, None, :]
    front_half = values[..., :half_dim]
    back_half = values[..., half_dim:]
    return jnp.concatenate(
        [front_half * cosine - back_half * sine_val, back_half * cosine + front_half * sine_val],
        axis=-1,
    )


def token_layout(lengths):
    local_idx = jnp.arange(TOK_DEV, dtype=jnp.int32)
    requests = jnp.where(local_idx < PRE, 0, local_idx - PRE + 1)
    offsets = jnp.where(local_idx < PRE, local_idx, 0)
    request_hot = (requests[:, None] == jnp.arange(REQS_DEV, dtype=jnp.int32)[None, :]).astype(
        jnp.int32
    )
    positions = jnp.sum(request_hot * lengths[None, :], axis=1) + offsets
    return (requests, positions)


def page_slots(table, lengths):
    pages_used = (lengths + PAGE - 1) // PAGE
    entry_live = jnp.arange(MAXPG, dtype=jnp.int32)[None, :] < pages_used[:, None]
    page_match = (
        (table[:, :, None] == jnp.arange(POOL, dtype=jnp.int32)[None, None, :])
        & entry_live[:, :, None]
    ).astype(jnp.int32)
    page_owner = jnp.sum(
        page_match * jnp.arange(REQS_DEV, dtype=jnp.int32)[:, None, None], axis=(0, 1)
    )
    page_start = jnp.sum(
        page_match * (jnp.arange(MAXPG, dtype=jnp.int32) * PAGE)[None, :, None], axis=(0, 1)
    )
    page_used = jnp.sum(page_match, axis=(0, 1)) > 0
    owner_length = jnp.sum(page_match * lengths[:, None, None], axis=(0, 1))
    slot_pos = page_start[:, None] + jnp.arange(PAGE, dtype=jnp.int32)[None, :]
    slot_live = page_used[:, None] & (slot_pos < owner_length[:, None])
    slot_owner = jnp.where(slot_live, page_owner[:, None], -1)
    return slot_owner.reshape(POOL * PAGE)


def attend(
    queries, keys_new, values_new, keys_cache, values_cache, requests, positions, slot_owner
):
    inv_root = 1.0 / math.sqrt(queries.shape[-1])
    cache_mask = slot_owner[None, :] == requests[:, None]
    new_mask = (requests[None, :] == requests[:, None]) & (positions[None, :] <= positions[:, None])
    score_cache = (
        jnp.einsum("tkgh,knh->kgtn", queries, keys_cache, preferred_element_type=jnp.float32)
        * inv_root
    )
    score_new = (
        jnp.einsum("tkgh,skh->kgts", queries, keys_new, preferred_element_type=jnp.float32)
        * inv_root
    )
    score_cache = jnp.where(cache_mask[None, None], score_cache, -1e30)
    score_new = jnp.where(new_mask[None, None], score_new, -1e30)
    row_max = jnp.maximum(
        jnp.max(score_cache, axis=-1, keepdims=True), jnp.max(score_new, axis=-1, keepdims=True)
    )
    exp_cache = jnp.where(cache_mask[None, None], jnp.exp(score_cache - row_max), 0.0)
    exp_new = jnp.where(new_mask[None, None], jnp.exp(score_new - row_max), 0.0)
    total = jnp.sum(exp_cache, axis=-1, keepdims=True) + jnp.sum(exp_new, axis=-1, keepdims=True)
    prob_cache = (exp_cache / total).astype(jnp.bfloat16)
    prob_new = (exp_new / total).astype(jnp.bfloat16)
    mixed = jnp.einsum(
        "kgtn,knh->tkgh", prob_cache, values_cache, preferred_element_type=jnp.float32
    )
    mixed = mixed + jnp.einsum(
        "kgts,skh->tkgh", prob_new, values_new, preferred_element_type=jnp.float32
    )
    return mixed.astype(jnp.bfloat16).reshape(queries.shape[0], -1)


def expert_apply(blocks, gate_weight, up_weight, down_weight):
    local_experts = gate_weight.shape[0]
    sources = blocks.shape[0] // local_experts
    slot_count = blocks.shape[1]
    grouped = blocks.reshape(sources, local_experts, slot_count, blocks.shape[2])
    gate_acts = jnp.einsum(
        "sekd,edf->sekf", grouped, gate_weight, preferred_element_type=jnp.float32
    )
    up_acts = jnp.einsum("sekd,edf->sekf", grouped, up_weight, preferred_element_type=jnp.float32)
    hidden_act = (jax.nn.silu(gate_acts) * up_acts).astype(jnp.bfloat16)
    part_sums = jnp.einsum(
        "sekf,efd->sekd", hidden_act, down_weight, preferred_element_type=jnp.float32
    ).astype(jnp.bfloat16)
    return part_sums.reshape(sources * local_experts, slot_count, part_sums.shape[3])


def build_buffer(normed, slot_index, top_count, expert_count, capacity):
    picked = jnp.repeat(normed, top_count, axis=0)
    buffer_rows = (
        jnp.zeros((expert_count * capacity, normed.shape[1]), normed.dtype)
        .at[slot_index]
        .set(picked)
    )
    return buffer_rows.reshape(expert_count, capacity, normed.shape[1])


def weigh_back(returned, slot_index, route_weights, token_count, top_count):
    row_width = returned.shape[2]
    back_rows = returned.reshape(returned.shape[0] * returned.shape[1], row_width)[slot_index]
    weighted = (
        back_rows.astype(jnp.float32) * route_weights.reshape(token_count * top_count)[:, None]
    )
    return jnp.sum(weighted.reshape(token_count, top_count, row_width), axis=1)


LANES = 128
VMEM = pl.BlockSpec(memory_space=pltpu.VMEM)
SMEM = pl.BlockSpec(memory_space=pltpu.SMEM)
VMEM_LIMIT = 24 * 1024 * 1024


def flip(value, axis, bits):
    return lax.ppermute(value, axis, [(i, i ^ bits) for i in range(lax.axis_size(axis))])


def attention_kernel(*refs):
    pieces, hbm_refs, (keep_out, near_out, far_out, cross_out) = refs[:4], refs[4:16], refs[16:20]
    local_refs, value_hbm = refs[20:31], hbm_refs[11]
    (length_ref, table_ref, gain_ref, frequency_ref, q_gain_ref, k_gain_ref) = local_refs[:6]
    (q_ref, k_ref, v_ref, key_ref, o_ref) = local_refs[6:]
    (
        value_ref, x_ref, query_ref, own_scores, top_ref, scores_ref, mix_ref, mixed_ref, part_ref,
        owner_ref, slots_ref, page_owner, page_live, sems,
    ) = refs[31:]
    tokens, head_dim = x_ref.shape[0], k_gain_ref.shape[1]
    targets = (*local_refs, value_ref.at[:, :, :head_dim])
    copies = [
        pltpu.make_async_copy(source, target, sems.at[i])
        for i, (source, target) in enumerate(zip(hbm_refs, targets))
    ]
    for copy in copies:
        copy.start()
    tp_index = lax.axis_index("tp")
    heads = q_ref.shape[1] // head_dim
    decodes = tokens - PRE
    rows = heads * tokens
    value_ref[:, :, head_dim:] = jnp.ones((POOL, PAGE, head_dim), jnp.bfloat16)
    for step, piece in enumerate(pieces):
        width = piece.shape[1]
        start = pl.multiple_of((tp_index ^ step) * width, width)
        x_ref[:, pl.ds(start, width)] = piece[...]
    for copy in copies[:6]:
        copy.wait()
    token = lax.broadcasted_iota(jnp.int32, (tokens, head_dim), 0)
    lane = lax.broadcasted_iota(jnp.int32, (tokens, head_dim), 1)
    position = length_ref[0] + token
    for i in range(decodes):
        position = jnp.where(token == PRE + i, length_ref[i + 1], position)
    angle = position.astype(jnp.float32) * frequency_ref[...]
    cosine, sine = jnp.cos(angle), jnp.sin(angle)
    sine = jnp.where(lane < head_dim // 2, -sine, sine)

    def turned(values, gain):
        values = rms_scale(values, gain)
        return values * cosine + pltpu.roll(values, head_dim // 2, 1) * sine

    normed = rms_scale(x_ref[...].astype(jnp.float32), gain_ref[...]).astype(jnp.bfloat16)
    contract = (((1,), (1,)), ((), ()))
    for copy in copies[6:9]:
        copy.wait()
    key_lin = jnp.dot(normed, k_ref[...], preferred_element_type=jnp.float32)
    values_new = jnp.dot(normed, v_ref[...], preferred_element_type=jnp.float32).astype(jnp.bfloat16)
    query_lin = jnp.dot(normed, q_ref[...], preferred_element_type=jnp.float32)
    keys_new = turned(key_lin, k_gain_ref[...]).astype(jnp.bfloat16)
    values_new = jnp.concatenate([values_new, jnp.ones_like(values_new)], axis=1)
    to_log2 = math.log2(math.e) / math.sqrt(head_dim)
    own_mask = (lane == token) | ((lane < token) & (token < PRE))
    decode_query, decode_own = [], []
    for head in range(heads):
        span = slice(head * tokens, (head + 1) * tokens)
        query = turned(query_lin[:, head * head_dim : (head + 1) * head_dim], q_gain_ref[...]) * to_log2
        rounded = query.astype(jnp.bfloat16)
        query_ref[span, :] = rounded
        scores = lax.dot_general(rounded, keys_new, contract, preferred_element_type=jnp.float32)
        scores = jnp.where(own_mask, scores, -1e30)
        own_scores[span, :] = scores
        top_ref[span, :] = scores
        decode_query.append(query[PRE:])
        decode_own.append(scores[PRE:])
    decode_query = jnp.concatenate(decode_query, axis=0).astype(jnp.bfloat16)
    decode_own = jnp.concatenate(decode_own, axis=0)
    for page in range(POOL):
        page_owner[page] = -1
        page_live[page] = 0
    for request in range(1, REQS_DEV):

        def name_page(entry, carry):
            page = table_ref[request, entry]
            page_owner[page] = request
            page_live[page] = jnp.minimum(length_ref[request] - entry * PAGE, PAGE)
            return carry

        lax.fori_loop(0, (length_ref[request] + PAGE - 1) // PAGE, name_page, 0)
    slot = lax.broadcasted_iota(jnp.int32, (1, PAGE), 1)
    for page in range(POOL):
        owner_ref[:, page * PAGE : (page + 1) * PAGE] = jnp.where(
            slot < page_live[page], page_owner[page], -1
        )
    copies[9].wait()
    pages = scores_ref.shape[2] // PAGE
    width = pages * PAGE
    length = length_ref[0]
    steps = (length + width - 1) // width
    column = lax.broadcasted_iota(jnp.int32, (1, width), 1)

    def named(ref, step):
        names = [table_ref[0, jnp.minimum(step * pages + i, MAXPG - 1)] for i in range(pages)]
        return jnp.concatenate([ref[name] for name in names], axis=0)

    def score(step, carry):
        scores = lax.dot_general(
            query_ref[...], named(key_ref, step), contract, preferred_element_type=jnp.float32
        )
        scores = jnp.where(column + step * width < length, scores, -1e30)
        scores_ref[step] = scores
        top = top_ref[...]
        for page in range(pages):
            top = jnp.maximum(top, scores[:, page * PAGE : (page + 1) * PAGE])
        top_ref[...] = top
        return carry

    lax.fori_loop(0, steps, score, 0)
    row_request = 1 + lax.broadcasted_iota(jnp.int32, (heads * decodes, 1), 0) % decodes
    top = decode_own
    span = 8 * PAGE
    for start in range(0, POOL * PAGE, span):
        keys = key_ref[start // PAGE : (start + span) // PAGE].reshape(span, head_dim)
        scores = lax.dot_general(decode_query, keys, contract, preferred_element_type=jnp.float32)
        scores = jnp.where(owner_ref[:, start : start + span] == row_request, scores, -1e30)
        slots_ref[:, start : start + span] = scores
        for page in range(8):
            top = jnp.maximum(top, scores[:, page * PAGE : (page + 1) * PAGE])
    top = jnp.max(top, axis=1, keepdims=True)
    copies[11].wait()
    decode_mix = jnp.dot(
        jnp.exp2(decode_own - top).astype(jnp.bfloat16), values_new, preferred_element_type=jnp.float32
    )
    for start in range(0, POOL * PAGE, span):
        weights = jnp.exp2(slots_ref[:, start : start + span] - top).astype(jnp.bfloat16)
        values = value_ref[start // PAGE : (start + span) // PAGE].reshape(span, 2 * head_dim)
        decode_mix = decode_mix + jnp.dot(weights, values, preferred_element_type=jnp.float32)
    decoded = decode_mix[:, :head_dim] / decode_mix[:, head_dim:]
    top = jnp.max(top_ref[...], axis=1, keepdims=True)
    top_ref[...] = jnp.broadcast_to(top, top_ref.shape)
    mix_ref[...] = jnp.dot(
        jnp.exp2(own_scores[...] - top).astype(jnp.bfloat16), values_new, preferred_element_type=jnp.float32
    )

    def mix(step, carry):
        weights = jnp.exp2(scores_ref[step] - top_ref[:, :1]).astype(jnp.bfloat16)
        mix_ref[...] += jnp.dot(weights, named(value_ref, step), preferred_element_type=jnp.float32)
        return carry

    lax.fori_loop(0, steps, mix, 0)
    for head in range(heads):
        part = mix_ref[head * tokens : (head + 1) * tokens, :]
        columns = slice(head * head_dim, (head + 1) * head_dim)
        mixed_ref[:, columns] = part[:, :head_dim] / part[:, head_dim:]
        mixed_ref[PRE:, columns] = decoded[head * decodes : (head + 1) * decodes]
    copies[10].wait()
    part_ref[...] = jnp.dot(
        mixed_ref[...].astype(jnp.bfloat16), o_ref[...], preferred_element_type=jnp.float32
    )
    share_rows = keep_out.shape[0]
    for step, out_ref in enumerate((keep_out, near_out, far_out, cross_out)):
        mine = pl.ds(pl.multiple_of((tp_index ^ step) * share_rows, share_rows), share_rows)
        part = part_ref[mine, :]
        if step == 0:
            part = part + x_ref[mine, :].astype(jnp.float32)
        out_ref[...] = part.astype(out_ref.dtype)


def attention_shares(
    hidden_in, norm_in_gain, q_weight, k_weight, v_weight, q_gain, k_gain, o_weight,
    key_pages, value_pages, page_table, cache_len,
):
    far = flip(hidden_in, "tp", 2)
    pieces = (hidden_in, flip(hidden_in, "tp", 1), far, flip(far, "tp", 1))
    tokens, width = hidden_in.shape[0], 4 * hidden_in.shape[1]
    head_dim = q_gain.shape[0]
    rows = q_weight.shape[1] // head_dim * tokens
    decode_rows = rows // tokens * (tokens - PRE)
    half = ROPE_BASE ** (-np.arange(head_dim // 2) / (head_dim // 2))
    frequency = jnp.asarray(np.concatenate([half, half])[None, :], jnp.float32)
    scalars = (cache_len, page_table)
    arrays = (
        norm_in_gain[None, :], frequency, q_gain[None, :], k_gain[None, :],
        q_weight, k_weight, v_weight, key_pages[0], o_weight,
    )
    share = (tokens // 4, width)
    score_pages = 4
    return pl.pallas_call(
        attention_kernel,
        out_shape=[jax.ShapeDtypeStruct(share, jnp.float32)]
        + [jax.ShapeDtypeStruct(share, jnp.bfloat16)] * 3,
        in_specs=[VMEM] * 4 + [pl.BlockSpec(memory_space=pltpu.HBM)] * 12,
        out_specs=[VMEM] * 4,
        scratch_shapes=[pltpu.SMEM(array.shape, array.dtype) for array in scalars]
        + [pltpu.VMEM(array.shape, array.dtype) for array in arrays]
        + [
            pltpu.VMEM((POOL, PAGE, 2 * head_dim), jnp.bfloat16),
            pltpu.VMEM((tokens, width), jnp.bfloat16),
            pltpu.VMEM((rows, head_dim), jnp.bfloat16),
            pltpu.VMEM((rows, tokens), jnp.float32),
            pltpu.VMEM((rows, head_dim), jnp.float32),
            pltpu.VMEM((MAXPG // score_pages, rows, score_pages * PAGE), jnp.float32),
            pltpu.VMEM((rows, 2 * head_dim), jnp.float32),
            pltpu.VMEM((tokens, q_weight.shape[1]), jnp.float32),
            pltpu.VMEM((tokens, width), jnp.float32),
            pltpu.VMEM((1, POOL * PAGE), jnp.int32),
            pltpu.VMEM((decode_rows, POOL * PAGE), jnp.float32),
            pltpu.SMEM((POOL,), jnp.int32),
            pltpu.SMEM((POOL,), jnp.int32),
            pltpu.SemaphoreType.DMA((12,)),
        ],
        compiler_params=pltpu.CompilerParams(vmem_limit_bytes=56 * 1024 * 1024),
        name="attention",
    )(*pieces, *scalars, *arrays, value_pages[0])


def pack_kernel(
    own_ref, near_ref, far_ref, cross_ref, gain_ref, ids_ref, routes_ref,
    rows_ref, residual_ref, spread_ref,
):
    tp_index = lax.axis_index("tp")
    share_rows, width = own_ref.shape
    mine = pl.ds(pl.multiple_of(tp_index * share_rows, share_rows), share_rows)
    residual = (own_ref[...] + near_ref[...].astype(jnp.float32)) + (
        far_ref[...].astype(jnp.float32) + cross_ref[...].astype(jnp.float32)
    )
    residual_ref[...] = residual
    rows_ref[:, :width] = rms_scale(residual, gain_ref[...]).astype(jnp.bfloat16)
    expert = lax.broadcasted_iota(jnp.int32, (LANES, spread_ref.shape[0]), 0) % (LANES // 2)
    spread = jnp.zeros(expert.shape, jnp.float32)
    for k in range(ids_ref.shape[0]):
        spread = spread + jnp.where(expert == ids_ref[k : k + 1, :], routes_ref[k : k + 1, :], 0.0)
    spread_ref[...] = spread.T
    spread = spread_ref[mine, :]
    lane = lax.broadcasted_iota(jnp.int32, spread.shape, 1)
    high = spread.astype(jnp.bfloat16).astype(jnp.float32)
    rows_ref[:, width:] = jnp.where(lane < LANES // 2, high, spread - high).astype(jnp.bfloat16)


def experts_kernel(plan, *refs):
    pieces, residual_refs = refs[: len(plan)], refs[len(plan) : -7]
    gate_ref, up_ref, down_ref, keep_ref, send_ref, rows_ref, sums_ref = refs[-7:]
    req_index, tp_index = lax.axis_index("req"), lax.axis_index("tp")
    columns, _, levels, group_rows, share_width = keep_ref.shape
    width = gate_ref.shape[1]
    units = gate_ref.shape[0] // 2
    for (column, step, first), piece in zip(plan, pieces):
        count = piece.shape[1]
        for level in range(levels):
            start = (column * levels + level) * group_rows + first
            start = start + (tp_index ^ step) * (group_rows // 4)
            rows_ref[pl.ds(pl.multiple_of(start, count), count), :] = piece[level]
    spread = rows_ref[:, width:].astype(jnp.float32)
    lane = lax.broadcasted_iota(jnp.int32, spread.shape, 1) % (LANES // 2)
    weights = [
        jnp.sum(jnp.where(lane == 2 * req_index + e, spread, 0.0), axis=1, keepdims=True)
        for e in range(2)
    ]
    contract = (((1,), (1,)), ((), ()))
    rows = rows_ref[:, :width]
    gate = lax.dot_general(rows, gate_ref[...], contract, preferred_element_type=jnp.float32)
    up = lax.dot_general(rows, up_ref[...], contract, preferred_element_type=jnp.float32)
    unit = lax.broadcasted_iota(jnp.int32, gate.shape, 1)
    weight = jnp.where(unit < units, weights[0], weights[1])
    acts = (gate / (1.0 + jnp.exp(-gate)) * up * weight).astype(jnp.bfloat16)
    for step in range(4):
        start = pl.multiple_of((tp_index ^ step) * share_width, share_width)
        part = jnp.dot(
            acts, down_ref[:, pl.ds(start, share_width)], preferred_element_type=jnp.float32
        )
        for residual_ref in residual_refs:
            count = residual_ref.shape[0]
            mine = pl.ds(pl.multiple_of(tp_index * count, count), count)
            sums_ref[...] = part
            sums_ref[mine, :] += residual_ref[:, pl.ds(start, share_width)]
            part = sums_ref[...]
        target = send_ref if step % 2 else keep_ref
        part = part.reshape(columns, levels, group_rows, share_width).astype(target.dtype)
        for column in range(columns):
            target[column, step // 2] = part[column]


def run_experts(pieces, weights, group_rows, *residual):
    plan = tuple(place for place, _ in pieces)
    pieces = [piece for _, piece in pieces]
    columns, levels, packed = 1 + max(place[0] for place in plan), *pieces[0].shape[::2]
    rows, share_width = columns * levels * group_rows, weights[2].shape[1] // 4
    out_shape = (columns, 2, levels, group_rows, share_width)
    return pl.pallas_call(
        functools.partial(experts_kernel, plan),
        out_shape=[
            jax.ShapeDtypeStruct(out_shape, jnp.float32),
            jax.ShapeDtypeStruct(out_shape, jnp.bfloat16),
        ],
        in_specs=[VMEM] * (len(pieces) + len(residual) + 3),
        out_specs=[VMEM] * 2,
        scratch_shapes=[
            pltpu.VMEM((rows, packed), jnp.bfloat16),
            pltpu.VMEM((rows, share_width), jnp.float32),
        ],
        compiler_params=pltpu.CompilerParams(vmem_limit_bytes=VMEM_LIMIT),
        name="experts",
    )(*pieces, *residual, *weights)


def finish_kernel(own_ref, x_ref, y_ref, z1_ref, z2_ref, z3_ref, out_ref):
    total = own_ref[0]
    for extra_ref in (x_ref, y_ref):
        total = total + extra_ref[0].astype(jnp.float32)
    for extra_ref in (z1_ref, z2_ref, z3_ref):
        total = total + extra_ref[...].astype(jnp.float32)
    out_ref[...] = total.astype(jnp.bfloat16)


def ordered(*values):
    return lax.optimization_barrier(values)


def across_parts(line_x, line_y):
    half = line_x.shape[1] // 2
    return flip(line_x[:, :half], "tp", 2), flip(line_y[:, half:], "req", 1)


def other_core(parts):
    return tuple(flip(part, "tp", 1) for part in parts)


def with_core(pair):
    return pair[0], flip(pair[1], "tp", 1)


def joined(pair, column, y):
    return pair[0][column, y] + pair[1][column, y].astype(jnp.float32)


def near_pieces(column, line, core):
    return [((column, 0, 0), line), ((column, 1, 0), core)]


def far_pieces(column, parts, cores):
    half = parts[0].shape[1]
    if len(parts) == 1:
        return [((column, 2, 0), parts[0]), ((column, 3, 0), cores[0])]
    return [((column, 2, i * half), part) for i, part in enumerate(parts)] + [
        ((column, 3, i * half), part) for i, part in enumerate(cores)
    ]


def relayed(side):
    part = side.astype(jnp.bfloat16)
    half = part.shape[1] // 2
    return flip(part[:, :half], "req", 1), flip(part[:, half:], "tp", 2)


def neighbours(to_x, to_y, by_x, by_y):
    half = by_x.shape[1]
    to_y = jnp.concatenate([to_y[:, :half] + by_x.astype(jnp.float32), to_y[:, half:]], axis=1)
    to_x = jnp.concatenate([to_x[:, :half], to_x[:, half:] + by_y.astype(jnp.float32)], axis=1)
    return flip(to_x.astype(jnp.bfloat16), "req", 1), flip(to_y.astype(jnp.bfloat16), "tp", 2)


def moe_dense(
    kept,
    sent,
    norm_post_gain,
    expert_ids,
    route_weights,
    gate_weight,
    up_weight,
    down_weight,
):
    share_rows, width = kept.shape
    token_count, share_width = 4 * share_rows, width // 4
    received = [flip(part, "tp", bits) for bits, part in enumerate(sent, 1)]
    rows, residual = pl.pallas_call(
        pack_kernel,
        out_shape=[
            jax.ShapeDtypeStruct((share_rows, width + LANES), jnp.bfloat16),
            jax.ShapeDtypeStruct((share_rows, width), jnp.float32),
        ],
        in_specs=[VMEM] * 7,
        out_specs=[VMEM] * 2,
        scratch_shapes=[pltpu.VMEM((token_count, LANES), jnp.float32)],
        compiler_params=pltpu.CompilerParams(vmem_limit_bytes=8 * 1024 * 1024),
        name="pack_rows",
    )(kept, *received, norm_post_gain[None, :], expert_ids.T, route_weights.T)
    gate_up = [w.transpose(0, 2, 1).reshape(-1, width) for w in (gate_weight, up_weight)]
    weights = (*gate_up, down_weight.reshape(-1, width))
    line_0 = rows[None]
    levels = [flip(rows, "req", 2 * bits) for bits in (1, 2, 3)]
    y_0, x_0 = flip(line_0, "tp", 2), flip(line_0, "req", 1)
    line_3, y_0, x_0 = ordered(jnp.stack(levels), y_0, x_0)
    core_0, across_0, y_3, x_3 = ordered(
        flip(line_0, "tp", 1),
        across_parts(x_0, y_0),
        flip(line_3, "tp", 2),
        flip(line_3, "req", 1),
    )
    core_3, y_core_3, x_core_3 = other_core((line_3, y_3, x_3))
    near_3 = run_experts(
        near_pieces(0, line_3, core_3) + far_pieces(0, (y_3,), (y_core_3,)), weights, token_count
    )
    near_3, x_core_0, y_core_0, x_core_3, across_3 = ordered(
        near_3, flip(x_0, "tp", 1), flip(y_0, "tp", 1), x_core_3, across_parts(x_3, y_3)
    )
    side_3 = run_experts(
        near_pieces(0, x_3, x_core_3) + far_pieces(0, across_3, other_core(across_3)),
        weights,
        token_count,
    )
    side_3, across_core_0 = ordered(side_3, other_core(across_0))
    side_3 = with_core(side_3)
    all_0 = run_experts(
        near_pieces(0, line_0, core_0)
        + far_pieces(0, (y_0,), (y_core_0,))
        + near_pieces(1, x_0, x_core_0)
        + far_pieces(1, across_0, across_core_0),
        weights,
        token_count,
        residual,
    )
    all_0, near_3, side_3 = ordered(all_0, near_3, side_3)
    near_3, all_0, relay_3 = ordered(
        with_core(near_3), with_core(all_0), relayed(joined(side_3, 0, 1))
    )
    relay_0, sums_3 = ordered(
        relayed(joined(all_0, 1, 1)),
        neighbours(joined(side_3, 0, 0), joined(near_3, 0, 1), *relay_3),
    )
    sent = joined(near_3, 0, 0) + sums_3[0].astype(jnp.float32) + sums_3[1].astype(jnp.float32)
    sent = sent.astype(jnp.bfloat16)
    from_z = [flip(sent[bits - 1], "req", 2 * bits) for bits in (1, 2, 3)]
    sums_0 = neighbours(joined(all_0, 1, 0), joined(all_0, 0, 1), *relay_0)
    return pl.pallas_call(
        finish_kernel,
        out_shape=jax.ShapeDtypeStruct((token_count, share_width), jnp.bfloat16),
        in_specs=[VMEM] * 6,
        out_specs=VMEM,
        compiler_params=pltpu.CompilerParams(vmem_limit_bytes=8 * 1024 * 1024),
        name="finish",
    )(joined(all_0, 0, 0), *sums_0, *from_z)


def moe_routed(
    x_full,
    head_part,
    norm_post_gain,
    expert_ids,
    route_weights,
    gate_weight,
    up_weight,
    down_weight,
):
    req_count = lax.axis_size("req")
    tp_index = lax.axis_index("tp")
    x_float = x_full.astype(jnp.float32)
    token_count = x_float.shape[0]
    share_width = x_float.shape[1] // lax.axis_size("tp")
    top_count = expert_ids.shape[1]
    expert_count = gate_weight.shape[0] * req_count
    capacity = max(2, 3 * token_count * top_count // (2 * expert_count))
    flat_expert = expert_ids.reshape(token_count * top_count)
    one_hot = (flat_expert[:, None] == jnp.arange(expert_count, dtype=jnp.int32)[None, :]).astype(
        jnp.int32
    )
    slot_rank = jnp.sum((jnp.cumsum(one_hot, axis=0) - one_hot) * one_hot, axis=1)
    slot_index = flat_expert * capacity + slot_rank
    head_sum = lax.psum(head_part.astype(jnp.bfloat16), "tp").astype(jnp.float32)
    residual_full = x_float + head_sum
    normed_post = rms_scale(residual_full, norm_post_gain).astype(jnp.bfloat16)
    residual = lax.dynamic_slice_in_dim(residual_full, tp_index * share_width, share_width, 1)
    send_buffer = build_buffer(normed_post, slot_index, top_count, expert_count, capacity)
    part_sums = expert_apply(
        lax.all_to_all(send_buffer, "req", split_axis=0, concat_axis=0, tiled=True),
        gate_weight,
        up_weight,
        down_weight,
    )
    returned = lax.all_to_all(part_sums, "req", split_axis=0, concat_axis=0, tiled=True)
    moe_term = weigh_back(returned, slot_index, route_weights, token_count, top_count)
    moe_share = lax.psum_scatter(
        moe_term.astype(jnp.bfloat16), "tp", scatter_dimension=1, tiled=True
    ).astype(jnp.float32)
    return (residual + moe_share).astype(jnp.bfloat16)


def attention_part(
    x_full,
    norm_in_gain,
    q_weight,
    k_weight,
    v_weight,
    q_gain,
    k_gain,
    o_weight,
    key_pages,
    value_pages,
    page_table,
    cache_len,
):
    head_dim = q_gain.shape[0]
    kv_local = key_pages.shape[0]
    group_size = q_weight.shape[1] // head_dim // kv_local
    token_count = x_full.shape[0]
    x_float = x_full.astype(jnp.float32)
    normed_in = rms_scale(x_float, norm_in_gain).astype(jnp.bfloat16)
    query_lin = jnp.dot(normed_in, q_weight, preferred_element_type=jnp.float32).reshape(
        token_count, kv_local * group_size, head_dim
    )
    key_lin = jnp.dot(normed_in, k_weight, preferred_element_type=jnp.float32).reshape(
        token_count, kv_local, head_dim
    )
    values_new = (
        jnp.dot(normed_in, v_weight, preferred_element_type=jnp.float32)
        .astype(jnp.bfloat16)
        .reshape(token_count, kv_local, head_dim)
    )
    requests, positions = token_layout(cache_len)
    queries = (
        rotate(rms_scale(query_lin, q_gain), positions)
        .astype(jnp.bfloat16)
        .reshape(token_count, kv_local, group_size, head_dim)
    )
    keys_new = rotate(rms_scale(key_lin, k_gain), positions).astype(jnp.bfloat16)
    slot_owner = page_slots(page_table, cache_len)
    cache_slots = key_pages.shape[1] * key_pages.shape[2]
    keys_cache = key_pages.reshape(kv_local, cache_slots, head_dim)
    values_cache = value_pages.reshape(kv_local, cache_slots, head_dim)
    attended = attend(
        queries, keys_new, values_new, keys_cache, values_cache, requests, positions, slot_owner
    )
    return jnp.dot(attended, o_weight, preferred_element_type=jnp.float32)


def body(
    hidden_in,
    norm_in_gain,
    q_weight,
    k_weight,
    v_weight,
    q_gain,
    k_gain,
    o_weight,
    key_pages,
    value_pages,
    page_table,
    cache_len,
    norm_post_gain,
    expert_ids,
    route_weights,
    gate_weight,
    up_weight,
    down_weight,
):
    req_count = lax.axis_size("req")
    attention = (
        norm_in_gain,
        q_weight,
        k_weight,
        v_weight,
        q_gain,
        k_gain,
        o_weight,
        key_pages,
        value_pages,
        page_table,
        cache_len,
    )
    experts = (norm_post_gain, expert_ids, route_weights, gate_weight, up_weight, down_weight)
    expert_count = gate_weight.shape[0] * req_count
    staged = (req_count, lax.axis_size("tp"), gate_weight.shape[0]) == (8, 4, 2)
    if staged and expert_count <= LANES // 2:
        kept, *sent = attention_shares(hidden_in, *attention)
        return moe_dense(kept, sent, *experts)
    x_full = lax.all_gather(hidden_in, "tp", axis=1, tiled=True)
    return moe_routed(x_full, attention_part(x_full, *attention), *experts)


def solution(mesh):
    return jax.shard_map(
        body,
        mesh=mesh,
        in_specs=(
            P("req", "tp"),
            P(),
            P(None, "tp"),
            P(None, "tp"),
            P(None, "tp"),
            P(),
            P(),
            P("tp", None),
            P("tp", "req", None, None),
            P("tp", "req", None, None),
            P("req", None),
            P("req"),
            P(),
            P("req", None),
            P("req", None),
            P("req", None, "tp"),
            P("req", None, "tp"),
            P("req", "tp", None),
        ),
        out_specs=P("req", "tp"),
        check_vma=False,
    )
```

```python
import functools
import math

import jax
import jax.numpy as jnp
import numpy as np
from jax import lax
from jax.experimental import pallas as pl
from jax.experimental.pallas import tpu as pltpu
from jax.sharding import PartitionSpec as P

PAGE = 128
MAXPG = 32
PRE = 120
TOK_DEV = 128
REQS_DEV = 9
POOL = 48


NORM_EPS = 1e-06
ROPE_BASE = 1000000.0


def rms_scale(values, gain_vec):
    mean_square = jnp.mean(values * values, axis=-1, keepdims=True)
    return values * lax.rsqrt(mean_square + NORM_EPS) * gain_vec


def rotate(values, positions):
    half_dim = values.shape[-1] // 2
    exponent = jnp.arange(half_dim, dtype=jnp.float32) * (2.0 / values.shape[-1])
    frequency = jnp.power(jnp.float32(ROPE_BASE), -exponent)
    angles = positions.astype(jnp.float32)[:, None] * frequency[None, :]
    cosine = jnp.cos(angles)[:, None, :]
    sine_val = jnp.sin(angles)[:, None, :]
    front_half = values[..., :half_dim]
    back_half = values[..., half_dim:]
    return jnp.concatenate(
        [front_half * cosine - back_half * sine_val, back_half * cosine + front_half * sine_val],
        axis=-1,
    )


def token_layout(lengths):
    local_idx = jnp.arange(TOK_DEV, dtype=jnp.int32)
    requests = jnp.where(local_idx < PRE, 0, local_idx - PRE + 1)
    offsets = jnp.where(local_idx < PRE, local_idx, 0)
    request_hot = (requests[:, None] == jnp.arange(REQS_DEV, dtype=jnp.int32)[None, :]).astype(
        jnp.int32
    )
    positions = jnp.sum(request_hot * lengths[None, :], axis=1) + offsets
    return (requests, positions)


def page_slots(table, lengths):
    pages_used = (lengths + PAGE - 1) // PAGE
    entry_live = jnp.arange(MAXPG, dtype=jnp.int32)[None, :] < pages_used[:, None]
    page_match = (
        (table[:, :, None] == jnp.arange(POOL, dtype=jnp.int32)[None, None, :])
        & entry_live[:, :, None]
    ).astype(jnp.int32)
    page_owner = jnp.sum(
        page_match * jnp.arange(REQS_DEV, dtype=jnp.int32)[:, None, None], axis=(0, 1)
    )
    page_start = jnp.sum(
        page_match * (jnp.arange(MAXPG, dtype=jnp.int32) * PAGE)[None, :, None], axis=(0, 1)
    )
    page_used = jnp.sum(page_match, axis=(0, 1)) > 0
    owner_length = jnp.sum(page_match * lengths[:, None, None], axis=(0, 1))
    slot_pos = page_start[:, None] + jnp.arange(PAGE, dtype=jnp.int32)[None, :]
    slot_live = page_used[:, None] & (slot_pos < owner_length[:, None])
    slot_owner = jnp.where(slot_live, page_owner[:, None], -1)
    return slot_owner.reshape(POOL * PAGE)


def attend(
    queries, keys_new, values_new, keys_cache, values_cache, requests, positions, slot_owner
):
    inv_root = 1.0 / math.sqrt(queries.shape[-1])
    cache_mask = slot_owner[None, :] == requests[:, None]
    new_mask = (requests[None, :] == requests[:, None]) & (positions[None, :] <= positions[:, None])
    score_cache = (
        jnp.einsum("tkgh,knh->kgtn", queries, keys_cache, preferred_element_type=jnp.float32)
        * inv_root
    )
    score_new = (
        jnp.einsum("tkgh,skh->kgts", queries, keys_new, preferred_element_type=jnp.float32)
        * inv_root
    )
    score_cache = jnp.where(cache_mask[None, None], score_cache, -1e30)
    score_new = jnp.where(new_mask[None, None], score_new, -1e30)
    row_max = jnp.maximum(
        jnp.max(score_cache, axis=-1, keepdims=True), jnp.max(score_new, axis=-1, keepdims=True)
    )
    exp_cache = jnp.where(cache_mask[None, None], jnp.exp(score_cache - row_max), 0.0)
    exp_new = jnp.where(new_mask[None, None], jnp.exp(score_new - row_max), 0.0)
    total = jnp.sum(exp_cache, axis=-1, keepdims=True) + jnp.sum(exp_new, axis=-1, keepdims=True)
    prob_cache = (exp_cache / total).astype(jnp.bfloat16)
    prob_new = (exp_new / total).astype(jnp.bfloat16)
    mixed = jnp.einsum(
        "kgtn,knh->tkgh", prob_cache, values_cache, preferred_element_type=jnp.float32
    )
    mixed = mixed + jnp.einsum(
        "kgts,skh->tkgh", prob_new, values_new, preferred_element_type=jnp.float32
    )
    return mixed.astype(jnp.bfloat16).reshape(queries.shape[0], -1)


def expert_apply(blocks, gate_weight, up_weight, down_weight):
    local_experts = gate_weight.shape[0]
    sources = blocks.shape[0] // local_experts
    slot_count = blocks.shape[1]
    grouped = blocks.reshape(sources, local_experts, slot_count, blocks.shape[2])
    gate_acts = jnp.einsum(
        "sekd,edf->sekf", grouped, gate_weight, preferred_element_type=jnp.float32
    )
    up_acts = jnp.einsum("sekd,edf->sekf", grouped, up_weight, preferred_element_type=jnp.float32)
    hidden_act = (jax.nn.silu(gate_acts) * up_acts).astype(jnp.bfloat16)
    part_sums = jnp.einsum(
        "sekf,efd->sekd", hidden_act, down_weight, preferred_element_type=jnp.float32
    ).astype(jnp.bfloat16)
    return part_sums.reshape(sources * local_experts, slot_count, part_sums.shape[3])


def build_buffer(normed, slot_index, top_count, expert_count, capacity):
    picked = jnp.repeat(normed, top_count, axis=0)
    buffer_rows = (
        jnp.zeros((expert_count * capacity, normed.shape[1]), normed.dtype)
        .at[slot_index]
        .set(picked)
    )
    return buffer_rows.reshape(expert_count, capacity, normed.shape[1])


def weigh_back(returned, slot_index, route_weights, token_count, top_count):
    row_width = returned.shape[2]
    back_rows = returned.reshape(returned.shape[0] * returned.shape[1], row_width)[slot_index]
    weighted = (
        back_rows.astype(jnp.float32) * route_weights.reshape(token_count * top_count)[:, None]
    )
    return jnp.sum(weighted.reshape(token_count, top_count, row_width), axis=1)


LANES = 128
VMEM = pl.BlockSpec(memory_space=pltpu.VMEM)
SMEM = pl.BlockSpec(memory_space=pltpu.SMEM)
VMEM_LIMIT = 24 * 1024 * 1024


def flip(value, axis, bits):
    return lax.ppermute(value, axis, [(i, i ^ bits) for i in range(lax.axis_size(axis))])


def layout_kernel(
    length_ref, table_ref, frequency_ref, cosine_ref, sine_ref, owner_ref, list_ref, count_ref, live_ref
):
    tokens, head_dim = cosine_ref.shape
    slots = list_ref.shape[0]
    owners = live_ref
    for entry in range(slots):
        list_ref[entry] = 0
        owners[0, entry] = -1
        owners[1, entry] = 0
    count = jnp.int32(0)
    for request in range(1, REQS_DEV):

        def name_page(entry, count):
            list_ref[count] = table_ref[request, entry]
            owners[0, count] = request
            owners[1, count] = jnp.minimum(length_ref[request] - entry * PAGE, PAGE)
            return count + 1

        count = lax.fori_loop(0, (length_ref[request] + PAGE - 1) // PAGE, name_page, count)
    count_ref[0] = count
    slot = lax.broadcasted_iota(jnp.int32, (1, PAGE), 1)
    for entry in range(slots):
        owner_ref[:, entry * PAGE : (entry + 1) * PAGE] = jnp.where(
            slot < owners[1, entry], owners[0, entry], -1
        )
    token = lax.broadcasted_iota(jnp.int32, (tokens, head_dim), 0)
    lane = lax.broadcasted_iota(jnp.int32, (tokens, head_dim), 1)
    position = length_ref[0] + token
    for i in range(tokens - PRE):
        position = jnp.where(token == PRE + i, length_ref[i + 1], position)
    angle = position.astype(jnp.float32) * frequency_ref[...]
    sine = jnp.sin(angle)
    cosine_ref[...] = jnp.cos(angle)
    sine_ref[...] = jnp.where(lane < head_dim // 2, -sine, sine)


def attention_kernel(*refs):
    pieces, hbm_refs, (keep_out, far_out, core_out) = refs[:4], refs[4:20], refs[20:23]
    local_refs = refs[23:39]
    (length_ref, table_ref, list_ref, count_ref, gain_ref, q_gain_ref, k_gain_ref) = local_refs[:7]
    (cosine_ref, sine_ref, owner_ref, q_ref, k_ref, v_ref, key_ref, value_ref, o_ref) = local_refs[7:]
    (
        x_ref, query_ref, own_scores, top_ref, scores_ref, mix_ref, mixed_ref, part_ref, slots_ref,
        decode_top, decode_mix, sems,
    ) = refs[39:]
    tokens, head_dim = x_ref.shape[0], k_gain_ref.shape[1]
    copies = [
        pltpu.make_async_copy(source, target, sems.at[i])
        for i, (source, target) in enumerate(zip(hbm_refs, local_refs))
    ]
    for copy in copies:
        copy.start()
    tp_index = lax.axis_index("tp")
    heads = q_ref.shape[1] // head_dim
    decodes = tokens - PRE
    for step, piece in enumerate(pieces):
        width = piece.shape[1]
        start = pl.multiple_of((tp_index ^ step) * width, width)
        x_ref[:, pl.ds(start, width)] = piece[...]
    for copy in copies[:10]:
        copy.wait()
    token = lax.broadcasted_iota(jnp.int32, (tokens, head_dim), 0)
    lane = lax.broadcasted_iota(jnp.int32, (tokens, head_dim), 1)

    def turned(values, gain):
        values = rms_scale(values, gain)
        return values * cosine_ref[...] + pltpu.roll(values, head_dim // 2, 1) * sine_ref[...]

    def with_ones(values):
        return jnp.concatenate([values, jnp.ones_like(values)], axis=1)

    normed = rms_scale(x_ref[...].astype(jnp.float32), gain_ref[...]).astype(jnp.bfloat16)
    contract = (((1,), (1,)), ((), ()))
    for copy in copies[10:13]:
        copy.wait()
    key_lin = jnp.dot(normed, k_ref[...], preferred_element_type=jnp.float32)
    values_new = jnp.dot(normed, v_ref[...], preferred_element_type=jnp.float32).astype(jnp.bfloat16)
    query_lin = jnp.dot(normed, q_ref[...], preferred_element_type=jnp.float32)
    keys_new = turned(key_lin, k_gain_ref[...]).astype(jnp.bfloat16)
    values_new = with_ones(values_new)
    to_log2 = math.log2(math.e) / math.sqrt(head_dim)
    own_mask = (lane == token) | ((lane < token) & (token < PRE))
    decode_query, decode_own = [], []
    for head in range(heads):
        span = slice(head * tokens, (head + 1) * tokens)
        query = turned(query_lin[:, head * head_dim : (head + 1) * head_dim], q_gain_ref[...]) * to_log2
        rounded = query.astype(jnp.bfloat16)
        query_ref[span, :] = rounded
        scores = lax.dot_general(rounded, keys_new, contract, preferred_element_type=jnp.float32)
        scores = jnp.where(own_mask, scores, -1e30)
        own_scores[span, :] = scores
        top_ref[span, :] = scores
        decode_query.append(query[PRE:])
        decode_own.append(scores[PRE:])
    decode_query = jnp.concatenate(decode_query, axis=0).astype(jnp.bfloat16)
    decode_own = jnp.concatenate(decode_own, axis=0)
    for copy in copies[13:15]:
        copy.wait()

    def raised(top, scores):
        for start in range(0, scores.shape[1], head_dim):
            top = jnp.maximum(top, scores[:, start : start + head_dim])
        return top

    pages = scores_ref.shape[2] // PAGE
    width = pages * PAGE
    length = length_ref[0]
    steps = (length + width - 1) // width
    column = lax.broadcasted_iota(jnp.int32, (1, width), 1)

    def own_pages(ref, step):
        names = [table_ref[0, jnp.minimum(step * pages + i, MAXPG - 1)] for i in range(pages)]
        return jnp.concatenate([ref[name] for name in names], axis=0)

    def score(step, carry):
        scores = lax.dot_general(
            query_ref[...], own_pages(key_ref, step), contract, preferred_element_type=jnp.float32
        )
        scores = jnp.where(column + step * width < length, scores, -1e30)
        scores_ref[step] = scores
        top_ref[...] = raised(top_ref[...], scores)
        return carry

    lax.fori_loop(0, steps, score, 0)
    listed = slots_ref.shape[2] // PAGE
    decode_steps = (count_ref[0] + listed - 1) // listed
    row_request = 1 + lax.broadcasted_iota(jnp.int32, (heads * decodes, 1), 0) % decodes
    decode_top[...] = decode_own

    def listed_pages(ref, step):
        return jnp.concatenate([ref[list_ref[step * listed + i]] for i in range(listed)], axis=0)

    def decode_score(step, carry):
        scores = lax.dot_general(
            decode_query, listed_pages(key_ref, step), contract, preferred_element_type=jnp.float32
        )
        start = pl.multiple_of(step * listed * PAGE, listed * PAGE)
        scores = jnp.where(owner_ref[:, pl.ds(start, listed * PAGE)] == row_request, scores, -1e30)
        slots_ref[step] = scores
        decode_top[...] = raised(decode_top[...], scores)
        return carry

    lax.fori_loop(0, decode_steps, decode_score, 0)
    top = jnp.max(decode_top[...], axis=1, keepdims=True)
    decode_mix[...] = jnp.dot(
        jnp.exp2(decode_own - top).astype(jnp.bfloat16), values_new, preferred_element_type=jnp.float32
    )

    def decode_mixed(step, carry):
        weights = jnp.exp2(slots_ref[step] - top).astype(jnp.bfloat16)
        decode_mix[...] += jnp.dot(
            weights, with_ones(listed_pages(value_ref, step)), preferred_element_type=jnp.float32
        )
        return carry

    lax.fori_loop(0, decode_steps, decode_mixed, 0)
    decoded = decode_mix[:, :head_dim] / decode_mix[:, head_dim:]
    top = jnp.max(top_ref[...], axis=1, keepdims=True)
    top_ref[...] = jnp.broadcast_to(top, top_ref.shape)
    mix_ref[...] = jnp.dot(
        jnp.exp2(own_scores[...] - top).astype(jnp.bfloat16), values_new, preferred_element_type=jnp.float32
    )

    def mix(step, carry):
        weights = jnp.exp2(scores_ref[step] - top_ref[:, :1]).astype(jnp.bfloat16)
        mix_ref[...] += jnp.dot(
            weights, with_ones(own_pages(value_ref, step)), preferred_element_type=jnp.float32
        )
        return carry

    lax.fori_loop(0, steps, mix, 0)
    for head in range(heads):
        part = mix_ref[head * tokens : (head + 1) * tokens, :]
        columns = slice(head * head_dim, (head + 1) * head_dim)
        mixed_ref[:, columns] = part[:, :head_dim] / part[:, head_dim:]
        mixed_ref[PRE:, columns] = decoded[head * decodes : (head + 1) * decodes]
    copies[15].wait()
    part_ref[...] = jnp.dot(
        mixed_ref[...].astype(jnp.bfloat16), o_ref[...], preferred_element_type=jnp.float32
    )
    share_rows = keep_out.shape[0]

    def quarter(step):
        return pl.ds(pl.multiple_of((tp_index ^ step) * share_rows, share_rows), share_rows)

    keep_out[...] = part_ref[quarter(0), :] + x_ref[quarter(0), :].astype(jnp.float32)
    far_out[...] = part_ref[quarter(2), :]
    core_out[0] = part_ref[quarter(1), :].astype(jnp.bfloat16)
    core_out[1] = part_ref[quarter(3), :].astype(jnp.bfloat16)


def attention_shares(
    hidden_in, norm_in_gain, q_weight, k_weight, v_weight, q_gain, k_gain, o_weight,
    key_pages, value_pages, page_table, cache_len,
):
    tokens, width = hidden_in.shape[0], 4 * hidden_in.shape[1]
    head_dim = q_gain.shape[0]
    rows = q_weight.shape[1] // head_dim * tokens
    decode_rows = rows // tokens * (tokens - PRE)
    half = ROPE_BASE ** (-np.arange(head_dim // 2) / (head_dim // 2))
    frequency = jnp.asarray(np.concatenate([half, half])[None, :], jnp.float32)
    params = pltpu.CompilerParams(vmem_limit_bytes=56 * 1024 * 1024)
    rope = jax.ShapeDtypeStruct((tokens, head_dim), jnp.float32)
    cosine, sine, owner, page_list, page_count = pl.pallas_call(
        layout_kernel,
        out_shape=[
            rope,
            rope,
            jax.ShapeDtypeStruct((1, POOL * PAGE), jnp.int32),
            jax.ShapeDtypeStruct((POOL,), jnp.int32),
            jax.ShapeDtypeStruct((1,), jnp.int32),
        ],
        in_specs=[SMEM, SMEM, VMEM],
        out_specs=[VMEM, VMEM, VMEM, SMEM, SMEM],
        scratch_shapes=[pltpu.SMEM((2, POOL), jnp.int32)],
        compiler_params=params,
        name="layout",
    )(cache_len, page_table, frequency)
    far, cosine, sine, owner, page_list, page_count = ordered(
        flip(hidden_in, "tp", 2), cosine, sine, owner, page_list, page_count
    )
    pieces = (hidden_in, flip(hidden_in, "tp", 1), far, flip(far, "tp", 1))
    scalars = (cache_len, page_table, page_list, page_count)
    arrays = (
        norm_in_gain[None, :], q_gain[None, :], k_gain[None, :], cosine, sine, owner,
        q_weight, k_weight, v_weight, key_pages[0], value_pages[0], o_weight,
    )
    share = (tokens // 4, width)
    score_pages, list_pages = 4, 8
    return pl.pallas_call(
        attention_kernel,
        out_shape=[
            jax.ShapeDtypeStruct(share, jnp.float32),
            jax.ShapeDtypeStruct(share, jnp.float32),
            jax.ShapeDtypeStruct((2, *share), jnp.bfloat16),
        ],
        in_specs=[VMEM] * 4 + [pl.BlockSpec(memory_space=pltpu.HBM)] * 16,
        out_specs=[VMEM] * 3,
        scratch_shapes=[pltpu.SMEM(array.shape, array.dtype) for array in scalars]
        + [pltpu.VMEM(array.shape, array.dtype) for array in arrays]
        + [
            pltpu.VMEM((tokens, width), jnp.bfloat16),
            pltpu.VMEM((rows, head_dim), jnp.bfloat16),
            pltpu.VMEM((rows, tokens), jnp.float32),
            pltpu.VMEM((rows, head_dim), jnp.float32),
            pltpu.VMEM((MAXPG // score_pages, rows, score_pages * PAGE), jnp.float32),
            pltpu.VMEM((rows, 2 * head_dim), jnp.float32),
            pltpu.VMEM((tokens, q_weight.shape[1]), jnp.float32),
            pltpu.VMEM((tokens, width), jnp.float32),
            pltpu.VMEM((POOL // list_pages, decode_rows, list_pages * PAGE), jnp.float32),
            pltpu.VMEM((decode_rows, head_dim), jnp.float32),
            pltpu.VMEM((decode_rows, 2 * head_dim), jnp.float32),
            pltpu.SemaphoreType.DMA((16,)),
        ],
        compiler_params=params,
        name="attention",
    )(*pieces, *scalars, *arrays)


def pack_kernel(
    own_ref, core_ref, far_ref, gain_ref, ids_ref, routes_ref,
    rows_ref, residual_ref, spread_ref,
):
    tp_index = lax.axis_index("tp")
    share_rows, width = own_ref.shape
    mine = pl.ds(pl.multiple_of(tp_index * share_rows, share_rows), share_rows)
    residual = own_ref[...] + core_ref[0].astype(jnp.float32) + far_ref[...].astype(jnp.float32)
    residual_ref[...] = residual
    rows_ref[:, :width] = rms_scale(residual, gain_ref[...]).astype(jnp.bfloat16)
    expert = lax.broadcasted_iota(jnp.int32, (LANES, spread_ref.shape[0]), 0) % (LANES // 2)
    spread = jnp.zeros(expert.shape, jnp.float32)
    for k in range(ids_ref.shape[0]):
        spread = spread + jnp.where(expert == ids_ref[k : k + 1, :], routes_ref[k : k + 1, :], 0.0)
    spread_ref[...] = spread.T
    spread = spread_ref[mine, :]
    lane = lax.broadcasted_iota(jnp.int32, spread.shape, 1)
    high = spread.astype(jnp.bfloat16).astype(jnp.float32)
    rows_ref[:, width:] = jnp.where(lane < LANES // 2, high, spread - high).astype(jnp.bfloat16)


def experts_kernel(plan, *refs):
    pieces, residual_refs = refs[: len(plan)], refs[len(plan) : -7]
    gate_ref, up_ref, down_ref, keep_ref, send_ref, rows_ref, sums_ref = refs[-7:]
    req_index, tp_index = lax.axis_index("req"), lax.axis_index("tp")
    columns, _, levels, group_rows, share_width = keep_ref.shape
    width = gate_ref.shape[1]
    units = gate_ref.shape[0] // 2
    for (column, step, first), piece in zip(plan, pieces):
        count = piece.shape[1]
        for level in range(levels):
            start = (column * levels + level) * group_rows + first
            start = start + (tp_index ^ step) * (group_rows // 4)
            rows_ref[pl.ds(pl.multiple_of(start, count), count), :] = piece[level]
    spread = rows_ref[:, width:].astype(jnp.float32)
    lane = lax.broadcasted_iota(jnp.int32, spread.shape, 1) % (LANES // 2)
    weights = [
        jnp.sum(jnp.where(lane == 2 * req_index + e, spread, 0.0), axis=1, keepdims=True)
        for e in range(2)
    ]
    contract = (((1,), (1,)), ((), ()))
    rows = rows_ref[:, :width]
    gate = lax.dot_general(rows, gate_ref[...], contract, preferred_element_type=jnp.float32)
    up = lax.dot_general(rows, up_ref[...], contract, preferred_element_type=jnp.float32)
    unit = lax.broadcasted_iota(jnp.int32, gate.shape, 1)
    weight = jnp.where(unit < units, weights[0], weights[1])
    acts = (gate / (1.0 + jnp.exp(-gate)) * up * weight).astype(jnp.bfloat16)
    for step in range(4):
        start = pl.multiple_of((tp_index ^ step) * share_width, share_width)
        part = jnp.dot(
            acts, down_ref[:, pl.ds(start, share_width)], preferred_element_type=jnp.float32
        )
        for residual_ref in residual_refs:
            count = residual_ref.shape[0]
            mine = pl.ds(pl.multiple_of(tp_index * count, count), count)
            sums_ref[...] = part
            sums_ref[mine, :] += residual_ref[:, pl.ds(start, share_width)]
            part = sums_ref[...]
        target = send_ref if step % 2 else keep_ref
        part = part.reshape(columns, levels, group_rows, share_width).astype(target.dtype)
        for column in range(columns):
            target[column, step // 2] = part[column]


def run_experts(pieces, weights, group_rows, *residual):
    plan = tuple(place for place, _ in pieces)
    pieces = [piece for _, piece in pieces]
    columns, levels, packed = 1 + max(place[0] for place in plan), *pieces[0].shape[::2]
    rows, share_width = columns * levels * group_rows, weights[2].shape[1] // 4
    out_shape = (columns, 2, levels, group_rows, share_width)
    return pl.pallas_call(
        functools.partial(experts_kernel, plan),
        out_shape=[
            jax.ShapeDtypeStruct(out_shape, jnp.float32),
            jax.ShapeDtypeStruct(out_shape, jnp.bfloat16),
        ],
        in_specs=[VMEM] * (len(pieces) + len(residual) + 3),
        out_specs=[VMEM] * 2,
        scratch_shapes=[
            pltpu.VMEM((rows, packed), jnp.bfloat16),
            pltpu.VMEM((rows, share_width), jnp.float32),
        ],
        compiler_params=pltpu.CompilerParams(vmem_limit_bytes=VMEM_LIMIT),
        name="experts",
    )(*pieces, *residual, *weights)


def finish_kernel(own_ref, x_ref, y_ref, z1_ref, z2_ref, z3_ref, out_ref):
    total = own_ref[0]
    for extra_ref in (x_ref, y_ref):
        total = total + extra_ref[0].astype(jnp.float32)
    for extra_ref in (z1_ref, z2_ref, z3_ref):
        total = total + extra_ref[...].astype(jnp.float32)
    out_ref[...] = total.astype(jnp.bfloat16)


def ordered(*values):
    return lax.optimization_barrier(values)


def across_parts(line_x, line_y):
    half = line_x.shape[1] // 2
    return flip(line_x[:, :half], "tp", 2), flip(line_y[:, half:], "req", 1)


def other_core(parts):
    return tuple(flip(part, "tp", 1) for part in parts)


def with_core(pair):
    return pair[0], flip(pair[1], "tp", 1)


def joined(pair, column, y):
    return pair[0][column, y] + pair[1][column, y].astype(jnp.float32)


def near_pieces(column, line, core):
    return [((column, 0, 0), line), ((column, 1, 0), core)]


def far_pieces(column, parts, cores):
    half = parts[0].shape[1]
    if len(parts) == 1:
        return [((column, 2, 0), parts[0]), ((column, 3, 0), cores[0])]
    return [((column, 2, i * half), part) for i, part in enumerate(parts)] + [
        ((column, 3, i * half), part) for i, part in enumerate(cores)
    ]


def relayed(side):
    part = side.astype(jnp.bfloat16)
    half = part.shape[1] // 2
    return flip(part[:, :half], "req", 1), flip(part[:, half:], "tp", 2)


def neighbours(to_x, to_y, by_x, by_y):
    half = by_x.shape[1]
    to_y = jnp.concatenate([to_y[:, :half] + by_x.astype(jnp.float32), to_y[:, half:]], axis=1)
    to_x = jnp.concatenate([to_x[:, :half], to_x[:, half:] + by_y.astype(jnp.float32)], axis=1)
    return flip(to_x.astype(jnp.bfloat16), "req", 1), flip(to_y.astype(jnp.bfloat16), "tp", 2)


def moe_dense(
    kept,
    far,
    core,
    norm_post_gain,
    expert_ids,
    route_weights,
    gate_weight,
    up_weight,
    down_weight,
):
    share_rows, width = kept.shape
    token_count, share_width = 4 * share_rows, width // 4
    core = flip(core, "tp", 1)
    far = flip((far + core[1].astype(jnp.float32)).astype(jnp.bfloat16), "tp", 2)
    rows, residual = pl.pallas_call(
        pack_kernel,
        out_shape=[
            jax.ShapeDtypeStruct((share_rows, width + LANES), jnp.bfloat16),
            jax.ShapeDtypeStruct((share_rows, width), jnp.float32),
        ],
        in_specs=[VMEM] * 6,
        out_specs=[VMEM] * 2,
        scratch_shapes=[pltpu.VMEM((token_count, LANES), jnp.float32)],
        compiler_params=pltpu.CompilerParams(vmem_limit_bytes=8 * 1024 * 1024),
        name="pack_rows",
    )(kept, core, far, norm_post_gain[None, :], expert_ids.T, route_weights.T)
    gate_up = [w.transpose(0, 2, 1).reshape(-1, width) for w in (gate_weight, up_weight)]
    weights = (*gate_up, down_weight.reshape(-1, width))
    line_0 = rows[None]
    levels = [flip(rows, "req", 2 * bits) for bits in (1, 2, 3)]
    y_0, x_0 = flip(line_0, "tp", 2), flip(line_0, "req", 1)
    line_3, y_0, x_0 = ordered(jnp.stack(levels), y_0, x_0)
    core_0, across_0, y_3, x_3 = ordered(
        flip(line_0, "tp", 1),
        across_parts(x_0, y_0),
        flip(line_3, "tp", 2),
        flip(line_3, "req", 1),
    )
    core_3, y_core_3, x_core_3 = other_core((line_3, y_3, x_3))
    near_3 = run_experts(
        near_pieces(0, line_3, core_3) + far_pieces(0, (y_3,), (y_core_3,)), weights, token_count
    )
    near_3, x_core_0, y_core_0, x_core_3, across_3 = ordered(
        near_3, flip(x_0, "tp", 1), flip(y_0, "tp", 1), x_core_3, across_parts(x_3, y_3)
    )
    side_3 = run_experts(
        near_pieces(0, x_3, x_core_3) + far_pieces(0, across_3, other_core(across_3)),
        weights,
        token_count,
    )
    side_3, across_core_0 = ordered(side_3, other_core(across_0))
    side_3 = with_core(side_3)
    all_0 = run_experts(
        near_pieces(0, line_0, core_0)
        + far_pieces(0, (y_0,), (y_core_0,))
        + near_pieces(1, x_0, x_core_0)
        + far_pieces(1, across_0, across_core_0),
        weights,
        token_count,
        residual,
    )
    all_0, near_3, side_3 = ordered(all_0, near_3, side_3)
    near_3, all_0, relay_3 = ordered(
        with_core(near_3), with_core(all_0), relayed(joined(side_3, 0, 1))
    )
    relay_0, sums_3 = ordered(
        relayed(joined(all_0, 1, 1)),
        neighbours(joined(side_3, 0, 0), joined(near_3, 0, 1), *relay_3),
    )
    sent = joined(near_3, 0, 0) + sums_3[0].astype(jnp.float32) + sums_3[1].astype(jnp.float32)
    sent = sent.astype(jnp.bfloat16)
    from_z = [flip(sent[bits - 1], "req", 2 * bits) for bits in (1, 2, 3)]
    sums_0 = neighbours(joined(all_0, 1, 0), joined(all_0, 0, 1), *relay_0)
    return pl.pallas_call(
        finish_kernel,
        out_shape=jax.ShapeDtypeStruct((token_count, share_width), jnp.bfloat16),
        in_specs=[VMEM] * 6,
        out_specs=VMEM,
        compiler_params=pltpu.CompilerParams(vmem_limit_bytes=8 * 1024 * 1024),
        name="finish",
    )(joined(all_0, 0, 0), *sums_0, *from_z)


def moe_routed(
    x_full,
    head_part,
    norm_post_gain,
    expert_ids,
    route_weights,
    gate_weight,
    up_weight,
    down_weight,
):
    req_count = lax.axis_size("req")
    tp_index = lax.axis_index("tp")
    x_float = x_full.astype(jnp.float32)
    token_count = x_float.shape[0]
    share_width = x_float.shape[1] // lax.axis_size("tp")
    top_count = expert_ids.shape[1]
    expert_count = gate_weight.shape[0] * req_count
    capacity = max(2, 3 * token_count * top_count // (2 * expert_count))
    flat_expert = expert_ids.reshape(token_count * top_count)
    one_hot = (flat_expert[:, None] == jnp.arange(expert_count, dtype=jnp.int32)[None, :]).astype(
        jnp.int32
    )
    slot_rank = jnp.sum((jnp.cumsum(one_hot, axis=0) - one_hot) * one_hot, axis=1)
    slot_index = flat_expert * capacity + slot_rank
    head_sum = lax.psum(head_part.astype(jnp.bfloat16), "tp").astype(jnp.float32)
    residual_full = x_float + head_sum
    normed_post = rms_scale(residual_full, norm_post_gain).astype(jnp.bfloat16)
    residual = lax.dynamic_slice_in_dim(residual_full, tp_index * share_width, share_width, 1)
    send_buffer = build_buffer(normed_post, slot_index, top_count, expert_count, capacity)
    part_sums = expert_apply(
        lax.all_to_all(send_buffer, "req", split_axis=0, concat_axis=0, tiled=True),
        gate_weight,
        up_weight,
        down_weight,
    )
    returned = lax.all_to_all(part_sums, "req", split_axis=0, concat_axis=0, tiled=True)
    moe_term = weigh_back(returned, slot_index, route_weights, token_count, top_count)
    moe_share = lax.psum_scatter(
        moe_term.astype(jnp.bfloat16), "tp", scatter_dimension=1, tiled=True
    ).astype(jnp.float32)
    return (residual + moe_share).astype(jnp.bfloat16)


def attention_part(
    x_full,
    norm_in_gain,
    q_weight,
    k_weight,
    v_weight,
    q_gain,
    k_gain,
    o_weight,
    key_pages,
    value_pages,
    page_table,
    cache_len,
):
    head_dim = q_gain.shape[0]
    kv_local = key_pages.shape[0]
    group_size = q_weight.shape[1] // head_dim // kv_local
    token_count = x_full.shape[0]
    x_float = x_full.astype(jnp.float32)
    normed_in = rms_scale(x_float, norm_in_gain).astype(jnp.bfloat16)
    query_lin = jnp.dot(normed_in, q_weight, preferred_element_type=jnp.float32).reshape(
        token_count, kv_local * group_size, head_dim
    )
    key_lin = jnp.dot(normed_in, k_weight, preferred_element_type=jnp.float32).reshape(
        token_count, kv_local, head_dim
    )
    values_new = (
        jnp.dot(normed_in, v_weight, preferred_element_type=jnp.float32)
        .astype(jnp.bfloat16)
        .reshape(token_count, kv_local, head_dim)
    )
    requests, positions = token_layout(cache_len)
    queries = (
        rotate(rms_scale(query_lin, q_gain), positions)
        .astype(jnp.bfloat16)
        .reshape(token_count, kv_local, group_size, head_dim)
    )
    keys_new = rotate(rms_scale(key_lin, k_gain), positions).astype(jnp.bfloat16)
    slot_owner = page_slots(page_table, cache_len)
    cache_slots = key_pages.shape[1] * key_pages.shape[2]
    keys_cache = key_pages.reshape(kv_local, cache_slots, head_dim)
    values_cache = value_pages.reshape(kv_local, cache_slots, head_dim)
    attended = attend(
        queries, keys_new, values_new, keys_cache, values_cache, requests, positions, slot_owner
    )
    return jnp.dot(attended, o_weight, preferred_element_type=jnp.float32)


def body(
    hidden_in,
    norm_in_gain,
    q_weight,
    k_weight,
    v_weight,
    q_gain,
    k_gain,
    o_weight,
    key_pages,
    value_pages,
    page_table,
    cache_len,
    norm_post_gain,
    expert_ids,
    route_weights,
    gate_weight,
    up_weight,
    down_weight,
):
    req_count = lax.axis_size("req")
    attention = (
        norm_in_gain,
        q_weight,
        k_weight,
        v_weight,
        q_gain,
        k_gain,
        o_weight,
        key_pages,
        value_pages,
        page_table,
        cache_len,
    )
    experts = (norm_post_gain, expert_ids, route_weights, gate_weight, up_weight, down_weight)
    expert_count = gate_weight.shape[0] * req_count
    staged = (req_count, lax.axis_size("tp"), gate_weight.shape[0]) == (8, 4, 2)
    if staged and expert_count <= LANES // 2:
        return moe_dense(*attention_shares(hidden_in, *attention), *experts)
    x_full = lax.all_gather(hidden_in, "tp", axis=1, tiled=True)
    return moe_routed(x_full, attention_part(x_full, *attention), *experts)


def solution(mesh):
    return jax.shard_map(
        body,
        mesh=mesh,
        in_specs=(
            P("req", "tp"),
            P(),
            P(None, "tp"),
            P(None, "tp"),
            P(None, "tp"),
            P(),
            P(),
            P("tp", None),
            P("tp", "req", None, None),
            P("tp", "req", None, None),
            P("req", None),
            P("req"),
            P(),
            P("req", None),
            P("req", None),
            P("req", None, "tp"),
            P("req", None, "tp"),
            P("req", "tp", None),
        ),
        out_specs=P("req", "tp"),
        check_vma=False,
    )
```

```python
import functools
import math

import jax
import jax.numpy as jnp
import numpy as np
from jax import lax
from jax.experimental import pallas as pl
from jax.experimental.pallas import tpu as pltpu
from jax.sharding import PartitionSpec as P

PAGE = 128
MAXPG = 32
PRE = 120
TOK_DEV = 128
REQS_DEV = 9
POOL = 48
SHORT_PG = 2
SHORT_LIST = (REQS_DEV - 1) * SHORT_PG


NORM_EPS = 1e-06
ROPE_BASE = 1000000.0


def rms_scale(values, gain_vec):
    mean_square = jnp.mean(values * values, axis=-1, keepdims=True)
    return values * lax.rsqrt(mean_square + NORM_EPS) * gain_vec


def rotate(values, positions):
    half_dim = values.shape[-1] // 2
    exponent = jnp.arange(half_dim, dtype=jnp.float32) * (2.0 / values.shape[-1])
    frequency = jnp.power(jnp.float32(ROPE_BASE), -exponent)
    angles = positions.astype(jnp.float32)[:, None] * frequency[None, :]
    cosine = jnp.cos(angles)[:, None, :]
    sine_val = jnp.sin(angles)[:, None, :]
    front_half = values[..., :half_dim]
    back_half = values[..., half_dim:]
    return jnp.concatenate(
        [front_half * cosine - back_half * sine_val, back_half * cosine + front_half * sine_val],
        axis=-1,
    )


def token_layout(lengths):
    local_idx = jnp.arange(TOK_DEV, dtype=jnp.int32)
    requests = jnp.where(local_idx < PRE, 0, local_idx - PRE + 1)
    offsets = jnp.where(local_idx < PRE, local_idx, 0)
    request_hot = (requests[:, None] == jnp.arange(REQS_DEV, dtype=jnp.int32)[None, :]).astype(
        jnp.int32
    )
    positions = jnp.sum(request_hot * lengths[None, :], axis=1) + offsets
    return (requests, positions)


def page_slots(table, lengths):
    pages_used = (lengths + PAGE - 1) // PAGE
    entry_live = jnp.arange(MAXPG, dtype=jnp.int32)[None, :] < pages_used[:, None]
    page_match = (
        (table[:, :, None] == jnp.arange(POOL, dtype=jnp.int32)[None, None, :])
        & entry_live[:, :, None]
    ).astype(jnp.int32)
    page_owner = jnp.sum(
        page_match * jnp.arange(REQS_DEV, dtype=jnp.int32)[:, None, None], axis=(0, 1)
    )
    page_start = jnp.sum(
        page_match * (jnp.arange(MAXPG, dtype=jnp.int32) * PAGE)[None, :, None], axis=(0, 1)
    )
    page_used = jnp.sum(page_match, axis=(0, 1)) > 0
    owner_length = jnp.sum(page_match * lengths[:, None, None], axis=(0, 1))
    slot_pos = page_start[:, None] + jnp.arange(PAGE, dtype=jnp.int32)[None, :]
    slot_live = page_used[:, None] & (slot_pos < owner_length[:, None])
    slot_owner = jnp.where(slot_live, page_owner[:, None], -1)
    return slot_owner.reshape(POOL * PAGE)


def attend(
    queries, keys_new, values_new, keys_cache, values_cache, requests, positions, slot_owner
):
    inv_root = 1.0 / math.sqrt(queries.shape[-1])
    cache_mask = slot_owner[None, :] == requests[:, None]
    new_mask = (requests[None, :] == requests[:, None]) & (positions[None, :] <= positions[:, None])
    score_cache = (
        jnp.einsum("tkgh,knh->kgtn", queries, keys_cache, preferred_element_type=jnp.float32)
        * inv_root
    )
    score_new = (
        jnp.einsum("tkgh,skh->kgts", queries, keys_new, preferred_element_type=jnp.float32)
        * inv_root
    )
    score_cache = jnp.where(cache_mask[None, None], score_cache, -1e30)
    score_new = jnp.where(new_mask[None, None], score_new, -1e30)
    row_max = jnp.maximum(
        jnp.max(score_cache, axis=-1, keepdims=True), jnp.max(score_new, axis=-1, keepdims=True)
    )
    exp_cache = jnp.where(cache_mask[None, None], jnp.exp(score_cache - row_max), 0.0)
    exp_new = jnp.where(new_mask[None, None], jnp.exp(score_new - row_max), 0.0)
    total = jnp.sum(exp_cache, axis=-1, keepdims=True) + jnp.sum(exp_new, axis=-1, keepdims=True)
    prob_cache = (exp_cache / total).astype(jnp.bfloat16)
    prob_new = (exp_new / total).astype(jnp.bfloat16)
    mixed = jnp.einsum(
        "kgtn,knh->tkgh", prob_cache, values_cache, preferred_element_type=jnp.float32
    )
    mixed = mixed + jnp.einsum(
        "kgts,skh->tkgh", prob_new, values_new, preferred_element_type=jnp.float32
    )
    return mixed.astype(jnp.bfloat16).reshape(queries.shape[0], -1)


def expert_apply(blocks, gate_weight, up_weight, down_weight):
    local_experts = gate_weight.shape[0]
    sources = blocks.shape[0] // local_experts
    slot_count = blocks.shape[1]
    grouped = blocks.reshape(sources, local_experts, slot_count, blocks.shape[2])
    gate_acts = jnp.einsum(
        "sekd,edf->sekf", grouped, gate_weight, preferred_element_type=jnp.float32
    )
    up_acts = jnp.einsum("sekd,edf->sekf", grouped, up_weight, preferred_element_type=jnp.float32)
    hidden_act = (jax.nn.silu(gate_acts) * up_acts).astype(jnp.bfloat16)
    part_sums = jnp.einsum(
        "sekf,efd->sekd", hidden_act, down_weight, preferred_element_type=jnp.float32
    ).astype(jnp.bfloat16)
    return part_sums.reshape(sources * local_experts, slot_count, part_sums.shape[3])


def build_buffer(normed, slot_index, top_count, expert_count, capacity):
    picked = jnp.repeat(normed, top_count, axis=0)
    buffer_rows = (
        jnp.zeros((expert_count * capacity, normed.shape[1]), normed.dtype)
        .at[slot_index]
        .set(picked)
    )
    return buffer_rows.reshape(expert_count, capacity, normed.shape[1])


def weigh_back(returned, slot_index, route_weights, token_count, top_count):
    row_width = returned.shape[2]
    back_rows = returned.reshape(returned.shape[0] * returned.shape[1], row_width)[slot_index]
    weighted = (
        back_rows.astype(jnp.float32) * route_weights.reshape(token_count * top_count)[:, None]
    )
    return jnp.sum(weighted.reshape(token_count, top_count, row_width), axis=1)


LANES = 128
VMEM = pl.BlockSpec(memory_space=pltpu.VMEM)
SMEM = pl.BlockSpec(memory_space=pltpu.SMEM)
VMEM_LIMIT = 24 * 1024 * 1024


def flip(value, axis, bits):
    return lax.ppermute(value, axis, [(i, i ^ bits) for i in range(lax.axis_size(axis))])


def layout_kernel(
    length_ref, table_ref, frequency_ref, cosine_ref, sine_ref, owner_ref, list_ref, owners
):
    tokens, head_dim = cosine_ref.shape
    for entry in range(POOL):
        list_ref[entry] = 0
        owners[0, entry] = -1
        owners[1, entry] = 0
    prefill_long = length_ref[0] > SHORT_PG * PAGE
    count = jnp.int32(0)
    for request in range(1, REQS_DEV):

        def name_page(entry, count):
            page = table_ref[request, entry]
            place = jnp.where(prefill_long, count, page)
            list_ref[place] = page
            owners[0, place] = request
            owners[1, place] = jnp.minimum(length_ref[request] - entry * PAGE, PAGE)
            return count + 1

        count = lax.fori_loop(0, (length_ref[request] + PAGE - 1) // PAGE, name_page, count)
    slot = lax.broadcasted_iota(jnp.int32, (1, PAGE), 1)
    for entry in range(POOL):
        owner_ref[:, entry * PAGE : (entry + 1) * PAGE] = jnp.where(
            slot < owners[1, entry], owners[0, entry], -1
        )
    token = lax.broadcasted_iota(jnp.int32, (tokens, head_dim), 0)
    lane = lax.broadcasted_iota(jnp.int32, (tokens, head_dim), 1)
    position = length_ref[0] + token
    for i in range(tokens - PRE):
        position = jnp.where(token == PRE + i, length_ref[i + 1], position)
    angle = position.astype(jnp.float32) * frequency_ref[...]
    sine = jnp.sin(angle)
    cosine_ref[...] = jnp.cos(angle)
    sine_ref[...] = jnp.where(lane < head_dim // 2, -sine, sine)


def attention_kernel(*refs):
    pieces, hbm_refs, (keep_out, far_out, core_out) = refs[:4], refs[4:19], refs[19:22]
    local_refs = refs[22:37]
    (length_ref, table_ref, list_ref, gain_ref, q_gain_ref, k_gain_ref) = local_refs[:6]
    (cosine_ref, sine_ref, owner_ref, q_ref, k_ref, v_ref, key_ref, value_ref, o_ref) = local_refs[6:]
    (
        x_ref, query_ref, own_scores, scores_ref, mix_ref, mixed_ref, part_ref, slots_ref, decoded_ref,
        sems,
    ) = refs[37:]
    tokens, head_dim = x_ref.shape[0], k_gain_ref.shape[1]
    copies = [
        pltpu.make_async_copy(source, target, sems.at[i])
        for i, (source, target) in enumerate(zip(hbm_refs, local_refs))
    ]
    for copy in copies:
        copy.start()
    tp_index = lax.axis_index("tp")
    heads = q_ref.shape[1] // head_dim
    decodes = tokens - PRE
    for step, piece in enumerate(pieces):
        width = piece.shape[1]
        start = pl.multiple_of((tp_index ^ step) * width, width)
        x_ref[:, pl.ds(start, width)] = piece[...]
    for copy in copies[:9]:
        copy.wait()
    token = lax.broadcasted_iota(jnp.int32, (tokens, head_dim), 0)
    lane = lax.broadcasted_iota(jnp.int32, (tokens, head_dim), 1)

    def turned(values, gain):
        values = rms_scale(values, gain)
        return values * cosine_ref[...] + pltpu.roll(values, head_dim // 2, 1) * sine_ref[...]

    def with_ones(values):
        return jnp.concatenate([values, jnp.ones_like(values)], axis=1)

    normed = rms_scale(x_ref[...].astype(jnp.float32), gain_ref[...]).astype(jnp.bfloat16)
    contract = (((1,), (1,)), ((), ()))
    for copy in copies[9:12]:
        copy.wait()
    key_lin = jnp.dot(normed, k_ref[...], preferred_element_type=jnp.float32)
    values_new = jnp.dot(normed, v_ref[...], preferred_element_type=jnp.float32).astype(jnp.bfloat16)
    query_lin = jnp.dot(normed, q_ref[...], preferred_element_type=jnp.float32)
    keys_new = turned(key_lin, k_gain_ref[...]).astype(jnp.bfloat16)
    values_new = with_ones(values_new)
    to_log2 = math.log2(math.e) / math.sqrt(head_dim)
    own_mask = (lane == token) | ((lane < token) & (token < PRE))
    decode_query, decode_own = [], []
    for head in range(heads):
        span = slice(head * tokens, (head + 1) * tokens)
        query = turned(query_lin[:, head * head_dim : (head + 1) * head_dim], q_gain_ref[...]) * to_log2
        rounded = query.astype(jnp.bfloat16)
        query_ref[span, :] = rounded
        scores = lax.dot_general(rounded, keys_new, contract, preferred_element_type=jnp.float32)
        scores = jnp.where(own_mask, scores, -1e30)
        own_scores[span, :] = scores
        decode_query.append(query[PRE:])
        decode_own.append(scores[PRE:])
    decode_query = jnp.concatenate(decode_query, axis=0).astype(jnp.bfloat16)
    decode_own = jnp.concatenate(decode_own, axis=0)
    for copy in copies[12:14]:
        copy.wait()

    def raised(top, scores):
        for start in range(0, scores.shape[1], head_dim):
            top = jnp.maximum(top, scores[:, start : start + head_dim])
        return top

    def weigh(own, score_steps, value_steps, scores_ref):
        top = own
        for step, score_step in enumerate(score_steps):
            scores = score_step()
            scores_ref[step, :, : scores.shape[1]] = scores
            top = raised(top, scores)
        top = jnp.max(top, axis=1, keepdims=True)
        mix = jnp.dot(
            jnp.exp2(own - top).astype(jnp.bfloat16), values_new, preferred_element_type=jnp.float32
        )
        for step, value_step in enumerate(value_steps):
            values = value_step()
            weights = jnp.exp2(scores_ref[step, :, : values.shape[0]] - top).astype(jnp.bfloat16)
            mix = mix + jnp.dot(weights, with_ones(values), preferred_element_type=jnp.float32)
        return mix

    def taken(ref, names):
        return jnp.concatenate([ref[name] for name in names], axis=0)

    def against(queries, keys):
        return lax.dot_general(queries, keys, contract, preferred_element_type=jnp.float32)

    def prefill(names, live):
        def score(pages):
            scores = against(query_ref[...], taken(key_ref, pages))
            return scores if live is None else jnp.where(live, scores, -1e30)

        mix_ref[...] = weigh(
            own_scores[...],
            [functools.partial(score, pages) for pages in names],
            [functools.partial(taken, value_ref, pages) for pages in names],
            scores_ref,
        )

    def decode(steps, pages_of):
        row_request = 1 + lax.broadcasted_iota(jnp.int32, (heads * decodes, 1), 0) % decodes
        width = slots_ref.shape[2]

        def score(step):
            scores = against(decode_query, pages_of(key_ref, step))
            owner = owner_ref[:, step * width : (step + 1) * width]
            return jnp.where(owner == row_request, scores, -1e30)

        mix = weigh(
            decode_own,
            [functools.partial(score, step) for step in range(steps)],
            [functools.partial(pages_of, value_ref, step) for step in range(steps)],
            slots_ref,
        )
        decoded_ref[...] = mix[:, :head_dim] / mix[:, head_dim:]

    length = length_ref[0]
    listed = slots_ref.shape[2] // PAGE
    pages = scores_ref.shape[2] // PAGE

    @pl.when(length > SHORT_PG * PAGE)
    def _():
        names = [table_ref[0, entry] for entry in range(MAXPG)]
        prefill([names[first : first + pages] for first in range(0, MAXPG, pages)], None)
        decode(
            SHORT_LIST // listed,
            lambda ref, step: taken(ref, [list_ref[step * listed + i] for i in range(listed)]),
        )

    @pl.when(length <= SHORT_PG * PAGE)
    def _():
        column = lax.broadcasted_iota(jnp.int32, (1, SHORT_PG * PAGE), 1)
        prefill([[table_ref[0, entry] for entry in range(SHORT_PG)]], column < length)
        decode(
            POOL // listed,
            lambda ref, step: ref[step * listed : (step + 1) * listed].reshape(-1, head_dim),
        )

    for head in range(heads):
        part = mix_ref[head * tokens : (head + 1) * tokens, :]
        columns = slice(head * head_dim, (head + 1) * head_dim)
        mixed_ref[:, columns] = part[:, :head_dim] / part[:, head_dim:]
        mixed_ref[PRE:, columns] = decoded_ref[head * decodes : (head + 1) * decodes]
    copies[14].wait()
    part_ref[...] = jnp.dot(
        mixed_ref[...].astype(jnp.bfloat16), o_ref[...], preferred_element_type=jnp.float32
    )
    share_rows = keep_out.shape[0]

    def quarter(step):
        return pl.ds(pl.multiple_of((tp_index ^ step) * share_rows, share_rows), share_rows)

    keep_out[...] = part_ref[quarter(0), :] + x_ref[quarter(0), :].astype(jnp.float32)
    far_out[...] = part_ref[quarter(2), :]
    core_out[0] = part_ref[quarter(1), :].astype(jnp.bfloat16)
    core_out[1] = part_ref[quarter(3), :].astype(jnp.bfloat16)


def attention_shares(
    hidden_in, norm_in_gain, q_weight, k_weight, v_weight, q_gain, k_gain, o_weight,
    key_pages, value_pages, page_table, cache_len,
):
    tokens, width = hidden_in.shape[0], 4 * hidden_in.shape[1]
    head_dim = q_gain.shape[0]
    rows = q_weight.shape[1] // head_dim * tokens
    decode_rows = rows // tokens * (tokens - PRE)
    half = ROPE_BASE ** (-np.arange(head_dim // 2) / (head_dim // 2))
    frequency = jnp.asarray(np.concatenate([half, half])[None, :], jnp.float32)
    params = pltpu.CompilerParams(vmem_limit_bytes=56 * 1024 * 1024)
    rope = jax.ShapeDtypeStruct((tokens, head_dim), jnp.float32)
    cosine, sine, owner, page_list = pl.pallas_call(
        layout_kernel,
        out_shape=[
            rope,
            rope,
            jax.ShapeDtypeStruct((1, POOL * PAGE), jnp.int32),
            jax.ShapeDtypeStruct((POOL,), jnp.int32),
        ],
        in_specs=[SMEM, SMEM, VMEM],
        out_specs=[VMEM, VMEM, VMEM, SMEM],
        scratch_shapes=[pltpu.SMEM((2, POOL), jnp.int32)],
        compiler_params=params,
        name="layout",
    )(cache_len, page_table, frequency)
    far, cosine, sine, owner, page_list = ordered(
        flip(hidden_in, "tp", 2), cosine, sine, owner, page_list
    )
    pieces = (hidden_in, flip(hidden_in, "tp", 1), far, flip(far, "tp", 1))
    scalars = (cache_len, page_table, page_list)
    arrays = (
        norm_in_gain[None, :], q_gain[None, :], k_gain[None, :], cosine, sine, owner,
        q_weight, k_weight, v_weight, key_pages[0], value_pages[0], o_weight,
    )
    share = (tokens // 4, width)
    score_pages, list_pages = 4, 8
    return pl.pallas_call(
        attention_kernel,
        out_shape=[
            jax.ShapeDtypeStruct(share, jnp.float32),
            jax.ShapeDtypeStruct(share, jnp.float32),
            jax.ShapeDtypeStruct((2, *share), jnp.bfloat16),
        ],
        in_specs=[VMEM] * 4 + [pl.BlockSpec(memory_space=pltpu.HBM)] * 15,
        out_specs=[VMEM] * 3,
        scratch_shapes=[pltpu.SMEM(array.shape, array.dtype) for array in scalars]
        + [pltpu.VMEM(array.shape, array.dtype) for array in arrays]
        + [
            pltpu.VMEM((tokens, width), jnp.bfloat16),
            pltpu.VMEM((rows, head_dim), jnp.bfloat16),
            pltpu.VMEM((rows, tokens), jnp.float32),
            pltpu.VMEM((MAXPG // score_pages, rows, score_pages * PAGE), jnp.float32),
            pltpu.VMEM((rows, 2 * head_dim), jnp.float32),
            pltpu.VMEM((tokens, q_weight.shape[1]), jnp.float32),
            pltpu.VMEM((tokens, width), jnp.float32),
            pltpu.VMEM((POOL // list_pages, decode_rows, list_pages * PAGE), jnp.float32),
            pltpu.VMEM((decode_rows, head_dim), jnp.float32),
            pltpu.SemaphoreType.DMA((15,)),
        ],
        compiler_params=params,
        name="attention",
    )(*pieces, *scalars, *arrays)


def pack_kernel(
    own_ref, far_ref, gain_ref, ids_ref, routes_ref,
    rows_ref, residual_ref, spread_ref,
):
    tp_index = lax.axis_index("tp")
    share_rows, width = own_ref.shape
    mine = pl.ds(pl.multiple_of(tp_index * share_rows, share_rows), share_rows)
    residual = own_ref[...] + far_ref[...].astype(jnp.float32)
    residual_ref[...] = residual
    rows_ref[:, :width] = rms_scale(residual, gain_ref[...]).astype(jnp.bfloat16)
    expert = lax.broadcasted_iota(jnp.int32, (LANES, spread_ref.shape[0]), 0) % (LANES // 2)
    spread = jnp.zeros(expert.shape, jnp.float32)
    for k in range(ids_ref.shape[0]):
        spread = spread + jnp.where(expert == ids_ref[k : k + 1, :], routes_ref[k : k + 1, :], 0.0)
    spread_ref[...] = spread.T
    spread = spread_ref[mine, :]
    lane = lax.broadcasted_iota(jnp.int32, spread.shape, 1)
    high = spread.astype(jnp.bfloat16).astype(jnp.float32)
    rows_ref[:, width:] = jnp.where(lane < LANES // 2, high, spread - high).astype(jnp.bfloat16)


def experts_kernel(plan, *refs):
    pieces, residual_refs = refs[: len(plan)], refs[len(plan) : -7]
    gate_ref, up_ref, down_ref, keep_ref, send_ref, rows_ref, sums_ref = refs[-7:]
    req_index, tp_index = lax.axis_index("req"), lax.axis_index("tp")
    columns, _, levels, group_rows, share_width = keep_ref.shape
    width = gate_ref.shape[1]
    units = gate_ref.shape[0] // 2
    for (column, step, first), piece in zip(plan, pieces):
        count = piece.shape[1]
        for level in range(levels):
            start = (column * levels + level) * group_rows + first
            start = start + (tp_index ^ step) * (group_rows // 4)
            rows_ref[pl.ds(pl.multiple_of(start, count), count), :] = piece[level]
    spread = rows_ref[:, width:].astype(jnp.float32)
    lane = lax.broadcasted_iota(jnp.int32, spread.shape, 1) % (LANES // 2)
    weights = [
        jnp.sum(jnp.where(lane == 2 * req_index + e, spread, 0.0), axis=1, keepdims=True)
        for e in range(2)
    ]
    contract = (((1,), (1,)), ((), ()))
    rows = rows_ref[:, :width]
    gate = lax.dot_general(rows, gate_ref[...], contract, preferred_element_type=jnp.float32)
    up = lax.dot_general(rows, up_ref[...], contract, preferred_element_type=jnp.float32)
    unit = lax.broadcasted_iota(jnp.int32, gate.shape, 1)
    weight = jnp.where(unit < units, weights[0], weights[1])
    acts = (gate / (1.0 + jnp.exp(-gate)) * up * weight).astype(jnp.bfloat16)
    for step in range(4):
        start = pl.multiple_of((tp_index ^ step) * share_width, share_width)
        part = jnp.dot(
            acts, down_ref[:, pl.ds(start, share_width)], preferred_element_type=jnp.float32
        )
        for residual_ref in residual_refs:
            count = residual_ref.shape[0]
            mine = pl.ds(pl.multiple_of(tp_index * count, count), count)
            sums_ref[...] = part
            sums_ref[mine, :] += residual_ref[:, pl.ds(start, share_width)]
            part = sums_ref[...]
        target = send_ref if step % 2 else keep_ref
        part = part.reshape(columns, levels, group_rows, share_width).astype(target.dtype)
        for column in range(columns):
            target[column, step // 2] = part[column]


def run_experts(pieces, weights, group_rows, *residual):
    plan = tuple(place for place, _ in pieces)
    pieces = [piece for _, piece in pieces]
    columns, levels, packed = 1 + max(place[0] for place in plan), *pieces[0].shape[::2]
    rows, share_width = columns * levels * group_rows, weights[2].shape[1] // 4
    out_shape = (columns, 2, levels, group_rows, share_width)
    return pl.pallas_call(
        functools.partial(experts_kernel, plan),
        out_shape=[
            jax.ShapeDtypeStruct(out_shape, jnp.float32),
            jax.ShapeDtypeStruct(out_shape, jnp.bfloat16),
        ],
        in_specs=[VMEM] * (len(pieces) + len(residual) + 3),
        out_specs=[VMEM] * 2,
        scratch_shapes=[
            pltpu.VMEM((rows, packed), jnp.bfloat16),
            pltpu.VMEM((rows, share_width), jnp.float32),
        ],
        compiler_params=pltpu.CompilerParams(vmem_limit_bytes=VMEM_LIMIT),
        name="experts",
    )(*pieces, *residual, *weights)


def finish_kernel(own_ref, x_ref, y_ref, z1_ref, z2_ref, z3_ref, out_ref):
    total = own_ref[0]
    for extra_ref in (x_ref, y_ref):
        total = total + extra_ref[0].astype(jnp.float32)
    for extra_ref in (z1_ref, z2_ref, z3_ref):
        total = total + extra_ref[...].astype(jnp.float32)
    out_ref[...] = total.astype(jnp.bfloat16)


def ordered(*values):
    return lax.optimization_barrier(values)


def across_parts(line_x, line_y):
    half = line_x.shape[1] // 2
    return flip(line_x[:, :half], "tp", 2), flip(line_y[:, half:], "req", 1)


def other_core(parts):
    return tuple(flip(part, "tp", 1) for part in parts)


def with_core(pair):
    return pair[0], flip(pair[1], "tp", 1)


def joined(pair, column, y):
    return pair[0][column, y] + pair[1][column, y].astype(jnp.float32)


def near_pieces(column, line, core):
    return [((column, 0, 0), line), ((column, 1, 0), core)]


def far_pieces(column, parts, cores):
    half = parts[0].shape[1]
    if len(parts) == 1:
        return [((column, 2, 0), parts[0]), ((column, 3, 0), cores[0])]
    return [((column, 2, i * half), part) for i, part in enumerate(parts)] + [
        ((column, 3, i * half), part) for i, part in enumerate(cores)
    ]


def relayed(side):
    part = side.astype(jnp.bfloat16)
    half = part.shape[1] // 2
    return flip(part[:, :half], "req", 1), flip(part[:, half:], "tp", 2)


def neighbours(to_x, to_y, by_x, by_y):
    half = by_x.shape[1]
    to_y = jnp.concatenate([to_y[:, :half] + by_x.astype(jnp.float32), to_y[:, half:]], axis=1)
    to_x = jnp.concatenate([to_x[:, :half], to_x[:, half:] + by_y.astype(jnp.float32)], axis=1)
    return flip(to_x.astype(jnp.bfloat16), "req", 1), flip(to_y.astype(jnp.bfloat16), "tp", 2)


def moe_dense(
    kept,
    far,
    core,
    norm_post_gain,
    expert_ids,
    route_weights,
    gate_weight,
    up_weight,
    down_weight,
):
    share_rows, width = kept.shape
    token_count, share_width = 4 * share_rows, width // 4
    core = flip(core, "tp", 1)
    far = flip((far + core[1].astype(jnp.float32)).astype(jnp.bfloat16), "tp", 2)
    kept, far = ordered(kept + core[0].astype(jnp.float32), far)
    rows, residual = pl.pallas_call(
        pack_kernel,
        out_shape=[
            jax.ShapeDtypeStruct((share_rows, width + LANES), jnp.bfloat16),
            jax.ShapeDtypeStruct((share_rows, width), jnp.float32),
        ],
        in_specs=[VMEM] * 5,
        out_specs=[VMEM] * 2,
        scratch_shapes=[pltpu.VMEM((token_count, LANES), jnp.float32)],
        compiler_params=pltpu.CompilerParams(vmem_limit_bytes=8 * 1024 * 1024),
        name="pack_rows",
    )(kept, far, norm_post_gain[None, :], expert_ids.T, route_weights.T)
    gate_up = [w.transpose(0, 2, 1).reshape(-1, width) for w in (gate_weight, up_weight)]
    weights = (*gate_up, down_weight.reshape(-1, width))
    line_0 = rows[None]
    levels = [flip(rows, "req", 2 * bits) for bits in (1, 2, 3)]
    y_0, x_0 = flip(line_0, "tp", 2), flip(line_0, "req", 1)
    line_3, y_0, x_0 = ordered(jnp.stack(levels), y_0, x_0)
    core_0, across_0, y_3, x_3 = ordered(
        flip(line_0, "tp", 1),
        across_parts(x_0, y_0),
        flip(line_3, "tp", 2),
        flip(line_3, "req", 1),
    )
    core_3, y_core_3, x_core_3 = other_core((line_3, y_3, x_3))
    near_3 = run_experts(
        near_pieces(0, line_3, core_3) + far_pieces(0, (y_3,), (y_core_3,)), weights, token_count
    )
    near_3, x_core_0, y_core_0, x_core_3, across_3 = ordered(
        near_3, flip(x_0, "tp", 1), flip(y_0, "tp", 1), x_core_3, across_parts(x_3, y_3)
    )
    side_3 = run_experts(
        near_pieces(0, x_3, x_core_3) + far_pieces(0, across_3, other_core(across_3)),
        weights,
        token_count,
    )
    side_3, across_core_0 = ordered(side_3, other_core(across_0))
    side_3 = with_core(side_3)
    all_0 = run_experts(
        near_pieces(0, line_0, core_0)
        + far_pieces(0, (y_0,), (y_core_0,))
        + near_pieces(1, x_0, x_core_0)
        + far_pieces(1, across_0, across_core_0),
        weights,
        token_count,
        residual,
    )
    all_0, near_3, side_3 = ordered(all_0, near_3, side_3)
    near_3, all_0, relay_3 = ordered(
        with_core(near_3), with_core(all_0), relayed(joined(side_3, 0, 1))
    )
    relay_0, sums_3 = ordered(
        relayed(joined(all_0, 1, 1)),
        neighbours(joined(side_3, 0, 0), joined(near_3, 0, 1), *relay_3),
    )
    sent = joined(near_3, 0, 0) + sums_3[0].astype(jnp.float32) + sums_3[1].astype(jnp.float32)
    sent = sent.astype(jnp.bfloat16)
    from_z = [flip(sent[bits - 1], "req", 2 * bits) for bits in (1, 2, 3)]
    sums_0 = neighbours(joined(all_0, 1, 0), joined(all_0, 0, 1), *relay_0)
    return pl.pallas_call(
        finish_kernel,
        out_shape=jax.ShapeDtypeStruct((token_count, share_width), jnp.bfloat16),
        in_specs=[VMEM] * 6,
        out_specs=VMEM,
        compiler_params=pltpu.CompilerParams(vmem_limit_bytes=8 * 1024 * 1024),
        name="finish",
    )(joined(all_0, 0, 0), *sums_0, *from_z)


def moe_routed(
    x_full,
    head_part,
    norm_post_gain,
    expert_ids,
    route_weights,
    gate_weight,
    up_weight,
    down_weight,
):
    req_count = lax.axis_size("req")
    tp_index = lax.axis_index("tp")
    x_float = x_full.astype(jnp.float32)
    token_count = x_float.shape[0]
    share_width = x_float.shape[1] // lax.axis_size("tp")
    top_count = expert_ids.shape[1]
    expert_count = gate_weight.shape[0] * req_count
    capacity = max(2, 3 * token_count * top_count // (2 * expert_count))
    flat_expert = expert_ids.reshape(token_count * top_count)
    one_hot = (flat_expert[:, None] == jnp.arange(expert_count, dtype=jnp.int32)[None, :]).astype(
        jnp.int32
    )
    slot_rank = jnp.sum((jnp.cumsum(one_hot, axis=0) - one_hot) * one_hot, axis=1)
    slot_index = flat_expert * capacity + slot_rank
    head_sum = lax.psum(head_part.astype(jnp.bfloat16), "tp").astype(jnp.float32)
    residual_full = x_float + head_sum
    normed_post = rms_scale(residual_full, norm_post_gain).astype(jnp.bfloat16)
    residual = lax.dynamic_slice_in_dim(residual_full, tp_index * share_width, share_width, 1)
    send_buffer = build_buffer(normed_post, slot_index, top_count, expert_count, capacity)
    part_sums = expert_apply(
        lax.all_to_all(send_buffer, "req", split_axis=0, concat_axis=0, tiled=True),
        gate_weight,
        up_weight,
        down_weight,
    )
    returned = lax.all_to_all(part_sums, "req", split_axis=0, concat_axis=0, tiled=True)
    moe_term = weigh_back(returned, slot_index, route_weights, token_count, top_count)
    moe_share = lax.psum_scatter(
        moe_term.astype(jnp.bfloat16), "tp", scatter_dimension=1, tiled=True
    ).astype(jnp.float32)
    return (residual + moe_share).astype(jnp.bfloat16)


def attention_part(
    x_full,
    norm_in_gain,
    q_weight,
    k_weight,
    v_weight,
    q_gain,
    k_gain,
    o_weight,
    key_pages,
    value_pages,
    page_table,
    cache_len,
):
    head_dim = q_gain.shape[0]
    kv_local = key_pages.shape[0]
    group_size = q_weight.shape[1] // head_dim // kv_local
    token_count = x_full.shape[0]
    x_float = x_full.astype(jnp.float32)
    normed_in = rms_scale(x_float, norm_in_gain).astype(jnp.bfloat16)
    query_lin = jnp.dot(normed_in, q_weight, preferred_element_type=jnp.float32).reshape(
        token_count, kv_local * group_size, head_dim
    )
    key_lin = jnp.dot(normed_in, k_weight, preferred_element_type=jnp.float32).reshape(
        token_count, kv_local, head_dim
    )
    values_new = (
        jnp.dot(normed_in, v_weight, preferred_element_type=jnp.float32)
        .astype(jnp.bfloat16)
        .reshape(token_count, kv_local, head_dim)
    )
    requests, positions = token_layout(cache_len)
    queries = (
        rotate(rms_scale(query_lin, q_gain), positions)
        .astype(jnp.bfloat16)
        .reshape(token_count, kv_local, group_size, head_dim)
    )
    keys_new = rotate(rms_scale(key_lin, k_gain), positions).astype(jnp.bfloat16)
    slot_owner = page_slots(page_table, cache_len)
    cache_slots = key_pages.shape[1] * key_pages.shape[2]
    keys_cache = key_pages.reshape(kv_local, cache_slots, head_dim)
    values_cache = value_pages.reshape(kv_local, cache_slots, head_dim)
    attended = attend(
        queries, keys_new, values_new, keys_cache, values_cache, requests, positions, slot_owner
    )
    return jnp.dot(attended, o_weight, preferred_element_type=jnp.float32)


def body(
    hidden_in,
    norm_in_gain,
    q_weight,
    k_weight,
    v_weight,
    q_gain,
    k_gain,
    o_weight,
    key_pages,
    value_pages,
    page_table,
    cache_len,
    norm_post_gain,
    expert_ids,
    route_weights,
    gate_weight,
    up_weight,
    down_weight,
):
    req_count = lax.axis_size("req")
    attention = (
        norm_in_gain,
        q_weight,
        k_weight,
        v_weight,
        q_gain,
        k_gain,
        o_weight,
        key_pages,
        value_pages,
        page_table,
        cache_len,
    )
    experts = (norm_post_gain, expert_ids, route_weights, gate_weight, up_weight, down_weight)
    expert_count = gate_weight.shape[0] * req_count
    staged = (req_count, lax.axis_size("tp"), gate_weight.shape[0]) == (8, 4, 2)
    if staged and expert_count <= LANES // 2:
        return moe_dense(*attention_shares(hidden_in, *attention), *experts)
    x_full = lax.all_gather(hidden_in, "tp", axis=1, tiled=True)
    return moe_routed(x_full, attention_part(x_full, *attention), *experts)


def solution(mesh):
    return jax.shard_map(
        body,
        mesh=mesh,
        in_specs=(
            P("req", "tp"),
            P(),
            P(None, "tp"),
            P(None, "tp"),
            P(None, "tp"),
            P(),
            P(),
            P("tp", None),
            P("tp", "req", None, None),
            P("tp", "req", None, None),
            P("req", None),
            P("req"),
            P(),
            P("req", None),
            P("req", None),
            P("req", None, "tp"),
            P("req", None, "tp"),
            P("req", "tp", None),
        ),
        out_specs=P("req", "tp"),
        check_vma=False,
    )
```

```python
import functools
import math

import jax
import jax.numpy as jnp
import numpy as np
from jax import lax
from jax.experimental import pallas as pl
from jax.experimental.pallas import tpu as pltpu
from jax.sharding import PartitionSpec as P

PAGE = 128
MAXPG = 32
PRE = 120
TOK_DEV = 128
REQS_DEV = 9
POOL = 48
SHORT_PG = 2
SHORT_LIST = (REQS_DEV - 1) * SHORT_PG


NORM_EPS = 1e-06
ROPE_BASE = 1000000.0


def rms_scale(values, gain_vec):
    mean_square = jnp.mean(values * values, axis=-1, keepdims=True)
    return values * lax.rsqrt(mean_square + NORM_EPS) * gain_vec


def rotate(values, positions):
    half_dim = values.shape[-1] // 2
    exponent = jnp.arange(half_dim, dtype=jnp.float32) * (2.0 / values.shape[-1])
    frequency = jnp.power(jnp.float32(ROPE_BASE), -exponent)
    angles = positions.astype(jnp.float32)[:, None] * frequency[None, :]
    cosine = jnp.cos(angles)[:, None, :]
    sine_val = jnp.sin(angles)[:, None, :]
    front_half = values[..., :half_dim]
    back_half = values[..., half_dim:]
    return jnp.concatenate(
        [front_half * cosine - back_half * sine_val, back_half * cosine + front_half * sine_val],
        axis=-1,
    )


def token_layout(lengths):
    local_idx = jnp.arange(TOK_DEV, dtype=jnp.int32)
    requests = jnp.where(local_idx < PRE, 0, local_idx - PRE + 1)
    offsets = jnp.where(local_idx < PRE, local_idx, 0)
    request_hot = (requests[:, None] == jnp.arange(REQS_DEV, dtype=jnp.int32)[None, :]).astype(
        jnp.int32
    )
    positions = jnp.sum(request_hot * lengths[None, :], axis=1) + offsets
    return (requests, positions)


def page_slots(table, lengths):
    pages_used = (lengths + PAGE - 1) // PAGE
    entry_live = jnp.arange(MAXPG, dtype=jnp.int32)[None, :] < pages_used[:, None]
    page_match = (
        (table[:, :, None] == jnp.arange(POOL, dtype=jnp.int32)[None, None, :])
        & entry_live[:, :, None]
    ).astype(jnp.int32)
    page_owner = jnp.sum(
        page_match * jnp.arange(REQS_DEV, dtype=jnp.int32)[:, None, None], axis=(0, 1)
    )
    page_start = jnp.sum(
        page_match * (jnp.arange(MAXPG, dtype=jnp.int32) * PAGE)[None, :, None], axis=(0, 1)
    )
    page_used = jnp.sum(page_match, axis=(0, 1)) > 0
    owner_length = jnp.sum(page_match * lengths[:, None, None], axis=(0, 1))
    slot_pos = page_start[:, None] + jnp.arange(PAGE, dtype=jnp.int32)[None, :]
    slot_live = page_used[:, None] & (slot_pos < owner_length[:, None])
    slot_owner = jnp.where(slot_live, page_owner[:, None], -1)
    return slot_owner.reshape(POOL * PAGE)


def attend(
    queries, keys_new, values_new, keys_cache, values_cache, requests, positions, slot_owner
):
    inv_root = 1.0 / math.sqrt(queries.shape[-1])
    cache_mask = slot_owner[None, :] == requests[:, None]
    new_mask = (requests[None, :] == requests[:, None]) & (positions[None, :] <= positions[:, None])
    score_cache = (
        jnp.einsum("tkgh,knh->kgtn", queries, keys_cache, preferred_element_type=jnp.float32)
        * inv_root
    )
    score_new = (
        jnp.einsum("tkgh,skh->kgts", queries, keys_new, preferred_element_type=jnp.float32)
        * inv_root
    )
    score_cache = jnp.where(cache_mask[None, None], score_cache, -1e30)
    score_new = jnp.where(new_mask[None, None], score_new, -1e30)
    row_max = jnp.maximum(
        jnp.max(score_cache, axis=-1, keepdims=True), jnp.max(score_new, axis=-1, keepdims=True)
    )
    exp_cache = jnp.where(cache_mask[None, None], jnp.exp(score_cache - row_max), 0.0)
    exp_new = jnp.where(new_mask[None, None], jnp.exp(score_new - row_max), 0.0)
    total = jnp.sum(exp_cache, axis=-1, keepdims=True) + jnp.sum(exp_new, axis=-1, keepdims=True)
    prob_cache = (exp_cache / total).astype(jnp.bfloat16)
    prob_new = (exp_new / total).astype(jnp.bfloat16)
    mixed = jnp.einsum(
        "kgtn,knh->tkgh", prob_cache, values_cache, preferred_element_type=jnp.float32
    )
    mixed = mixed + jnp.einsum(
        "kgts,skh->tkgh", prob_new, values_new, preferred_element_type=jnp.float32
    )
    return mixed.astype(jnp.bfloat16).reshape(queries.shape[0], -1)


def expert_apply(blocks, gate_weight, up_weight, down_weight):
    local_experts = gate_weight.shape[0]
    sources = blocks.shape[0] // local_experts
    slot_count = blocks.shape[1]
    grouped = blocks.reshape(sources, local_experts, slot_count, blocks.shape[2])
    gate_acts = jnp.einsum(
        "sekd,edf->sekf", grouped, gate_weight, preferred_element_type=jnp.float32
    )
    up_acts = jnp.einsum("sekd,edf->sekf", grouped, up_weight, preferred_element_type=jnp.float32)
    hidden_act = (jax.nn.silu(gate_acts) * up_acts).astype(jnp.bfloat16)
    part_sums = jnp.einsum(
        "sekf,efd->sekd", hidden_act, down_weight, preferred_element_type=jnp.float32
    ).astype(jnp.bfloat16)
    return part_sums.reshape(sources * local_experts, slot_count, part_sums.shape[3])


def build_buffer(normed, slot_index, top_count, expert_count, capacity):
    picked = jnp.repeat(normed, top_count, axis=0)
    buffer_rows = (
        jnp.zeros((expert_count * capacity, normed.shape[1]), normed.dtype)
        .at[slot_index]
        .set(picked)
    )
    return buffer_rows.reshape(expert_count, capacity, normed.shape[1])


def weigh_back(returned, slot_index, route_weights, token_count, top_count):
    row_width = returned.shape[2]
    back_rows = returned.reshape(returned.shape[0] * returned.shape[1], row_width)[slot_index]
    weighted = (
        back_rows.astype(jnp.float32) * route_weights.reshape(token_count * top_count)[:, None]
    )
    return jnp.sum(weighted.reshape(token_count, top_count, row_width), axis=1)


LANES = 128
VMEM = pl.BlockSpec(memory_space=pltpu.VMEM)
SMEM = pl.BlockSpec(memory_space=pltpu.SMEM)
VMEM_LIMIT = 24 * 1024 * 1024


def flip(value, axis, bits):
    return lax.ppermute(value, axis, [(i, i ^ bits) for i in range(lax.axis_size(axis))])


def layout_kernel(
    length_ref, table_ref, frequency_ref, cosine_ref, sine_ref, owner_ref, list_ref, owners
):
    tokens, head_dim = cosine_ref.shape
    for entry in range(POOL):
        list_ref[entry] = 0
        owners[0, entry] = -1
        owners[1, entry] = 0
    prefill_long = length_ref[0] > SHORT_PG * PAGE
    count = jnp.int32(0)
    for request in range(1, REQS_DEV):

        def name_page(entry, count):
            page = table_ref[request, entry]
            place = jnp.where(prefill_long, count, page)
            list_ref[place] = page
            owners[0, place] = request
            owners[1, place] = jnp.minimum(length_ref[request] - entry * PAGE, PAGE)
            return count + 1

        count = lax.fori_loop(0, (length_ref[request] + PAGE - 1) // PAGE, name_page, count)
    slot = lax.broadcasted_iota(jnp.int32, (1, PAGE), 1)
    for entry in range(POOL):
        owner_ref[:, entry * PAGE : (entry + 1) * PAGE] = jnp.where(
            slot < owners[1, entry], owners[0, entry], -1
        )
    token = lax.broadcasted_iota(jnp.int32, (tokens, head_dim), 0)
    lane = lax.broadcasted_iota(jnp.int32, (tokens, head_dim), 1)
    position = length_ref[0] + token
    for i in range(tokens - PRE):
        position = jnp.where(token == PRE + i, length_ref[i + 1], position)
    angle = position.astype(jnp.float32) * frequency_ref[...]
    sine = jnp.sin(angle)
    cosine_ref[...] = jnp.cos(angle)
    sine_ref[...] = jnp.where(lane < head_dim // 2, -sine, sine)


def attention_kernel(*refs):
    pieces, hbm_refs, (keep_out, far_out, core_out) = refs[:4], refs[4:19], refs[19:22]
    local_refs = refs[22:37]
    (length_ref, table_ref, list_ref, gain_ref, q_gain_ref, k_gain_ref) = local_refs[:6]
    (cosine_ref, sine_ref, owner_ref, q_ref, k_ref, v_ref, key_ref, value_ref, o_ref) = local_refs[6:]
    (
        x_ref, query_ref, own_scores, scores_ref, mix_ref, mixed_ref, part_ref, slots_ref, decoded_ref,
        sems,
    ) = refs[37:]
    tokens, head_dim = x_ref.shape[0], k_gain_ref.shape[1]
    copies = [
        pltpu.make_async_copy(source, target, sems.at[i])
        for i, (source, target) in enumerate(zip(hbm_refs, local_refs))
    ]
    for copy in copies[:12]:
        copy.start()
    tp_index = lax.axis_index("tp")
    heads = q_ref.shape[1] // head_dim
    decodes = tokens - PRE
    for step, piece in enumerate(pieces):
        width = piece.shape[1]
        start = pl.multiple_of((tp_index ^ step) * width, width)
        x_ref[:, pl.ds(start, width)] = piece[...]
    for copy in copies[:9]:
        copy.wait()
    token = lax.broadcasted_iota(jnp.int32, (tokens, head_dim), 0)
    lane = lax.broadcasted_iota(jnp.int32, (tokens, head_dim), 1)

    def turned(values, gain):
        values = rms_scale(values, gain)
        return values * cosine_ref[...] + pltpu.roll(values, head_dim // 2, 1) * sine_ref[...]

    def with_ones(values):
        return jnp.concatenate([values, jnp.ones_like(values)], axis=1)

    normed = rms_scale(x_ref[...].astype(jnp.float32), gain_ref[...]).astype(jnp.bfloat16)
    contract = (((1,), (1,)), ((), ()))
    for copy in copies[9:12]:
        copy.wait()
    for copy in copies[12:]:
        copy.start()
    key_lin = jnp.dot(normed, k_ref[...], preferred_element_type=jnp.float32)
    values_new = jnp.dot(normed, v_ref[...], preferred_element_type=jnp.float32).astype(jnp.bfloat16)
    query_lin = jnp.dot(normed, q_ref[...], preferred_element_type=jnp.float32)
    keys_new = turned(key_lin, k_gain_ref[...]).astype(jnp.bfloat16)
    values_new = with_ones(values_new)
    to_log2 = math.log2(math.e) / math.sqrt(head_dim)
    own_mask = (lane == token) | ((lane < token) & (token < PRE))
    decode_query, decode_own = [], []
    for head in range(heads):
        span = slice(head * tokens, (head + 1) * tokens)
        query = turned(query_lin[:, head * head_dim : (head + 1) * head_dim], q_gain_ref[...]) * to_log2
        rounded = query.astype(jnp.bfloat16)
        query_ref[span, :] = rounded
        scores = lax.dot_general(rounded, keys_new, contract, preferred_element_type=jnp.float32)
        scores = jnp.where(own_mask, scores, -1e30)
        own_scores[span, :] = scores
        decode_query.append(query[PRE:])
        decode_own.append(scores[PRE:])
    decode_query = jnp.concatenate(decode_query, axis=0).astype(jnp.bfloat16)
    decode_own = jnp.concatenate(decode_own, axis=0)
    for copy in copies[12:14]:
        copy.wait()

    def raised(top, scores):
        for start in range(0, scores.shape[1], head_dim):
            top = jnp.maximum(top, scores[:, start : start + head_dim])
        return top

    def weigh(own, score_steps, value_steps, scores_ref):
        top = own
        for step, score_step in enumerate(score_steps):
            scores = score_step()
            scores_ref[step, :, : scores.shape[1]] = scores
            top = raised(top, scores)
        top = jnp.max(top, axis=1, keepdims=True)
        mix = jnp.dot(
            jnp.exp2(own - top).astype(jnp.bfloat16), values_new, preferred_element_type=jnp.float32
        )
        for step, value_step in enumerate(value_steps):
            values = value_step()
            weights = jnp.exp2(scores_ref[step, :, : values.shape[0]] - top).astype(jnp.bfloat16)
            mix = mix + jnp.dot(weights, with_ones(values), preferred_element_type=jnp.float32)
        return mix

    def taken(ref, names):
        return jnp.concatenate([ref[name] for name in names], axis=0)

    def against(queries, keys):
        return lax.dot_general(queries, keys, contract, preferred_element_type=jnp.float32)

    def prefill(names, live):
        def score(pages):
            scores = against(query_ref[...], taken(key_ref, pages))
            return scores if live is None else jnp.where(live, scores, -1e30)

        mix_ref[...] = weigh(
            own_scores[...],
            [functools.partial(score, pages) for pages in names],
            [functools.partial(taken, value_ref, pages) for pages in names],
            scores_ref,
        )

    def decode(steps, pages_of):
        row_request = 1 + lax.broadcasted_iota(jnp.int32, (heads * decodes, 1), 0) % decodes
        width = slots_ref.shape[2]

        def score(step):
            scores = against(decode_query, pages_of(key_ref, step))
            owner = owner_ref[:, step * width : (step + 1) * width]
            return jnp.where(owner == row_request, scores, -1e30)

        mix = weigh(
            decode_own,
            [functools.partial(score, step) for step in range(steps)],
            [functools.partial(pages_of, value_ref, step) for step in range(steps)],
            slots_ref,
        )
        decoded_ref[...] = mix[:, :head_dim] / mix[:, head_dim:]

    length = length_ref[0]
    listed = slots_ref.shape[2] // PAGE
    pages = scores_ref.shape[2] // PAGE

    @pl.when(length > SHORT_PG * PAGE)
    def _():
        names = [table_ref[0, entry] for entry in range(MAXPG)]
        prefill([names[first : first + pages] for first in range(0, MAXPG, pages)], None)
        decode(
            SHORT_LIST // listed,
            lambda ref, step: taken(ref, [list_ref[step * listed + i] for i in range(listed)]),
        )

    @pl.when(length <= SHORT_PG * PAGE)
    def _():
        column = lax.broadcasted_iota(jnp.int32, (1, SHORT_PG * PAGE), 1)
        prefill([[table_ref[0, entry] for entry in range(SHORT_PG)]], column < length)
        decode(
            POOL // listed,
            lambda ref, step: ref[step * listed : (step + 1) * listed].reshape(-1, head_dim),
        )

    for head in range(heads):
        part = mix_ref[head * tokens : (head + 1) * tokens, :]
        columns = slice(head * head_dim, (head + 1) * head_dim)
        mixed_ref[:, columns] = part[:, :head_dim] / part[:, head_dim:]
        mixed_ref[PRE:, columns] = decoded_ref[head * decodes : (head + 1) * decodes]
    copies[14].wait()
    part_ref[...] = jnp.dot(
        mixed_ref[...].astype(jnp.bfloat16), o_ref[...], preferred_element_type=jnp.float32
    )
    share_rows = keep_out.shape[0]

    def quarter(step):
        return pl.ds(pl.multiple_of((tp_index ^ step) * share_rows, share_rows), share_rows)

    keep_out[...] = part_ref[quarter(0), :] + x_ref[quarter(0), :].astype(jnp.float32)
    far_out[...] = part_ref[quarter(2), :]
    core_out[0] = part_ref[quarter(1), :].astype(jnp.bfloat16)
    core_out[1] = part_ref[quarter(3), :].astype(jnp.bfloat16)


def attention_shares(
    hidden_in, norm_in_gain, q_weight, k_weight, v_weight, q_gain, k_gain, o_weight,
    key_pages, value_pages, page_table, cache_len,
):
    tokens, width = hidden_in.shape[0], 4 * hidden_in.shape[1]
    head_dim = q_gain.shape[0]
    rows = q_weight.shape[1] // head_dim * tokens
    decode_rows = rows // tokens * (tokens - PRE)
    half = ROPE_BASE ** (-np.arange(head_dim // 2) / (head_dim // 2))
    frequency = jnp.asarray(np.concatenate([half, half])[None, :], jnp.float32)
    params = pltpu.CompilerParams(vmem_limit_bytes=56 * 1024 * 1024)
    rope = jax.ShapeDtypeStruct((tokens, head_dim), jnp.float32)
    cosine, sine, owner, page_list = pl.pallas_call(
        layout_kernel,
        out_shape=[
            rope,
            rope,
            jax.ShapeDtypeStruct((1, POOL * PAGE), jnp.int32),
            jax.ShapeDtypeStruct((POOL,), jnp.int32),
        ],
        in_specs=[SMEM, SMEM, VMEM],
        out_specs=[VMEM, VMEM, VMEM, SMEM],
        scratch_shapes=[pltpu.SMEM((2, POOL), jnp.int32)],
        compiler_params=params,
        name="layout",
    )(cache_len, page_table, frequency)
    far, cosine, sine, owner, page_list = ordered(
        flip(hidden_in, "tp", 2), cosine, sine, owner, page_list
    )
    pieces = (hidden_in, flip(hidden_in, "tp", 1), far, flip(far, "tp", 1))
    scalars = (cache_len, page_table, page_list)
    arrays = (
        norm_in_gain[None, :], q_gain[None, :], k_gain[None, :], cosine, sine, owner,
        q_weight, k_weight, v_weight, key_pages[0], value_pages[0], o_weight,
    )
    share = (tokens // 4, width)
    score_pages, list_pages = 4, 8
    return pl.pallas_call(
        attention_kernel,
        out_shape=[
            jax.ShapeDtypeStruct(share, jnp.float32),
            jax.ShapeDtypeStruct(share, jnp.float32),
            jax.ShapeDtypeStruct((2, *share), jnp.bfloat16),
        ],
        in_specs=[VMEM] * 4 + [pl.BlockSpec(memory_space=pltpu.HBM)] * 15,
        out_specs=[VMEM] * 3,
        scratch_shapes=[pltpu.SMEM(array.shape, array.dtype) for array in scalars]
        + [pltpu.VMEM(array.shape, array.dtype) for array in arrays]
        + [
            pltpu.VMEM((tokens, width), jnp.bfloat16),
            pltpu.VMEM((rows, head_dim), jnp.bfloat16),
            pltpu.VMEM((rows, tokens), jnp.float32),
            pltpu.VMEM((MAXPG // score_pages, rows, score_pages * PAGE), jnp.float32),
            pltpu.VMEM((rows, 2 * head_dim), jnp.float32),
            pltpu.VMEM((tokens, q_weight.shape[1]), jnp.float32),
            pltpu.VMEM((tokens, width), jnp.float32),
            pltpu.VMEM((POOL // list_pages, decode_rows, list_pages * PAGE), jnp.float32),
            pltpu.VMEM((decode_rows, head_dim), jnp.float32),
            pltpu.SemaphoreType.DMA((15,)),
        ],
        compiler_params=params,
        name="attention",
    )(*pieces, *scalars, *arrays)


def pack_kernel(
    own_ref, far_ref, gain_ref, ids_ref, routes_ref,
    rows_ref, residual_ref, spread_ref,
):
    tp_index = lax.axis_index("tp")
    share_rows, width = own_ref.shape
    mine = pl.ds(pl.multiple_of(tp_index * share_rows, share_rows), share_rows)
    residual = own_ref[...] + far_ref[...].astype(jnp.float32)
    residual_ref[...] = residual
    rows_ref[:, :width] = rms_scale(residual, gain_ref[...]).astype(jnp.bfloat16)
    expert = lax.broadcasted_iota(jnp.int32, (LANES, spread_ref.shape[0]), 0) % (LANES // 2)
    spread = jnp.zeros(expert.shape, jnp.float32)
    for k in range(ids_ref.shape[0]):
        spread = spread + jnp.where(expert == ids_ref[k : k + 1, :], routes_ref[k : k + 1, :], 0.0)
    spread_ref[...] = spread.T
    spread = spread_ref[mine, :]
    lane = lax.broadcasted_iota(jnp.int32, spread.shape, 1)
    high = spread.astype(jnp.bfloat16).astype(jnp.float32)
    rows_ref[:, width:] = jnp.where(lane < LANES // 2, high, spread - high).astype(jnp.bfloat16)


def experts_kernel(plan, *refs):
    pieces, residual_refs = refs[: len(plan)], refs[len(plan) : -7]
    gate_ref, up_ref, down_ref, keep_ref, send_ref, rows_ref, sums_ref = refs[-7:]
    req_index, tp_index = lax.axis_index("req"), lax.axis_index("tp")
    columns, _, levels, group_rows, share_width = keep_ref.shape
    width = gate_ref.shape[1]
    units = gate_ref.shape[0] // 2
    for (column, step, first), piece in zip(plan, pieces):
        count = piece.shape[1]
        for level in range(levels):
            start = (column * levels + level) * group_rows + first
            start = start + (tp_index ^ step) * (group_rows // 4)
            rows_ref[pl.ds(pl.multiple_of(start, count), count), :] = piece[level]
    spread = rows_ref[:, width:].astype(jnp.float32)
    lane = lax.broadcasted_iota(jnp.int32, spread.shape, 1) % (LANES // 2)
    weights = [
        jnp.sum(jnp.where(lane == 2 * req_index + e, spread, 0.0), axis=1, keepdims=True)
        for e in range(2)
    ]
    contract = (((1,), (1,)), ((), ()))
    rows = rows_ref[:, :width]
    gate = lax.dot_general(rows, gate_ref[...], contract, preferred_element_type=jnp.float32)
    up = lax.dot_general(rows, up_ref[...], contract, preferred_element_type=jnp.float32)
    unit = lax.broadcasted_iota(jnp.int32, gate.shape, 1)
    weight = jnp.where(unit < units, weights[0], weights[1])
    acts = (gate / (1.0 + jnp.exp(-gate)) * up * weight).astype(jnp.bfloat16)
    for step in range(4):
        start = pl.multiple_of((tp_index ^ step) * share_width, share_width)
        part = jnp.dot(
            acts, down_ref[:, pl.ds(start, share_width)], preferred_element_type=jnp.float32
        )
        for residual_ref in residual_refs:
            count = residual_ref.shape[0]
            mine = pl.ds(pl.multiple_of(tp_index * count, count), count)
            sums_ref[...] = part
            sums_ref[mine, :] += residual_ref[:, pl.ds(start, share_width)]
            part = sums_ref[...]
        target = send_ref if step % 2 else keep_ref
        part = part.reshape(columns, levels, group_rows, share_width).astype(target.dtype)
        for column in range(columns):
            target[column, step // 2] = part[column]


def run_experts(pieces, weights, group_rows, *residual):
    plan = tuple(place for place, _ in pieces)
    pieces = [piece for _, piece in pieces]
    columns, levels, packed = 1 + max(place[0] for place in plan), *pieces[0].shape[::2]
    rows, share_width = columns * levels * group_rows, weights[2].shape[1] // 4
    out_shape = (columns, 2, levels, group_rows, share_width)
    return pl.pallas_call(
        functools.partial(experts_kernel, plan),
        out_shape=[
            jax.ShapeDtypeStruct(out_shape, jnp.float32),
            jax.ShapeDtypeStruct(out_shape, jnp.bfloat16),
        ],
        in_specs=[VMEM] * (len(pieces) + len(residual) + 3),
        out_specs=[VMEM] * 2,
        scratch_shapes=[
            pltpu.VMEM((rows, packed), jnp.bfloat16),
            pltpu.VMEM((rows, share_width), jnp.float32),
        ],
        compiler_params=pltpu.CompilerParams(vmem_limit_bytes=VMEM_LIMIT),
        name="experts",
    )(*pieces, *residual, *weights)


def finish_kernel(own_ref, z1_ref, z2_ref, x_ref, y_ref, out_ref):
    total = own_ref[0]
    for extra_ref in (x_ref, y_ref):
        total = total + extra_ref[0].astype(jnp.float32)
    for extra_ref in (z1_ref, z2_ref):
        total = total + extra_ref[...].astype(jnp.float32)
    out_ref[...] = total.astype(jnp.bfloat16)


def ordered(*values):
    return lax.optimization_barrier(values)


def across_parts(line_x, line_y):
    half = line_x.shape[1] // 2
    return flip(line_x[:, :half], "tp", 2), flip(line_y[:, half:], "req", 1)


def other_core(parts):
    return tuple(flip(part, "tp", 1) for part in parts)


def with_core(pair):
    return pair[0], flip(pair[1], "tp", 1)


def joined(pair, column, y):
    return pair[0][column, y] + pair[1][column, y].astype(jnp.float32)


def near_pieces(column, line, core):
    return [((column, 0, 0), line), ((column, 1, 0), core)]


def far_pieces(column, parts, cores):
    half = parts[0].shape[1]
    if len(parts) == 1:
        return [((column, 2, 0), parts[0]), ((column, 3, 0), cores[0])]
    return [((column, 2, i * half), part) for i, part in enumerate(parts)] + [
        ((column, 3, i * half), part) for i, part in enumerate(cores)
    ]


def relayed(side):
    part = side.astype(jnp.bfloat16)
    half = part.shape[1] // 2
    return flip(part[:, :half], "req", 1), flip(part[:, half:], "tp", 2)


def neighbours(to_x, to_y, by_x, by_y):
    half = by_x.shape[1]
    to_y = jnp.concatenate([to_y[:, :half] + by_x.astype(jnp.float32), to_y[:, half:]], axis=1)
    to_x = jnp.concatenate([to_x[:, :half], to_x[:, half:] + by_y.astype(jnp.float32)], axis=1)
    return flip(to_x.astype(jnp.bfloat16), "req", 1), flip(to_y.astype(jnp.bfloat16), "tp", 2)


def moe_dense(
    kept,
    far,
    core,
    norm_post_gain,
    expert_ids,
    route_weights,
    gate_weight,
    up_weight,
    down_weight,
):
    share_rows, width = kept.shape
    token_count, share_width = 4 * share_rows, width // 4
    core = flip(core, "tp", 1)
    far = flip((far + core[1].astype(jnp.float32)).astype(jnp.bfloat16), "tp", 2)
    kept, far = ordered(kept + core[0].astype(jnp.float32), far)
    rows, residual = pl.pallas_call(
        pack_kernel,
        out_shape=[
            jax.ShapeDtypeStruct((share_rows, width + LANES), jnp.bfloat16),
            jax.ShapeDtypeStruct((share_rows, width), jnp.float32),
        ],
        in_specs=[VMEM] * 5,
        out_specs=[VMEM] * 2,
        scratch_shapes=[pltpu.VMEM((token_count, LANES), jnp.float32)],
        compiler_params=pltpu.CompilerParams(vmem_limit_bytes=8 * 1024 * 1024),
        name="pack_rows",
    )(kept, far, norm_post_gain[None, :], expert_ids.T, route_weights.T)
    gate_up = [w.transpose(0, 2, 1).reshape(-1, width) for w in (gate_weight, up_weight)]
    weights = (*gate_up, down_weight.reshape(-1, width))
    line_0 = rows[None]
    z_1, z_2 = flip(line_0, "req", 2), flip(line_0, "req", 4)
    y_0, x_0 = flip(line_0, "tp", 2), flip(line_0, "req", 1)
    line_12, z_2, y_0, x_0 = ordered(jnp.concatenate([z_1, z_2]), z_2, y_0, x_0)
    line_3, across_0, core_0, y_core_0 = ordered(
        jnp.concatenate([line_12, flip(z_2, "req", 2)]),
        across_parts(x_0, y_0),
        flip(line_0, "tp", 1),
        flip(y_0, "tp", 1),
    )
    y_3, x_3 = flip(line_3, "tp", 2), flip(line_3, "req", 1)
    all_0 = run_experts(
        near_pieces(0, line_0, core_0)
        + far_pieces(0, (y_0,), (y_core_0,))
        + near_pieces(1, x_0, flip(x_0, "tp", 1))
        + far_pieces(1, across_0, other_core(across_0)),
        weights,
        token_count,
        residual,
    )
    all_0, core_3, y_3, x_3 = ordered(all_0, flip(line_3, "tp", 1), y_3, x_3)
    y_core_3, x_core_3 = other_core((y_3, x_3))
    near_3 = run_experts(
        near_pieces(0, line_3, core_3) + far_pieces(0, (y_3,), (y_core_3,)), weights, token_count
    )
    near_3, x_core_3, across_3 = ordered(near_3, x_core_3, across_parts(x_3, y_3))
    side_3 = run_experts(
        near_pieces(0, x_3, x_core_3) + far_pieces(0, across_3, other_core(across_3)),
        weights,
        token_count,
    )
    all_0, near_3, side_3 = ordered(all_0, near_3, side_3)
    all_0, near_3, side_3 = ordered(all_0, near_3, with_core(side_3))
    near_3, all_0, relay_3 = ordered(
        with_core(near_3), with_core(all_0), relayed(joined(side_3, 0, 1))
    )
    sums_3 = ordered(*neighbours(joined(side_3, 0, 0), joined(near_3, 0, 1), *relay_3))
    sent = joined(near_3, 0, 0) + sums_3[0].astype(jnp.float32) + sums_3[1].astype(jnp.float32)
    sent_3, relay_0 = ordered(
        flip(sent[2].astype(jnp.bfloat16), "req", 2), relayed(joined(all_0, 1, 1))
    )
    sent_2, relay_0 = ordered(
        (sent[1] + sent_3.astype(jnp.float32)).astype(jnp.bfloat16), relay_0
    )
    from_z = [flip(sent[0].astype(jnp.bfloat16), "req", 2), flip(sent_2, "req", 4)]
    sums_0 = neighbours(joined(all_0, 1, 0), joined(all_0, 0, 1), *relay_0)
    return pl.pallas_call(
        finish_kernel,
        out_shape=jax.ShapeDtypeStruct((token_count, share_width), jnp.bfloat16),
        in_specs=[VMEM] * 5,
        out_specs=VMEM,
        compiler_params=pltpu.CompilerParams(vmem_limit_bytes=8 * 1024 * 1024),
        name="finish",
    )(joined(all_0, 0, 0), *from_z, *sums_0)


def moe_routed(
    x_full,
    head_part,
    norm_post_gain,
    expert_ids,
    route_weights,
    gate_weight,
    up_weight,
    down_weight,
):
    req_count = lax.axis_size("req")
    tp_index = lax.axis_index("tp")
    x_float = x_full.astype(jnp.float32)
    token_count = x_float.shape[0]
    share_width = x_float.shape[1] // lax.axis_size("tp")
    top_count = expert_ids.shape[1]
    expert_count = gate_weight.shape[0] * req_count
    capacity = max(2, 3 * token_count * top_count // (2 * expert_count))
    flat_expert = expert_ids.reshape(token_count * top_count)
    one_hot = (flat_expert[:, None] == jnp.arange(expert_count, dtype=jnp.int32)[None, :]).astype(
        jnp.int32
    )
    slot_rank = jnp.sum((jnp.cumsum(one_hot, axis=0) - one_hot) * one_hot, axis=1)
    slot_index = flat_expert * capacity + slot_rank
    head_sum = lax.psum(head_part.astype(jnp.bfloat16), "tp").astype(jnp.float32)
    residual_full = x_float + head_sum
    normed_post = rms_scale(residual_full, norm_post_gain).astype(jnp.bfloat16)
    residual = lax.dynamic_slice_in_dim(residual_full, tp_index * share_width, share_width, 1)
    send_buffer = build_buffer(normed_post, slot_index, top_count, expert_count, capacity)
    part_sums = expert_apply(
        lax.all_to_all(send_buffer, "req", split_axis=0, concat_axis=0, tiled=True),
        gate_weight,
        up_weight,
        down_weight,
    )
    returned = lax.all_to_all(part_sums, "req", split_axis=0, concat_axis=0, tiled=True)
    moe_term = weigh_back(returned, slot_index, route_weights, token_count, top_count)
    moe_share = lax.psum_scatter(
        moe_term.astype(jnp.bfloat16), "tp", scatter_dimension=1, tiled=True
    ).astype(jnp.float32)
    return (residual + moe_share).astype(jnp.bfloat16)


def attention_part(
    x_full,
    norm_in_gain,
    q_weight,
    k_weight,
    v_weight,
    q_gain,
    k_gain,
    o_weight,
    key_pages,
    value_pages,
    page_table,
    cache_len,
):
    head_dim = q_gain.shape[0]
    kv_local = key_pages.shape[0]
    group_size = q_weight.shape[1] // head_dim // kv_local
    token_count = x_full.shape[0]
    x_float = x_full.astype(jnp.float32)
    normed_in = rms_scale(x_float, norm_in_gain).astype(jnp.bfloat16)
    query_lin = jnp.dot(normed_in, q_weight, preferred_element_type=jnp.float32).reshape(
        token_count, kv_local * group_size, head_dim
    )
    key_lin = jnp.dot(normed_in, k_weight, preferred_element_type=jnp.float32).reshape(
        token_count, kv_local, head_dim
    )
    values_new = (
        jnp.dot(normed_in, v_weight, preferred_element_type=jnp.float32)
        .astype(jnp.bfloat16)
        .reshape(token_count, kv_local, head_dim)
    )
    requests, positions = token_layout(cache_len)
    queries = (
        rotate(rms_scale(query_lin, q_gain), positions)
        .astype(jnp.bfloat16)
        .reshape(token_count, kv_local, group_size, head_dim)
    )
    keys_new = rotate(rms_scale(key_lin, k_gain), positions).astype(jnp.bfloat16)
    slot_owner = page_slots(page_table, cache_len)
    cache_slots = key_pages.shape[1] * key_pages.shape[2]
    keys_cache = key_pages.reshape(kv_local, cache_slots, head_dim)
    values_cache = value_pages.reshape(kv_local, cache_slots, head_dim)
    attended = attend(
        queries, keys_new, values_new, keys_cache, values_cache, requests, positions, slot_owner
    )
    return jnp.dot(attended, o_weight, preferred_element_type=jnp.float32)


def body(
    hidden_in,
    norm_in_gain,
    q_weight,
    k_weight,
    v_weight,
    q_gain,
    k_gain,
    o_weight,
    key_pages,
    value_pages,
    page_table,
    cache_len,
    norm_post_gain,
    expert_ids,
    route_weights,
    gate_weight,
    up_weight,
    down_weight,
):
    req_count = lax.axis_size("req")
    attention = (
        norm_in_gain,
        q_weight,
        k_weight,
        v_weight,
        q_gain,
        k_gain,
        o_weight,
        key_pages,
        value_pages,
        page_table,
        cache_len,
    )
    experts = (norm_post_gain, expert_ids, route_weights, gate_weight, up_weight, down_weight)
    expert_count = gate_weight.shape[0] * req_count
    staged = (req_count, lax.axis_size("tp"), gate_weight.shape[0]) == (8, 4, 2)
    if staged and expert_count <= LANES // 2:
        return moe_dense(*attention_shares(hidden_in, *attention), *experts)
    x_full = lax.all_gather(hidden_in, "tp", axis=1, tiled=True)
    return moe_routed(x_full, attention_part(x_full, *attention), *experts)


def solution(mesh):
    return jax.shard_map(
        body,
        mesh=mesh,
        in_specs=(
            P("req", "tp"),
            P(),
            P(None, "tp"),
            P(None, "tp"),
            P(None, "tp"),
            P(),
            P(),
            P("tp", None),
            P("tp", "req", None, None),
            P("tp", "req", None, None),
            P("req", None),
            P("req"),
            P(),
            P("req", None),
            P("req", None),
            P("req", None, "tp"),
            P("req", None, "tp"),
            P("req", "tp", None),
        ),
        out_specs=P("req", "tp"),
        check_vma=False,
    )
```

```python
import functools
import math

import jax
import jax.numpy as jnp
import numpy as np
from jax import lax
from jax.experimental import pallas as pl
from jax.experimental.pallas import tpu as pltpu
from jax.sharding import PartitionSpec as P

PAGE = 128
MAXPG = 32
PRE = 120
TOK_DEV = 128
REQS_DEV = 9
POOL = 48
SHORT_PG = 2
SHORT_LIST = (REQS_DEV - 1) * SHORT_PG


NORM_EPS = 1e-06
ROPE_BASE = 1000000.0


def rms_scale(values, gain_vec):
    mean_square = jnp.mean(values * values, axis=-1, keepdims=True)
    return values * lax.rsqrt(mean_square + NORM_EPS) * gain_vec


def rotate(values, positions):
    half_dim = values.shape[-1] // 2
    exponent = jnp.arange(half_dim, dtype=jnp.float32) * (2.0 / values.shape[-1])
    frequency = jnp.power(jnp.float32(ROPE_BASE), -exponent)
    angles = positions.astype(jnp.float32)[:, None] * frequency[None, :]
    cosine = jnp.cos(angles)[:, None, :]
    sine_val = jnp.sin(angles)[:, None, :]
    front_half = values[..., :half_dim]
    back_half = values[..., half_dim:]
    return jnp.concatenate(
        [front_half * cosine - back_half * sine_val, back_half * cosine + front_half * sine_val],
        axis=-1,
    )


def token_layout(lengths):
    local_idx = jnp.arange(TOK_DEV, dtype=jnp.int32)
    requests = jnp.where(local_idx < PRE, 0, local_idx - PRE + 1)
    offsets = jnp.where(local_idx < PRE, local_idx, 0)
    request_hot = (requests[:, None] == jnp.arange(REQS_DEV, dtype=jnp.int32)[None, :]).astype(
        jnp.int32
    )
    positions = jnp.sum(request_hot * lengths[None, :], axis=1) + offsets
    return (requests, positions)


def page_slots(table, lengths):
    pages_used = (lengths + PAGE - 1) // PAGE
    entry_live = jnp.arange(MAXPG, dtype=jnp.int32)[None, :] < pages_used[:, None]
    page_match = (
        (table[:, :, None] == jnp.arange(POOL, dtype=jnp.int32)[None, None, :])
        & entry_live[:, :, None]
    ).astype(jnp.int32)
    page_owner = jnp.sum(
        page_match * jnp.arange(REQS_DEV, dtype=jnp.int32)[:, None, None], axis=(0, 1)
    )
    page_start = jnp.sum(
        page_match * (jnp.arange(MAXPG, dtype=jnp.int32) * PAGE)[None, :, None], axis=(0, 1)
    )
    page_used = jnp.sum(page_match, axis=(0, 1)) > 0
    owner_length = jnp.sum(page_match * lengths[:, None, None], axis=(0, 1))
    slot_pos = page_start[:, None] + jnp.arange(PAGE, dtype=jnp.int32)[None, :]
    slot_live = page_used[:, None] & (slot_pos < owner_length[:, None])
    slot_owner = jnp.where(slot_live, page_owner[:, None], -1)
    return slot_owner.reshape(POOL * PAGE)


def attend(
    queries, keys_new, values_new, keys_cache, values_cache, requests, positions, slot_owner
):
    inv_root = 1.0 / math.sqrt(queries.shape[-1])
    cache_mask = slot_owner[None, :] == requests[:, None]
    new_mask = (requests[None, :] == requests[:, None]) & (positions[None, :] <= positions[:, None])
    score_cache = (
        jnp.einsum("tkgh,knh->kgtn", queries, keys_cache, preferred_element_type=jnp.float32)
        * inv_root
    )
    score_new = (
        jnp.einsum("tkgh,skh->kgts", queries, keys_new, preferred_element_type=jnp.float32)
        * inv_root
    )
    score_cache = jnp.where(cache_mask[None, None], score_cache, -1e30)
    score_new = jnp.where(new_mask[None, None], score_new, -1e30)
    row_max = jnp.maximum(
        jnp.max(score_cache, axis=-1, keepdims=True), jnp.max(score_new, axis=-1, keepdims=True)
    )
    exp_cache = jnp.where(cache_mask[None, None], jnp.exp(score_cache - row_max), 0.0)
    exp_new = jnp.where(new_mask[None, None], jnp.exp(score_new - row_max), 0.0)
    total = jnp.sum(exp_cache, axis=-1, keepdims=True) + jnp.sum(exp_new, axis=-1, keepdims=True)
    prob_cache = (exp_cache / total).astype(jnp.bfloat16)
    prob_new = (exp_new / total).astype(jnp.bfloat16)
    mixed = jnp.einsum(
        "kgtn,knh->tkgh", prob_cache, values_cache, preferred_element_type=jnp.float32
    )
    mixed = mixed + jnp.einsum(
        "kgts,skh->tkgh", prob_new, values_new, preferred_element_type=jnp.float32
    )
    return mixed.astype(jnp.bfloat16).reshape(queries.shape[0], -1)


def expert_apply(blocks, gate_weight, up_weight, down_weight):
    local_experts = gate_weight.shape[0]
    sources = blocks.shape[0] // local_experts
    slot_count = blocks.shape[1]
    grouped = blocks.reshape(sources, local_experts, slot_count, blocks.shape[2])
    gate_acts = jnp.einsum(
        "sekd,edf->sekf", grouped, gate_weight, preferred_element_type=jnp.float32
    )
    up_acts = jnp.einsum("sekd,edf->sekf", grouped, up_weight, preferred_element_type=jnp.float32)
    hidden_act = (jax.nn.silu(gate_acts) * up_acts).astype(jnp.bfloat16)
    part_sums = jnp.einsum(
        "sekf,efd->sekd", hidden_act, down_weight, preferred_element_type=jnp.float32
    ).astype(jnp.bfloat16)
    return part_sums.reshape(sources * local_experts, slot_count, part_sums.shape[3])


def build_buffer(normed, slot_index, top_count, expert_count, capacity):
    picked = jnp.repeat(normed, top_count, axis=0)
    buffer_rows = (
        jnp.zeros((expert_count * capacity, normed.shape[1]), normed.dtype)
        .at[slot_index]
        .set(picked)
    )
    return buffer_rows.reshape(expert_count, capacity, normed.shape[1])


def weigh_back(returned, slot_index, route_weights, token_count, top_count):
    row_width = returned.shape[2]
    back_rows = returned.reshape(returned.shape[0] * returned.shape[1], row_width)[slot_index]
    weighted = (
        back_rows.astype(jnp.float32) * route_weights.reshape(token_count * top_count)[:, None]
    )
    return jnp.sum(weighted.reshape(token_count, top_count, row_width), axis=1)


LANES = 128
VMEM = pl.BlockSpec(memory_space=pltpu.VMEM)
SMEM = pl.BlockSpec(memory_space=pltpu.SMEM)
VMEM_LIMIT = 24 * 1024 * 1024


def flip(value, axis, bits):
    return lax.ppermute(value, axis, [(i, i ^ bits) for i in range(lax.axis_size(axis))])


def layout_kernel(
    length_ref, table_ref, frequency_ref, cosine_ref, sine_ref, owner_ref, list_ref, owners
):
    tokens, head_dim = cosine_ref.shape
    for entry in range(POOL):
        list_ref[entry] = 0
        owners[0, entry] = -1
        owners[1, entry] = 0
    prefill_long = length_ref[0] > SHORT_PG * PAGE
    count = jnp.int32(0)
    for request in range(1, REQS_DEV):

        def name_page(entry, count):
            page = table_ref[request, entry]
            place = jnp.where(prefill_long, count, page)
            list_ref[place] = page
            owners[0, place] = request
            owners[1, place] = jnp.minimum(length_ref[request] - entry * PAGE, PAGE)
            return count + 1

        count = lax.fori_loop(0, (length_ref[request] + PAGE - 1) // PAGE, name_page, count)
    slot = lax.broadcasted_iota(jnp.int32, (1, PAGE), 1)
    for entry in range(POOL):
        owner_ref[:, entry * PAGE : (entry + 1) * PAGE] = jnp.where(
            slot < owners[1, entry], owners[0, entry], -1
        )
    token = lax.broadcasted_iota(jnp.int32, (tokens, head_dim), 0)
    lane = lax.broadcasted_iota(jnp.int32, (tokens, head_dim), 1)
    position = length_ref[0] + token
    for i in range(tokens - PRE):
        position = jnp.where(token == PRE + i, length_ref[i + 1], position)
    angle = position.astype(jnp.float32) * frequency_ref[...]
    sine = jnp.sin(angle)
    cosine_ref[...] = jnp.cos(angle)
    sine_ref[...] = jnp.where(lane < head_dim // 2, -sine, sine)


def attention_kernel(*refs):
    pieces, hbm_refs, (keep_out, far_out, core_out) = refs[:4], refs[4:19], refs[19:22]
    local_refs = refs[22:37]
    (length_ref, table_ref, list_ref, gain_ref, q_gain_ref, k_gain_ref) = local_refs[:6]
    (cosine_ref, sine_ref, owner_ref, q_ref, k_ref, v_ref, key_ref, value_ref, o_ref) = local_refs[6:]
    (
        x_ref, query_ref, own_scores, scores_ref, mix_ref, mixed_ref, part_ref, slots_ref, decoded_ref,
        sems,
    ) = refs[37:]
    tokens, head_dim = x_ref.shape[0], k_gain_ref.shape[1]
    copies = [
        pltpu.make_async_copy(source, target, sems.at[i])
        for i, (source, target) in enumerate(zip(hbm_refs, local_refs))
    ]
    for copy in copies:
        copy.start()
    tp_index = lax.axis_index("tp")
    heads = q_ref.shape[1] // head_dim
    decodes = tokens - PRE
    for step, piece in enumerate(pieces):
        width = piece.shape[1]
        start = pl.multiple_of((tp_index ^ step) * width, width)
        x_ref[:, pl.ds(start, width)] = piece[...]
    for copy in copies[:9]:
        copy.wait()
    token = lax.broadcasted_iota(jnp.int32, (tokens, head_dim), 0)
    lane = lax.broadcasted_iota(jnp.int32, (tokens, head_dim), 1)

    def turned(values, gain):
        values = rms_scale(values, gain)
        return values * cosine_ref[...] + pltpu.roll(values, head_dim // 2, 1) * sine_ref[...]

    def with_ones(values):
        return jnp.concatenate([values, jnp.ones_like(values)], axis=1)

    normed = rms_scale(x_ref[...].astype(jnp.float32), gain_ref[...]).astype(jnp.bfloat16)
    contract = (((1,), (1,)), ((), ()))
    for copy in copies[9:12]:
        copy.wait()
    key_lin = jnp.dot(normed, k_ref[...], preferred_element_type=jnp.float32)
    values_new = jnp.dot(normed, v_ref[...], preferred_element_type=jnp.float32).astype(jnp.bfloat16)
    query_lin = jnp.dot(normed, q_ref[...], preferred_element_type=jnp.float32)
    keys_new = turned(key_lin, k_gain_ref[...]).astype(jnp.bfloat16)
    values_new = with_ones(values_new)
    to_log2 = math.log2(math.e) / math.sqrt(head_dim)
    own_mask = (lane == token) | ((lane < token) & (token < PRE))
    decode_query, decode_own = [], []
    for head in range(heads):
        span = slice(head * tokens, (head + 1) * tokens)
        query = turned(query_lin[:, head * head_dim : (head + 1) * head_dim], q_gain_ref[...]) * to_log2
        rounded = query.astype(jnp.bfloat16)
        query_ref[span, :] = rounded
        scores = lax.dot_general(rounded, keys_new, contract, preferred_element_type=jnp.float32)
        scores = jnp.where(own_mask, scores, -1e30)
        own_scores[span, :] = scores
        decode_query.append(query[PRE:])
        decode_own.append(scores[PRE:])
    decode_query = jnp.concatenate(decode_query, axis=0).astype(jnp.bfloat16)
    decode_own = jnp.concatenate(decode_own, axis=0)
    for copy in copies[12:14]:
        copy.wait()

    def raised(top, scores):
        for start in range(0, scores.shape[1], head_dim):
            top = jnp.maximum(top, scores[:, start : start + head_dim])
        return top

    def weigh(own, score_steps, value_steps, scores_ref):
        top = own
        for step, score_step in enumerate(score_steps):
            scores = score_step()
            scores_ref[step, :, : scores.shape[1]] = scores
            top = raised(top, scores)
        top = jnp.max(top, axis=1, keepdims=True)
        mix = jnp.dot(
            jnp.exp2(own - top).astype(jnp.bfloat16), values_new, preferred_element_type=jnp.float32
        )
        for step, value_step in enumerate(value_steps):
            values = value_step()
            weights = jnp.exp2(scores_ref[step, :, : values.shape[0]] - top).astype(jnp.bfloat16)
            mix = mix + jnp.dot(weights, with_ones(values), preferred_element_type=jnp.float32)
        return mix

    def taken(ref, names):
        return jnp.concatenate([ref[name] for name in names], axis=0)

    def against(queries, keys):
        return lax.dot_general(queries, keys, contract, preferred_element_type=jnp.float32)

    def prefill(names, live):
        def score(pages):
            scores = against(query_ref[...], taken(key_ref, pages))
            return scores if live is None else jnp.where(live, scores, -1e30)

        mix_ref[...] = weigh(
            own_scores[...],
            [functools.partial(score, pages) for pages in names],
            [functools.partial(taken, value_ref, pages) for pages in names],
            scores_ref,
        )

    def decode(steps, pages_of):
        row_request = 1 + lax.broadcasted_iota(jnp.int32, (heads * decodes, 1), 0) % decodes
        width = slots_ref.shape[2]

        def score(step):
            scores = against(decode_query, pages_of(key_ref, step))
            owner = owner_ref[:, step * width : (step + 1) * width]
            return jnp.where(owner == row_request, scores, -1e30)

        mix = weigh(
            decode_own,
            [functools.partial(score, step) for step in range(steps)],
            [functools.partial(pages_of, value_ref, step) for step in range(steps)],
            slots_ref,
        )
        decoded_ref[...] = mix[:, :head_dim] / mix[:, head_dim:]

    length = length_ref[0]
    listed = slots_ref.shape[2] // PAGE
    pages = scores_ref.shape[2] // PAGE

    @pl.when(length > SHORT_PG * PAGE)
    def _():
        names = [table_ref[0, entry] for entry in range(MAXPG)]
        prefill([names[first : first + pages] for first in range(0, MAXPG, pages)], None)
        decode(
            SHORT_LIST // listed,
            lambda ref, step: taken(ref, [list_ref[step * listed + i] for i in range(listed)]),
        )

    @pl.when(length <= SHORT_PG * PAGE)
    def _():
        column = lax.broadcasted_iota(jnp.int32, (1, SHORT_PG * PAGE), 1)
        prefill([[table_ref[0, entry] for entry in range(SHORT_PG)]], column < length)
        decode(
            POOL // listed,
            lambda ref, step: ref[step * listed : (step + 1) * listed].reshape(-1, head_dim),
        )

    for head in range(heads):
        part = mix_ref[head * tokens : (head + 1) * tokens, :]
        columns = slice(head * head_dim, (head + 1) * head_dim)
        mixed_ref[:, columns] = part[:, :head_dim] / part[:, head_dim:]
        mixed_ref[PRE:, columns] = decoded_ref[head * decodes : (head + 1) * decodes]
    copies[14].wait()
    part_ref[...] = jnp.dot(
        mixed_ref[...].astype(jnp.bfloat16), o_ref[...], preferred_element_type=jnp.float32
    )
    share_rows = keep_out.shape[0]

    def quarter(step):
        return pl.ds(pl.multiple_of((tp_index ^ step) * share_rows, share_rows), share_rows)

    keep_out[...] = part_ref[quarter(0), :] + x_ref[quarter(0), :].astype(jnp.float32)
    far_out[...] = part_ref[quarter(2), :]
    core_out[0] = part_ref[quarter(1), :].astype(jnp.bfloat16)
    core_out[1] = part_ref[quarter(3), :].astype(jnp.bfloat16)


def attention_shares(
    hidden_in, norm_in_gain, q_weight, k_weight, v_weight, q_gain, k_gain, o_weight,
    key_pages, value_pages, page_table, cache_len,
):
    tokens, width = hidden_in.shape[0], 4 * hidden_in.shape[1]
    head_dim = q_gain.shape[0]
    rows = q_weight.shape[1] // head_dim * tokens
    decode_rows = rows // tokens * (tokens - PRE)
    half = ROPE_BASE ** (-np.arange(head_dim // 2) / (head_dim // 2))
    frequency = jnp.asarray(np.concatenate([half, half])[None, :], jnp.float32)
    params = pltpu.CompilerParams(vmem_limit_bytes=56 * 1024 * 1024)
    rope = jax.ShapeDtypeStruct((tokens, head_dim), jnp.float32)
    cosine, sine, owner, page_list = pl.pallas_call(
        layout_kernel,
        out_shape=[
            rope,
            rope,
            jax.ShapeDtypeStruct((1, POOL * PAGE), jnp.int32),
            jax.ShapeDtypeStruct((POOL,), jnp.int32),
        ],
        in_specs=[SMEM, SMEM, VMEM],
        out_specs=[VMEM, VMEM, VMEM, SMEM],
        scratch_shapes=[pltpu.SMEM((2, POOL), jnp.int32)],
        compiler_params=params,
        name="layout",
    )(cache_len, page_table, frequency)
    far, cosine, sine, owner, page_list = ordered(
        flip(hidden_in, "tp", 2), cosine, sine, owner, page_list
    )
    pieces = (hidden_in, flip(hidden_in, "tp", 1), far, flip(far, "tp", 1))
    scalars = (cache_len, page_table, page_list)
    arrays = (
        norm_in_gain[None, :], q_gain[None, :], k_gain[None, :], cosine, sine, owner,
        q_weight, k_weight, v_weight, key_pages[0], value_pages[0], o_weight,
    )
    share = (tokens // 4, width)
    score_pages, list_pages = 4, 8
    return pl.pallas_call(
        attention_kernel,
        out_shape=[
            jax.ShapeDtypeStruct(share, jnp.float32),
            jax.ShapeDtypeStruct(share, jnp.float32),
            jax.ShapeDtypeStruct((2, *share), jnp.bfloat16),
        ],
        in_specs=[VMEM] * 4 + [pl.BlockSpec(memory_space=pltpu.HBM)] * 15,
        out_specs=[VMEM] * 3,
        scratch_shapes=[pltpu.SMEM(array.shape, array.dtype) for array in scalars]
        + [pltpu.VMEM(array.shape, array.dtype) for array in arrays]
        + [
            pltpu.VMEM((tokens, width), jnp.bfloat16),
            pltpu.VMEM((rows, head_dim), jnp.bfloat16),
            pltpu.VMEM((rows, tokens), jnp.float32),
            pltpu.VMEM((MAXPG // score_pages, rows, score_pages * PAGE), jnp.float32),
            pltpu.VMEM((rows, 2 * head_dim), jnp.float32),
            pltpu.VMEM((tokens, q_weight.shape[1]), jnp.float32),
            pltpu.VMEM((tokens, width), jnp.float32),
            pltpu.VMEM((POOL // list_pages, decode_rows, list_pages * PAGE), jnp.float32),
            pltpu.VMEM((decode_rows, head_dim), jnp.float32),
            pltpu.SemaphoreType.DMA((15,)),
        ],
        compiler_params=params,
        name="attention",
    )(*pieces, *scalars, *arrays)


def pack_kernel(
    own_ref, far_ref, gain_ref, ids_ref, routes_ref,
    rows_ref, residual_ref, spread_ref,
):
    tp_index = lax.axis_index("tp")
    share_rows, width = own_ref.shape
    mine = pl.ds(pl.multiple_of(tp_index * share_rows, share_rows), share_rows)
    residual = own_ref[...] + far_ref[...].astype(jnp.float32)
    residual_ref[...] = residual
    rows_ref[:, :width] = rms_scale(residual, gain_ref[...]).astype(jnp.bfloat16)
    expert = lax.broadcasted_iota(jnp.int32, (LANES, spread_ref.shape[0]), 0) % (LANES // 2)
    spread = jnp.zeros(expert.shape, jnp.float32)
    for k in range(ids_ref.shape[0]):
        spread = spread + jnp.where(expert == ids_ref[k : k + 1, :], routes_ref[k : k + 1, :], 0.0)
    spread_ref[...] = spread.T
    spread = spread_ref[mine, :]
    lane = lax.broadcasted_iota(jnp.int32, spread.shape, 1)
    high = spread.astype(jnp.bfloat16).astype(jnp.float32)
    rows_ref[:, width:] = jnp.where(lane < LANES // 2, high, spread - high).astype(jnp.bfloat16)


def experts_kernel(plan, residuals, *refs):
    pieces, residual_refs = refs[: len(plan)], refs[len(plan) : len(plan) + residuals]
    gate_ref, up_ref, down_ref, keep_ref, *send_refs, rows_ref, sums_ref = refs[len(plan) + residuals :]
    req_index, tp_index = lax.axis_index("req"), lax.axis_index("tp")
    columns, _, levels, group_rows, share_width = keep_ref.shape
    width = gate_ref.shape[1]
    units = gate_ref.shape[0] // 2
    for (column, step, first), piece in zip(plan, pieces):
        count = piece.shape[1]
        for level in range(levels):
            start = (column * levels + level) * group_rows + first
            start = start + (tp_index ^ step) * (group_rows // 4)
            rows_ref[pl.ds(pl.multiple_of(start, count), count), :] = piece[level]
    spread = rows_ref[:, width:].astype(jnp.float32)
    lane = lax.broadcasted_iota(jnp.int32, spread.shape, 1) % (LANES // 2)
    weights = [
        jnp.sum(jnp.where(lane == 2 * req_index + e, spread, 0.0), axis=1, keepdims=True)
        for e in range(2)
    ]
    contract = (((1,), (1,)), ((), ()))
    rows = rows_ref[:, :width]
    gate = lax.dot_general(rows, gate_ref[...], contract, preferred_element_type=jnp.float32)
    up = lax.dot_general(rows, up_ref[...], contract, preferred_element_type=jnp.float32)
    unit = lax.broadcasted_iota(jnp.int32, gate.shape, 1)
    weight = jnp.where(unit < units, weights[0], weights[1])
    acts = (gate / (1.0 + jnp.exp(-gate)) * up * weight).astype(jnp.bfloat16)
    for step in range(4):
        start = pl.multiple_of((tp_index ^ step) * share_width, share_width)
        part = jnp.dot(
            acts, down_ref[:, pl.ds(start, share_width)], preferred_element_type=jnp.float32
        )
        for residual_ref in residual_refs:
            count = residual_ref.shape[0]
            mine = pl.ds(pl.multiple_of(tp_index * count, count), count)
            sums_ref[...] = part
            sums_ref[mine, :] += residual_ref[:, pl.ds(start, share_width)]
            part = sums_ref[...]
        part = part.reshape(columns, levels, group_rows, share_width)
        if step % 2:
            send_refs[step // 2][...] = part.astype(jnp.bfloat16)
            continue
        for column in range(columns):
            keep_ref[column, step // 2] = part[column]


def run_experts(pieces, weights, group_rows, *residual):
    plan = tuple(place for place, _ in pieces)
    pieces = [piece for _, piece in pieces]
    columns, levels, packed = 1 + max(place[0] for place in plan), *pieces[0].shape[::2]
    rows, share_width = columns * levels * group_rows, weights[2].shape[1] // 4
    sums = (levels, group_rows, share_width)
    keep, *send = pl.pallas_call(
        functools.partial(experts_kernel, plan, len(residual)),
        out_shape=[jax.ShapeDtypeStruct((columns, 2, *sums), jnp.float32)]
        + [jax.ShapeDtypeStruct((columns, *sums), jnp.bfloat16)] * 2,
        in_specs=[VMEM] * (len(pieces) + len(residual) + 3),
        out_specs=[VMEM] * 3,
        scratch_shapes=[
            pltpu.VMEM((rows, packed), jnp.bfloat16),
            pltpu.VMEM((rows, share_width), jnp.float32),
        ],
        compiler_params=pltpu.CompilerParams(vmem_limit_bytes=VMEM_LIMIT),
        name="experts",
    )(*pieces, *residual, *weights)
    return keep, send


def finish_kernel(own_ref, z1_ref, z2_ref, x_ref, y_ref, out_ref):
    total = own_ref[0]
    for extra_ref in (x_ref, y_ref):
        total = total + extra_ref[0].astype(jnp.float32)
    for extra_ref in (z1_ref, z2_ref):
        total = total + extra_ref[...].astype(jnp.float32)
    out_ref[...] = total.astype(jnp.bfloat16)


def ordered(*values):
    return lax.optimization_barrier(values)


def across_parts(line_x, line_y):
    half = line_x.shape[1] // 2
    return flip(line_x[:, :half], "tp", 2), flip(line_y[:, half:], "req", 1)


def other_core(parts):
    return tuple(flip(part, "tp", 1) for part in parts)


def with_core(pair):
    return pair[0], list(other_core(pair[1]))


def joined(pair, column, y):
    return pair[0][column, y] + pair[1][y][column].astype(jnp.float32)


def near_pieces(column, line, core):
    return [((column, 0, 0), line), ((column, 1, 0), core)]


def far_pieces(column, parts, cores):
    half = parts[0].shape[1]
    if len(parts) == 1:
        return [((column, 2, 0), parts[0]), ((column, 3, 0), cores[0])]
    return [((column, 2, i * half), part) for i, part in enumerate(parts)] + [
        ((column, 3, i * half), part) for i, part in enumerate(cores)
    ]


def relayed(side):
    part = side.astype(jnp.bfloat16)
    half = part.shape[1] // 2
    return flip(part[:, :half], "req", 1), flip(part[:, half:], "tp", 2)


def neighbours(to_x, to_y, by_x, by_y):
    half = by_x.shape[1]
    to_y = jnp.concatenate([to_y[:, :half] + by_x.astype(jnp.float32), to_y[:, half:]], axis=1)
    to_x = jnp.concatenate([to_x[:, :half], to_x[:, half:] + by_y.astype(jnp.float32)], axis=1)
    return flip(to_x.astype(jnp.bfloat16), "req", 1), flip(to_y.astype(jnp.bfloat16), "tp", 2)


def moe_dense(
    kept,
    far,
    core,
    norm_post_gain,
    expert_ids,
    route_weights,
    gate_weight,
    up_weight,
    down_weight,
):
    share_rows, width = kept.shape
    token_count, share_width = 4 * share_rows, width // 4
    core = flip(core, "tp", 1)
    far, kept, core = ordered((far + core[1].astype(jnp.float32)).astype(jnp.bfloat16), kept, core)
    kept, far = ordered(kept + core[0].astype(jnp.float32), flip(far, "tp", 2))
    rows, residual = pl.pallas_call(
        pack_kernel,
        out_shape=[
            jax.ShapeDtypeStruct((share_rows, width + LANES), jnp.bfloat16),
            jax.ShapeDtypeStruct((share_rows, width), jnp.float32),
        ],
        in_specs=[VMEM] * 5,
        out_specs=[VMEM] * 2,
        scratch_shapes=[pltpu.VMEM((token_count, LANES), jnp.float32)],
        compiler_params=pltpu.CompilerParams(vmem_limit_bytes=8 * 1024 * 1024),
        name="pack_rows",
    )(kept, far, norm_post_gain[None, :], expert_ids.T, route_weights.T)
    gate_up = [w.transpose(0, 2, 1).reshape(-1, width) for w in (gate_weight, up_weight)]
    weights = (*gate_up, down_weight.reshape(-1, width))
    line_0 = rows[None]
    z_1, z_2 = flip(line_0, "req", 2), flip(line_0, "req", 4)
    y_0, x_0 = flip(line_0, "tp", 2), flip(line_0, "req", 1)
    line_12, z_2, y_0, x_0 = ordered(jnp.concatenate([z_1, z_2]), z_2, y_0, x_0)
    line_3, across_0, core_0, y_core_0 = ordered(
        jnp.concatenate([line_12, flip(z_2, "req", 2)]),
        across_parts(x_0, y_0),
        flip(line_0, "tp", 1),
        flip(y_0, "tp", 1),
    )
    y_3, x_3 = flip(line_3, "tp", 2), flip(line_3, "req", 1)
    all_0 = run_experts(
        near_pieces(0, line_0, core_0)
        + far_pieces(0, (y_0,), (y_core_0,))
        + near_pieces(1, x_0, flip(x_0, "tp", 1))
        + far_pieces(1, across_0, other_core(across_0)),
        weights,
        token_count,
        residual,
    )
    all_0, core_3, y_3, x_3 = ordered(all_0, flip(line_3, "tp", 1), y_3, x_3)
    y_core_3, x_core_3 = other_core((y_3, x_3))
    near_3 = run_experts(
        near_pieces(0, line_3, core_3) + far_pieces(0, (y_3,), (y_core_3,)), weights, token_count
    )
    near_3, x_core_3, across_3 = ordered(near_3, x_core_3, across_parts(x_3, y_3))
    side_3 = run_experts(
        near_pieces(0, x_3, x_core_3) + far_pieces(0, across_3, other_core(across_3)),
        weights,
        token_count,
    )
    all_0, near_3, side_3 = ordered(all_0, near_3, side_3)
    keep, (send, first) = side_3
    all_0, near_3, keep, send, first = ordered(all_0, near_3, keep, send, flip(first, "tp", 1))
    relay_3 = relayed(joined((keep, (send, first)), 0, 1))
    near_3, all_0, side_3, relay_3 = ordered(
        with_core(near_3), with_core(all_0), (keep, [flip(send, "tp", 1), first]), relay_3
    )
    sums_3 = ordered(*neighbours(joined(side_3, 0, 0), joined(near_3, 0, 1), *relay_3))
    sent = joined(near_3, 0, 0) + sums_3[0].astype(jnp.float32) + sums_3[1].astype(jnp.float32)
    sent_3, relay_0 = ordered(
        flip(sent[2].astype(jnp.bfloat16), "req", 2), relayed(joined(all_0, 1, 1))
    )
    sent_2, relay_0 = ordered(
        (sent[1] + sent_3.astype(jnp.float32)).astype(jnp.bfloat16), relay_0
    )
    from_z = [flip(sent[0].astype(jnp.bfloat16), "req", 2), flip(sent_2, "req", 4)]
    sums_0 = neighbours(joined(all_0, 1, 0), joined(all_0, 0, 1), *relay_0)
    return pl.pallas_call(
        finish_kernel,
        out_shape=jax.ShapeDtypeStruct((token_count, share_width), jnp.bfloat16),
        in_specs=[VMEM] * 5,
        out_specs=VMEM,
        compiler_params=pltpu.CompilerParams(vmem_limit_bytes=8 * 1024 * 1024),
        name="finish",
    )(joined(all_0, 0, 0), *from_z, *sums_0)


def moe_routed(
    x_full,
    head_part,
    norm_post_gain,
    expert_ids,
    route_weights,
    gate_weight,
    up_weight,
    down_weight,
):
    req_count = lax.axis_size("req")
    tp_index = lax.axis_index("tp")
    x_float = x_full.astype(jnp.float32)
    token_count = x_float.shape[0]
    share_width = x_float.shape[1] // lax.axis_size("tp")
    top_count = expert_ids.shape[1]
    expert_count = gate_weight.shape[0] * req_count
    capacity = max(2, 3 * token_count * top_count // (2 * expert_count))
    flat_expert = expert_ids.reshape(token_count * top_count)
    one_hot = (flat_expert[:, None] == jnp.arange(expert_count, dtype=jnp.int32)[None, :]).astype(
        jnp.int32
    )
    slot_rank = jnp.sum((jnp.cumsum(one_hot, axis=0) - one_hot) * one_hot, axis=1)
    slot_index = flat_expert * capacity + slot_rank
    head_sum = lax.psum(head_part.astype(jnp.bfloat16), "tp").astype(jnp.float32)
    residual_full = x_float + head_sum
    normed_post = rms_scale(residual_full, norm_post_gain).astype(jnp.bfloat16)
    residual = lax.dynamic_slice_in_dim(residual_full, tp_index * share_width, share_width, 1)
    send_buffer = build_buffer(normed_post, slot_index, top_count, expert_count, capacity)
    part_sums = expert_apply(
        lax.all_to_all(send_buffer, "req", split_axis=0, concat_axis=0, tiled=True),
        gate_weight,
        up_weight,
        down_weight,
    )
    returned = lax.all_to_all(part_sums, "req", split_axis=0, concat_axis=0, tiled=True)
    moe_term = weigh_back(returned, slot_index, route_weights, token_count, top_count)
    moe_share = lax.psum_scatter(
        moe_term.astype(jnp.bfloat16), "tp", scatter_dimension=1, tiled=True
    ).astype(jnp.float32)
    return (residual + moe_share).astype(jnp.bfloat16)


def attention_part(
    x_full,
    norm_in_gain,
    q_weight,
    k_weight,
    v_weight,
    q_gain,
    k_gain,
    o_weight,
    key_pages,
    value_pages,
    page_table,
    cache_len,
):
    head_dim = q_gain.shape[0]
    kv_local = key_pages.shape[0]
    group_size = q_weight.shape[1] // head_dim // kv_local
    token_count = x_full.shape[0]
    x_float = x_full.astype(jnp.float32)
    normed_in = rms_scale(x_float, norm_in_gain).astype(jnp.bfloat16)
    query_lin = jnp.dot(normed_in, q_weight, preferred_element_type=jnp.float32).reshape(
        token_count, kv_local * group_size, head_dim
    )
    key_lin = jnp.dot(normed_in, k_weight, preferred_element_type=jnp.float32).reshape(
        token_count, kv_local, head_dim
    )
    values_new = (
        jnp.dot(normed_in, v_weight, preferred_element_type=jnp.float32)
        .astype(jnp.bfloat16)
        .reshape(token_count, kv_local, head_dim)
    )
    requests, positions = token_layout(cache_len)
    queries = (
        rotate(rms_scale(query_lin, q_gain), positions)
        .astype(jnp.bfloat16)
        .reshape(token_count, kv_local, group_size, head_dim)
    )
    keys_new = rotate(rms_scale(key_lin, k_gain), positions).astype(jnp.bfloat16)
    slot_owner = page_slots(page_table, cache_len)
    cache_slots = key_pages.shape[1] * key_pages.shape[2]
    keys_cache = key_pages.reshape(kv_local, cache_slots, head_dim)
    values_cache = value_pages.reshape(kv_local, cache_slots, head_dim)
    attended = attend(
        queries, keys_new, values_new, keys_cache, values_cache, requests, positions, slot_owner
    )
    return jnp.dot(attended, o_weight, preferred_element_type=jnp.float32)


def body(
    hidden_in,
    norm_in_gain,
    q_weight,
    k_weight,
    v_weight,
    q_gain,
    k_gain,
    o_weight,
    key_pages,
    value_pages,
    page_table,
    cache_len,
    norm_post_gain,
    expert_ids,
    route_weights,
    gate_weight,
    up_weight,
    down_weight,
):
    req_count = lax.axis_size("req")
    attention = (
        norm_in_gain,
        q_weight,
        k_weight,
        v_weight,
        q_gain,
        k_gain,
        o_weight,
        key_pages,
        value_pages,
        page_table,
        cache_len,
    )
    experts = (norm_post_gain, expert_ids, route_weights, gate_weight, up_weight, down_weight)
    expert_count = gate_weight.shape[0] * req_count
    staged = (req_count, lax.axis_size("tp"), gate_weight.shape[0]) == (8, 4, 2)
    if staged and expert_count <= LANES // 2:
        return moe_dense(*attention_shares(hidden_in, *attention), *experts)
    x_full = lax.all_gather(hidden_in, "tp", axis=1, tiled=True)
    return moe_routed(x_full, attention_part(x_full, *attention), *experts)


def solution(mesh):
    return jax.shard_map(
        body,
        mesh=mesh,
        in_specs=(
            P("req", "tp"),
            P(),
            P(None, "tp"),
            P(None, "tp"),
            P(None, "tp"),
            P(),
            P(),
            P("tp", None),
            P("tp", "req", None, None),
            P("tp", "req", None, None),
            P("req", None),
            P("req"),
            P(),
            P("req", None),
            P("req", None),
            P("req", None, "tp"),
            P("req", None, "tp"),
            P("req", "tp", None),
        ),
        out_specs=P("req", "tp"),
        check_vma=False,
    )
```

```python
import functools
import math

import jax
import jax.numpy as jnp
import numpy as np
from jax import lax
from jax.experimental import pallas as pl
from jax.experimental.pallas import tpu as pltpu
from jax.sharding import PartitionSpec as P

PAGE = 128
MAXPG = 32
PRE = 120
TOK_DEV = 128
REQS_DEV = 9
POOL = 48
SHORT_PG = 2
SHORT_LIST = (REQS_DEV - 1) * SHORT_PG


NORM_EPS = 1e-06
ROPE_BASE = 1000000.0


def rms_scale(values, gain_vec):
    mean_square = jnp.mean(values * values, axis=-1, keepdims=True)
    return values * lax.rsqrt(mean_square + NORM_EPS) * gain_vec


def rotate(values, positions):
    half_dim = values.shape[-1] // 2
    exponent = jnp.arange(half_dim, dtype=jnp.float32) * (2.0 / values.shape[-1])
    frequency = jnp.power(jnp.float32(ROPE_BASE), -exponent)
    angles = positions.astype(jnp.float32)[:, None] * frequency[None, :]
    cosine = jnp.cos(angles)[:, None, :]
    sine_val = jnp.sin(angles)[:, None, :]
    front_half = values[..., :half_dim]
    back_half = values[..., half_dim:]
    return jnp.concatenate(
        [front_half * cosine - back_half * sine_val, back_half * cosine + front_half * sine_val],
        axis=-1,
    )


def token_layout(lengths):
    local_idx = jnp.arange(TOK_DEV, dtype=jnp.int32)
    requests = jnp.where(local_idx < PRE, 0, local_idx - PRE + 1)
    offsets = jnp.where(local_idx < PRE, local_idx, 0)
    request_hot = (requests[:, None] == jnp.arange(REQS_DEV, dtype=jnp.int32)[None, :]).astype(
        jnp.int32
    )
    positions = jnp.sum(request_hot * lengths[None, :], axis=1) + offsets
    return (requests, positions)


def page_slots(table, lengths):
    pages_used = (lengths + PAGE - 1) // PAGE
    entry_live = jnp.arange(MAXPG, dtype=jnp.int32)[None, :] < pages_used[:, None]
    page_match = (
        (table[:, :, None] == jnp.arange(POOL, dtype=jnp.int32)[None, None, :])
        & entry_live[:, :, None]
    ).astype(jnp.int32)
    page_owner = jnp.sum(
        page_match * jnp.arange(REQS_DEV, dtype=jnp.int32)[:, None, None], axis=(0, 1)
    )
    page_start = jnp.sum(
        page_match * (jnp.arange(MAXPG, dtype=jnp.int32) * PAGE)[None, :, None], axis=(0, 1)
    )
    page_used = jnp.sum(page_match, axis=(0, 1)) > 0
    owner_length = jnp.sum(page_match * lengths[:, None, None], axis=(0, 1))
    slot_pos = page_start[:, None] + jnp.arange(PAGE, dtype=jnp.int32)[None, :]
    slot_live = page_used[:, None] & (slot_pos < owner_length[:, None])
    slot_owner = jnp.where(slot_live, page_owner[:, None], -1)
    return slot_owner.reshape(POOL * PAGE)


def attend(
    queries, keys_new, values_new, keys_cache, values_cache, requests, positions, slot_owner
):
    inv_root = 1.0 / math.sqrt(queries.shape[-1])
    cache_mask = slot_owner[None, :] == requests[:, None]
    new_mask = (requests[None, :] == requests[:, None]) & (positions[None, :] <= positions[:, None])
    score_cache = (
        jnp.einsum("tkgh,knh->kgtn", queries, keys_cache, preferred_element_type=jnp.float32)
        * inv_root
    )
    score_new = (
        jnp.einsum("tkgh,skh->kgts", queries, keys_new, preferred_element_type=jnp.float32)
        * inv_root
    )
    score_cache = jnp.where(cache_mask[None, None], score_cache, -1e30)
    score_new = jnp.where(new_mask[None, None], score_new, -1e30)
    row_max = jnp.maximum(
        jnp.max(score_cache, axis=-1, keepdims=True), jnp.max(score_new, axis=-1, keepdims=True)
    )
    exp_cache = jnp.where(cache_mask[None, None], jnp.exp(score_cache - row_max), 0.0)
    exp_new = jnp.where(new_mask[None, None], jnp.exp(score_new - row_max), 0.0)
    total = jnp.sum(exp_cache, axis=-1, keepdims=True) + jnp.sum(exp_new, axis=-1, keepdims=True)
    prob_cache = (exp_cache / total).astype(jnp.bfloat16)
    prob_new = (exp_new / total).astype(jnp.bfloat16)
    mixed = jnp.einsum(
        "kgtn,knh->tkgh", prob_cache, values_cache, preferred_element_type=jnp.float32
    )
    mixed = mixed + jnp.einsum(
        "kgts,skh->tkgh", prob_new, values_new, preferred_element_type=jnp.float32
    )
    return mixed.astype(jnp.bfloat16).reshape(queries.shape[0], -1)


def expert_apply(blocks, gate_weight, up_weight, down_weight):
    local_experts = gate_weight.shape[0]
    sources = blocks.shape[0] // local_experts
    slot_count = blocks.shape[1]
    grouped = blocks.reshape(sources, local_experts, slot_count, blocks.shape[2])
    gate_acts = jnp.einsum(
        "sekd,edf->sekf", grouped, gate_weight, preferred_element_type=jnp.float32
    )
    up_acts = jnp.einsum("sekd,edf->sekf", grouped, up_weight, preferred_element_type=jnp.float32)
    hidden_act = (jax.nn.silu(gate_acts) * up_acts).astype(jnp.bfloat16)
    part_sums = jnp.einsum(
        "sekf,efd->sekd", hidden_act, down_weight, preferred_element_type=jnp.float32
    ).astype(jnp.bfloat16)
    return part_sums.reshape(sources * local_experts, slot_count, part_sums.shape[3])


def build_buffer(normed, slot_index, top_count, expert_count, capacity):
    picked = jnp.repeat(normed, top_count, axis=0)
    buffer_rows = (
        jnp.zeros((expert_count * capacity, normed.shape[1]), normed.dtype)
        .at[slot_index]
        .set(picked)
    )
    return buffer_rows.reshape(expert_count, capacity, normed.shape[1])


def weigh_back(returned, slot_index, route_weights, token_count, top_count):
    row_width = returned.shape[2]
    back_rows = returned.reshape(returned.shape[0] * returned.shape[1], row_width)[slot_index]
    weighted = (
        back_rows.astype(jnp.float32) * route_weights.reshape(token_count * top_count)[:, None]
    )
    return jnp.sum(weighted.reshape(token_count, top_count, row_width), axis=1)


LANES = 128
VMEM = pl.BlockSpec(memory_space=pltpu.VMEM)
SMEM = pl.BlockSpec(memory_space=pltpu.SMEM)
VMEM_LIMIT = 24 * 1024 * 1024


def flip(value, axis, bits):
    return lax.ppermute(value, axis, [(i, i ^ bits) for i in range(lax.axis_size(axis))])


def stage_kernel(*refs):
    length_hbm, table_hbm, frequency_hbm, *large = refs[:12]
    cosine_ref, sine_ref, owner_ref, *staged = refs[12:24]
    list_ref, length_out, table_out = refs[24:27]
    frequency_ref, owners, sems = refs[27:]
    length_ref, table_ref = length_out, table_out
    sources = (length_hbm, table_hbm, frequency_hbm, *large)
    targets = (length_out, table_out, frequency_ref, *staged)
    copies = [
        pltpu.make_async_copy(source, target, sems.at[i])
        for i, (source, target) in enumerate(zip(sources, targets))
    ]
    for copy in copies:
        copy.start()
    for copy in copies[:3]:
        copy.wait()
    tokens, head_dim = cosine_ref.shape
    for entry in range(POOL):
        list_ref[entry] = 0
        owners[0, entry] = -1
        owners[1, entry] = 0
    prefill_long = length_ref[0] > SHORT_PG * PAGE
    count = jnp.int32(0)
    for request in range(1, REQS_DEV):

        def name_page(entry, count):
            page = table_ref[request, entry]
            place = jnp.where(prefill_long, count, page)
            list_ref[place] = page
            owners[0, place] = request
            owners[1, place] = jnp.minimum(length_ref[request] - entry * PAGE, PAGE)
            return count + 1

        count = lax.fori_loop(0, (length_ref[request] + PAGE - 1) // PAGE, name_page, count)
    slot = lax.broadcasted_iota(jnp.int32, (1, PAGE), 1)
    for entry in range(POOL):
        owner_ref[:, entry * PAGE : (entry + 1) * PAGE] = jnp.where(
            slot < owners[1, entry], owners[0, entry], -1
        )
    token = lax.broadcasted_iota(jnp.int32, (tokens, head_dim), 0)
    lane = lax.broadcasted_iota(jnp.int32, (tokens, head_dim), 1)
    position = length_ref[0] + token
    for i in range(tokens - PRE):
        position = jnp.where(token == PRE + i, length_ref[i + 1], position)
    angle = position.astype(jnp.float32) * frequency_ref[...]
    sine = jnp.sin(angle)
    cosine_ref[...] = jnp.cos(angle)
    sine_ref[...] = jnp.where(lane < head_dim // 2, -sine, sine)
    for copy in copies[3:]:
        copy.wait()


def attention_kernel(*refs):
    pieces, (keep_out, far_out, core_out) = refs[:4], refs[19:22]
    (cosine_ref, sine_ref, owner_ref, gain_ref, q_gain_ref, k_gain_ref) = refs[4:10]
    (q_ref, k_ref, v_ref, key_ref, value_ref, o_ref, list_ref, length_ref, table_ref) = refs[10:19]
    (
        x_ref, query_ref, own_scores, scores_ref, mix_ref, mixed_ref, part_ref, slots_ref, decoded_ref,
    ) = refs[22:]
    tokens, head_dim = x_ref.shape[0], k_gain_ref.shape[1]
    tp_index = lax.axis_index("tp")
    heads = q_ref.shape[1] // head_dim
    decodes = tokens - PRE
    for step, piece in enumerate(pieces):
        width = piece.shape[1]
        start = pl.multiple_of((tp_index ^ step) * width, width)
        x_ref[:, pl.ds(start, width)] = piece[...]
    token = lax.broadcasted_iota(jnp.int32, (tokens, head_dim), 0)
    lane = lax.broadcasted_iota(jnp.int32, (tokens, head_dim), 1)

    def turned(values, gain):
        values = rms_scale(values, gain)
        return values * cosine_ref[...] + pltpu.roll(values, head_dim // 2, 1) * sine_ref[...]

    def with_ones(values):
        return jnp.concatenate([values, jnp.ones_like(values)], axis=1)

    normed = rms_scale(x_ref[...].astype(jnp.float32), gain_ref[...]).astype(jnp.bfloat16)
    contract = (((1,), (1,)), ((), ()))
    key_lin = jnp.dot(normed, k_ref[...], preferred_element_type=jnp.float32)
    values_new = jnp.dot(normed, v_ref[...], preferred_element_type=jnp.float32).astype(jnp.bfloat16)
    query_lin = jnp.dot(normed, q_ref[...], preferred_element_type=jnp.float32)
    keys_new = turned(key_lin, k_gain_ref[...]).astype(jnp.bfloat16)
    values_new = with_ones(values_new)
    to_log2 = math.log2(math.e) / math.sqrt(head_dim)
    own_mask = (lane == token) | ((lane < token) & (token < PRE))
    decode_query, decode_own = [], []
    for head in range(heads):
        span = slice(head * tokens, (head + 1) * tokens)
        query = turned(query_lin[:, head * head_dim : (head + 1) * head_dim], q_gain_ref[...]) * to_log2
        rounded = query.astype(jnp.bfloat16)
        query_ref[span, :] = rounded
        scores = lax.dot_general(rounded, keys_new, contract, preferred_element_type=jnp.float32)
        scores = jnp.where(own_mask, scores, -1e30)
        own_scores[span, :] = scores
        decode_query.append(query[PRE:])
        decode_own.append(scores[PRE:])
    decode_query = jnp.concatenate(decode_query, axis=0).astype(jnp.bfloat16)
    decode_own = jnp.concatenate(decode_own, axis=0)

    def raised(top, scores):
        for start in range(0, scores.shape[1], head_dim):
            top = jnp.maximum(top, scores[:, start : start + head_dim])
        return top

    def weigh(own, score_steps, value_steps, scores_ref):
        top = own
        for step, score_step in enumerate(score_steps):
            scores = score_step()
            scores_ref[step, :, : scores.shape[1]] = scores
            top = raised(top, scores)
        top = jnp.max(top, axis=1, keepdims=True)
        mix = jnp.dot(
            jnp.exp2(own - top).astype(jnp.bfloat16), values_new, preferred_element_type=jnp.float32
        )
        for step, value_step in enumerate(value_steps):
            values = value_step()
            weights = jnp.exp2(scores_ref[step, :, : values.shape[0]] - top).astype(jnp.bfloat16)
            mix = mix + jnp.dot(weights, with_ones(values), preferred_element_type=jnp.float32)
        return mix

    def taken(ref, names):
        return jnp.concatenate([ref[name] for name in names], axis=0)

    def against(queries, keys):
        return lax.dot_general(queries, keys, contract, preferred_element_type=jnp.float32)

    def prefill(names, live):
        def score(pages):
            scores = against(query_ref[...], taken(key_ref, pages))
            return scores if live is None else jnp.where(live, scores, -1e30)

        mix_ref[...] = weigh(
            own_scores[...],
            [functools.partial(score, pages) for pages in names],
            [functools.partial(taken, value_ref, pages) for pages in names],
            scores_ref,
        )

    def decode(steps, pages_of):
        row_request = 1 + lax.broadcasted_iota(jnp.int32, (heads * decodes, 1), 0) % decodes
        width = slots_ref.shape[2]

        def score(step):
            scores = against(decode_query, pages_of(key_ref, step))
            owner = owner_ref[:, step * width : (step + 1) * width]
            return jnp.where(owner == row_request, scores, -1e30)

        mix = weigh(
            decode_own,
            [functools.partial(score, step) for step in range(steps)],
            [functools.partial(pages_of, value_ref, step) for step in range(steps)],
            slots_ref,
        )
        decoded_ref[...] = mix[:, :head_dim] / mix[:, head_dim:]

    length = length_ref[0]
    listed = slots_ref.shape[2] // PAGE
    pages = scores_ref.shape[2] // PAGE

    @pl.when(length > SHORT_PG * PAGE)
    def _():
        names = [table_ref[0, entry] for entry in range(MAXPG)]
        prefill([names[first : first + pages] for first in range(0, MAXPG, pages)], None)
        decode(
            SHORT_LIST // listed,
            lambda ref, step: taken(ref, [list_ref[step * listed + i] for i in range(listed)]),
        )

    @pl.when(length <= SHORT_PG * PAGE)
    def _():
        column = lax.broadcasted_iota(jnp.int32, (1, SHORT_PG * PAGE), 1)
        prefill([[table_ref[0, entry] for entry in range(SHORT_PG)]], column < length)
        decode(
            POOL // listed,
            lambda ref, step: ref[step * listed : (step + 1) * listed].reshape(-1, head_dim),
        )

    for head in range(heads):
        part = mix_ref[head * tokens : (head + 1) * tokens, :]
        columns = slice(head * head_dim, (head + 1) * head_dim)
        mixed_ref[:, columns] = part[:, :head_dim] / part[:, head_dim:]
        mixed_ref[PRE:, columns] = decoded_ref[head * decodes : (head + 1) * decodes]
    part_ref[...] = jnp.dot(
        mixed_ref[...].astype(jnp.bfloat16), o_ref[...], preferred_element_type=jnp.float32
    )
    share_rows = keep_out.shape[0]

    def quarter(step):
        return pl.ds(pl.multiple_of((tp_index ^ step) * share_rows, share_rows), share_rows)

    keep_out[...] = part_ref[quarter(0), :] + x_ref[quarter(0), :].astype(jnp.float32)
    far_out[...] = part_ref[quarter(2), :]
    core_out[0] = part_ref[quarter(1), :].astype(jnp.bfloat16)
    core_out[1] = part_ref[quarter(3), :].astype(jnp.bfloat16)


def attention_shares(
    hidden_in, norm_in_gain, q_weight, k_weight, v_weight, q_gain, k_gain, o_weight,
    key_pages, value_pages, page_table, cache_len,
):
    tokens, width = hidden_in.shape[0], 4 * hidden_in.shape[1]
    head_dim = q_gain.shape[0]
    rows = q_weight.shape[1] // head_dim * tokens
    decode_rows = rows // tokens * (tokens - PRE)
    half = ROPE_BASE ** (-np.arange(head_dim // 2) / (head_dim // 2))
    frequency = jnp.asarray(np.concatenate([half, half])[None, :], jnp.float32)
    large = (
        norm_in_gain[None, :], q_gain[None, :], k_gain[None, :], q_weight, k_weight, v_weight,
        key_pages[0], value_pages[0], o_weight,
    )
    scalars = (cache_len, page_table)
    sources = [
        pltpu.with_memory_space_constraint(array, pltpu.HBM)
        for array in (*scalars, frequency, *large)
    ]
    rope = pltpu.VMEM((tokens, head_dim), jnp.float32)
    *staged, page_list, lengths, table = pl.pallas_call(
        stage_kernel,
        out_shape=[rope, rope, pltpu.VMEM((1, POOL * PAGE), jnp.int32)]
        + [pltpu.VMEM(array.shape, array.dtype) for array in large]
        + [jax.ShapeDtypeStruct((POOL,), jnp.int32)]
        + [jax.ShapeDtypeStruct(array.shape, array.dtype) for array in scalars],
        in_specs=[pl.BlockSpec(memory_space=pltpu.HBM)] * 12,
        out_specs=[VMEM] * 12 + [SMEM] * 3,
        scratch_shapes=[
            pltpu.VMEM(frequency.shape, frequency.dtype),
            pltpu.SMEM((2, POOL), jnp.int32),
            pltpu.SemaphoreType.DMA((12,)),
        ],
        compiler_params=pltpu.CompilerParams(vmem_limit_bytes=4 * 1024 * 1024),
        name="stage",
    )(*sources)
    far, *staged = ordered(flip(hidden_in, "tp", 2), *staged, page_list, lengths, table)
    pieces = (hidden_in, flip(hidden_in, "tp", 1), far, flip(far, "tp", 1))
    share = (tokens // 4, width)
    score_pages, list_pages = 4, 8
    return pl.pallas_call(
        attention_kernel,
        out_shape=[
            jax.ShapeDtypeStruct(share, jnp.float32),
            jax.ShapeDtypeStruct(share, jnp.float32),
            jax.ShapeDtypeStruct((2, *share), jnp.bfloat16),
        ],
        in_specs=[VMEM] * 16 + [SMEM] * 3,
        out_specs=[VMEM] * 3,
        scratch_shapes=[
            pltpu.VMEM((tokens, width), jnp.bfloat16),
            pltpu.VMEM((rows, head_dim), jnp.bfloat16),
            pltpu.VMEM((rows, tokens), jnp.float32),
            pltpu.VMEM((MAXPG // score_pages, rows, score_pages * PAGE), jnp.float32),
            pltpu.VMEM((rows, 2 * head_dim), jnp.float32),
            pltpu.VMEM((tokens, q_weight.shape[1]), jnp.float32),
            pltpu.VMEM((tokens, width), jnp.float32),
            pltpu.VMEM((POOL // list_pages, decode_rows, list_pages * PAGE), jnp.float32),
            pltpu.VMEM((decode_rows, head_dim), jnp.float32),
        ],
        compiler_params=pltpu.CompilerParams(vmem_limit_bytes=24 * 1024 * 1024),
        name="attention",
    )(*pieces, *staged)


def pack_kernel(
    own_ref, far_ref, gain_ref, ids_ref, routes_ref,
    rows_ref, residual_ref, spread_ref,
):
    tp_index = lax.axis_index("tp")
    share_rows, width = own_ref.shape
    mine = pl.ds(pl.multiple_of(tp_index * share_rows, share_rows), share_rows)
    residual = own_ref[...] + far_ref[...].astype(jnp.float32)
    residual_ref[...] = residual
    rows_ref[:, :width] = rms_scale(residual, gain_ref[...]).astype(jnp.bfloat16)
    expert = lax.broadcasted_iota(jnp.int32, (LANES, spread_ref.shape[0]), 0) % (LANES // 2)
    spread = jnp.zeros(expert.shape, jnp.float32)
    for k in range(ids_ref.shape[0]):
        spread = spread + jnp.where(expert == ids_ref[k : k + 1, :], routes_ref[k : k + 1, :], 0.0)
    spread_ref[...] = spread.T
    spread = spread_ref[mine, :]
    lane = lax.broadcasted_iota(jnp.int32, spread.shape, 1)
    high = spread.astype(jnp.bfloat16).astype(jnp.float32)
    rows_ref[:, width:] = jnp.where(lane < LANES // 2, high, spread - high).astype(jnp.bfloat16)


def experts_kernel(plan, residuals, *refs):
    pieces, residual_refs = refs[: len(plan)], refs[len(plan) : len(plan) + residuals]
    gate_ref, up_ref, down_ref, keep_ref, *send_refs, rows_ref, sums_ref = refs[len(plan) + residuals :]
    req_index, tp_index = lax.axis_index("req"), lax.axis_index("tp")
    columns, _, levels, group_rows, share_width = keep_ref.shape
    width = gate_ref.shape[1]
    units = gate_ref.shape[0] // 2
    for (column, step, first), piece in zip(plan, pieces):
        count = piece.shape[1]
        for level in range(levels):
            start = (column * levels + level) * group_rows + first
            start = start + (tp_index ^ step) * (group_rows // 4)
            rows_ref[pl.ds(pl.multiple_of(start, count), count), :] = piece[level]
    spread = rows_ref[:, width:].astype(jnp.float32)
    lane = lax.broadcasted_iota(jnp.int32, spread.shape, 1) % (LANES // 2)
    weights = [
        jnp.sum(jnp.where(lane == 2 * req_index + e, spread, 0.0), axis=1, keepdims=True)
        for e in range(2)
    ]
    contract = (((1,), (1,)), ((), ()))
    rows = rows_ref[:, :width]
    gate = lax.dot_general(rows, gate_ref[...], contract, preferred_element_type=jnp.float32)
    up = lax.dot_general(rows, up_ref[...], contract, preferred_element_type=jnp.float32)
    unit = lax.broadcasted_iota(jnp.int32, gate.shape, 1)
    weight = jnp.where(unit < units, weights[0], weights[1])
    acts = (gate / (1.0 + jnp.exp(-gate)) * up * weight).astype(jnp.bfloat16)
    for step in range(4):
        start = pl.multiple_of((tp_index ^ step) * share_width, share_width)
        part = jnp.dot(
            acts, down_ref[:, pl.ds(start, share_width)], preferred_element_type=jnp.float32
        )
        for residual_ref in residual_refs:
            count = residual_ref.shape[0]
            mine = pl.ds(pl.multiple_of(tp_index * count, count), count)
            sums_ref[...] = part
            sums_ref[mine, :] += residual_ref[:, pl.ds(start, share_width)]
            part = sums_ref[...]
        part = part.reshape(columns, levels, group_rows, share_width)
        if step % 2:
            send_refs[step // 2][...] = part.astype(jnp.bfloat16)
            continue
        for column in range(columns):
            keep_ref[column, step // 2] = part[column]


def run_experts(pieces, weights, group_rows, *residual):
    plan = tuple(place for place, _ in pieces)
    pieces = [piece for _, piece in pieces]
    columns, levels, packed = 1 + max(place[0] for place in plan), *pieces[0].shape[::2]
    rows, share_width = columns * levels * group_rows, weights[2].shape[1] // 4
    sums = (levels, group_rows, share_width)
    keep, *send = pl.pallas_call(
        functools.partial(experts_kernel, plan, len(residual)),
        out_shape=[jax.ShapeDtypeStruct((columns, 2, *sums), jnp.float32)]
        + [jax.ShapeDtypeStruct((columns, *sums), jnp.bfloat16)] * 2,
        in_specs=[VMEM] * (len(pieces) + len(residual) + 3),
        out_specs=[VMEM] * 3,
        scratch_shapes=[
            pltpu.VMEM((rows, packed), jnp.bfloat16),
            pltpu.VMEM((rows, share_width), jnp.float32),
        ],
        compiler_params=pltpu.CompilerParams(vmem_limit_bytes=VMEM_LIMIT),
        name="experts",
    )(*pieces, *residual, *weights)
    return keep, send


def finish_kernel(own_ref, z1_ref, z2_ref, x_ref, y_ref, out_ref):
    total = own_ref[0]
    for extra_ref in (x_ref, y_ref):
        total = total + extra_ref[0].astype(jnp.float32)
    for extra_ref in (z1_ref, z2_ref):
        total = total + extra_ref[...].astype(jnp.float32)
    out_ref[...] = total.astype(jnp.bfloat16)


def ordered(*values):
    return lax.optimization_barrier(values)


def across_parts(line_x, line_y):
    half = line_x.shape[1] // 2
    return flip(line_x[:, :half], "tp", 2), flip(line_y[:, half:], "req", 1)


def other_core(parts):
    return tuple(flip(part, "tp", 1) for part in parts)


def with_core(pair):
    return pair[0], list(other_core(pair[1]))


def joined(pair, column, y):
    return pair[0][column, y] + pair[1][y][column].astype(jnp.float32)


def near_pieces(column, line, core):
    return [((column, 0, 0), line), ((column, 1, 0), core)]


def far_pieces(column, parts, cores):
    half = parts[0].shape[1]
    if len(parts) == 1:
        return [((column, 2, 0), parts[0]), ((column, 3, 0), cores[0])]
    return [((column, 2, i * half), part) for i, part in enumerate(parts)] + [
        ((column, 3, i * half), part) for i, part in enumerate(cores)
    ]


def relayed(side):
    part = side.astype(jnp.bfloat16)
    half = part.shape[1] // 2
    return flip(part[:, :half], "req", 1), flip(part[:, half:], "tp", 2)


def neighbours(to_x, to_y, by_x, by_y):
    half = by_x.shape[1]
    to_y = jnp.concatenate([to_y[:, :half] + by_x.astype(jnp.float32), to_y[:, half:]], axis=1)
    to_x = jnp.concatenate([to_x[:, :half], to_x[:, half:] + by_y.astype(jnp.float32)], axis=1)
    return flip(to_x.astype(jnp.bfloat16), "req", 1), flip(to_y.astype(jnp.bfloat16), "tp", 2)


def moe_dense(
    kept,
    far,
    core,
    norm_post_gain,
    expert_ids,
    route_weights,
    gate_weight,
    up_weight,
    down_weight,
):
    share_rows, width = kept.shape
    token_count, share_width = 4 * share_rows, width // 4
    core = flip(core, "tp", 1)
    far, kept, core = ordered((far + core[1].astype(jnp.float32)).astype(jnp.bfloat16), kept, core)
    kept, far = ordered(kept + core[0].astype(jnp.float32), flip(far, "tp", 2))
    rows, residual = pl.pallas_call(
        pack_kernel,
        out_shape=[
            jax.ShapeDtypeStruct((share_rows, width + LANES), jnp.bfloat16),
            jax.ShapeDtypeStruct((share_rows, width), jnp.float32),
        ],
        in_specs=[VMEM] * 5,
        out_specs=[VMEM] * 2,
        scratch_shapes=[pltpu.VMEM((token_count, LANES), jnp.float32)],
        compiler_params=pltpu.CompilerParams(vmem_limit_bytes=8 * 1024 * 1024),
        name="pack_rows",
    )(kept, far, norm_post_gain[None, :], expert_ids.T, route_weights.T)
    gate_up = [w.transpose(0, 2, 1).reshape(-1, width) for w in (gate_weight, up_weight)]
    weights = (*gate_up, down_weight.reshape(-1, width))
    line_0 = rows[None]
    z_1, z_2 = flip(line_0, "req", 2), flip(line_0, "req", 4)
    y_0, x_0 = flip(line_0, "tp", 2), flip(line_0, "req", 1)
    line_12, z_2, y_0, x_0 = ordered(jnp.concatenate([z_1, z_2]), z_2, y_0, x_0)
    line_3, across_0, core_0, y_core_0 = ordered(
        jnp.concatenate([line_12, flip(z_2, "req", 2)]),
        across_parts(x_0, y_0),
        flip(line_0, "tp", 1),
        flip(y_0, "tp", 1),
    )
    y_3, x_3 = flip(line_3, "tp", 2), flip(line_3, "req", 1)
    all_0 = run_experts(
        near_pieces(0, line_0, core_0)
        + far_pieces(0, (y_0,), (y_core_0,))
        + near_pieces(1, x_0, flip(x_0, "tp", 1))
        + far_pieces(1, across_0, other_core(across_0)),
        weights,
        token_count,
        residual,
    )
    all_0, core_3, y_3, x_3 = ordered(all_0, flip(line_3, "tp", 1), y_3, x_3)
    y_core_3, x_core_3 = other_core((y_3, x_3))
    near_3 = run_experts(
        near_pieces(0, line_3, core_3) + far_pieces(0, (y_3,), (y_core_3,)), weights, token_count
    )
    near_3, x_core_3, across_3 = ordered(near_3, x_core_3, across_parts(x_3, y_3))
    side_3 = run_experts(
        near_pieces(0, x_3, x_core_3) + far_pieces(0, across_3, other_core(across_3)),
        weights,
        token_count,
    )
    all_0, near_3, side_3 = ordered(all_0, near_3, side_3)
    keep, (send, first) = side_3
    all_0, near_3, keep, send, first = ordered(all_0, near_3, keep, send, flip(first, "tp", 1))
    relay_3 = relayed(joined((keep, (send, first)), 0, 1))
    near_keep, (near_send, near_first) = near_3
    all_0, near_send, near_first, send, relay_3 = ordered(
        all_0, near_send, flip(near_first, "tp", 1), flip(send, "tp", 1), relay_3
    )
    sums_3 = neighbours(
        joined((keep, (send, first)), 0, 0), joined((near_keep, (near_send, near_first)), 0, 1), *relay_3
    )
    all_0, near_send, sums_3 = ordered(with_core(all_0), flip(near_send, "tp", 1), sums_3)
    near_3 = (near_keep, (near_send, near_first))
    sent = joined(near_3, 0, 0) + sums_3[0].astype(jnp.float32) + sums_3[1].astype(jnp.float32)
    sent_3, relay_0 = ordered(
        flip(sent[2].astype(jnp.bfloat16), "req", 2), relayed(joined(all_0, 1, 1))
    )
    sent_2, relay_0 = ordered(
        (sent[1] + sent_3.astype(jnp.float32)).astype(jnp.bfloat16), relay_0
    )
    from_z = [flip(sent[0].astype(jnp.bfloat16), "req", 2), flip(sent_2, "req", 4)]
    sums_0 = neighbours(joined(all_0, 1, 0), joined(all_0, 0, 1), *relay_0)
    return pl.pallas_call(
        finish_kernel,
        out_shape=jax.ShapeDtypeStruct((token_count, share_width), jnp.bfloat16),
        in_specs=[VMEM] * 5,
        out_specs=VMEM,
        compiler_params=pltpu.CompilerParams(vmem_limit_bytes=8 * 1024 * 1024),
        name="finish",
    )(joined(all_0, 0, 0), *from_z, *sums_0)


def moe_routed(
    x_full,
    head_part,
    norm_post_gain,
    expert_ids,
    route_weights,
    gate_weight,
    up_weight,
    down_weight,
):
    req_count = lax.axis_size("req")
    tp_index = lax.axis_index("tp")
    x_float = x_full.astype(jnp.float32)
    token_count = x_float.shape[0]
    share_width = x_float.shape[1] // lax.axis_size("tp")
    top_count = expert_ids.shape[1]
    expert_count = gate_weight.shape[0] * req_count
    capacity = max(2, 3 * token_count * top_count // (2 * expert_count))
    flat_expert = expert_ids.reshape(token_count * top_count)
    one_hot = (flat_expert[:, None] == jnp.arange(expert_count, dtype=jnp.int32)[None, :]).astype(
        jnp.int32
    )
    slot_rank = jnp.sum((jnp.cumsum(one_hot, axis=0) - one_hot) * one_hot, axis=1)
    slot_index = flat_expert * capacity + slot_rank
    head_sum = lax.psum(head_part.astype(jnp.bfloat16), "tp").astype(jnp.float32)
    residual_full = x_float + head_sum
    normed_post = rms_scale(residual_full, norm_post_gain).astype(jnp.bfloat16)
    residual = lax.dynamic_slice_in_dim(residual_full, tp_index * share_width, share_width, 1)
    send_buffer = build_buffer(normed_post, slot_index, top_count, expert_count, capacity)
    part_sums = expert_apply(
        lax.all_to_all(send_buffer, "req", split_axis=0, concat_axis=0, tiled=True),
        gate_weight,
        up_weight,
        down_weight,
    )
    returned = lax.all_to_all(part_sums, "req", split_axis=0, concat_axis=0, tiled=True)
    moe_term = weigh_back(returned, slot_index, route_weights, token_count, top_count)
    moe_share = lax.psum_scatter(
        moe_term.astype(jnp.bfloat16), "tp", scatter_dimension=1, tiled=True
    ).astype(jnp.float32)
    return (residual + moe_share).astype(jnp.bfloat16)


def attention_part(
    x_full,
    norm_in_gain,
    q_weight,
    k_weight,
    v_weight,
    q_gain,
    k_gain,
    o_weight,
    key_pages,
    value_pages,
    page_table,
    cache_len,
):
    head_dim = q_gain.shape[0]
    kv_local = key_pages.shape[0]
    group_size = q_weight.shape[1] // head_dim // kv_local
    token_count = x_full.shape[0]
    x_float = x_full.astype(jnp.float32)
    normed_in = rms_scale(x_float, norm_in_gain).astype(jnp.bfloat16)
    query_lin = jnp.dot(normed_in, q_weight, preferred_element_type=jnp.float32).reshape(
        token_count, kv_local * group_size, head_dim
    )
    key_lin = jnp.dot(normed_in, k_weight, preferred_element_type=jnp.float32).reshape(
        token_count, kv_local, head_dim
    )
    values_new = (
        jnp.dot(normed_in, v_weight, preferred_element_type=jnp.float32)
        .astype(jnp.bfloat16)
        .reshape(token_count, kv_local, head_dim)
    )
    requests, positions = token_layout(cache_len)
    queries = (
        rotate(rms_scale(query_lin, q_gain), positions)
        .astype(jnp.bfloat16)
        .reshape(token_count, kv_local, group_size, head_dim)
    )
    keys_new = rotate(rms_scale(key_lin, k_gain), positions).astype(jnp.bfloat16)
    slot_owner = page_slots(page_table, cache_len)
    cache_slots = key_pages.shape[1] * key_pages.shape[2]
    keys_cache = key_pages.reshape(kv_local, cache_slots, head_dim)
    values_cache = value_pages.reshape(kv_local, cache_slots, head_dim)
    attended = attend(
        queries, keys_new, values_new, keys_cache, values_cache, requests, positions, slot_owner
    )
    return jnp.dot(attended, o_weight, preferred_element_type=jnp.float32)


def body(
    hidden_in,
    norm_in_gain,
    q_weight,
    k_weight,
    v_weight,
    q_gain,
    k_gain,
    o_weight,
    key_pages,
    value_pages,
    page_table,
    cache_len,
    norm_post_gain,
    expert_ids,
    route_weights,
    gate_weight,
    up_weight,
    down_weight,
):
    req_count = lax.axis_size("req")
    attention = (
        norm_in_gain,
        q_weight,
        k_weight,
        v_weight,
        q_gain,
        k_gain,
        o_weight,
        key_pages,
        value_pages,
        page_table,
        cache_len,
    )
    experts = (norm_post_gain, expert_ids, route_weights, gate_weight, up_weight, down_weight)
    expert_count = gate_weight.shape[0] * req_count
    staged = (req_count, lax.axis_size("tp"), gate_weight.shape[0]) == (8, 4, 2)
    if staged and expert_count <= LANES // 2:
        return moe_dense(*attention_shares(hidden_in, *attention), *experts)
    x_full = lax.all_gather(hidden_in, "tp", axis=1, tiled=True)
    return moe_routed(x_full, attention_part(x_full, *attention), *experts)


def solution(mesh):
    return jax.shard_map(
        body,
        mesh=mesh,
        in_specs=(
            P("req", "tp"),
            P(),
            P(None, "tp"),
            P(None, "tp"),
            P(None, "tp"),
            P(),
            P(),
            P("tp", None),
            P("tp", "req", None, None),
            P("tp", "req", None, None),
            P("req", None),
            P("req"),
            P(),
            P("req", None),
            P("req", None),
            P("req", None, "tp"),
            P("req", None, "tp"),
            P("req", "tp", None),
        ),
        out_specs=P("req", "tp"),
        check_vma=False,
    )
```

```python
import functools
import math

import jax
import jax.numpy as jnp
import numpy as np
from jax import lax
from jax.experimental import pallas as pl
from jax.experimental.pallas import tpu as pltpu
from jax.sharding import PartitionSpec as P

PAGE = 128
MAXPG = 32
PRE = 120
TOK_DEV = 128
REQS_DEV = 9
POOL = 48
SHORT_PG = 2
SHORT_LIST = (REQS_DEV - 1) * SHORT_PG


NORM_EPS = 1e-06
ROPE_BASE = 1000000.0


def rms_scale(values, gain_vec):
    mean_square = jnp.mean(values * values, axis=-1, keepdims=True)
    return values * lax.rsqrt(mean_square + NORM_EPS) * gain_vec


def rotate(values, positions):
    half_dim = values.shape[-1] // 2
    exponent = jnp.arange(half_dim, dtype=jnp.float32) * (2.0 / values.shape[-1])
    frequency = jnp.power(jnp.float32(ROPE_BASE), -exponent)
    angles = positions.astype(jnp.float32)[:, None] * frequency[None, :]
    cosine = jnp.cos(angles)[:, None, :]
    sine_val = jnp.sin(angles)[:, None, :]
    front_half = values[..., :half_dim]
    back_half = values[..., half_dim:]
    return jnp.concatenate(
        [front_half * cosine - back_half * sine_val, back_half * cosine + front_half * sine_val],
        axis=-1,
    )


def token_layout(lengths):
    local_idx = jnp.arange(TOK_DEV, dtype=jnp.int32)
    requests = jnp.where(local_idx < PRE, 0, local_idx - PRE + 1)
    offsets = jnp.where(local_idx < PRE, local_idx, 0)
    request_hot = (requests[:, None] == jnp.arange(REQS_DEV, dtype=jnp.int32)[None, :]).astype(
        jnp.int32
    )
    positions = jnp.sum(request_hot * lengths[None, :], axis=1) + offsets
    return (requests, positions)


def page_slots(table, lengths):
    pages_used = (lengths + PAGE - 1) // PAGE
    entry_live = jnp.arange(MAXPG, dtype=jnp.int32)[None, :] < pages_used[:, None]
    page_match = (
        (table[:, :, None] == jnp.arange(POOL, dtype=jnp.int32)[None, None, :])
        & entry_live[:, :, None]
    ).astype(jnp.int32)
    page_owner = jnp.sum(
        page_match * jnp.arange(REQS_DEV, dtype=jnp.int32)[:, None, None], axis=(0, 1)
    )
    page_start = jnp.sum(
        page_match * (jnp.arange(MAXPG, dtype=jnp.int32) * PAGE)[None, :, None], axis=(0, 1)
    )
    page_used = jnp.sum(page_match, axis=(0, 1)) > 0
    owner_length = jnp.sum(page_match * lengths[:, None, None], axis=(0, 1))
    slot_pos = page_start[:, None] + jnp.arange(PAGE, dtype=jnp.int32)[None, :]
    slot_live = page_used[:, None] & (slot_pos < owner_length[:, None])
    slot_owner = jnp.where(slot_live, page_owner[:, None], -1)
    return slot_owner.reshape(POOL * PAGE)


def attend(
    queries, keys_new, values_new, keys_cache, values_cache, requests, positions, slot_owner
):
    inv_root = 1.0 / math.sqrt(queries.shape[-1])
    cache_mask = slot_owner[None, :] == requests[:, None]
    new_mask = (requests[None, :] == requests[:, None]) & (positions[None, :] <= positions[:, None])
    score_cache = (
        jnp.einsum("tkgh,knh->kgtn", queries, keys_cache, preferred_element_type=jnp.float32)
        * inv_root
    )
    score_new = (
        jnp.einsum("tkgh,skh->kgts", queries, keys_new, preferred_element_type=jnp.float32)
        * inv_root
    )
    score_cache = jnp.where(cache_mask[None, None], score_cache, -1e30)
    score_new = jnp.where(new_mask[None, None], score_new, -1e30)
    row_max = jnp.maximum(
        jnp.max(score_cache, axis=-1, keepdims=True), jnp.max(score_new, axis=-1, keepdims=True)
    )
    exp_cache = jnp.where(cache_mask[None, None], jnp.exp(score_cache - row_max), 0.0)
    exp_new = jnp.where(new_mask[None, None], jnp.exp(score_new - row_max), 0.0)
    total = jnp.sum(exp_cache, axis=-1, keepdims=True) + jnp.sum(exp_new, axis=-1, keepdims=True)
    prob_cache = (exp_cache / total).astype(jnp.bfloat16)
    prob_new = (exp_new / total).astype(jnp.bfloat16)
    mixed = jnp.einsum(
        "kgtn,knh->tkgh", prob_cache, values_cache, preferred_element_type=jnp.float32
    )
    mixed = mixed + jnp.einsum(
        "kgts,skh->tkgh", prob_new, values_new, preferred_element_type=jnp.float32
    )
    return mixed.astype(jnp.bfloat16).reshape(queries.shape[0], -1)


def expert_apply(blocks, gate_weight, up_weight, down_weight):
    local_experts = gate_weight.shape[0]
    sources = blocks.shape[0] // local_experts
    slot_count = blocks.shape[1]
    grouped = blocks.reshape(sources, local_experts, slot_count, blocks.shape[2])
    gate_acts = jnp.einsum(
        "sekd,edf->sekf", grouped, gate_weight, preferred_element_type=jnp.float32
    )
    up_acts = jnp.einsum("sekd,edf->sekf", grouped, up_weight, preferred_element_type=jnp.float32)
    hidden_act = (jax.nn.silu(gate_acts) * up_acts).astype(jnp.bfloat16)
    part_sums = jnp.einsum(
        "sekf,efd->sekd", hidden_act, down_weight, preferred_element_type=jnp.float32
    ).astype(jnp.bfloat16)
    return part_sums.reshape(sources * local_experts, slot_count, part_sums.shape[3])


def build_buffer(normed, slot_index, top_count, expert_count, capacity):
    picked = jnp.repeat(normed, top_count, axis=0)
    buffer_rows = (
        jnp.zeros((expert_count * capacity, normed.shape[1]), normed.dtype)
        .at[slot_index]
        .set(picked)
    )
    return buffer_rows.reshape(expert_count, capacity, normed.shape[1])


def weigh_back(returned, slot_index, route_weights, token_count, top_count):
    row_width = returned.shape[2]
    back_rows = returned.reshape(returned.shape[0] * returned.shape[1], row_width)[slot_index]
    weighted = (
        back_rows.astype(jnp.float32) * route_weights.reshape(token_count * top_count)[:, None]
    )
    return jnp.sum(weighted.reshape(token_count, top_count, row_width), axis=1)


LANES = 128
VMEM = pl.BlockSpec(memory_space=pltpu.VMEM)
SMEM = pl.BlockSpec(memory_space=pltpu.SMEM)
VMEM_LIMIT = 24 * 1024 * 1024


def flip(value, axis, bits):
    return lax.ppermute(value, axis, [(i, i ^ bits) for i in range(lax.axis_size(axis))])


def stage_kernel(*refs):
    length_hbm, table_hbm, frequency_hbm, *large = refs[:12]
    cosine_ref, sine_ref, owner_ref, *staged = refs[12:24]
    list_ref, length_out, table_out = refs[24:27]
    frequency_ref, owners, sems = refs[27:]
    length_ref, table_ref = length_out, table_out
    sources = (length_hbm, table_hbm, frequency_hbm, *large)
    targets = (length_out, table_out, frequency_ref, *staged)
    copies = [
        pltpu.make_async_copy(source, target, sems.at[i])
        for i, (source, target) in enumerate(zip(sources, targets))
    ]
    for copy in copies:
        copy.start()
    for copy in copies[:3]:
        copy.wait()
    tokens, head_dim = cosine_ref.shape
    for entry in range(POOL):
        list_ref[entry] = 0
        owners[0, entry] = -1
        owners[1, entry] = 0
    prefill_long = length_ref[0] > SHORT_PG * PAGE
    count = jnp.int32(0)
    for request in range(1, REQS_DEV):

        def name_page(entry, count):
            page = table_ref[request, entry]
            place = jnp.where(prefill_long, count, page)
            list_ref[place] = page
            owners[0, place] = request
            owners[1, place] = jnp.minimum(length_ref[request] - entry * PAGE, PAGE)
            return count + 1

        count = lax.fori_loop(0, (length_ref[request] + PAGE - 1) // PAGE, name_page, count)
    slot = lax.broadcasted_iota(jnp.int32, (1, PAGE), 1)
    for entry in range(POOL):
        owner_ref[:, entry * PAGE : (entry + 1) * PAGE] = jnp.where(
            slot < owners[1, entry], owners[0, entry], -1
        )
    token = lax.broadcasted_iota(jnp.int32, (tokens, head_dim), 0)
    lane = lax.broadcasted_iota(jnp.int32, (tokens, head_dim), 1)
    position = length_ref[0] + token
    for i in range(tokens - PRE):
        position = jnp.where(token == PRE + i, length_ref[i + 1], position)
    angle = position.astype(jnp.float32) * frequency_ref[...]
    sine = jnp.sin(angle)
    cosine_ref[...] = jnp.cos(angle)
    sine_ref[...] = jnp.where(lane < head_dim // 2, -sine, sine)
    for copy in copies[3:]:
        copy.wait()


def attention_kernel(*refs):
    pieces, (keep_out, far_out, core_out) = refs[:4], refs[19:22]
    (cosine_ref, sine_ref, owner_ref, gain_ref, q_gain_ref, k_gain_ref) = refs[4:10]
    (q_ref, k_ref, v_ref, key_ref, value_ref, o_ref, list_ref, length_ref, table_ref) = refs[10:19]
    (
        x_ref, query_ref, own_scores, scores_ref, mix_ref, mixed_ref, part_ref, slots_ref, decoded_ref,
    ) = refs[22:]
    tokens, head_dim = x_ref.shape[0], k_gain_ref.shape[1]
    tp_index = lax.axis_index("tp")
    heads = q_ref.shape[1] // head_dim
    decodes = tokens - PRE
    for step, piece in enumerate(pieces):
        width = piece.shape[1]
        start = pl.multiple_of((tp_index ^ step) * width, width)
        x_ref[:, pl.ds(start, width)] = piece[...]
    token = lax.broadcasted_iota(jnp.int32, (tokens, head_dim), 0)
    lane = lax.broadcasted_iota(jnp.int32, (tokens, head_dim), 1)

    def turned(values, gain):
        values = rms_scale(values, gain)
        return values * cosine_ref[...] + pltpu.roll(values, head_dim // 2, 1) * sine_ref[...]

    def with_ones(values):
        return jnp.concatenate([values, jnp.ones_like(values)], axis=1)

    normed = rms_scale(x_ref[...].astype(jnp.float32), gain_ref[...]).astype(jnp.bfloat16)
    contract = (((1,), (1,)), ((), ()))
    key_lin = jnp.dot(normed, k_ref[...], preferred_element_type=jnp.float32)
    values_new = jnp.dot(normed, v_ref[...], preferred_element_type=jnp.float32).astype(jnp.bfloat16)
    query_lin = jnp.dot(normed, q_ref[...], preferred_element_type=jnp.float32)
    keys_new = turned(key_lin, k_gain_ref[...]).astype(jnp.bfloat16)
    values_new = with_ones(values_new)
    to_log2 = math.log2(math.e) / math.sqrt(head_dim)
    own_mask = (lane == token) | ((lane < token) & (token < PRE))
    decode_query, decode_own = [], []
    for head in range(heads):
        span = slice(head * tokens, (head + 1) * tokens)
        query = turned(query_lin[:, head * head_dim : (head + 1) * head_dim], q_gain_ref[...]) * to_log2
        rounded = query.astype(jnp.bfloat16)
        query_ref[span, :] = rounded
        scores = lax.dot_general(rounded, keys_new, contract, preferred_element_type=jnp.float32)
        scores = jnp.where(own_mask, scores, -1e30)
        own_scores[span, :] = scores
        decode_query.append(query[PRE:])
        decode_own.append(scores[PRE:])
    decode_query = jnp.concatenate(decode_query, axis=0).astype(jnp.bfloat16)
    decode_own = jnp.concatenate(decode_own, axis=0)

    def raised(top, scores):
        for start in range(0, scores.shape[1], head_dim):
            top = jnp.maximum(top, scores[:, start : start + head_dim])
        return top

    def weigh(own, score_steps, value_steps, scores_ref):
        top = own
        for step, score_step in enumerate(score_steps):
            scores = score_step()
            scores_ref[step, :, : scores.shape[1]] = scores
            top = raised(top, scores)
        top = jnp.max(top, axis=1, keepdims=True)
        mix = jnp.dot(
            jnp.exp2(own - top).astype(jnp.bfloat16), values_new, preferred_element_type=jnp.float32
        )
        for step, value_step in enumerate(value_steps):
            values = value_step()
            weights = jnp.exp2(scores_ref[step, :, : values.shape[0]] - top).astype(jnp.bfloat16)
            mix = mix + jnp.dot(weights, with_ones(values), preferred_element_type=jnp.float32)
        return mix

    def taken(ref, names):
        return jnp.concatenate([ref[name] for name in names], axis=0)

    def against(queries, keys):
        return lax.dot_general(queries, keys, contract, preferred_element_type=jnp.float32)

    def prefill(names, live):
        def score(pages):
            scores = against(query_ref[...], taken(key_ref, pages))
            return scores if live is None else jnp.where(live, scores, -1e30)

        mix_ref[...] = weigh(
            own_scores[...],
            [functools.partial(score, pages) for pages in names],
            [functools.partial(taken, value_ref, pages) for pages in names],
            scores_ref,
        )

    def decode(steps, pages_of):
        row_request = 1 + lax.broadcasted_iota(jnp.int32, (heads * decodes, 1), 0) % decodes
        width = slots_ref.shape[2]

        def score(step):
            scores = against(decode_query, pages_of(key_ref, step))
            owner = owner_ref[:, step * width : (step + 1) * width]
            return jnp.where(owner == row_request, scores, -1e30)

        mix = weigh(
            decode_own,
            [functools.partial(score, step) for step in range(steps)],
            [functools.partial(pages_of, value_ref, step) for step in range(steps)],
            slots_ref,
        )
        decoded_ref[...] = mix[:, :head_dim] / mix[:, head_dim:]

    length = length_ref[0]
    listed = slots_ref.shape[2] // PAGE
    pages = scores_ref.shape[2] // PAGE

    @pl.when(length > SHORT_PG * PAGE)
    def _():
        names = [table_ref[0, entry] for entry in range(MAXPG)]
        prefill([names[first : first + pages] for first in range(0, MAXPG, pages)], None)
        decode(
            SHORT_LIST // listed,
            lambda ref, step: taken(ref, [list_ref[step * listed + i] for i in range(listed)]),
        )

    @pl.when(length <= SHORT_PG * PAGE)
    def _():
        column = lax.broadcasted_iota(jnp.int32, (1, SHORT_PG * PAGE), 1)
        prefill([[table_ref[0, entry] for entry in range(SHORT_PG)]], column < length)
        decode(
            POOL // listed,
            lambda ref, step: ref[step * listed : (step + 1) * listed].reshape(-1, head_dim),
        )

    for head in range(heads):
        part = mix_ref[head * tokens : (head + 1) * tokens, :]
        columns = slice(head * head_dim, (head + 1) * head_dim)
        mixed_ref[:, columns] = part[:, :head_dim] / part[:, head_dim:]
        mixed_ref[PRE:, columns] = decoded_ref[head * decodes : (head + 1) * decodes]
    part_ref[...] = jnp.dot(
        mixed_ref[...].astype(jnp.bfloat16), o_ref[...], preferred_element_type=jnp.float32
    )
    share_rows = keep_out.shape[0]

    def quarter(step):
        return pl.ds(pl.multiple_of((tp_index ^ step) * share_rows, share_rows), share_rows)

    keep_out[...] = part_ref[quarter(0), :] + x_ref[quarter(0), :].astype(jnp.float32)
    far_out[...] = part_ref[quarter(2), :]
    core_out[0] = part_ref[quarter(1), :].astype(jnp.bfloat16)
    core_out[1] = part_ref[quarter(3), :].astype(jnp.bfloat16)


def attention_shares(
    hidden_in, norm_in_gain, q_weight, k_weight, v_weight, q_gain, k_gain, o_weight,
    key_pages, value_pages, page_table, cache_len,
):
    tokens, width = hidden_in.shape[0], 4 * hidden_in.shape[1]
    head_dim = q_gain.shape[0]
    rows = q_weight.shape[1] // head_dim * tokens
    decode_rows = rows // tokens * (tokens - PRE)
    half = ROPE_BASE ** (-np.arange(head_dim // 2) / (head_dim // 2))
    frequency = jnp.asarray(np.concatenate([half, half])[None, :], jnp.float32)
    large = (
        norm_in_gain[None, :], q_gain[None, :], k_gain[None, :], q_weight, k_weight, v_weight,
        key_pages[0], value_pages[0], o_weight,
    )
    scalars = (cache_len, page_table)
    sources = [
        pltpu.with_memory_space_constraint(array, pltpu.HBM)
        for array in (*scalars, frequency, *large)
    ]
    rope = pltpu.VMEM((tokens, head_dim), jnp.float32)
    *staged, page_list, lengths, table = pl.pallas_call(
        stage_kernel,
        out_shape=[rope, rope, pltpu.VMEM((1, POOL * PAGE), jnp.int32)]
        + [pltpu.VMEM(array.shape, array.dtype) for array in large]
        + [jax.ShapeDtypeStruct((POOL,), jnp.int32)]
        + [jax.ShapeDtypeStruct(array.shape, array.dtype) for array in scalars],
        in_specs=[pl.BlockSpec(memory_space=pltpu.HBM)] * 12,
        out_specs=[VMEM] * 12 + [SMEM] * 3,
        scratch_shapes=[
            pltpu.VMEM(frequency.shape, frequency.dtype),
            pltpu.SMEM((2, POOL), jnp.int32),
            pltpu.SemaphoreType.DMA((12,)),
        ],
        compiler_params=pltpu.CompilerParams(vmem_limit_bytes=4 * 1024 * 1024),
        name="stage",
    )(*sources)
    far, *staged = ordered(flip(hidden_in, "tp", 2), *staged, page_list, lengths, table)
    pieces = (hidden_in, flip(hidden_in, "tp", 1), far, flip(far, "tp", 1))
    share = (tokens // 4, width)
    score_pages, list_pages = 4, 8
    return pl.pallas_call(
        attention_kernel,
        out_shape=[
            jax.ShapeDtypeStruct(share, jnp.float32),
            jax.ShapeDtypeStruct(share, jnp.float32),
            jax.ShapeDtypeStruct((2, *share), jnp.bfloat16),
        ],
        in_specs=[VMEM] * 16 + [SMEM] * 3,
        out_specs=[VMEM] * 3,
        scratch_shapes=[
            pltpu.VMEM((tokens, width), jnp.bfloat16),
            pltpu.VMEM((rows, head_dim), jnp.bfloat16),
            pltpu.VMEM((rows, tokens), jnp.float32),
            pltpu.VMEM((MAXPG // score_pages, rows, score_pages * PAGE), jnp.float32),
            pltpu.VMEM((rows, 2 * head_dim), jnp.float32),
            pltpu.VMEM((tokens, q_weight.shape[1]), jnp.float32),
            pltpu.VMEM((tokens, width), jnp.float32),
            pltpu.VMEM((POOL // list_pages, decode_rows, list_pages * PAGE), jnp.float32),
            pltpu.VMEM((decode_rows, head_dim), jnp.float32),
        ],
        compiler_params=pltpu.CompilerParams(vmem_limit_bytes=24 * 1024 * 1024),
        name="attention",
    )(*pieces, *staged)


def pack_kernel(
    own_ref, far_ref, gain_ref, ids_ref, routes_ref,
    rows_ref, residual_ref, spread_ref,
):
    tp_index = lax.axis_index("tp")
    share_rows, width = own_ref.shape
    mine = pl.ds(pl.multiple_of(tp_index * share_rows, share_rows), share_rows)
    residual = own_ref[...] + far_ref[...].astype(jnp.float32)
    residual_ref[...] = residual
    rows_ref[:, :width] = rms_scale(residual, gain_ref[...]).astype(jnp.bfloat16)
    expert = lax.broadcasted_iota(jnp.int32, (LANES, spread_ref.shape[0]), 0) % (LANES // 2)
    spread = jnp.zeros(expert.shape, jnp.float32)
    for k in range(ids_ref.shape[0]):
        spread = spread + jnp.where(expert == ids_ref[k : k + 1, :], routes_ref[k : k + 1, :], 0.0)
    spread_ref[...] = spread.T
    spread = spread_ref[mine, :]
    lane = lax.broadcasted_iota(jnp.int32, spread.shape, 1)
    high = spread.astype(jnp.bfloat16).astype(jnp.float32)
    rows_ref[:, width:] = jnp.where(lane < LANES // 2, high, spread - high).astype(jnp.bfloat16)


def experts_kernel(plan, residuals, *refs):
    pieces, residual_refs = refs[: len(plan)], refs[len(plan) : len(plan) + residuals]
    gate_ref, up_ref, down_ref, keep_ref, *send_refs, rows_ref, sums_ref = refs[len(plan) + residuals :]
    req_index, tp_index = lax.axis_index("req"), lax.axis_index("tp")
    columns, _, levels, group_rows, share_width = keep_ref.shape
    width = gate_ref.shape[1]
    units = gate_ref.shape[0] // 2
    for (column, step, first), piece in zip(plan, pieces):
        count = piece.shape[1]
        for level in range(levels):
            start = (column * levels + level) * group_rows + first
            start = start + (tp_index ^ step) * (group_rows // 4)
            rows_ref[pl.ds(pl.multiple_of(start, count), count), :] = piece[level]
    spread = rows_ref[:, width:].astype(jnp.float32)
    lane = lax.broadcasted_iota(jnp.int32, spread.shape, 1) % (LANES // 2)
    weights = [
        jnp.sum(jnp.where(lane == 2 * req_index + e, spread, 0.0), axis=1, keepdims=True)
        for e in range(2)
    ]
    contract = (((1,), (1,)), ((), ()))
    rows = rows_ref[:, :width]
    gate = lax.dot_general(rows, gate_ref[...], contract, preferred_element_type=jnp.float32)
    up = lax.dot_general(rows, up_ref[...], contract, preferred_element_type=jnp.float32)
    unit = lax.broadcasted_iota(jnp.int32, gate.shape, 1)
    weight = jnp.where(unit < units, weights[0], weights[1])
    acts = (gate / (1.0 + jnp.exp(-gate)) * up * weight).astype(jnp.bfloat16)
    for step in range(4):
        start = pl.multiple_of((tp_index ^ step) * share_width, share_width)
        part = jnp.dot(
            acts, down_ref[:, pl.ds(start, share_width)], preferred_element_type=jnp.float32
        )
        for residual_ref in residual_refs:
            count = residual_ref.shape[0]
            mine = pl.ds(pl.multiple_of(tp_index * count, count), count)
            sums_ref[...] = part
            sums_ref[mine, :] += residual_ref[:, pl.ds(start, share_width)]
            part = sums_ref[...]
        part = part.reshape(columns, levels, group_rows, share_width)
        if step % 2:
            send_refs[step // 2][...] = part.astype(jnp.bfloat16)
            continue
        for column in range(columns):
            keep_ref[column, step // 2] = part[column]


def run_experts(pieces, weights, group_rows, *residual):
    plan = tuple(place for place, _ in pieces)
    pieces = [piece for _, piece in pieces]
    columns, levels, packed = 1 + max(place[0] for place in plan), *pieces[0].shape[::2]
    rows, share_width = columns * levels * group_rows, weights[2].shape[1] // 4
    sums = (levels, group_rows, share_width)
    keep, *send = pl.pallas_call(
        functools.partial(experts_kernel, plan, len(residual)),
        out_shape=[jax.ShapeDtypeStruct((columns, 2, *sums), jnp.float32)]
        + [jax.ShapeDtypeStruct((columns, *sums), jnp.bfloat16)] * 2,
        in_specs=[VMEM] * (len(pieces) + len(residual) + 3),
        out_specs=[VMEM] * 3,
        scratch_shapes=[
            pltpu.VMEM((rows, packed), jnp.bfloat16),
            pltpu.VMEM((rows, share_width), jnp.float32),
        ],
        compiler_params=pltpu.CompilerParams(vmem_limit_bytes=VMEM_LIMIT),
        name="experts",
    )(*pieces, *residual, *weights)
    return keep, send


def finish_kernel(own_ref, z1_ref, z2_ref, x_ref, y_ref, out_ref):
    total = own_ref[0]
    for extra_ref in (x_ref, y_ref):
        total = total + extra_ref[0].astype(jnp.float32)
    for extra_ref in (z1_ref, z2_ref):
        total = total + extra_ref[...].astype(jnp.float32)
    out_ref[...] = total.astype(jnp.bfloat16)


def ordered(*values):
    return lax.optimization_barrier(values)


def across_parts(line_x, line_y):
    half = line_x.shape[1] // 2
    return flip(line_x[:, :half], "tp", 2), flip(line_y[:, half:], "req", 1)


def other_core(parts):
    return tuple(flip(part, "tp", 1) for part in parts)


def with_core(pair):
    return pair[0], list(other_core(pair[1]))


def joined(pair, column, y):
    return pair[0][column, y] + pair[1][y][column].astype(jnp.float32)


def near_pieces(column, line, core):
    return [((column, 0, 0), line), ((column, 1, 0), core)]


def far_pieces(column, parts, cores):
    half = parts[0].shape[1]
    if len(parts) == 1:
        return [((column, 2, 0), parts[0]), ((column, 3, 0), cores[0])]
    return [((column, 2, i * half), part) for i, part in enumerate(parts)] + [
        ((column, 3, i * half), part) for i, part in enumerate(cores)
    ]


def relayed(side):
    part = side.astype(jnp.bfloat16)
    half = part.shape[1] // 2
    return flip(part[:, :half], "req", 1), flip(part[:, half:], "tp", 2)


def neighbours(to_x, to_y, by_x, by_y):
    half = by_x.shape[1]
    to_y = jnp.concatenate([to_y[:, :half] + by_x.astype(jnp.float32), to_y[:, half:]], axis=1)
    to_x = jnp.concatenate([to_x[:, :half], to_x[:, half:] + by_y.astype(jnp.float32)], axis=1)
    return flip(to_x.astype(jnp.bfloat16), "req", 1), flip(to_y.astype(jnp.bfloat16), "tp", 2)


def moe_dense(
    kept,
    far,
    core,
    norm_post_gain,
    expert_ids,
    route_weights,
    gate_weight,
    up_weight,
    down_weight,
):
    share_rows, width = kept.shape
    token_count, share_width = 4 * share_rows, width // 4
    core = flip(core, "tp", 1)
    far, kept, core = ordered((far + core[1].astype(jnp.float32)).astype(jnp.bfloat16), kept, core)
    kept, far = ordered(kept + core[0].astype(jnp.float32), flip(far, "tp", 2))
    rows, residual = pl.pallas_call(
        pack_kernel,
        out_shape=[
            jax.ShapeDtypeStruct((share_rows, width + LANES), jnp.bfloat16),
            jax.ShapeDtypeStruct((share_rows, width), jnp.float32),
        ],
        in_specs=[VMEM] * 5,
        out_specs=[VMEM] * 2,
        scratch_shapes=[pltpu.VMEM((token_count, LANES), jnp.float32)],
        compiler_params=pltpu.CompilerParams(vmem_limit_bytes=8 * 1024 * 1024),
        name="pack_rows",
    )(kept, far, norm_post_gain[None, :], expert_ids.T, route_weights.T)
    gate_up = [w.transpose(0, 2, 1).reshape(-1, width) for w in (gate_weight, up_weight)]
    weights = (*gate_up, down_weight.reshape(-1, width))
    line_0 = rows[None]
    levels = [flip(line_0, "req", 2 * bits) for bits in (1, 2, 3)]
    y_0, x_0 = flip(line_0, "tp", 2), flip(line_0, "req", 1)
    line_3, y_0, x_0 = ordered(jnp.concatenate(levels), y_0, x_0)
    core_0, core_3, across_0, y_3, x_3 = ordered(
        *other_core((line_0, line_3)),
        across_parts(x_0, y_0),
        flip(line_3, "tp", 2),
        flip(line_3, "req", 1),
    )
    y_core_3, x_core_3 = other_core((y_3, x_3))
    near_3 = run_experts(
        near_pieces(0, line_3, core_3) + far_pieces(0, (y_3,), (y_core_3,)), weights, token_count
    )
    near_3, y_core_0, x_core_0, across_core_0, x_core_3, across_3 = ordered(
        near_3,
        *other_core((y_0, x_0)),
        other_core(across_0),
        x_core_3,
        across_parts(x_3, y_3),
    )
    keep, (send, first) = run_experts(
        near_pieces(0, x_3, x_core_3) + far_pieces(0, across_3, other_core(across_3)),
        weights,
        token_count,
    )
    near_3, keep, send, first = ordered(near_3, keep, send, first)
    all_0 = run_experts(
        near_pieces(0, line_0, core_0)
        + far_pieces(0, (y_0,), (y_core_0,))
        + near_pieces(1, x_0, x_core_0)
        + far_pieces(1, across_0, across_core_0),
        weights,
        token_count,
        residual,
    )
    all_0, near_3, keep, send, first = ordered(all_0, near_3, keep, send, flip(first, "tp", 1))
    relay_3 = relayed(joined((keep, (send, first)), 0, 1))
    near_keep, (near_send, near_first) = near_3
    all_0, near_send, near_first, send, relay_3 = ordered(
        all_0, near_send, flip(near_first, "tp", 1), flip(send, "tp", 1), relay_3
    )
    sums_3 = neighbours(
        joined((keep, (send, first)), 0, 0), joined((near_keep, (near_send, near_first)), 0, 1), *relay_3
    )
    all_0, near_send, sums_3 = ordered(with_core(all_0), flip(near_send, "tp", 1), sums_3)
    near_3 = (near_keep, (near_send, near_first))
    sent = joined(near_3, 0, 0) + sums_3[0].astype(jnp.float32) + sums_3[1].astype(jnp.float32)
    sent_3, relay_0 = ordered(
        flip(sent[2].astype(jnp.bfloat16), "req", 2), relayed(joined(all_0, 1, 1))
    )
    sent_2, relay_0 = ordered(
        (sent[1] + sent_3.astype(jnp.float32)).astype(jnp.bfloat16), relay_0
    )
    from_z = [flip(sent[0].astype(jnp.bfloat16), "req", 2), flip(sent_2, "req", 4)]
    sums_0 = neighbours(joined(all_0, 1, 0), joined(all_0, 0, 1), *relay_0)
    return pl.pallas_call(
        finish_kernel,
        out_shape=jax.ShapeDtypeStruct((token_count, share_width), jnp.bfloat16),
        in_specs=[VMEM] * 5,
        out_specs=VMEM,
        compiler_params=pltpu.CompilerParams(vmem_limit_bytes=8 * 1024 * 1024),
        name="finish",
    )(joined(all_0, 0, 0), *from_z, *sums_0)


def moe_routed(
    x_full,
    head_part,
    norm_post_gain,
    expert_ids,
    route_weights,
    gate_weight,
    up_weight,
    down_weight,
):
    req_count = lax.axis_size("req")
    tp_index = lax.axis_index("tp")
    x_float = x_full.astype(jnp.float32)
    token_count = x_float.shape[0]
    share_width = x_float.shape[1] // lax.axis_size("tp")
    top_count = expert_ids.shape[1]
    expert_count = gate_weight.shape[0] * req_count
    capacity = max(2, 3 * token_count * top_count // (2 * expert_count))
    flat_expert = expert_ids.reshape(token_count * top_count)
    one_hot = (flat_expert[:, None] == jnp.arange(expert_count, dtype=jnp.int32)[None, :]).astype(
        jnp.int32
    )
    slot_rank = jnp.sum((jnp.cumsum(one_hot, axis=0) - one_hot) * one_hot, axis=1)
    slot_index = flat_expert * capacity + slot_rank
    head_sum = lax.psum(head_part.astype(jnp.bfloat16), "tp").astype(jnp.float32)
    residual_full = x_float + head_sum
    normed_post = rms_scale(residual_full, norm_post_gain).astype(jnp.bfloat16)
    residual = lax.dynamic_slice_in_dim(residual_full, tp_index * share_width, share_width, 1)
    send_buffer = build_buffer(normed_post, slot_index, top_count, expert_count, capacity)
    part_sums = expert_apply(
        lax.all_to_all(send_buffer, "req", split_axis=0, concat_axis=0, tiled=True),
        gate_weight,
        up_weight,
        down_weight,
    )
    returned = lax.all_to_all(part_sums, "req", split_axis=0, concat_axis=0, tiled=True)
    moe_term = weigh_back(returned, slot_index, route_weights, token_count, top_count)
    moe_share = lax.psum_scatter(
        moe_term.astype(jnp.bfloat16), "tp", scatter_dimension=1, tiled=True
    ).astype(jnp.float32)
    return (residual + moe_share).astype(jnp.bfloat16)


def attention_part(
    x_full,
    norm_in_gain,
    q_weight,
    k_weight,
    v_weight,
    q_gain,
    k_gain,
    o_weight,
    key_pages,
    value_pages,
    page_table,
    cache_len,
):
    head_dim = q_gain.shape[0]
    kv_local = key_pages.shape[0]
    group_size = q_weight.shape[1] // head_dim // kv_local
    token_count = x_full.shape[0]
    x_float = x_full.astype(jnp.float32)
    normed_in = rms_scale(x_float, norm_in_gain).astype(jnp.bfloat16)
    query_lin = jnp.dot(normed_in, q_weight, preferred_element_type=jnp.float32).reshape(
        token_count, kv_local * group_size, head_dim
    )
    key_lin = jnp.dot(normed_in, k_weight, preferred_element_type=jnp.float32).reshape(
        token_count, kv_local, head_dim
    )
    values_new = (
        jnp.dot(normed_in, v_weight, preferred_element_type=jnp.float32)
        .astype(jnp.bfloat16)
        .reshape(token_count, kv_local, head_dim)
    )
    requests, positions = token_layout(cache_len)
    queries = (
        rotate(rms_scale(query_lin, q_gain), positions)
        .astype(jnp.bfloat16)
        .reshape(token_count, kv_local, group_size, head_dim)
    )
    keys_new = rotate(rms_scale(key_lin, k_gain), positions).astype(jnp.bfloat16)
    slot_owner = page_slots(page_table, cache_len)
    cache_slots = key_pages.shape[1] * key_pages.shape[2]
    keys_cache = key_pages.reshape(kv_local, cache_slots, head_dim)
    values_cache = value_pages.reshape(kv_local, cache_slots, head_dim)
    attended = attend(
        queries, keys_new, values_new, keys_cache, values_cache, requests, positions, slot_owner
    )
    return jnp.dot(attended, o_weight, preferred_element_type=jnp.float32)


def body(
    hidden_in,
    norm_in_gain,
    q_weight,
    k_weight,
    v_weight,
    q_gain,
    k_gain,
    o_weight,
    key_pages,
    value_pages,
    page_table,
    cache_len,
    norm_post_gain,
    expert_ids,
    route_weights,
    gate_weight,
    up_weight,
    down_weight,
):
    req_count = lax.axis_size("req")
    attention = (
        norm_in_gain,
        q_weight,
        k_weight,
        v_weight,
        q_gain,
        k_gain,
        o_weight,
        key_pages,
        value_pages,
        page_table,
        cache_len,
    )
    experts = (norm_post_gain, expert_ids, route_weights, gate_weight, up_weight, down_weight)
    expert_count = gate_weight.shape[0] * req_count
    staged = (req_count, lax.axis_size("tp"), gate_weight.shape[0]) == (8, 4, 2)
    if staged and expert_count <= LANES // 2:
        return moe_dense(*attention_shares(hidden_in, *attention), *experts)
    x_full = lax.all_gather(hidden_in, "tp", axis=1, tiled=True)
    return moe_routed(x_full, attention_part(x_full, *attention), *experts)


def solution(mesh):
    return jax.shard_map(
        body,
        mesh=mesh,
        in_specs=(
            P("req", "tp"),
            P(),
            P(None, "tp"),
            P(None, "tp"),
            P(None, "tp"),
            P(),
            P(),
            P("tp", None),
            P("tp", "req", None, None),
            P("tp", "req", None, None),
            P("req", None),
            P("req"),
            P(),
            P("req", None),
            P("req", None),
            P("req", None, "tp"),
            P("req", None, "tp"),
            P("req", "tp", None),
        ),
        out_specs=P("req", "tp"),
        check_vma=False,
    )
```

```python
import functools
import math

import jax
import jax.numpy as jnp
import numpy as np
from jax import lax
from jax.experimental import pallas as pl
from jax.experimental.pallas import tpu as pltpu
from jax.sharding import PartitionSpec as P

PAGE = 128
MAXPG = 32
PRE = 120
TOK_DEV = 128
REQS_DEV = 9
POOL = 48
SHORT_PG = 2
SHORT_LIST = (REQS_DEV - 1) * SHORT_PG


NORM_EPS = 1e-06
ROPE_BASE = 1000000.0


def rms_scale(values, gain_vec):
    mean_square = jnp.mean(values * values, axis=-1, keepdims=True)
    return values * lax.rsqrt(mean_square + NORM_EPS) * gain_vec


def rotate(values, positions):
    half_dim = values.shape[-1] // 2
    exponent = jnp.arange(half_dim, dtype=jnp.float32) * (2.0 / values.shape[-1])
    frequency = jnp.power(jnp.float32(ROPE_BASE), -exponent)
    angles = positions.astype(jnp.float32)[:, None] * frequency[None, :]
    cosine = jnp.cos(angles)[:, None, :]
    sine_val = jnp.sin(angles)[:, None, :]
    front_half = values[..., :half_dim]
    back_half = values[..., half_dim:]
    return jnp.concatenate(
        [front_half * cosine - back_half * sine_val, back_half * cosine + front_half * sine_val],
        axis=-1,
    )


def token_layout(lengths):
    local_idx = jnp.arange(TOK_DEV, dtype=jnp.int32)
    requests = jnp.where(local_idx < PRE, 0, local_idx - PRE + 1)
    offsets = jnp.where(local_idx < PRE, local_idx, 0)
    request_hot = (requests[:, None] == jnp.arange(REQS_DEV, dtype=jnp.int32)[None, :]).astype(
        jnp.int32
    )
    positions = jnp.sum(request_hot * lengths[None, :], axis=1) + offsets
    return (requests, positions)


def page_slots(table, lengths):
    pages_used = (lengths + PAGE - 1) // PAGE
    entry_live = jnp.arange(MAXPG, dtype=jnp.int32)[None, :] < pages_used[:, None]
    page_match = (
        (table[:, :, None] == jnp.arange(POOL, dtype=jnp.int32)[None, None, :])
        & entry_live[:, :, None]
    ).astype(jnp.int32)
    page_owner = jnp.sum(
        page_match * jnp.arange(REQS_DEV, dtype=jnp.int32)[:, None, None], axis=(0, 1)
    )
    page_start = jnp.sum(
        page_match * (jnp.arange(MAXPG, dtype=jnp.int32) * PAGE)[None, :, None], axis=(0, 1)
    )
    page_used = jnp.sum(page_match, axis=(0, 1)) > 0
    owner_length = jnp.sum(page_match * lengths[:, None, None], axis=(0, 1))
    slot_pos = page_start[:, None] + jnp.arange(PAGE, dtype=jnp.int32)[None, :]
    slot_live = page_used[:, None] & (slot_pos < owner_length[:, None])
    slot_owner = jnp.where(slot_live, page_owner[:, None], -1)
    return slot_owner.reshape(POOL * PAGE)


def attend(
    queries, keys_new, values_new, keys_cache, values_cache, requests, positions, slot_owner
):
    inv_root = 1.0 / math.sqrt(queries.shape[-1])
    cache_mask = slot_owner[None, :] == requests[:, None]
    new_mask = (requests[None, :] == requests[:, None]) & (positions[None, :] <= positions[:, None])
    score_cache = (
        jnp.einsum("tkgh,knh->kgtn", queries, keys_cache, preferred_element_type=jnp.float32)
        * inv_root
    )
    score_new = (
        jnp.einsum("tkgh,skh->kgts", queries, keys_new, preferred_element_type=jnp.float32)
        * inv_root
    )
    score_cache = jnp.where(cache_mask[None, None], score_cache, -1e30)
    score_new = jnp.where(new_mask[None, None], score_new, -1e30)
    row_max = jnp.maximum(
        jnp.max(score_cache, axis=-1, keepdims=True), jnp.max(score_new, axis=-1, keepdims=True)
    )
    exp_cache = jnp.where(cache_mask[None, None], jnp.exp(score_cache - row_max), 0.0)
    exp_new = jnp.where(new_mask[None, None], jnp.exp(score_new - row_max), 0.0)
    total = jnp.sum(exp_cache, axis=-1, keepdims=True) + jnp.sum(exp_new, axis=-1, keepdims=True)
    prob_cache = (exp_cache / total).astype(jnp.bfloat16)
    prob_new = (exp_new / total).astype(jnp.bfloat16)
    mixed = jnp.einsum(
        "kgtn,knh->tkgh", prob_cache, values_cache, preferred_element_type=jnp.float32
    )
    mixed = mixed + jnp.einsum(
        "kgts,skh->tkgh", prob_new, values_new, preferred_element_type=jnp.float32
    )
    return mixed.astype(jnp.bfloat16).reshape(queries.shape[0], -1)


def expert_apply(blocks, gate_weight, up_weight, down_weight):
    local_experts = gate_weight.shape[0]
    sources = blocks.shape[0] // local_experts
    slot_count = blocks.shape[1]
    grouped = blocks.reshape(sources, local_experts, slot_count, blocks.shape[2])
    gate_acts = jnp.einsum(
        "sekd,edf->sekf", grouped, gate_weight, preferred_element_type=jnp.float32
    )
    up_acts = jnp.einsum("sekd,edf->sekf", grouped, up_weight, preferred_element_type=jnp.float32)
    hidden_act = (jax.nn.silu(gate_acts) * up_acts).astype(jnp.bfloat16)
    part_sums = jnp.einsum(
        "sekf,efd->sekd", hidden_act, down_weight, preferred_element_type=jnp.float32
    ).astype(jnp.bfloat16)
    return part_sums.reshape(sources * local_experts, slot_count, part_sums.shape[3])


def build_buffer(normed, slot_index, top_count, expert_count, capacity):
    picked = jnp.repeat(normed, top_count, axis=0)
    buffer_rows = (
        jnp.zeros((expert_count * capacity, normed.shape[1]), normed.dtype)
        .at[slot_index]
        .set(picked)
    )
    return buffer_rows.reshape(expert_count, capacity, normed.shape[1])


def weigh_back(returned, slot_index, route_weights, token_count, top_count):
    row_width = returned.shape[2]
    back_rows = returned.reshape(returned.shape[0] * returned.shape[1], row_width)[slot_index]
    weighted = (
        back_rows.astype(jnp.float32) * route_weights.reshape(token_count * top_count)[:, None]
    )
    return jnp.sum(weighted.reshape(token_count, top_count, row_width), axis=1)


LANES = 128
VMEM = pl.BlockSpec(memory_space=pltpu.VMEM)
SMEM = pl.BlockSpec(memory_space=pltpu.SMEM)
VMEM_LIMIT = 24 * 1024 * 1024


def flip(value, axis, bits):
    return lax.ppermute(value, axis, [(i, i ^ bits) for i in range(lax.axis_size(axis))])


def stage_kernel(*refs):
    length_hbm, table_hbm, frequency_hbm, *large = refs[:12]
    cosine_ref, sine_ref, owner_ref, *staged = refs[12:24]
    list_ref, length_out, table_out = refs[24:27]
    frequency_ref, owners, sems = refs[27:]
    length_ref, table_ref = length_out, table_out
    sources = (length_hbm, table_hbm, frequency_hbm, *large)
    targets = (length_out, table_out, frequency_ref, *staged)
    copies = [
        pltpu.make_async_copy(source, target, sems.at[i])
        for i, (source, target) in enumerate(zip(sources, targets))
    ]
    for copy in copies:
        copy.start()
    for copy in copies[:3]:
        copy.wait()
    tokens, head_dim = cosine_ref.shape
    for entry in range(POOL):
        list_ref[entry] = 0
        owners[0, entry] = -1
        owners[1, entry] = 0
    prefill_long = length_ref[0] > SHORT_PG * PAGE
    count = jnp.int32(0)
    for request in range(1, REQS_DEV):

        def name_page(entry, count):
            page = table_ref[request, entry]
            place = jnp.where(prefill_long, count, page)
            list_ref[place] = page
            owners[0, place] = request
            owners[1, place] = jnp.minimum(length_ref[request] - entry * PAGE, PAGE)
            return count + 1

        count = lax.fori_loop(0, (length_ref[request] + PAGE - 1) // PAGE, name_page, count)
    slot = lax.broadcasted_iota(jnp.int32, (1, PAGE), 1)
    for entry in range(POOL):
        owner_ref[:, entry * PAGE : (entry + 1) * PAGE] = jnp.where(
            slot < owners[1, entry], owners[0, entry], -1
        )
    token = lax.broadcasted_iota(jnp.int32, (tokens, head_dim), 0)
    lane = lax.broadcasted_iota(jnp.int32, (tokens, head_dim), 1)
    position = length_ref[0] + token
    for i in range(tokens - PRE):
        position = jnp.where(token == PRE + i, length_ref[i + 1], position)
    angle = position.astype(jnp.float32) * frequency_ref[...]
    sine = jnp.sin(angle)
    cosine_ref[...] = jnp.cos(angle)
    sine_ref[...] = jnp.where(lane < head_dim // 2, -sine, sine)
    for copy in copies[3:]:
        copy.wait()


def attention_kernel(*refs):
    pieces, (keep_out, far_out, core_out) = refs[:4], refs[19:22]
    (cosine_ref, sine_ref, owner_ref, gain_ref, q_gain_ref, k_gain_ref) = refs[4:10]
    (q_ref, k_ref, v_ref, key_ref, value_ref, o_ref, list_ref, length_ref, table_ref) = refs[10:19]
    (
        x_ref, query_ref, own_scores, scores_ref, mix_ref, mixed_ref, part_ref, slots_ref, decoded_ref,
    ) = refs[22:]
    tokens, head_dim = x_ref.shape[0], k_gain_ref.shape[1]
    tp_index = lax.axis_index("tp")
    heads = q_ref.shape[1] // head_dim
    decodes = tokens - PRE
    for step, piece in enumerate(pieces):
        width = piece.shape[1]
        start = pl.multiple_of((tp_index ^ step) * width, width)
        x_ref[:, pl.ds(start, width)] = piece[...]
    token = lax.broadcasted_iota(jnp.int32, (tokens, head_dim), 0)
    lane = lax.broadcasted_iota(jnp.int32, (tokens, head_dim), 1)

    def turned(values, gain):
        values = rms_scale(values, gain)
        return values * cosine_ref[...] + pltpu.roll(values, head_dim // 2, 1) * sine_ref[...]

    def with_ones(values):
        return jnp.concatenate([values, jnp.ones_like(values)], axis=1)

    normed = rms_scale(x_ref[...].astype(jnp.float32), gain_ref[...]).astype(jnp.bfloat16)
    contract = (((1,), (1,)), ((), ()))
    key_lin = jnp.dot(normed, k_ref[...], preferred_element_type=jnp.float32)
    values_new = jnp.dot(normed, v_ref[...], preferred_element_type=jnp.float32).astype(jnp.bfloat16)
    query_lin = jnp.dot(normed, q_ref[...], preferred_element_type=jnp.float32)
    keys_new = turned(key_lin, k_gain_ref[...]).astype(jnp.bfloat16)
    values_new = with_ones(values_new)
    to_log2 = math.log2(math.e) / math.sqrt(head_dim)
    own_mask = (lane == token) | ((lane < token) & (token < PRE))
    decode_query, decode_own = [], []
    for head in range(heads):
        span = slice(head * tokens, (head + 1) * tokens)
        query = turned(query_lin[:, head * head_dim : (head + 1) * head_dim], q_gain_ref[...]) * to_log2
        rounded = query.astype(jnp.bfloat16)
        query_ref[span, :] = rounded
        scores = lax.dot_general(rounded, keys_new, contract, preferred_element_type=jnp.float32)
        scores = jnp.where(own_mask, scores, -1e30)
        own_scores[span, :] = scores
        decode_query.append(query[PRE:])
        decode_own.append(scores[PRE:])
    decode_query = jnp.concatenate(decode_query, axis=0).astype(jnp.bfloat16)
    decode_own = jnp.concatenate(decode_own, axis=0)

    def raised(top, scores):
        for start in range(0, scores.shape[1], head_dim):
            top = jnp.maximum(top, scores[:, start : start + head_dim])
        return top

    def weigh(own, score_steps, value_steps, scores_ref):
        top = own
        for step, score_step in enumerate(score_steps):
            scores = score_step()
            scores_ref[step, :, : scores.shape[1]] = scores
            top = raised(top, scores)
        top = jnp.max(top, axis=1, keepdims=True)
        mix = jnp.dot(
            jnp.exp2(own - top).astype(jnp.bfloat16), values_new, preferred_element_type=jnp.float32
        )
        for step, value_step in enumerate(value_steps):
            values = value_step()
            weights = jnp.exp2(scores_ref[step, :, : values.shape[0]] - top).astype(jnp.bfloat16)
            mix = mix + jnp.dot(weights, with_ones(values), preferred_element_type=jnp.float32)
        return mix

    def taken(ref, names):
        return jnp.concatenate([ref[name] for name in names], axis=0)

    def against(queries, keys):
        return lax.dot_general(queries, keys, contract, preferred_element_type=jnp.float32)

    def prefill(names, live):
        def score(pages):
            scores = against(query_ref[...], taken(key_ref, pages))
            return scores if live is None else jnp.where(live, scores, -1e30)

        mix_ref[...] = weigh(
            own_scores[...],
            [functools.partial(score, pages) for pages in names],
            [functools.partial(taken, value_ref, pages) for pages in names],
            scores_ref,
        )

    def decode(steps, pages_of):
        row_request = 1 + lax.broadcasted_iota(jnp.int32, (heads * decodes, 1), 0) % decodes
        width = slots_ref.shape[2]

        def score(step):
            scores = against(decode_query, pages_of(key_ref, step))
            owner = owner_ref[:, step * width : (step + 1) * width]
            return jnp.where(owner == row_request, scores, -1e30)

        mix = weigh(
            decode_own,
            [functools.partial(score, step) for step in range(steps)],
            [functools.partial(pages_of, value_ref, step) for step in range(steps)],
            slots_ref,
        )
        decoded_ref[...] = mix[:, :head_dim] / mix[:, head_dim:]

    length = length_ref[0]
    listed = slots_ref.shape[2] // PAGE
    pages = scores_ref.shape[2] // PAGE

    @pl.when(length > SHORT_PG * PAGE)
    def _():
        names = [table_ref[0, entry] for entry in range(MAXPG)]
        prefill([names[first : first + pages] for first in range(0, MAXPG, pages)], None)
        decode(
            SHORT_LIST // listed,
            lambda ref, step: taken(ref, [list_ref[step * listed + i] for i in range(listed)]),
        )

    @pl.when(length <= SHORT_PG * PAGE)
    def _():
        column = lax.broadcasted_iota(jnp.int32, (1, SHORT_PG * PAGE), 1)
        prefill([[table_ref[0, entry] for entry in range(SHORT_PG)]], column < length)
        decode(
            POOL // listed,
            lambda ref, step: ref[step * listed : (step + 1) * listed].reshape(-1, head_dim),
        )

    for head in range(heads):
        part = mix_ref[head * tokens : (head + 1) * tokens, :]
        columns = slice(head * head_dim, (head + 1) * head_dim)
        mixed_ref[:, columns] = part[:, :head_dim] / part[:, head_dim:]
        mixed_ref[PRE:, columns] = decoded_ref[head * decodes : (head + 1) * decodes]
    part_ref[...] = jnp.dot(
        mixed_ref[...].astype(jnp.bfloat16), o_ref[...], preferred_element_type=jnp.float32
    )
    share_rows = keep_out.shape[0]

    def quarter(step):
        return pl.ds(pl.multiple_of((tp_index ^ step) * share_rows, share_rows), share_rows)

    keep_out[...] = part_ref[quarter(0), :] + x_ref[quarter(0), :].astype(jnp.float32)
    far_out[...] = part_ref[quarter(2), :]
    core_out[0] = part_ref[quarter(1), :].astype(jnp.bfloat16)
    core_out[1] = part_ref[quarter(3), :].astype(jnp.bfloat16)


def attention_shares(
    hidden_in, norm_in_gain, q_weight, k_weight, v_weight, q_gain, k_gain, o_weight,
    key_pages, value_pages, page_table, cache_len,
):
    tokens, width = hidden_in.shape[0], 4 * hidden_in.shape[1]
    head_dim = q_gain.shape[0]
    rows = q_weight.shape[1] // head_dim * tokens
    decode_rows = rows // tokens * (tokens - PRE)
    half = ROPE_BASE ** (-np.arange(head_dim // 2) / (head_dim // 2))
    frequency = jnp.asarray(np.concatenate([half, half])[None, :], jnp.float32)
    large = (
        norm_in_gain[None, :], q_gain[None, :], k_gain[None, :], q_weight, k_weight, v_weight,
        key_pages[0], value_pages[0], o_weight,
    )
    scalars = (cache_len, page_table)
    sources = [
        pltpu.with_memory_space_constraint(array, pltpu.HBM)
        for array in (*scalars, frequency, *large)
    ]
    rope = pltpu.VMEM((tokens, head_dim), jnp.float32)
    *staged, page_list, lengths, table = pl.pallas_call(
        stage_kernel,
        out_shape=[rope, rope, pltpu.VMEM((1, POOL * PAGE), jnp.int32)]
        + [pltpu.VMEM(array.shape, array.dtype) for array in large]
        + [jax.ShapeDtypeStruct((POOL,), jnp.int32)]
        + [jax.ShapeDtypeStruct(array.shape, array.dtype) for array in scalars],
        in_specs=[pl.BlockSpec(memory_space=pltpu.HBM)] * 12,
        out_specs=[VMEM] * 12 + [SMEM] * 3,
        scratch_shapes=[
            pltpu.VMEM(frequency.shape, frequency.dtype),
            pltpu.SMEM((2, POOL), jnp.int32),
            pltpu.SemaphoreType.DMA((12,)),
        ],
        compiler_params=pltpu.CompilerParams(vmem_limit_bytes=4 * 1024 * 1024),
        name="stage",
    )(*sources)
    far, *staged = ordered(flip(hidden_in, "tp", 2), *staged, page_list, lengths, table)
    pieces = (hidden_in, flip(hidden_in, "tp", 1), far, flip(far, "tp", 1))
    share = (tokens // 4, width)
    score_pages, list_pages = 4, 8
    return pl.pallas_call(
        attention_kernel,
        out_shape=[
            jax.ShapeDtypeStruct(share, jnp.float32),
            jax.ShapeDtypeStruct(share, jnp.float32),
            jax.ShapeDtypeStruct((2, *share), jnp.bfloat16),
        ],
        in_specs=[VMEM] * 16 + [SMEM] * 3,
        out_specs=[VMEM] * 3,
        scratch_shapes=[
            pltpu.VMEM((tokens, width), jnp.bfloat16),
            pltpu.VMEM((rows, head_dim), jnp.bfloat16),
            pltpu.VMEM((rows, tokens), jnp.float32),
            pltpu.VMEM((MAXPG // score_pages, rows, score_pages * PAGE), jnp.float32),
            pltpu.VMEM((rows, 2 * head_dim), jnp.float32),
            pltpu.VMEM((tokens, q_weight.shape[1]), jnp.float32),
            pltpu.VMEM((tokens, width), jnp.float32),
            pltpu.VMEM((POOL // list_pages, decode_rows, list_pages * PAGE), jnp.float32),
            pltpu.VMEM((decode_rows, head_dim), jnp.float32),
        ],
        compiler_params=pltpu.CompilerParams(vmem_limit_bytes=24 * 1024 * 1024),
        name="attention",
    )(*pieces, *staged)


def pack_kernel(
    own_ref, far_ref, gain_ref, ids_ref, routes_ref,
    rows_ref, residual_ref, spread_ref,
):
    tp_index = lax.axis_index("tp")
    share_rows, width = own_ref.shape
    mine = pl.ds(pl.multiple_of(tp_index * share_rows, share_rows), share_rows)
    residual = own_ref[...] + far_ref[...].astype(jnp.float32)
    residual_ref[...] = residual
    rows_ref[:, :width] = rms_scale(residual, gain_ref[...]).astype(jnp.bfloat16)
    expert = lax.broadcasted_iota(jnp.int32, (LANES, spread_ref.shape[0]), 0) % (LANES // 2)
    spread = jnp.zeros(expert.shape, jnp.float32)
    for k in range(ids_ref.shape[0]):
        spread = spread + jnp.where(expert == ids_ref[k : k + 1, :], routes_ref[k : k + 1, :], 0.0)
    spread_ref[...] = spread.T
    spread = spread_ref[mine, :]
    lane = lax.broadcasted_iota(jnp.int32, spread.shape, 1)
    high = spread.astype(jnp.bfloat16).astype(jnp.float32)
    rows_ref[:, width:] = jnp.where(lane < LANES // 2, high, spread - high).astype(jnp.bfloat16)


def experts_kernel(plan, residuals, *refs):
    pieces, residual_refs = refs[: len(plan)], refs[len(plan) : len(plan) + residuals]
    gate_ref, up_ref, down_ref, keep_ref, *send_refs, rows_ref, sums_ref = refs[len(plan) + residuals :]
    req_index, tp_index = lax.axis_index("req"), lax.axis_index("tp")
    columns, _, levels, group_rows, share_width = keep_ref.shape
    width = gate_ref.shape[1]
    units = gate_ref.shape[0] // 2
    for (column, step, first), piece in zip(plan, pieces):
        count = piece.shape[1]
        for level in range(levels):
            start = (column * levels + level) * group_rows + first
            start = start + (tp_index ^ step) * (group_rows // 4)
            rows_ref[pl.ds(pl.multiple_of(start, count), count), :] = piece[level]
    spread = rows_ref[:, width:].astype(jnp.float32)
    lane = lax.broadcasted_iota(jnp.int32, spread.shape, 1) % (LANES // 2)
    weights = [
        jnp.sum(jnp.where(lane == 2 * req_index + e, spread, 0.0), axis=1, keepdims=True)
        for e in range(2)
    ]
    contract = (((1,), (1,)), ((), ()))
    rows = rows_ref[:, :width]
    gate = lax.dot_general(rows, gate_ref[...], contract, preferred_element_type=jnp.float32)
    up = lax.dot_general(rows, up_ref[...], contract, preferred_element_type=jnp.float32)
    unit = lax.broadcasted_iota(jnp.int32, gate.shape, 1)
    weight = jnp.where(unit < units, weights[0], weights[1])
    acts = (gate / (1.0 + jnp.exp(-gate)) * up * weight).astype(jnp.bfloat16)
    for step in range(4):
        start = pl.multiple_of((tp_index ^ step) * share_width, share_width)
        part = jnp.dot(
            acts, down_ref[:, pl.ds(start, share_width)], preferred_element_type=jnp.float32
        )
        for residual_ref in residual_refs:
            count = residual_ref.shape[0]
            mine = pl.ds(pl.multiple_of(tp_index * count, count), count)
            sums_ref[...] = part
            sums_ref[mine, :] += residual_ref[:, pl.ds(start, share_width)]
            part = sums_ref[...]
        part = part.reshape(columns, levels, group_rows, share_width)
        if step % 2:
            send_refs[step // 2][...] = part.astype(jnp.bfloat16)
            continue
        for column in range(columns):
            keep_ref[column, step // 2] = part[column]


def run_experts(pieces, weights, group_rows, *residual):
    plan = tuple(place for place, _ in pieces)
    pieces = [piece for _, piece in pieces]
    columns, levels, packed = 1 + max(place[0] for place in plan), *pieces[0].shape[::2]
    rows, share_width = columns * levels * group_rows, weights[2].shape[1] // 4
    sums = (levels, group_rows, share_width)
    keep, *send = pl.pallas_call(
        functools.partial(experts_kernel, plan, len(residual)),
        out_shape=[jax.ShapeDtypeStruct((columns, 2, *sums), jnp.float32)]
        + [jax.ShapeDtypeStruct((columns, *sums), jnp.bfloat16)] * 2,
        in_specs=[VMEM] * (len(pieces) + len(residual) + 3),
        out_specs=[VMEM] * 3,
        scratch_shapes=[
            pltpu.VMEM((rows, packed), jnp.bfloat16),
            pltpu.VMEM((rows, share_width), jnp.float32),
        ],
        compiler_params=pltpu.CompilerParams(vmem_limit_bytes=VMEM_LIMIT),
        name="experts",
    )(*pieces, *residual, *weights)
    return keep, send


def finish_kernel(own_ref, z1_ref, z2_ref, x_ref, y_ref, out_ref):
    total = own_ref[0]
    for extra_ref in (x_ref, y_ref):
        total = total + extra_ref[0].astype(jnp.float32)
    for extra_ref in (z1_ref, z2_ref):
        total = total + extra_ref[...].astype(jnp.float32)
    out_ref[...] = total.astype(jnp.bfloat16)


def ordered(*values):
    return lax.optimization_barrier(values)


def across_parts(line_x, line_y):
    half = line_x.shape[1] // 2
    return flip(line_x[:, :half], "tp", 2), flip(line_y[:, half:], "req", 1)


def other_core(parts):
    return tuple(flip(part, "tp", 1) for part in parts)


def with_core(pair):
    return pair[0], list(other_core(pair[1]))


def joined(pair, column, y):
    return pair[0][column, y] + pair[1][y][column].astype(jnp.float32)


def near_pieces(column, line, core):
    return [((column, 0, 0), line), ((column, 1, 0), core)]


def far_pieces(column, parts, cores):
    half = parts[0].shape[1]
    if len(parts) == 1:
        return [((column, 2, 0), parts[0]), ((column, 3, 0), cores[0])]
    return [((column, 2, i * half), part) for i, part in enumerate(parts)] + [
        ((column, 3, i * half), part) for i, part in enumerate(cores)
    ]


def relayed(side):
    part = side.astype(jnp.bfloat16)
    half = part.shape[1] // 2
    return flip(part[:, :half], "req", 1), flip(part[:, half:], "tp", 2)


def with_lower(sums, part):
    half = part.shape[1]
    sums = [sums[:, :half] + part.astype(jnp.float32), sums[:, half:]]
    return jnp.concatenate(sums, axis=1).astype(jnp.bfloat16)


def with_upper(sums, part):
    half = part.shape[1]
    sums = [sums[:, :half], sums[:, half:] + part.astype(jnp.float32)]
    return jnp.concatenate(sums, axis=1).astype(jnp.bfloat16)


def neighbours(to_x, to_y, by_x, by_y):
    return flip(with_upper(to_x, by_y), "req", 1), flip(with_lower(to_y, by_x), "tp", 2)


def moe_dense(
    kept,
    far,
    core,
    norm_post_gain,
    expert_ids,
    route_weights,
    gate_weight,
    up_weight,
    down_weight,
):
    share_rows, width = kept.shape
    token_count, share_width = 4 * share_rows, width // 4
    core = flip(core, "tp", 1)
    far, kept, core = ordered((far + core[1].astype(jnp.float32)).astype(jnp.bfloat16), kept, core)
    kept, far = ordered(kept + core[0].astype(jnp.float32), flip(far, "tp", 2))
    rows, residual = pl.pallas_call(
        pack_kernel,
        out_shape=[
            jax.ShapeDtypeStruct((share_rows, width + LANES), jnp.bfloat16),
            jax.ShapeDtypeStruct((share_rows, width), jnp.float32),
        ],
        in_specs=[VMEM] * 5,
        out_specs=[VMEM] * 2,
        scratch_shapes=[pltpu.VMEM((token_count, LANES), jnp.float32)],
        compiler_params=pltpu.CompilerParams(vmem_limit_bytes=8 * 1024 * 1024),
        name="pack_rows",
    )(kept, far, norm_post_gain[None, :], expert_ids.T, route_weights.T)
    gate_up = [w.transpose(0, 2, 1).reshape(-1, width) for w in (gate_weight, up_weight)]
    weights = (*gate_up, down_weight.reshape(-1, width))
    line_0 = rows[None]
    z_1, z_2 = flip(line_0, "req", 2), flip(line_0, "req", 4)
    y_0, x_0 = flip(line_0, "tp", 2), flip(line_0, "req", 1)
    line_12, z_2, y_0, x_0 = ordered(jnp.concatenate([z_1, z_2]), z_2, y_0, x_0)
    line_3, across_0, core_0, y_core_0 = ordered(
        jnp.concatenate([line_12, flip(z_2, "req", 2)]),
        across_parts(x_0, y_0),
        flip(line_0, "tp", 1),
        flip(y_0, "tp", 1),
    )
    y_3, x_3 = flip(line_3, "tp", 2), flip(line_3, "req", 1)
    x_core_0, across_core_0, core_3, y_3, x_3 = ordered(
        flip(x_0, "tp", 1), other_core(across_0), flip(line_3, "tp", 1), y_3, x_3
    )
    all_0 = run_experts(
        near_pieces(0, line_0, core_0)
        + far_pieces(0, (y_0,), (y_core_0,))
        + near_pieces(1, x_0, x_core_0)
        + far_pieces(1, across_0, across_core_0),
        weights,
        token_count,
        residual,
    )
    x_core_3, all_0, y_3, across_3 = ordered(
        flip(x_3, "tp", 1), all_0, y_3, jnp.concatenate(across_parts(x_3, y_3), axis=1)
    )
    side_3 = run_experts(
        near_pieces(0, x_3, x_core_3) + far_pieces(0, (across_3,), (flip(across_3, "tp", 1),)),
        weights,
        token_count,
    )
    y_core_3, all_0, (keep, (send, first)) = ordered(flip(y_3, "tp", 1), all_0, side_3)
    all_0, y_core_3, keep, send, first = ordered(all_0, y_core_3, keep, send, flip(first, "tp", 1))
    diagonal, keep, send = ordered(joined((keep, (send, first)), 0, 1).astype(jnp.bfloat16), keep, send)
    by_x, by_y = relayed(diagonal)
    near_keep, (near_send, near_first) = run_experts(
        near_pieces(0, line_3, core_3) + far_pieces(0, (y_3,), (y_core_3,)), weights, token_count
    )
    send = flip(send, "tp", 1)
    all_0, near_keep, near_send, near_first, by_x, to_x = ordered(
        all_0,
        near_keep,
        near_send,
        flip(near_first, "tp", 1),
        by_x.astype(jnp.float32),
        with_upper(joined((keep, (send, first)), 0, 0), by_y),
    )
    to_y = with_lower(joined((near_keep, (near_send, near_first)), 0, 1), by_x)
    sums_3 = flip(to_x, "req", 1), flip(to_y, "tp", 2)
    all_0, near_send, sums_3 = ordered(with_core(all_0), flip(near_send, "tp", 1), sums_3)
    near_3 = (near_keep, (near_send, near_first))
    sent = joined(near_3, 0, 0) + sums_3[0].astype(jnp.float32) + sums_3[1].astype(jnp.float32)
    sent_3, relay_0 = ordered(
        flip(sent[2].astype(jnp.bfloat16), "req", 2), relayed(joined(all_0, 1, 1))
    )
    sent_2, relay_0 = ordered(
        (sent[1] + sent_3.astype(jnp.float32)).astype(jnp.bfloat16), relay_0
    )
    from_z = [flip(sent[0].astype(jnp.bfloat16), "req", 2), flip(sent_2, "req", 4)]
    sums_0 = neighbours(joined(all_0, 1, 0), joined(all_0, 0, 1), *relay_0)
    return pl.pallas_call(
        finish_kernel,
        out_shape=jax.ShapeDtypeStruct((token_count, share_width), jnp.bfloat16),
        in_specs=[VMEM] * 5,
        out_specs=VMEM,
        compiler_params=pltpu.CompilerParams(vmem_limit_bytes=8 * 1024 * 1024),
        name="finish",
    )(joined(all_0, 0, 0), *from_z, *sums_0)


def moe_routed(
    x_full,
    head_part,
    norm_post_gain,
    expert_ids,
    route_weights,
    gate_weight,
    up_weight,
    down_weight,
):
    req_count = lax.axis_size("req")
    tp_index = lax.axis_index("tp")
    x_float = x_full.astype(jnp.float32)
    token_count = x_float.shape[0]
    share_width = x_float.shape[1] // lax.axis_size("tp")
    top_count = expert_ids.shape[1]
    expert_count = gate_weight.shape[0] * req_count
    capacity = max(2, 3 * token_count * top_count // (2 * expert_count))
    flat_expert = expert_ids.reshape(token_count * top_count)
    one_hot = (flat_expert[:, None] == jnp.arange(expert_count, dtype=jnp.int32)[None, :]).astype(
        jnp.int32
    )
    slot_rank = jnp.sum((jnp.cumsum(one_hot, axis=0) - one_hot) * one_hot, axis=1)
    slot_index = flat_expert * capacity + slot_rank
    head_sum = lax.psum(head_part.astype(jnp.bfloat16), "tp").astype(jnp.float32)
    residual_full = x_float + head_sum
    normed_post = rms_scale(residual_full, norm_post_gain).astype(jnp.bfloat16)
    residual = lax.dynamic_slice_in_dim(residual_full, tp_index * share_width, share_width, 1)
    send_buffer = build_buffer(normed_post, slot_index, top_count, expert_count, capacity)
    part_sums = expert_apply(
        lax.all_to_all(send_buffer, "req", split_axis=0, concat_axis=0, tiled=True),
        gate_weight,
        up_weight,
        down_weight,
    )
    returned = lax.all_to_all(part_sums, "req", split_axis=0, concat_axis=0, tiled=True)
    moe_term = weigh_back(returned, slot_index, route_weights, token_count, top_count)
    moe_share = lax.psum_scatter(
        moe_term.astype(jnp.bfloat16), "tp", scatter_dimension=1, tiled=True
    ).astype(jnp.float32)
    return (residual + moe_share).astype(jnp.bfloat16)


def attention_part(
    x_full,
    norm_in_gain,
    q_weight,
    k_weight,
    v_weight,
    q_gain,
    k_gain,
    o_weight,
    key_pages,
    value_pages,
    page_table,
    cache_len,
):
    head_dim = q_gain.shape[0]
    kv_local = key_pages.shape[0]
    group_size = q_weight.shape[1] // head_dim // kv_local
    token_count = x_full.shape[0]
    x_float = x_full.astype(jnp.float32)
    normed_in = rms_scale(x_float, norm_in_gain).astype(jnp.bfloat16)
    query_lin = jnp.dot(normed_in, q_weight, preferred_element_type=jnp.float32).reshape(
        token_count, kv_local * group_size, head_dim
    )
    key_lin = jnp.dot(normed_in, k_weight, preferred_element_type=jnp.float32).reshape(
        token_count, kv_local, head_dim
    )
    values_new = (
        jnp.dot(normed_in, v_weight, preferred_element_type=jnp.float32)
        .astype(jnp.bfloat16)
        .reshape(token_count, kv_local, head_dim)
    )
    requests, positions = token_layout(cache_len)
    queries = (
        rotate(rms_scale(query_lin, q_gain), positions)
        .astype(jnp.bfloat16)
        .reshape(token_count, kv_local, group_size, head_dim)
    )
    keys_new = rotate(rms_scale(key_lin, k_gain), positions).astype(jnp.bfloat16)
    slot_owner = page_slots(page_table, cache_len)
    cache_slots = key_pages.shape[1] * key_pages.shape[2]
    keys_cache = key_pages.reshape(kv_local, cache_slots, head_dim)
    values_cache = value_pages.reshape(kv_local, cache_slots, head_dim)
    attended = attend(
        queries, keys_new, values_new, keys_cache, values_cache, requests, positions, slot_owner
    )
    return jnp.dot(attended, o_weight, preferred_element_type=jnp.float32)


def body(
    hidden_in,
    norm_in_gain,
    q_weight,
    k_weight,
    v_weight,
    q_gain,
    k_gain,
    o_weight,
    key_pages,
    value_pages,
    page_table,
    cache_len,
    norm_post_gain,
    expert_ids,
    route_weights,
    gate_weight,
    up_weight,
    down_weight,
):
    req_count = lax.axis_size("req")
    attention = (
        norm_in_gain,
        q_weight,
        k_weight,
        v_weight,
        q_gain,
        k_gain,
        o_weight,
        key_pages,
        value_pages,
        page_table,
        cache_len,
    )
    experts = (norm_post_gain, expert_ids, route_weights, gate_weight, up_weight, down_weight)
    expert_count = gate_weight.shape[0] * req_count
    staged = (req_count, lax.axis_size("tp"), gate_weight.shape[0]) == (8, 4, 2)
    if staged and expert_count <= LANES // 2:
        return moe_dense(*attention_shares(hidden_in, *attention), *experts)
    x_full = lax.all_gather(hidden_in, "tp", axis=1, tiled=True)
    return moe_routed(x_full, attention_part(x_full, *attention), *experts)


def solution(mesh):
    return jax.shard_map(
        body,
        mesh=mesh,
        in_specs=(
            P("req", "tp"),
            P(),
            P(None, "tp"),
            P(None, "tp"),
            P(None, "tp"),
            P(),
            P(),
            P("tp", None),
            P("tp", "req", None, None),
            P("tp", "req", None, None),
            P("req", None),
            P("req"),
            P(),
            P("req", None),
            P("req", None),
            P("req", None, "tp"),
            P("req", None, "tp"),
            P("req", "tp", None),
        ),
        out_specs=P("req", "tp"),
        check_vma=False,
    )
```

```python
import functools
import math

import jax
import jax.numpy as jnp
import numpy as np
from jax import lax
from jax.experimental import pallas as pl
from jax.experimental.pallas import tpu as pltpu
from jax.sharding import PartitionSpec as P

PAGE = 128
MAXPG = 32
PRE = 120
TOK_DEV = 128
REQS_DEV = 9
POOL = 48
SHORT_PG = 2
SHORT_LIST = (REQS_DEV - 1) * SHORT_PG


NORM_EPS = 1e-06
ROPE_BASE = 1000000.0


def rms_scale(values, gain_vec):
    mean_square = jnp.mean(values * values, axis=-1, keepdims=True)
    return values * lax.rsqrt(mean_square + NORM_EPS) * gain_vec


def rotate(values, positions):
    half_dim = values.shape[-1] // 2
    exponent = jnp.arange(half_dim, dtype=jnp.float32) * (2.0 / values.shape[-1])
    frequency = jnp.power(jnp.float32(ROPE_BASE), -exponent)
    angles = positions.astype(jnp.float32)[:, None] * frequency[None, :]
    cosine = jnp.cos(angles)[:, None, :]
    sine_val = jnp.sin(angles)[:, None, :]
    front_half = values[..., :half_dim]
    back_half = values[..., half_dim:]
    return jnp.concatenate(
        [front_half * cosine - back_half * sine_val, back_half * cosine + front_half * sine_val],
        axis=-1,
    )


def token_layout(lengths):
    local_idx = jnp.arange(TOK_DEV, dtype=jnp.int32)
    requests = jnp.where(local_idx < PRE, 0, local_idx - PRE + 1)
    offsets = jnp.where(local_idx < PRE, local_idx, 0)
    request_hot = (requests[:, None] == jnp.arange(REQS_DEV, dtype=jnp.int32)[None, :]).astype(
        jnp.int32
    )
    positions = jnp.sum(request_hot * lengths[None, :], axis=1) + offsets
    return (requests, positions)


def page_slots(table, lengths):
    pages_used = (lengths + PAGE - 1) // PAGE
    entry_live = jnp.arange(MAXPG, dtype=jnp.int32)[None, :] < pages_used[:, None]
    page_match = (
        (table[:, :, None] == jnp.arange(POOL, dtype=jnp.int32)[None, None, :])
        & entry_live[:, :, None]
    ).astype(jnp.int32)
    page_owner = jnp.sum(
        page_match * jnp.arange(REQS_DEV, dtype=jnp.int32)[:, None, None], axis=(0, 1)
    )
    page_start = jnp.sum(
        page_match * (jnp.arange(MAXPG, dtype=jnp.int32) * PAGE)[None, :, None], axis=(0, 1)
    )
    page_used = jnp.sum(page_match, axis=(0, 1)) > 0
    owner_length = jnp.sum(page_match * lengths[:, None, None], axis=(0, 1))
    slot_pos = page_start[:, None] + jnp.arange(PAGE, dtype=jnp.int32)[None, :]
    slot_live = page_used[:, None] & (slot_pos < owner_length[:, None])
    slot_owner = jnp.where(slot_live, page_owner[:, None], -1)
    return slot_owner.reshape(POOL * PAGE)


def attend(
    queries, keys_new, values_new, keys_cache, values_cache, requests, positions, slot_owner
):
    inv_root = 1.0 / math.sqrt(queries.shape[-1])
    cache_mask = slot_owner[None, :] == requests[:, None]
    new_mask = (requests[None, :] == requests[:, None]) & (positions[None, :] <= positions[:, None])
    score_cache = (
        jnp.einsum("tkgh,knh->kgtn", queries, keys_cache, preferred_element_type=jnp.float32)
        * inv_root
    )
    score_new = (
        jnp.einsum("tkgh,skh->kgts", queries, keys_new, preferred_element_type=jnp.float32)
        * inv_root
    )
    score_cache = jnp.where(cache_mask[None, None], score_cache, -1e30)
    score_new = jnp.where(new_mask[None, None], score_new, -1e30)
    row_max = jnp.maximum(
        jnp.max(score_cache, axis=-1, keepdims=True), jnp.max(score_new, axis=-1, keepdims=True)
    )
    exp_cache = jnp.where(cache_mask[None, None], jnp.exp(score_cache - row_max), 0.0)
    exp_new = jnp.where(new_mask[None, None], jnp.exp(score_new - row_max), 0.0)
    total = jnp.sum(exp_cache, axis=-1, keepdims=True) + jnp.sum(exp_new, axis=-1, keepdims=True)
    prob_cache = (exp_cache / total).astype(jnp.bfloat16)
    prob_new = (exp_new / total).astype(jnp.bfloat16)
    mixed = jnp.einsum(
        "kgtn,knh->tkgh", prob_cache, values_cache, preferred_element_type=jnp.float32
    )
    mixed = mixed + jnp.einsum(
        "kgts,skh->tkgh", prob_new, values_new, preferred_element_type=jnp.float32
    )
    return mixed.astype(jnp.bfloat16).reshape(queries.shape[0], -1)


def expert_apply(blocks, gate_weight, up_weight, down_weight):
    local_experts = gate_weight.shape[0]
    sources = blocks.shape[0] // local_experts
    slot_count = blocks.shape[1]
    grouped = blocks.reshape(sources, local_experts, slot_count, blocks.shape[2])
    gate_acts = jnp.einsum(
        "sekd,edf->sekf", grouped, gate_weight, preferred_element_type=jnp.float32
    )
    up_acts = jnp.einsum("sekd,edf->sekf", grouped, up_weight, preferred_element_type=jnp.float32)
    hidden_act = (jax.nn.silu(gate_acts) * up_acts).astype(jnp.bfloat16)
    part_sums = jnp.einsum(
        "sekf,efd->sekd", hidden_act, down_weight, preferred_element_type=jnp.float32
    ).astype(jnp.bfloat16)
    return part_sums.reshape(sources * local_experts, slot_count, part_sums.shape[3])


def build_buffer(normed, slot_index, top_count, expert_count, capacity):
    picked = jnp.repeat(normed, top_count, axis=0)
    buffer_rows = (
        jnp.zeros((expert_count * capacity, normed.shape[1]), normed.dtype)
        .at[slot_index]
        .set(picked)
    )
    return buffer_rows.reshape(expert_count, capacity, normed.shape[1])


def weigh_back(returned, slot_index, route_weights, token_count, top_count):
    row_width = returned.shape[2]
    back_rows = returned.reshape(returned.shape[0] * returned.shape[1], row_width)[slot_index]
    weighted = (
        back_rows.astype(jnp.float32) * route_weights.reshape(token_count * top_count)[:, None]
    )
    return jnp.sum(weighted.reshape(token_count, top_count, row_width), axis=1)


LANES = 128
VMEM = pl.BlockSpec(memory_space=pltpu.VMEM)
SMEM = pl.BlockSpec(memory_space=pltpu.SMEM)
VMEM_LIMIT = 24 * 1024 * 1024


def flip(value, axis, bits):
    return lax.ppermute(value, axis, [(i, i ^ bits) for i in range(lax.axis_size(axis))])


def stage_kernel(*refs):
    length_hbm, table_hbm, frequency_hbm, *large = refs[:10]
    cosine_ref, sine_ref, owner_ref, *staged = refs[10:20]
    list_ref, length_out, table_out = refs[20:23]
    frequency_ref, owners, sems = refs[23:]
    length_ref, table_ref = length_out, table_out
    sources = (length_hbm, table_hbm, frequency_hbm, *large)
    targets = (length_out, table_out, frequency_ref, *staged)
    copies = [
        pltpu.make_async_copy(source, target, sems.at[i])
        for i, (source, target) in enumerate(zip(sources, targets))
    ]
    for copy in copies:
        copy.start()
    for copy in copies[:3]:
        copy.wait()
    tokens, head_dim = cosine_ref.shape
    for entry in range(POOL):
        list_ref[entry] = 0
        owners[0, entry] = -1
        owners[1, entry] = 0
    prefill_long = length_ref[0] > SHORT_PG * PAGE
    count = jnp.int32(0)
    for request in range(1, REQS_DEV):

        def name_page(entry, count):
            page = table_ref[request, entry]
            place = jnp.where(prefill_long, count, page)
            list_ref[place] = page
            owners[0, place] = request
            owners[1, place] = jnp.minimum(length_ref[request] - entry * PAGE, PAGE)
            return count + 1

        count = lax.fori_loop(0, (length_ref[request] + PAGE - 1) // PAGE, name_page, count)
    slot = lax.broadcasted_iota(jnp.int32, (1, PAGE), 1)
    for entry in range(POOL):
        owner_ref[:, entry * PAGE : (entry + 1) * PAGE] = jnp.where(
            slot < owners[1, entry], owners[0, entry], -1
        )
    token = lax.broadcasted_iota(jnp.int32, (tokens, head_dim), 0)
    lane = lax.broadcasted_iota(jnp.int32, (tokens, head_dim), 1)
    position = length_ref[0] + token
    for i in range(tokens - PRE):
        position = jnp.where(token == PRE + i, length_ref[i + 1], position)
    angle = position.astype(jnp.float32) * frequency_ref[...]
    sine = jnp.sin(angle)
    cosine_ref[...] = jnp.cos(angle)
    sine_ref[...] = jnp.where(lane < head_dim // 2, -sine, sine)
    for copy in copies[3:]:
        copy.wait()


def attention_kernel(*refs):
    pieces, (keep_out, far_out, core_out) = refs[:4], refs[19:22]
    (cosine_ref, sine_ref, owner_ref, gain_ref, q_gain_ref, k_gain_ref) = refs[4:10]
    (q_ref, k_ref, v_ref, key_ref, list_ref, length_ref, table_ref) = refs[10:17]
    (
        x_ref, query_ref, own_scores, scores_ref, mix_ref, mixed_ref, part_ref, slots_ref, decoded_ref,
        value_ref, o_ref, sems,
    ) = refs[22:]
    value_copy, o_copy = (
        pltpu.make_async_copy(source, target, sems.at[i])
        for i, (source, target) in enumerate(zip(refs[17:19], (value_ref, o_ref)))
    )
    value_copy.start()
    o_copy.start()
    tokens, head_dim = x_ref.shape[0], k_gain_ref.shape[1]
    tp_index = lax.axis_index("tp")
    heads = q_ref.shape[1] // head_dim
    decodes = tokens - PRE
    for step, piece in enumerate(pieces):
        width = piece.shape[1]
        start = pl.multiple_of((tp_index ^ step) * width, width)
        x_ref[:, pl.ds(start, width)] = piece[...]
    token = lax.broadcasted_iota(jnp.int32, (tokens, head_dim), 0)
    lane = lax.broadcasted_iota(jnp.int32, (tokens, head_dim), 1)

    def turned(values, gain):
        values = rms_scale(values, gain)
        return values * cosine_ref[...] + pltpu.roll(values, head_dim // 2, 1) * sine_ref[...]

    def with_ones(values):
        return jnp.concatenate([values, jnp.ones_like(values)], axis=1)

    normed = rms_scale(x_ref[...].astype(jnp.float32), gain_ref[...]).astype(jnp.bfloat16)
    contract = (((1,), (1,)), ((), ()))
    key_lin = jnp.dot(normed, k_ref[...], preferred_element_type=jnp.float32)
    values_new = jnp.dot(normed, v_ref[...], preferred_element_type=jnp.float32).astype(jnp.bfloat16)
    query_lin = jnp.dot(normed, q_ref[...], preferred_element_type=jnp.float32)
    keys_new = turned(key_lin, k_gain_ref[...]).astype(jnp.bfloat16)
    values_new = with_ones(values_new)
    to_log2 = math.log2(math.e) / math.sqrt(head_dim)
    own_mask = (lane == token) | ((lane < token) & (token < PRE))
    decode_query, decode_own = [], []
    for head in range(heads):
        span = slice(head * tokens, (head + 1) * tokens)
        query = turned(query_lin[:, head * head_dim : (head + 1) * head_dim], q_gain_ref[...]) * to_log2
        rounded = query.astype(jnp.bfloat16)
        query_ref[span, :] = rounded
        scores = lax.dot_general(rounded, keys_new, contract, preferred_element_type=jnp.float32)
        scores = jnp.where(own_mask, scores, -1e30)
        own_scores[span, :] = scores
        decode_query.append(query[PRE:])
        decode_own.append(scores[PRE:])
    decode_query = jnp.concatenate(decode_query, axis=0).astype(jnp.bfloat16)
    decode_own = jnp.concatenate(decode_own, axis=0)

    def raised(top, scores):
        for start in range(0, scores.shape[1], head_dim):
            top = jnp.maximum(top, scores[:, start : start + head_dim])
        return top

    def weigh(own, score_steps, value_steps, scores_ref):
        top = own
        for step, score_step in enumerate(score_steps):
            scores = score_step()
            scores_ref[step, :, : scores.shape[1]] = scores
            top = raised(top, scores)
        top = jnp.max(top, axis=1, keepdims=True)
        mix = jnp.dot(
            jnp.exp2(own - top).astype(jnp.bfloat16), values_new, preferred_element_type=jnp.float32
        )
        for step, value_step in enumerate(value_steps):
            values = value_step()
            weights = jnp.exp2(scores_ref[step, :, : values.shape[0]] - top).astype(jnp.bfloat16)
            mix = mix + jnp.dot(weights, with_ones(values), preferred_element_type=jnp.float32)
        return mix

    def taken(ref, names):
        return jnp.concatenate([ref[name] for name in names], axis=0)

    def against(queries, keys):
        return lax.dot_general(queries, keys, contract, preferred_element_type=jnp.float32)

    def prefill(names, live):
        def score(pages):
            scores = against(query_ref[...], taken(key_ref, pages))
            return scores if live is None else jnp.where(live, scores, -1e30)

        mix_ref[...] = weigh(
            own_scores[...],
            [functools.partial(score, pages) for pages in names],
            [functools.partial(taken, value_ref, pages) for pages in names],
            scores_ref,
        )

    def decode(steps, pages_of):
        row_request = 1 + lax.broadcasted_iota(jnp.int32, (heads * decodes, 1), 0) % decodes
        width = slots_ref.shape[2]

        def score(step):
            scores = against(decode_query, pages_of(key_ref, step))
            owner = owner_ref[:, step * width : (step + 1) * width]
            return jnp.where(owner == row_request, scores, -1e30)

        mix = weigh(
            decode_own,
            [functools.partial(score, step) for step in range(steps)],
            [functools.partial(pages_of, value_ref, step) for step in range(steps)],
            slots_ref,
        )
        decoded_ref[...] = mix[:, :head_dim] / mix[:, head_dim:]

    value_copy.wait()
    length = length_ref[0]
    listed = slots_ref.shape[2] // PAGE
    pages = scores_ref.shape[2] // PAGE

    @pl.when(length > SHORT_PG * PAGE)
    def _():
        names = [table_ref[0, entry] for entry in range(MAXPG)]
        prefill([names[first : first + pages] for first in range(0, MAXPG, pages)], None)
        decode(
            SHORT_LIST // listed,
            lambda ref, step: taken(ref, [list_ref[step * listed + i] for i in range(listed)]),
        )

    @pl.when(length <= SHORT_PG * PAGE)
    def _():
        column = lax.broadcasted_iota(jnp.int32, (1, SHORT_PG * PAGE), 1)
        prefill([[table_ref[0, entry] for entry in range(SHORT_PG)]], column < length)
        decode(
            POOL // listed,
            lambda ref, step: ref[step * listed : (step + 1) * listed].reshape(-1, head_dim),
        )

    for head in range(heads):
        part = mix_ref[head * tokens : (head + 1) * tokens, :]
        columns = slice(head * head_dim, (head + 1) * head_dim)
        mixed_ref[:, columns] = part[:, :head_dim] / part[:, head_dim:]
        mixed_ref[PRE:, columns] = decoded_ref[head * decodes : (head + 1) * decodes]
    o_copy.wait()
    part_ref[...] = jnp.dot(
        mixed_ref[...].astype(jnp.bfloat16), o_ref[...], preferred_element_type=jnp.float32
    )
    share_rows = keep_out.shape[0]

    def quarter(step):
        return pl.ds(pl.multiple_of((tp_index ^ step) * share_rows, share_rows), share_rows)

    keep_out[...] = part_ref[quarter(0), :] + x_ref[quarter(0), :].astype(jnp.float32)
    far_out[...] = part_ref[quarter(2), :]
    core_out[0] = part_ref[quarter(1), :].astype(jnp.bfloat16)
    core_out[1] = part_ref[quarter(3), :].astype(jnp.bfloat16)


def attention_shares(
    hidden_in, norm_in_gain, q_weight, k_weight, v_weight, q_gain, k_gain, o_weight,
    key_pages, value_pages, page_table, cache_len,
):
    tokens, width = hidden_in.shape[0], 4 * hidden_in.shape[1]
    head_dim = q_gain.shape[0]
    rows = q_weight.shape[1] // head_dim * tokens
    decode_rows = rows // tokens * (tokens - PRE)
    half = ROPE_BASE ** (-np.arange(head_dim // 2) / (head_dim // 2))
    frequency = jnp.asarray(np.concatenate([half, half])[None, :], jnp.float32)
    large = (
        norm_in_gain[None, :], q_gain[None, :], k_gain[None, :], q_weight, k_weight, v_weight,
        key_pages[0],
    )
    scalars = (cache_len, page_table)
    later = (value_pages[0], o_weight)
    sources = [
        pltpu.with_memory_space_constraint(array, pltpu.HBM)
        for array in (*scalars, frequency, *large, *later)
    ]
    rope = pltpu.VMEM((tokens, head_dim), jnp.float32)
    *staged, page_list, lengths, table = pl.pallas_call(
        stage_kernel,
        out_shape=[rope, rope, pltpu.VMEM((1, POOL * PAGE), jnp.int32)]
        + [pltpu.VMEM(array.shape, array.dtype) for array in large]
        + [jax.ShapeDtypeStruct((POOL,), jnp.int32)]
        + [jax.ShapeDtypeStruct(array.shape, array.dtype) for array in scalars],
        in_specs=[pl.BlockSpec(memory_space=pltpu.HBM)] * 10,
        out_specs=[VMEM] * 10 + [SMEM] * 3,
        scratch_shapes=[
            pltpu.VMEM(frequency.shape, frequency.dtype),
            pltpu.SMEM((2, POOL), jnp.int32),
            pltpu.SemaphoreType.DMA((10,)),
        ],
        compiler_params=pltpu.CompilerParams(vmem_limit_bytes=4 * 1024 * 1024),
        name="stage",
    )(*sources[:10])
    far, *staged = ordered(flip(hidden_in, "tp", 2), *staged, page_list, lengths, table)
    pieces = (hidden_in, flip(hidden_in, "tp", 1), far, flip(far, "tp", 1))
    share = (tokens // 4, width)
    score_pages, list_pages = 4, 8
    return pl.pallas_call(
        attention_kernel,
        out_shape=[
            jax.ShapeDtypeStruct(share, jnp.float32),
            jax.ShapeDtypeStruct(share, jnp.float32),
            jax.ShapeDtypeStruct((2, *share), jnp.bfloat16),
        ],
        in_specs=[VMEM] * 14 + [SMEM] * 3 + [pl.BlockSpec(memory_space=pltpu.HBM)] * 2,
        out_specs=[VMEM] * 3,
        scratch_shapes=[
            pltpu.VMEM((tokens, width), jnp.bfloat16),
            pltpu.VMEM((rows, head_dim), jnp.bfloat16),
            pltpu.VMEM((rows, tokens), jnp.float32),
            pltpu.VMEM((MAXPG // score_pages, rows, score_pages * PAGE), jnp.float32),
            pltpu.VMEM((rows, 2 * head_dim), jnp.float32),
            pltpu.VMEM((tokens, q_weight.shape[1]), jnp.float32),
            pltpu.VMEM((tokens, width), jnp.float32),
            pltpu.VMEM((POOL // list_pages, decode_rows, list_pages * PAGE), jnp.float32),
            pltpu.VMEM((decode_rows, head_dim), jnp.float32),
            *(pltpu.VMEM(array.shape, array.dtype) for array in later),
            pltpu.SemaphoreType.DMA((2,)),
        ],
        compiler_params=pltpu.CompilerParams(vmem_limit_bytes=28 * 1024 * 1024),
        name="attention",
    )(*pieces, *staged, *sources[10:])


def pack_kernel(
    own_ref, far_ref, gain_ref, ids_ref, routes_ref,
    rows_ref, residual_ref, spread_ref,
):
    tp_index = lax.axis_index("tp")
    share_rows, width = own_ref.shape
    mine = pl.ds(pl.multiple_of(tp_index * share_rows, share_rows), share_rows)
    residual = own_ref[...] + far_ref[...].astype(jnp.float32)
    residual_ref[...] = residual
    rows_ref[:, :width] = rms_scale(residual, gain_ref[...]).astype(jnp.bfloat16)
    expert = lax.broadcasted_iota(jnp.int32, (LANES, spread_ref.shape[0]), 0) % (LANES // 2)
    spread = jnp.zeros(expert.shape, jnp.float32)
    for k in range(ids_ref.shape[0]):
        spread = spread + jnp.where(expert == ids_ref[k : k + 1, :], routes_ref[k : k + 1, :], 0.0)
    spread_ref[...] = spread.T
    spread = spread_ref[mine, :]
    lane = lax.broadcasted_iota(jnp.int32, spread.shape, 1)
    high = spread.astype(jnp.bfloat16).astype(jnp.float32)
    rows_ref[:, width:] = jnp.where(lane < LANES // 2, high, spread - high).astype(jnp.bfloat16)


def experts_kernel(plan, residuals, *refs):
    pieces, residual_refs = refs[: len(plan)], refs[len(plan) : len(plan) + residuals]
    gate_ref, up_ref, down_ref, keep_ref, *send_refs, rows_ref, sums_ref = refs[len(plan) + residuals :]
    req_index, tp_index = lax.axis_index("req"), lax.axis_index("tp")
    columns, _, levels, group_rows, share_width = keep_ref.shape
    width = gate_ref.shape[1]
    units = gate_ref.shape[0] // 2
    for (column, step, first), piece in zip(plan, pieces):
        count = piece.shape[1]
        for level in range(levels):
            start = (column * levels + level) * group_rows + first
            start = start + (tp_index ^ step) * (group_rows // 4)
            rows_ref[pl.ds(pl.multiple_of(start, count), count), :] = piece[level]
    spread = rows_ref[:, width:].astype(jnp.float32)
    lane = lax.broadcasted_iota(jnp.int32, spread.shape, 1) % (LANES // 2)
    weights = [
        jnp.sum(jnp.where(lane == 2 * req_index + e, spread, 0.0), axis=1, keepdims=True)
        for e in range(2)
    ]
    contract = (((1,), (1,)), ((), ()))
    rows = rows_ref[:, :width]
    gate = lax.dot_general(rows, gate_ref[...], contract, preferred_element_type=jnp.float32)
    up = lax.dot_general(rows, up_ref[...], contract, preferred_element_type=jnp.float32)
    unit = lax.broadcasted_iota(jnp.int32, gate.shape, 1)
    weight = jnp.where(unit < units, weights[0], weights[1])
    acts = (gate / (1.0 + jnp.exp(-gate)) * up * weight).astype(jnp.bfloat16)
    for step in range(4):
        start = pl.multiple_of((tp_index ^ step) * share_width, share_width)
        part = jnp.dot(
            acts, down_ref[:, pl.ds(start, share_width)], preferred_element_type=jnp.float32
        )
        for residual_ref in residual_refs:
            count = residual_ref.shape[0]
            mine = pl.ds(pl.multiple_of(tp_index * count, count), count)
            sums_ref[...] = part
            sums_ref[mine, :] += residual_ref[:, pl.ds(start, share_width)]
            part = sums_ref[...]
        part = part.reshape(columns, levels, group_rows, share_width)
        if step % 2:
            send_refs[step // 2][...] = part.astype(jnp.bfloat16)
            continue
        for column in range(columns):
            keep_ref[column, step // 2] = part[column]


def run_experts(pieces, weights, group_rows, *residual):
    plan = tuple(place for place, _ in pieces)
    pieces = [piece for _, piece in pieces]
    columns, levels, packed = 1 + max(place[0] for place in plan), *pieces[0].shape[::2]
    rows, share_width = columns * levels * group_rows, weights[2].shape[1] // 4
    sums = (levels, group_rows, share_width)
    keep, *send = pl.pallas_call(
        functools.partial(experts_kernel, plan, len(residual)),
        out_shape=[jax.ShapeDtypeStruct((columns, 2, *sums), jnp.float32)]
        + [jax.ShapeDtypeStruct((columns, *sums), jnp.bfloat16)] * 2,
        in_specs=[VMEM] * (len(pieces) + len(residual) + 3),
        out_specs=[VMEM] * 3,
        scratch_shapes=[
            pltpu.VMEM((rows, packed), jnp.bfloat16),
            pltpu.VMEM((rows, share_width), jnp.float32),
        ],
        compiler_params=pltpu.CompilerParams(vmem_limit_bytes=VMEM_LIMIT),
        name="experts",
    )(*pieces, *residual, *weights)
    return keep, send


def ordered(*values):
    return lax.optimization_barrier(values)


def across_parts(line_x, line_y):
    half = line_x.shape[1] // 2
    return flip(line_x[:, :half], "tp", 2), flip(line_y[:, half:], "req", 1)


def other_core(parts):
    return tuple(flip(part, "tp", 1) for part in parts)


def with_core(pair):
    return pair[0], list(other_core(pair[1]))


def joined(pair, column, y):
    return pair[0][column, y] + pair[1][y][column].astype(jnp.float32)


def near_pieces(column, line, core):
    return [((column, 0, 0), line), ((column, 1, 0), core)]


def far_pieces(column, parts, cores):
    half = parts[0].shape[1]
    if len(parts) == 1:
        return [((column, 2, 0), parts[0]), ((column, 3, 0), cores[0])]
    return [((column, 2, i * half), part) for i, part in enumerate(parts)] + [
        ((column, 3, i * half), part) for i, part in enumerate(cores)
    ]


def relayed(side):
    part = side.astype(jnp.bfloat16)
    half = part.shape[1] // 2
    return flip(part[:, :half], "req", 1), flip(part[:, half:], "tp", 2)


def with_lower(sums, part):
    half = part.shape[1]
    sums = [sums[:, :half] + part.astype(jnp.float32), sums[:, half:]]
    return jnp.concatenate(sums, axis=1).astype(jnp.bfloat16)


def with_upper(sums, part):
    half = part.shape[1]
    sums = [sums[:, :half], sums[:, half:] + part.astype(jnp.float32)]
    return jnp.concatenate(sums, axis=1).astype(jnp.bfloat16)


def neighbours(to_x, to_y, by_x, by_y):
    return flip(with_upper(to_x, by_y), "req", 1), flip(with_lower(to_y, by_x), "tp", 2)


def moe_dense(
    kept,
    far,
    core,
    norm_post_gain,
    expert_ids,
    route_weights,
    gate_weight,
    up_weight,
    down_weight,
):
    share_rows, width = kept.shape
    token_count, share_width = 4 * share_rows, width // 4
    core = flip(core, "tp", 1)
    far, kept, core = ordered((far + core[1].astype(jnp.float32)).astype(jnp.bfloat16), kept, core)
    kept, far = ordered(kept + core[0].astype(jnp.float32), flip(far, "tp", 2))
    rows, residual = pl.pallas_call(
        pack_kernel,
        out_shape=[
            jax.ShapeDtypeStruct((share_rows, width + LANES), jnp.bfloat16),
            jax.ShapeDtypeStruct((share_rows, width), jnp.float32),
        ],
        in_specs=[VMEM] * 5,
        out_specs=[VMEM] * 2,
        scratch_shapes=[pltpu.VMEM((token_count, LANES), jnp.float32)],
        compiler_params=pltpu.CompilerParams(vmem_limit_bytes=8 * 1024 * 1024),
        name="pack_rows",
    )(kept, far, norm_post_gain[None, :], expert_ids.T, route_weights.T)
    gate_up = [w.transpose(0, 2, 1).reshape(-1, width) for w in (gate_weight, up_weight)]
    weights = (*gate_up, down_weight.reshape(-1, width))
    line_0 = rows[None]
    z_1, z_2 = flip(line_0, "req", 2), flip(line_0, "req", 4)
    y_0, x_0 = flip(line_0, "tp", 2), flip(line_0, "req", 1)
    line_12, z_2, y_0, x_0 = ordered(jnp.concatenate([z_1, z_2]), z_2, y_0, x_0)
    line_3, across_0, core_0, y_core_0 = ordered(
        jnp.concatenate([line_12, flip(z_2, "req", 2)]),
        across_parts(x_0, y_0),
        flip(line_0, "tp", 1),
        flip(y_0, "tp", 1),
    )
    y_3, x_3 = flip(line_3, "tp", 2), flip(line_3, "req", 1)
    x_core_0, across_core_0, core_3, y_3, x_3 = ordered(
        flip(x_0, "tp", 1), other_core(across_0), flip(line_3, "tp", 1), y_3, x_3
    )
    all_0 = run_experts(
        near_pieces(0, line_0, core_0)
        + far_pieces(0, (y_0,), (y_core_0,))
        + near_pieces(1, x_0, x_core_0)
        + far_pieces(1, across_0, across_core_0),
        weights,
        token_count,
        residual,
    )
    x_core_3, all_0, y_3, across_3 = ordered(
        flip(x_3, "tp", 1), all_0, y_3, jnp.concatenate(across_parts(x_3, y_3), axis=1)
    )
    side_3 = run_experts(
        near_pieces(0, x_3, x_core_3) + far_pieces(0, (across_3,), (flip(across_3, "tp", 1),)),
        weights,
        token_count,
    )
    y_core_3, all_0, (keep, (send, first)) = ordered(flip(y_3, "tp", 1), all_0, side_3)
    all_0, y_core_3, keep, send, first = ordered(all_0, y_core_3, keep, send, flip(first, "tp", 1))
    diagonal, keep, send = ordered(joined((keep, (send, first)), 0, 1).astype(jnp.bfloat16), keep, send)
    by_x, by_y = relayed(diagonal)
    near_keep, (near_send, near_first) = run_experts(
        near_pieces(0, line_3, core_3) + far_pieces(0, (y_3,), (y_core_3,)), weights, token_count
    )
    send = flip(send, "tp", 1)
    all_0, near_keep, near_send, near_first, by_x, to_x = ordered(
        all_0,
        near_keep,
        near_send,
        flip(near_first, "tp", 1),
        by_x.astype(jnp.float32),
        with_upper(joined((keep, (send, first)), 0, 0), by_y),
    )
    to_y = with_lower(joined((near_keep, (near_send, near_first)), 0, 1), by_x)
    sums_3 = flip(to_x, "req", 1).astype(jnp.float32) + flip(to_y, "tp", 2).astype(jnp.float32)
    all_0, near_send, sums_3 = ordered(with_core(all_0), flip(near_send, "tp", 1), sums_3)
    sent = joined((near_keep, (near_send, near_first)), 0, 0) + sums_3
    sent_3, relay_0 = ordered(
        flip(sent[2].astype(jnp.bfloat16), "req", 2), relayed(joined(all_0, 1, 1))
    )
    sent_2, relay_0 = ordered(
        (sent[1] + sent_3.astype(jnp.float32)).astype(jnp.bfloat16), relay_0
    )
    from_z = [flip(sent[0].astype(jnp.bfloat16), "req", 2), flip(sent_2, "req", 4)]
    sums_0 = neighbours(joined(all_0, 1, 0), joined(all_0, 0, 1), *relay_0)
    total = joined(all_0, 0, 0) + from_z[0].astype(jnp.float32) + from_z[1].astype(jnp.float32)
    total, from_x, from_y = ordered(total[0], *sums_0)
    return (total + from_x[0].astype(jnp.float32) + from_y[0].astype(jnp.float32)).astype(jnp.bfloat16)


def moe_routed(
    x_full,
    head_part,
    norm_post_gain,
    expert_ids,
    route_weights,
    gate_weight,
    up_weight,
    down_weight,
):
    req_count = lax.axis_size("req")
    tp_index = lax.axis_index("tp")
    x_float = x_full.astype(jnp.float32)
    token_count = x_float.shape[0]
    share_width = x_float.shape[1] // lax.axis_size("tp")
    top_count = expert_ids.shape[1]
    expert_count = gate_weight.shape[0] * req_count
    capacity = max(2, 3 * token_count * top_count // (2 * expert_count))
    flat_expert = expert_ids.reshape(token_count * top_count)
    one_hot = (flat_expert[:, None] == jnp.arange(expert_count, dtype=jnp.int32)[None, :]).astype(
        jnp.int32
    )
    slot_rank = jnp.sum((jnp.cumsum(one_hot, axis=0) - one_hot) * one_hot, axis=1)
    slot_index = flat_expert * capacity + slot_rank
    head_sum = lax.psum(head_part.astype(jnp.bfloat16), "tp").astype(jnp.float32)
    residual_full = x_float + head_sum
    normed_post = rms_scale(residual_full, norm_post_gain).astype(jnp.bfloat16)
    residual = lax.dynamic_slice_in_dim(residual_full, tp_index * share_width, share_width, 1)
    send_buffer = build_buffer(normed_post, slot_index, top_count, expert_count, capacity)
    part_sums = expert_apply(
        lax.all_to_all(send_buffer, "req", split_axis=0, concat_axis=0, tiled=True),
        gate_weight,
        up_weight,
        down_weight,
    )
    returned = lax.all_to_all(part_sums, "req", split_axis=0, concat_axis=0, tiled=True)
    moe_term = weigh_back(returned, slot_index, route_weights, token_count, top_count)
    moe_share = lax.psum_scatter(
        moe_term.astype(jnp.bfloat16), "tp", scatter_dimension=1, tiled=True
    ).astype(jnp.float32)
    return (residual + moe_share).astype(jnp.bfloat16)


def attention_part(
    x_full,
    norm_in_gain,
    q_weight,
    k_weight,
    v_weight,
    q_gain,
    k_gain,
    o_weight,
    key_pages,
    value_pages,
    page_table,
    cache_len,
):
    head_dim = q_gain.shape[0]
    kv_local = key_pages.shape[0]
    group_size = q_weight.shape[1] // head_dim // kv_local
    token_count = x_full.shape[0]
    x_float = x_full.astype(jnp.float32)
    normed_in = rms_scale(x_float, norm_in_gain).astype(jnp.bfloat16)
    query_lin = jnp.dot(normed_in, q_weight, preferred_element_type=jnp.float32).reshape(
        token_count, kv_local * group_size, head_dim
    )
    key_lin = jnp.dot(normed_in, k_weight, preferred_element_type=jnp.float32).reshape(
        token_count, kv_local, head_dim
    )
    values_new = (
        jnp.dot(normed_in, v_weight, preferred_element_type=jnp.float32)
        .astype(jnp.bfloat16)
        .reshape(token_count, kv_local, head_dim)
    )
    requests, positions = token_layout(cache_len)
    queries = (
        rotate(rms_scale(query_lin, q_gain), positions)
        .astype(jnp.bfloat16)
        .reshape(token_count, kv_local, group_size, head_dim)
    )
    keys_new = rotate(rms_scale(key_lin, k_gain), positions).astype(jnp.bfloat16)
    slot_owner = page_slots(page_table, cache_len)
    cache_slots = key_pages.shape[1] * key_pages.shape[2]
    keys_cache = key_pages.reshape(kv_local, cache_slots, head_dim)
    values_cache = value_pages.reshape(kv_local, cache_slots, head_dim)
    attended = attend(
        queries, keys_new, values_new, keys_cache, values_cache, requests, positions, slot_owner
    )
    return jnp.dot(attended, o_weight, preferred_element_type=jnp.float32)


def body(
    hidden_in,
    norm_in_gain,
    q_weight,
    k_weight,
    v_weight,
    q_gain,
    k_gain,
    o_weight,
    key_pages,
    value_pages,
    page_table,
    cache_len,
    norm_post_gain,
    expert_ids,
    route_weights,
    gate_weight,
    up_weight,
    down_weight,
):
    req_count = lax.axis_size("req")
    attention = (
        norm_in_gain,
        q_weight,
        k_weight,
        v_weight,
        q_gain,
        k_gain,
        o_weight,
        key_pages,
        value_pages,
        page_table,
        cache_len,
    )
    experts = (norm_post_gain, expert_ids, route_weights, gate_weight, up_weight, down_weight)
    expert_count = gate_weight.shape[0] * req_count
    staged = (req_count, lax.axis_size("tp"), gate_weight.shape[0]) == (8, 4, 2)
    if staged and expert_count <= LANES // 2:
        return moe_dense(*attention_shares(hidden_in, *attention), *experts)
    x_full = lax.all_gather(hidden_in, "tp", axis=1, tiled=True)
    return moe_routed(x_full, attention_part(x_full, *attention), *experts)


def solution(mesh):
    return jax.shard_map(
        body,
        mesh=mesh,
        in_specs=(
            P("req", "tp"),
            P(),
            P(None, "tp"),
            P(None, "tp"),
            P(None, "tp"),
            P(),
            P(),
            P("tp", None),
            P("tp", "req", None, None),
            P("tp", "req", None, None),
            P("req", None),
            P("req"),
            P(),
            P("req", None),
            P("req", None),
            P("req", None, "tp"),
            P("req", None, "tp"),
            P("req", "tp", None),
        ),
        out_specs=P("req", "tp"),
        check_vma=False,
    )
```

```python
import functools
import math

import jax
import jax.numpy as jnp
import numpy as np
from jax import lax
from jax.experimental import pallas as pl
from jax.experimental.pallas import tpu as pltpu
from jax.sharding import PartitionSpec as P

PAGE = 128
MAXPG = 32
PRE = 120
TOK_DEV = 128
REQS_DEV = 9
POOL = 48
SHORT_PG = 2
SHORT_LIST = (REQS_DEV - 1) * SHORT_PG


NORM_EPS = 1e-06
ROPE_BASE = 1000000.0


def rms_scale(values, gain_vec):
    mean_square = jnp.mean(values * values, axis=-1, keepdims=True)
    return values * lax.rsqrt(mean_square + NORM_EPS) * gain_vec


def rotate(values, positions):
    half_dim = values.shape[-1] // 2
    exponent = jnp.arange(half_dim, dtype=jnp.float32) * (2.0 / values.shape[-1])
    frequency = jnp.power(jnp.float32(ROPE_BASE), -exponent)
    angles = positions.astype(jnp.float32)[:, None] * frequency[None, :]
    cosine = jnp.cos(angles)[:, None, :]
    sine_val = jnp.sin(angles)[:, None, :]
    front_half = values[..., :half_dim]
    back_half = values[..., half_dim:]
    return jnp.concatenate(
        [front_half * cosine - back_half * sine_val, back_half * cosine + front_half * sine_val],
        axis=-1,
    )


def token_layout(lengths):
    local_idx = jnp.arange(TOK_DEV, dtype=jnp.int32)
    requests = jnp.where(local_idx < PRE, 0, local_idx - PRE + 1)
    offsets = jnp.where(local_idx < PRE, local_idx, 0)
    request_hot = (requests[:, None] == jnp.arange(REQS_DEV, dtype=jnp.int32)[None, :]).astype(
        jnp.int32
    )
    positions = jnp.sum(request_hot * lengths[None, :], axis=1) + offsets
    return (requests, positions)


def page_slots(table, lengths):
    pages_used = (lengths + PAGE - 1) // PAGE
    entry_live = jnp.arange(MAXPG, dtype=jnp.int32)[None, :] < pages_used[:, None]
    page_match = (
        (table[:, :, None] == jnp.arange(POOL, dtype=jnp.int32)[None, None, :])
        & entry_live[:, :, None]
    ).astype(jnp.int32)
    page_owner = jnp.sum(
        page_match * jnp.arange(REQS_DEV, dtype=jnp.int32)[:, None, None], axis=(0, 1)
    )
    page_start = jnp.sum(
        page_match * (jnp.arange(MAXPG, dtype=jnp.int32) * PAGE)[None, :, None], axis=(0, 1)
    )
    page_used = jnp.sum(page_match, axis=(0, 1)) > 0
    owner_length = jnp.sum(page_match * lengths[:, None, None], axis=(0, 1))
    slot_pos = page_start[:, None] + jnp.arange(PAGE, dtype=jnp.int32)[None, :]
    slot_live = page_used[:, None] & (slot_pos < owner_length[:, None])
    slot_owner = jnp.where(slot_live, page_owner[:, None], -1)
    return slot_owner.reshape(POOL * PAGE)


def attend(
    queries, keys_new, values_new, keys_cache, values_cache, requests, positions, slot_owner
):
    inv_root = 1.0 / math.sqrt(queries.shape[-1])
    cache_mask = slot_owner[None, :] == requests[:, None]
    new_mask = (requests[None, :] == requests[:, None]) & (positions[None, :] <= positions[:, None])
    score_cache = (
        jnp.einsum("tkgh,knh->kgtn", queries, keys_cache, preferred_element_type=jnp.float32)
        * inv_root
    )
    score_new = (
        jnp.einsum("tkgh,skh->kgts", queries, keys_new, preferred_element_type=jnp.float32)
        * inv_root
    )
    score_cache = jnp.where(cache_mask[None, None], score_cache, -1e30)
    score_new = jnp.where(new_mask[None, None], score_new, -1e30)
    row_max = jnp.maximum(
        jnp.max(score_cache, axis=-1, keepdims=True), jnp.max(score_new, axis=-1, keepdims=True)
    )
    exp_cache = jnp.where(cache_mask[None, None], jnp.exp(score_cache - row_max), 0.0)
    exp_new = jnp.where(new_mask[None, None], jnp.exp(score_new - row_max), 0.0)
    total = jnp.sum(exp_cache, axis=-1, keepdims=True) + jnp.sum(exp_new, axis=-1, keepdims=True)
    prob_cache = (exp_cache / total).astype(jnp.bfloat16)
    prob_new = (exp_new / total).astype(jnp.bfloat16)
    mixed = jnp.einsum(
        "kgtn,knh->tkgh", prob_cache, values_cache, preferred_element_type=jnp.float32
    )
    mixed = mixed + jnp.einsum(
        "kgts,skh->tkgh", prob_new, values_new, preferred_element_type=jnp.float32
    )
    return mixed.astype(jnp.bfloat16).reshape(queries.shape[0], -1)


def expert_apply(blocks, gate_weight, up_weight, down_weight):
    local_experts = gate_weight.shape[0]
    sources = blocks.shape[0] // local_experts
    slot_count = blocks.shape[1]
    grouped = blocks.reshape(sources, local_experts, slot_count, blocks.shape[2])
    gate_acts = jnp.einsum(
        "sekd,edf->sekf", grouped, gate_weight, preferred_element_type=jnp.float32
    )
    up_acts = jnp.einsum("sekd,edf->sekf", grouped, up_weight, preferred_element_type=jnp.float32)
    hidden_act = (jax.nn.silu(gate_acts) * up_acts).astype(jnp.bfloat16)
    part_sums = jnp.einsum(
        "sekf,efd->sekd", hidden_act, down_weight, preferred_element_type=jnp.float32
    ).astype(jnp.bfloat16)
    return part_sums.reshape(sources * local_experts, slot_count, part_sums.shape[3])


def build_buffer(normed, slot_index, top_count, expert_count, capacity):
    picked = jnp.repeat(normed, top_count, axis=0)
    buffer_rows = (
        jnp.zeros((expert_count * capacity, normed.shape[1]), normed.dtype)
        .at[slot_index]
        .set(picked)
    )
    return buffer_rows.reshape(expert_count, capacity, normed.shape[1])


def weigh_back(returned, slot_index, route_weights, token_count, top_count):
    row_width = returned.shape[2]
    back_rows = returned.reshape(returned.shape[0] * returned.shape[1], row_width)[slot_index]
    weighted = (
        back_rows.astype(jnp.float32) * route_weights.reshape(token_count * top_count)[:, None]
    )
    return jnp.sum(weighted.reshape(token_count, top_count, row_width), axis=1)


LANES = 128
VMEM = pl.BlockSpec(memory_space=pltpu.VMEM)
SMEM = pl.BlockSpec(memory_space=pltpu.SMEM)
VMEM_LIMIT = 24 * 1024 * 1024


def flip(value, axis, bits):
    return lax.ppermute(value, axis, [(i, i ^ bits) for i in range(lax.axis_size(axis))])


def stage_kernel(*refs):
    length_hbm, table_hbm, frequency_hbm, *large = refs[:12]
    cosine_ref, sine_ref, owner_ref, *staged = refs[12:24]
    list_ref, length_out, table_out = refs[24:27]
    frequency_ref, owners, sems = refs[27:]
    length_ref, table_ref = length_out, table_out
    sources = (length_hbm, table_hbm, frequency_hbm, *large)
    targets = (length_out, table_out, frequency_ref, *staged)
    copies = [
        pltpu.make_async_copy(source, target, sems.at[i])
        for i, (source, target) in enumerate(zip(sources, targets))
    ]
    for copy in copies:
        copy.start()
    for copy in copies[:3]:
        copy.wait()
    tokens, head_dim = cosine_ref.shape
    for entry in range(POOL):
        list_ref[entry] = 0
        owners[0, entry] = -1
        owners[1, entry] = 0
    prefill_long = length_ref[0] > SHORT_PG * PAGE
    count = jnp.int32(0)
    for request in range(1, REQS_DEV):

        def name_page(entry, count):
            page = table_ref[request, entry]
            place = jnp.where(prefill_long, count, page)
            list_ref[place] = page
            owners[0, place] = request
            owners[1, place] = jnp.minimum(length_ref[request] - entry * PAGE, PAGE)
            return count + 1

        count = lax.fori_loop(0, (length_ref[request] + PAGE - 1) // PAGE, name_page, count)
    slot = lax.broadcasted_iota(jnp.int32, (1, PAGE), 1)
    for entry in range(POOL):
        owner_ref[:, entry * PAGE : (entry + 1) * PAGE] = jnp.where(
            slot < owners[1, entry], owners[0, entry], -1
        )
    token = lax.broadcasted_iota(jnp.int32, (tokens, head_dim), 0)
    lane = lax.broadcasted_iota(jnp.int32, (tokens, head_dim), 1)
    position = length_ref[0] + token
    for i in range(tokens - PRE):
        position = jnp.where(token == PRE + i, length_ref[i + 1], position)
    angle = position.astype(jnp.float32) * frequency_ref[...]
    sine = jnp.sin(angle)
    cosine_ref[...] = jnp.cos(angle)
    sine_ref[...] = jnp.where(lane < head_dim // 2, -sine, sine)
    for copy in copies[3:]:
        copy.wait()


def attention_kernel(*refs):
    pieces, (keep_out, far_out, core_out) = refs[:4], refs[19:22]
    (cosine_ref, sine_ref, owner_ref, gain_ref, q_gain_ref, k_gain_ref) = refs[4:10]
    (q_ref, k_ref, v_ref, key_ref, value_ref, o_ref, list_ref, length_ref, table_ref) = refs[10:19]
    (
        x_ref, query_ref, own_scores, scores_ref, mix_ref, mixed_ref, part_ref, slots_ref, decoded_ref,
    ) = refs[22:]
    tokens, head_dim = x_ref.shape[0], k_gain_ref.shape[1]
    tp_index = lax.axis_index("tp")
    heads = q_ref.shape[1] // head_dim
    decodes = tokens - PRE
    for step, piece in enumerate(pieces):
        width = piece.shape[1]
        start = pl.multiple_of((tp_index ^ step) * width, width)
        x_ref[:, pl.ds(start, width)] = piece[...]
    token = lax.broadcasted_iota(jnp.int32, (tokens, head_dim), 0)
    lane = lax.broadcasted_iota(jnp.int32, (tokens, head_dim), 1)

    def turned(values, gain):
        values = rms_scale(values, gain)
        return values * cosine_ref[...] + pltpu.roll(values, head_dim // 2, 1) * sine_ref[...]

    def with_ones(values):
        return jnp.concatenate([values, jnp.ones_like(values)], axis=1)

    normed = rms_scale(x_ref[...].astype(jnp.float32), gain_ref[...]).astype(jnp.bfloat16)
    contract = (((1,), (1,)), ((), ()))
    key_lin = jnp.dot(normed, k_ref[...], preferred_element_type=jnp.float32)
    values_new = jnp.dot(normed, v_ref[...], preferred_element_type=jnp.float32).astype(jnp.bfloat16)
    query_lin = jnp.dot(normed, q_ref[...], preferred_element_type=jnp.float32)
    keys_new = turned(key_lin, k_gain_ref[...]).astype(jnp.bfloat16)
    values_new = with_ones(values_new)
    to_log2 = math.log2(math.e) / math.sqrt(head_dim)
    own_mask = (lane == token) | ((lane < token) & (token < PRE))
    decode_query, decode_own = [], []
    for head in range(heads):
        span = slice(head * tokens, (head + 1) * tokens)
        query = turned(query_lin[:, head * head_dim : (head + 1) * head_dim], q_gain_ref[...]) * to_log2
        rounded = query.astype(jnp.bfloat16)
        query_ref[span, :] = rounded
        scores = lax.dot_general(rounded, keys_new, contract, preferred_element_type=jnp.float32)
        scores = jnp.where(own_mask, scores, -1e30)
        own_scores[span, :] = scores
        decode_query.append(query[PRE:])
        decode_own.append(scores[PRE:])
    decode_query = jnp.concatenate(decode_query, axis=0).astype(jnp.bfloat16)
    decode_own = jnp.concatenate(decode_own, axis=0)

    def raised(top, scores):
        for start in range(0, scores.shape[1], head_dim):
            top = jnp.maximum(top, scores[:, start : start + head_dim])
        return top

    def weigh(own, score_steps, value_steps, scores_ref):
        top = own
        for step, score_step in enumerate(score_steps):
            scores = score_step()
            scores_ref[step, :, : scores.shape[1]] = scores
            top = raised(top, scores)
        top = jnp.max(top, axis=1, keepdims=True)
        mix = jnp.dot(
            jnp.exp2(own - top).astype(jnp.bfloat16), values_new, preferred_element_type=jnp.float32
        )
        for step, value_step in enumerate(value_steps):
            values = value_step()
            weights = jnp.exp2(scores_ref[step, :, : values.shape[0]] - top).astype(jnp.bfloat16)
            mix = mix + jnp.dot(weights, with_ones(values), preferred_element_type=jnp.float32)
        return mix

    def taken(ref, names):
        return jnp.concatenate([ref[name] for name in names], axis=0)

    def against(queries, keys):
        return lax.dot_general(queries, keys, contract, preferred_element_type=jnp.float32)

    def prefill(names, live):
        def score(pages):
            scores = against(query_ref[...], taken(key_ref, pages))
            return scores if live is None else jnp.where(live, scores, -1e30)

        mix_ref[...] = weigh(
            own_scores[...],
            [functools.partial(score, pages) for pages in names],
            [functools.partial(taken, value_ref, pages) for pages in names],
            scores_ref,
        )

    def decode(steps, pages_of):
        row_request = 1 + lax.broadcasted_iota(jnp.int32, (heads * decodes, 1), 0) % decodes
        width = slots_ref.shape[2]

        def score(step):
            scores = against(decode_query, pages_of(key_ref, step))
            owner = owner_ref[:, step * width : (step + 1) * width]
            return jnp.where(owner == row_request, scores, -1e30)

        mix = weigh(
            decode_own,
            [functools.partial(score, step) for step in range(steps)],
            [functools.partial(pages_of, value_ref, step) for step in range(steps)],
            slots_ref,
        )
        decoded_ref[...] = mix[:, :head_dim] / mix[:, head_dim:]

    length = length_ref[0]
    listed = slots_ref.shape[2] // PAGE
    pages = scores_ref.shape[2] // PAGE

    @pl.when(length > SHORT_PG * PAGE)
    def _():
        names = [table_ref[0, entry] for entry in range(MAXPG)]
        prefill([names[first : first + pages] for first in range(0, MAXPG, pages)], None)
        decode(
            SHORT_LIST // listed,
            lambda ref, step: taken(ref, [list_ref[step * listed + i] for i in range(listed)]),
        )

    @pl.when(length <= SHORT_PG * PAGE)
    def _():
        column = lax.broadcasted_iota(jnp.int32, (1, SHORT_PG * PAGE), 1)
        prefill([[table_ref[0, entry] for entry in range(SHORT_PG)]], column < length)
        decode(
            POOL // listed,
            lambda ref, step: ref[step * listed : (step + 1) * listed].reshape(-1, head_dim),
        )

    for head in range(heads):
        part = mix_ref[head * tokens : (head + 1) * tokens, :]
        columns = slice(head * head_dim, (head + 1) * head_dim)
        mixed_ref[:, columns] = part[:, :head_dim] / part[:, head_dim:]
        mixed_ref[PRE:, columns] = decoded_ref[head * decodes : (head + 1) * decodes]
    part_ref[...] = jnp.dot(
        mixed_ref[...].astype(jnp.bfloat16), o_ref[...], preferred_element_type=jnp.float32
    )
    share_rows = keep_out.shape[0]

    def quarter(step):
        return pl.ds(pl.multiple_of((tp_index ^ step) * share_rows, share_rows), share_rows)

    keep_out[...] = part_ref[quarter(0), :] + x_ref[quarter(0), :].astype(jnp.float32)
    far_out[...] = part_ref[quarter(2), :]
    core_out[0] = part_ref[quarter(1), :].astype(jnp.bfloat16)
    core_out[1] = part_ref[quarter(3), :].astype(jnp.bfloat16)


def attention_shares(
    hidden_in, norm_in_gain, q_weight, k_weight, v_weight, q_gain, k_gain, o_weight,
    key_pages, value_pages, page_table, cache_len,
):
    tokens, width = hidden_in.shape[0], 4 * hidden_in.shape[1]
    head_dim = q_gain.shape[0]
    rows = q_weight.shape[1] // head_dim * tokens
    decode_rows = rows // tokens * (tokens - PRE)
    half = ROPE_BASE ** (-np.arange(head_dim // 2) / (head_dim // 2))
    frequency = jnp.asarray(np.concatenate([half, half])[None, :], jnp.float32)
    large = (
        norm_in_gain[None, :], q_gain[None, :], k_gain[None, :], q_weight, k_weight, v_weight,
        key_pages[0], value_pages[0], o_weight,
    )
    scalars = (cache_len, page_table)
    sources = [
        pltpu.with_memory_space_constraint(array, pltpu.HBM)
        for array in (*scalars, frequency, *large)
    ]
    rope = pltpu.VMEM((tokens, head_dim), jnp.float32)
    *staged, page_list, lengths, table = pl.pallas_call(
        stage_kernel,
        out_shape=[rope, rope, pltpu.VMEM((1, POOL * PAGE), jnp.int32)]
        + [pltpu.VMEM(array.shape, array.dtype) for array in large]
        + [jax.ShapeDtypeStruct((POOL,), jnp.int32)]
        + [jax.ShapeDtypeStruct(array.shape, array.dtype) for array in scalars],
        in_specs=[pl.BlockSpec(memory_space=pltpu.HBM)] * 12,
        out_specs=[VMEM] * 12 + [SMEM] * 3,
        scratch_shapes=[
            pltpu.VMEM(frequency.shape, frequency.dtype),
            pltpu.SMEM((2, POOL), jnp.int32),
            pltpu.SemaphoreType.DMA((12,)),
        ],
        compiler_params=pltpu.CompilerParams(vmem_limit_bytes=4 * 1024 * 1024),
        name="stage",
    )(*sources)
    far, *staged = ordered(flip(hidden_in, "tp", 2), *staged, page_list, lengths, table)
    pieces = (hidden_in, flip(hidden_in, "tp", 1), far, flip(far, "tp", 1))
    share = (tokens // 4, width)
    score_pages, list_pages = 4, 8
    return pl.pallas_call(
        attention_kernel,
        out_shape=[
            jax.ShapeDtypeStruct(share, jnp.float32),
            jax.ShapeDtypeStruct(share, jnp.float32),
            jax.ShapeDtypeStruct((2, *share), jnp.bfloat16),
        ],
        in_specs=[VMEM] * 16 + [SMEM] * 3,
        out_specs=[VMEM] * 3,
        scratch_shapes=[
            pltpu.VMEM((tokens, width), jnp.bfloat16),
            pltpu.VMEM((rows, head_dim), jnp.bfloat16),
            pltpu.VMEM((rows, tokens), jnp.float32),
            pltpu.VMEM((MAXPG // score_pages, rows, score_pages * PAGE), jnp.float32),
            pltpu.VMEM((rows, 2 * head_dim), jnp.float32),
            pltpu.VMEM((tokens, q_weight.shape[1]), jnp.float32),
            pltpu.VMEM((tokens, width), jnp.float32),
            pltpu.VMEM((POOL // list_pages, decode_rows, list_pages * PAGE), jnp.float32),
            pltpu.VMEM((decode_rows, head_dim), jnp.float32),
        ],
        compiler_params=pltpu.CompilerParams(vmem_limit_bytes=24 * 1024 * 1024),
        name="attention",
    )(*pieces, *staged)


def pack_kernel(
    own_ref, far_ref, gain_ref, ids_ref, routes_ref,
    rows_ref, residual_ref, spread_ref,
):
    tp_index = lax.axis_index("tp")
    share_rows, width = own_ref.shape
    mine = pl.ds(pl.multiple_of(tp_index * share_rows, share_rows), share_rows)
    residual = own_ref[...] + far_ref[...].astype(jnp.float32)
    residual_ref[...] = residual
    rows_ref[:, :width] = rms_scale(residual, gain_ref[...]).astype(jnp.bfloat16)
    expert = lax.broadcasted_iota(jnp.int32, (LANES, spread_ref.shape[0]), 0) % (LANES // 2)
    spread = jnp.zeros(expert.shape, jnp.float32)
    for k in range(ids_ref.shape[0]):
        spread = spread + jnp.where(expert == ids_ref[k : k + 1, :], routes_ref[k : k + 1, :], 0.0)
    spread_ref[...] = spread.T
    spread = spread_ref[mine, :]
    lane = lax.broadcasted_iota(jnp.int32, spread.shape, 1)
    high = spread.astype(jnp.bfloat16).astype(jnp.float32)
    rows_ref[:, width:] = jnp.where(lane < LANES // 2, high, spread - high).astype(jnp.bfloat16)


def experts_kernel(plan, residuals, *refs):
    pieces, residual_refs = refs[: len(plan)], refs[len(plan) : len(plan) + residuals]
    gate_ref, up_ref, down_ref, keep_ref, *send_refs, rows_ref, sums_ref = refs[len(plan) + residuals :]
    req_index, tp_index = lax.axis_index("req"), lax.axis_index("tp")
    columns, _, levels, group_rows, share_width = keep_ref.shape
    width = gate_ref.shape[1]
    units = gate_ref.shape[0] // 2
    for (column, step, first), piece in zip(plan, pieces):
        count = piece.shape[1]
        for level in range(levels):
            start = (column * levels + level) * group_rows + first
            start = start + (tp_index ^ step) * (group_rows // 4)
            rows_ref[pl.ds(pl.multiple_of(start, count), count), :] = piece[level]
    spread = rows_ref[:, width:].astype(jnp.float32)
    lane = lax.broadcasted_iota(jnp.int32, spread.shape, 1) % (LANES // 2)
    weights = [
        jnp.sum(jnp.where(lane == 2 * req_index + e, spread, 0.0), axis=1, keepdims=True)
        for e in range(2)
    ]
    contract = (((1,), (1,)), ((), ()))
    rows = rows_ref[:, :width]
    gate = lax.dot_general(rows, gate_ref[...], contract, preferred_element_type=jnp.float32)
    up = lax.dot_general(rows, up_ref[...], contract, preferred_element_type=jnp.float32)
    unit = lax.broadcasted_iota(jnp.int32, gate.shape, 1)
    weight = jnp.where(unit < units, weights[0], weights[1])
    acts = (gate / (1.0 + jnp.exp(-gate)) * up * weight).astype(jnp.bfloat16)
    for step in range(4):
        start = pl.multiple_of((tp_index ^ step) * share_width, share_width)
        part = jnp.dot(
            acts, down_ref[:, pl.ds(start, share_width)], preferred_element_type=jnp.float32
        )
        for residual_ref in residual_refs:
            count = residual_ref.shape[0]
            mine = pl.ds(pl.multiple_of(tp_index * count, count), count)
            sums_ref[...] = part
            sums_ref[mine, :] += residual_ref[:, pl.ds(start, share_width)]
            part = sums_ref[...]
        part = part.reshape(columns, levels, group_rows, share_width)
        if step % 2:
            send_refs[step // 2][...] = part.astype(jnp.bfloat16)
            continue
        for column in range(columns):
            keep_ref[column, step // 2] = part[column]


def run_experts(pieces, weights, group_rows, *residual):
    plan = tuple(place for place, _ in pieces)
    pieces = [piece for _, piece in pieces]
    columns, levels, packed = 1 + max(place[0] for place in plan), *pieces[0].shape[::2]
    rows, share_width = columns * levels * group_rows, weights[2].shape[1] // 4
    sums = (levels, group_rows, share_width)
    keep, *send = pl.pallas_call(
        functools.partial(experts_kernel, plan, len(residual)),
        out_shape=[jax.ShapeDtypeStruct((columns, 2, *sums), jnp.float32)]
        + [jax.ShapeDtypeStruct((columns, *sums), jnp.bfloat16)] * 2,
        in_specs=[VMEM] * (len(pieces) + len(residual) + 3),
        out_specs=[VMEM] * 3,
        scratch_shapes=[
            pltpu.VMEM((rows, packed), jnp.bfloat16),
            pltpu.VMEM((rows, share_width), jnp.float32),
        ],
        compiler_params=pltpu.CompilerParams(vmem_limit_bytes=VMEM_LIMIT),
        name="experts",
    )(*pieces, *residual, *weights)
    return keep, send


def ordered(*values):
    return lax.optimization_barrier(values)


def across_parts(line_x, line_y):
    half = line_x.shape[1] // 2
    return flip(line_x[:, :half], "tp", 2), flip(line_y[:, half:], "req", 1)


def other_core(parts):
    return tuple(flip(part, "tp", 1) for part in parts)


def with_core(pair):
    return pair[0], list(other_core(pair[1]))


def joined(pair, column, y):
    return pair[0][column, y] + pair[1][y][column].astype(jnp.float32)


def near_pieces(column, line, core):
    return [((column, 0, 0), line), ((column, 1, 0), core)]


def far_pieces(column, parts, cores):
    half = parts[0].shape[1]
    if len(parts) == 1:
        return [((column, 2, 0), parts[0]), ((column, 3, 0), cores[0])]
    return [((column, 2, i * half), part) for i, part in enumerate(parts)] + [
        ((column, 3, i * half), part) for i, part in enumerate(cores)
    ]


def relayed(side):
    part = side.astype(jnp.bfloat16)
    half = part.shape[1] // 2
    return flip(part[:, :half], "req", 1), flip(part[:, half:], "tp", 2)


def with_lower(sums, part):
    half = part.shape[1]
    sums = [sums[:, :half] + part.astype(jnp.float32), sums[:, half:]]
    return jnp.concatenate(sums, axis=1).astype(jnp.bfloat16)


def with_upper(sums, part):
    half = part.shape[1]
    sums = [sums[:, :half], sums[:, half:] + part.astype(jnp.float32)]
    return jnp.concatenate(sums, axis=1).astype(jnp.bfloat16)


def neighbours(to_x, to_y, by_x, by_y):
    return flip(with_upper(to_x, by_y), "req", 1), flip(with_lower(to_y, by_x), "tp", 2)


def moe_dense(
    kept,
    far,
    core,
    norm_post_gain,
    expert_ids,
    route_weights,
    gate_weight,
    up_weight,
    down_weight,
):
    share_rows, width = kept.shape
    token_count, share_width = 4 * share_rows, width // 4
    core = flip(core, "tp", 1)
    far, kept, core = ordered((far + core[1].astype(jnp.float32)).astype(jnp.bfloat16), kept, core)
    kept, far = ordered(kept + core[0].astype(jnp.float32), flip(far, "tp", 2))
    rows, residual = pl.pallas_call(
        pack_kernel,
        out_shape=[
            jax.ShapeDtypeStruct((share_rows, width + LANES), jnp.bfloat16),
            jax.ShapeDtypeStruct((share_rows, width), jnp.float32),
        ],
        in_specs=[VMEM] * 5,
        out_specs=[VMEM] * 2,
        scratch_shapes=[pltpu.VMEM((token_count, LANES), jnp.float32)],
        compiler_params=pltpu.CompilerParams(vmem_limit_bytes=8 * 1024 * 1024),
        name="pack_rows",
    )(kept, far, norm_post_gain[None, :], expert_ids.T, route_weights.T)
    gate_up = [w.transpose(0, 2, 1).reshape(-1, width) for w in (gate_weight, up_weight)]
    weights = (*gate_up, down_weight.reshape(-1, width))
    line_0 = rows[None]
    z_1, z_2 = flip(line_0, "req", 2), flip(line_0, "req", 4)
    y_0, x_0 = flip(line_0, "tp", 2), flip(line_0, "req", 1)
    line_12, z_2, y_0, x_0 = ordered(jnp.concatenate([z_1, z_2]), z_2, y_0, x_0)
    line_3, across_0, core_0, y_core_0 = ordered(
        jnp.concatenate([line_12, flip(z_2, "req", 2)]),
        across_parts(x_0, y_0),
        flip(line_0, "tp", 1),
        flip(y_0, "tp", 1),
    )
    y_3, x_3 = flip(line_3, "tp", 2), flip(line_3, "req", 1)
    x_core_0, across_core_0, core_3, y_3, x_3 = ordered(
        flip(x_0, "tp", 1), other_core(across_0), flip(line_3, "tp", 1), y_3, x_3
    )
    all_0 = run_experts(
        near_pieces(0, line_0, core_0)
        + far_pieces(0, (y_0,), (y_core_0,))
        + near_pieces(1, x_0, x_core_0)
        + far_pieces(1, across_0, across_core_0),
        weights,
        token_count,
        residual,
    )
    x_core_3, all_0, y_3, across_3 = ordered(
        flip(x_3, "tp", 1), all_0, y_3, jnp.concatenate(across_parts(x_3, y_3), axis=1)
    )
    side_3 = run_experts(
        near_pieces(0, x_3, x_core_3) + far_pieces(0, (across_3,), (flip(across_3, "tp", 1),)),
        weights,
        token_count,
    )
    y_core_3, all_0, (keep, (send, first)) = ordered(flip(y_3, "tp", 1), all_0, side_3)
    all_0, y_core_3, keep, send, first = ordered(all_0, y_core_3, keep, send, flip(first, "tp", 1))
    diagonal, keep, send = ordered(joined((keep, (send, first)), 0, 1).astype(jnp.bfloat16), keep, send)
    by_x, by_y = relayed(diagonal)
    near_keep, (near_send, near_first) = run_experts(
        near_pieces(0, line_3, core_3) + far_pieces(0, (y_3,), (y_core_3,)), weights, token_count
    )
    send = flip(send, "tp", 1)
    all_0, near_keep, near_send, near_first, by_x, to_x = ordered(
        all_0,
        near_keep,
        near_send,
        flip(near_first, "tp", 1),
        by_x.astype(jnp.float32),
        with_upper(joined((keep, (send, first)), 0, 0), by_y),
    )
    to_y = with_lower(joined((near_keep, (near_send, near_first)), 0, 1), by_x)
    sums_3 = flip(to_x, "req", 1).astype(jnp.float32) + flip(to_y, "tp", 2).astype(jnp.float32)
    all_0, near_send, sums_3 = ordered(with_core(all_0), flip(near_send, "tp", 1), sums_3)
    sent = joined((near_keep, (near_send, near_first)), 0, 0) + sums_3
    sent_3, relay_0 = ordered(
        flip(sent[2].astype(jnp.bfloat16), "req", 2), relayed(joined(all_0, 1, 1))
    )
    sent_2, relay_0 = ordered(
        (sent[1] + sent_3.astype(jnp.float32)).astype(jnp.bfloat16), relay_0
    )
    from_z = [flip(sent[0].astype(jnp.bfloat16), "req", 2), flip(sent_2, "req", 4)]
    sums_0 = neighbours(joined(all_0, 1, 0), joined(all_0, 0, 1), *relay_0)
    total = joined(all_0, 0, 0) + from_z[0].astype(jnp.float32) + from_z[1].astype(jnp.float32)
    total, from_x, from_y = ordered(total[0], *sums_0)
    return (total + from_x[0].astype(jnp.float32) + from_y[0].astype(jnp.float32)).astype(jnp.bfloat16)


def moe_routed(
    x_full,
    head_part,
    norm_post_gain,
    expert_ids,
    route_weights,
    gate_weight,
    up_weight,
    down_weight,
):
    req_count = lax.axis_size("req")
    tp_index = lax.axis_index("tp")
    x_float = x_full.astype(jnp.float32)
    token_count = x_float.shape[0]
    share_width = x_float.shape[1] // lax.axis_size("tp")
    top_count = expert_ids.shape[1]
    expert_count = gate_weight.shape[0] * req_count
    capacity = max(2, 3 * token_count * top_count // (2 * expert_count))
    flat_expert = expert_ids.reshape(token_count * top_count)
    one_hot = (flat_expert[:, None] == jnp.arange(expert_count, dtype=jnp.int32)[None, :]).astype(
        jnp.int32
    )
    slot_rank = jnp.sum((jnp.cumsum(one_hot, axis=0) - one_hot) * one_hot, axis=1)
    slot_index = flat_expert * capacity + slot_rank
    head_sum = lax.psum(head_part.astype(jnp.bfloat16), "tp").astype(jnp.float32)
    residual_full = x_float + head_sum
    normed_post = rms_scale(residual_full, norm_post_gain).astype(jnp.bfloat16)
    residual = lax.dynamic_slice_in_dim(residual_full, tp_index * share_width, share_width, 1)
    send_buffer = build_buffer(normed_post, slot_index, top_count, expert_count, capacity)
    part_sums = expert_apply(
        lax.all_to_all(send_buffer, "req", split_axis=0, concat_axis=0, tiled=True),
        gate_weight,
        up_weight,
        down_weight,
    )
    returned = lax.all_to_all(part_sums, "req", split_axis=0, concat_axis=0, tiled=True)
    moe_term = weigh_back(returned, slot_index, route_weights, token_count, top_count)
    moe_share = lax.psum_scatter(
        moe_term.astype(jnp.bfloat16), "tp", scatter_dimension=1, tiled=True
    ).astype(jnp.float32)
    return (residual + moe_share).astype(jnp.bfloat16)


def attention_part(
    x_full,
    norm_in_gain,
    q_weight,
    k_weight,
    v_weight,
    q_gain,
    k_gain,
    o_weight,
    key_pages,
    value_pages,
    page_table,
    cache_len,
):
    head_dim = q_gain.shape[0]
    kv_local = key_pages.shape[0]
    group_size = q_weight.shape[1] // head_dim // kv_local
    token_count = x_full.shape[0]
    x_float = x_full.astype(jnp.float32)
    normed_in = rms_scale(x_float, norm_in_gain).astype(jnp.bfloat16)
    query_lin = jnp.dot(normed_in, q_weight, preferred_element_type=jnp.float32).reshape(
        token_count, kv_local * group_size, head_dim
    )
    key_lin = jnp.dot(normed_in, k_weight, preferred_element_type=jnp.float32).reshape(
        token_count, kv_local, head_dim
    )
    values_new = (
        jnp.dot(normed_in, v_weight, preferred_element_type=jnp.float32)
        .astype(jnp.bfloat16)
        .reshape(token_count, kv_local, head_dim)
    )
    requests, positions = token_layout(cache_len)
    queries = (
        rotate(rms_scale(query_lin, q_gain), positions)
        .astype(jnp.bfloat16)
        .reshape(token_count, kv_local, group_size, head_dim)
    )
    keys_new = rotate(rms_scale(key_lin, k_gain), positions).astype(jnp.bfloat16)
    slot_owner = page_slots(page_table, cache_len)
    cache_slots = key_pages.shape[1] * key_pages.shape[2]
    keys_cache = key_pages.reshape(kv_local, cache_slots, head_dim)
    values_cache = value_pages.reshape(kv_local, cache_slots, head_dim)
    attended = attend(
        queries, keys_new, values_new, keys_cache, values_cache, requests, positions, slot_owner
    )
    return jnp.dot(attended, o_weight, preferred_element_type=jnp.float32)


def body(
    hidden_in,
    norm_in_gain,
    q_weight,
    k_weight,
    v_weight,
    q_gain,
    k_gain,
    o_weight,
    key_pages,
    value_pages,
    page_table,
    cache_len,
    norm_post_gain,
    expert_ids,
    route_weights,
    gate_weight,
    up_weight,
    down_weight,
):
    req_count = lax.axis_size("req")
    attention = (
        norm_in_gain,
        q_weight,
        k_weight,
        v_weight,
        q_gain,
        k_gain,
        o_weight,
        key_pages,
        value_pages,
        page_table,
        cache_len,
    )
    experts = (norm_post_gain, expert_ids, route_weights, gate_weight, up_weight, down_weight)
    expert_count = gate_weight.shape[0] * req_count
    staged = (req_count, lax.axis_size("tp"), gate_weight.shape[0]) == (8, 4, 2)
    if staged and expert_count <= LANES // 2:
        return moe_dense(*attention_shares(hidden_in, *attention), *experts)
    x_full = lax.all_gather(hidden_in, "tp", axis=1, tiled=True)
    return moe_routed(x_full, attention_part(x_full, *attention), *experts)


def solution(mesh):
    return jax.shard_map(
        body,
        mesh=mesh,
        in_specs=(
            P("req", "tp"),
            P(),
            P(None, "tp"),
            P(None, "tp"),
            P(None, "tp"),
            P(),
            P(),
            P("tp", None),
            P("tp", "req", None, None),
            P("tp", "req", None, None),
            P("req", None),
            P("req"),
            P(),
            P("req", None),
            P("req", None),
            P("req", None, "tp"),
            P("req", None, "tp"),
            P("req", "tp", None),
        ),
        out_specs=P("req", "tp"),
        check_vma=False,
    )
```

```python
import functools
import math

import jax
import jax.numpy as jnp
import numpy as np
from jax import lax
from jax.experimental import pallas as pl
from jax.experimental.pallas import tpu as pltpu
from jax.sharding import PartitionSpec as P

PAGE = 128
MAXPG = 32
PRE = 120
TOK_DEV = 128
REQS_DEV = 9
POOL = 48
SHORT_PG = 2
SHORT_LIST = (REQS_DEV - 1) * SHORT_PG


NORM_EPS = 1e-06
ROPE_BASE = 1000000.0


def rms_scale(values, gain_vec):
    mean_square = jnp.mean(values * values, axis=-1, keepdims=True)
    return values * lax.rsqrt(mean_square + NORM_EPS) * gain_vec


def rotate(values, positions):
    half_dim = values.shape[-1] // 2
    exponent = jnp.arange(half_dim, dtype=jnp.float32) * (2.0 / values.shape[-1])
    frequency = jnp.power(jnp.float32(ROPE_BASE), -exponent)
    angles = positions.astype(jnp.float32)[:, None] * frequency[None, :]
    cosine = jnp.cos(angles)[:, None, :]
    sine_val = jnp.sin(angles)[:, None, :]
    front_half = values[..., :half_dim]
    back_half = values[..., half_dim:]
    return jnp.concatenate(
        [front_half * cosine - back_half * sine_val, back_half * cosine + front_half * sine_val],
        axis=-1,
    )


def token_layout(lengths):
    local_idx = jnp.arange(TOK_DEV, dtype=jnp.int32)
    requests = jnp.where(local_idx < PRE, 0, local_idx - PRE + 1)
    offsets = jnp.where(local_idx < PRE, local_idx, 0)
    request_hot = (requests[:, None] == jnp.arange(REQS_DEV, dtype=jnp.int32)[None, :]).astype(
        jnp.int32
    )
    positions = jnp.sum(request_hot * lengths[None, :], axis=1) + offsets
    return (requests, positions)


def page_slots(table, lengths):
    pages_used = (lengths + PAGE - 1) // PAGE
    entry_live = jnp.arange(MAXPG, dtype=jnp.int32)[None, :] < pages_used[:, None]
    page_match = (
        (table[:, :, None] == jnp.arange(POOL, dtype=jnp.int32)[None, None, :])
        & entry_live[:, :, None]
    ).astype(jnp.int32)
    page_owner = jnp.sum(
        page_match * jnp.arange(REQS_DEV, dtype=jnp.int32)[:, None, None], axis=(0, 1)
    )
    page_start = jnp.sum(
        page_match * (jnp.arange(MAXPG, dtype=jnp.int32) * PAGE)[None, :, None], axis=(0, 1)
    )
    page_used = jnp.sum(page_match, axis=(0, 1)) > 0
    owner_length = jnp.sum(page_match * lengths[:, None, None], axis=(0, 1))
    slot_pos = page_start[:, None] + jnp.arange(PAGE, dtype=jnp.int32)[None, :]
    slot_live = page_used[:, None] & (slot_pos < owner_length[:, None])
    slot_owner = jnp.where(slot_live, page_owner[:, None], -1)
    return slot_owner.reshape(POOL * PAGE)


def attend(
    queries, keys_new, values_new, keys_cache, values_cache, requests, positions, slot_owner
):
    inv_root = 1.0 / math.sqrt(queries.shape[-1])
    cache_mask = slot_owner[None, :] == requests[:, None]
    new_mask = (requests[None, :] == requests[:, None]) & (positions[None, :] <= positions[:, None])
    score_cache = (
        jnp.einsum("tkgh,knh->kgtn", queries, keys_cache, preferred_element_type=jnp.float32)
        * inv_root
    )
    score_new = (
        jnp.einsum("tkgh,skh->kgts", queries, keys_new, preferred_element_type=jnp.float32)
        * inv_root
    )
    score_cache = jnp.where(cache_mask[None, None], score_cache, -1e30)
    score_new = jnp.where(new_mask[None, None], score_new, -1e30)
    row_max = jnp.maximum(
        jnp.max(score_cache, axis=-1, keepdims=True), jnp.max(score_new, axis=-1, keepdims=True)
    )
    exp_cache = jnp.where(cache_mask[None, None], jnp.exp(score_cache - row_max), 0.0)
    exp_new = jnp.where(new_mask[None, None], jnp.exp(score_new - row_max), 0.0)
    total = jnp.sum(exp_cache, axis=-1, keepdims=True) + jnp.sum(exp_new, axis=-1, keepdims=True)
    prob_cache = (exp_cache / total).astype(jnp.bfloat16)
    prob_new = (exp_new / total).astype(jnp.bfloat16)
    mixed = jnp.einsum(
        "kgtn,knh->tkgh", prob_cache, values_cache, preferred_element_type=jnp.float32
    )
    mixed = mixed + jnp.einsum(
        "kgts,skh->tkgh", prob_new, values_new, preferred_element_type=jnp.float32
    )
    return mixed.astype(jnp.bfloat16).reshape(queries.shape[0], -1)


def expert_apply(blocks, gate_weight, up_weight, down_weight):
    local_experts = gate_weight.shape[0]
    sources = blocks.shape[0] // local_experts
    slot_count = blocks.shape[1]
    grouped = blocks.reshape(sources, local_experts, slot_count, blocks.shape[2])
    gate_acts = jnp.einsum(
        "sekd,edf->sekf", grouped, gate_weight, preferred_element_type=jnp.float32
    )
    up_acts = jnp.einsum("sekd,edf->sekf", grouped, up_weight, preferred_element_type=jnp.float32)
    hidden_act = (jax.nn.silu(gate_acts) * up_acts).astype(jnp.bfloat16)
    part_sums = jnp.einsum(
        "sekf,efd->sekd", hidden_act, down_weight, preferred_element_type=jnp.float32
    ).astype(jnp.bfloat16)
    return part_sums.reshape(sources * local_experts, slot_count, part_sums.shape[3])


def build_buffer(normed, slot_index, top_count, expert_count, capacity):
    picked = jnp.repeat(normed, top_count, axis=0)
    buffer_rows = (
        jnp.zeros((expert_count * capacity, normed.shape[1]), normed.dtype)
        .at[slot_index]
        .set(picked)
    )
    return buffer_rows.reshape(expert_count, capacity, normed.shape[1])


def weigh_back(returned, slot_index, route_weights, token_count, top_count):
    row_width = returned.shape[2]
    back_rows = returned.reshape(returned.shape[0] * returned.shape[1], row_width)[slot_index]
    weighted = (
        back_rows.astype(jnp.float32) * route_weights.reshape(token_count * top_count)[:, None]
    )
    return jnp.sum(weighted.reshape(token_count, top_count, row_width), axis=1)


LANES = 128
VMEM = pl.BlockSpec(memory_space=pltpu.VMEM)
SMEM = pl.BlockSpec(memory_space=pltpu.SMEM)
VMEM_LIMIT = 24 * 1024 * 1024


def flip(value, axis, bits):
    return lax.ppermute(value, axis, [(i, i ^ bits) for i in range(lax.axis_size(axis))])


def stage_kernel(*refs):
    length_hbm, table_hbm, frequency_hbm, *large = refs[:12]
    cosine_ref, sine_ref, owner_ref, *staged = refs[12:24]
    list_ref, length_out, table_out = refs[24:27]
    frequency_ref, owners, sems = refs[27:]
    length_ref, table_ref = length_out, table_out
    sources = (length_hbm, table_hbm, frequency_hbm, *large)
    targets = (length_out, table_out, frequency_ref, *staged)
    copies = [
        pltpu.make_async_copy(source, target, sems.at[i])
        for i, (source, target) in enumerate(zip(sources, targets))
    ]
    for copy in copies:
        copy.start()
    for copy in copies[:3]:
        copy.wait()
    tokens, head_dim = cosine_ref.shape
    for entry in range(POOL):
        list_ref[entry] = 0
        owners[0, entry] = -1
        owners[1, entry] = 0
    prefill_long = length_ref[0] > SHORT_PG * PAGE
    count = jnp.int32(0)
    for request in range(1, REQS_DEV):

        def name_page(entry, count):
            page = table_ref[request, entry]
            place = jnp.where(prefill_long, count, page)
            list_ref[place] = page
            owners[0, place] = request
            owners[1, place] = jnp.minimum(length_ref[request] - entry * PAGE, PAGE)
            return count + 1

        count = lax.fori_loop(0, (length_ref[request] + PAGE - 1) // PAGE, name_page, count)
    slot = lax.broadcasted_iota(jnp.int32, (1, PAGE), 1)
    for entry in range(POOL):
        owner_ref[:, entry * PAGE : (entry + 1) * PAGE] = jnp.where(
            slot < owners[1, entry], owners[0, entry], -1
        )
    token = lax.broadcasted_iota(jnp.int32, (tokens, head_dim), 0)
    lane = lax.broadcasted_iota(jnp.int32, (tokens, head_dim), 1)
    position = length_ref[0] + token
    for i in range(tokens - PRE):
        position = jnp.where(token == PRE + i, length_ref[i + 1], position)
    angle = position.astype(jnp.float32) * frequency_ref[...]
    sine = jnp.sin(angle)
    cosine_ref[...] = jnp.cos(angle)
    sine_ref[...] = jnp.where(lane < head_dim // 2, -sine, sine)
    for copy in copies[3:]:
        copy.wait()


def attention_kernel(*refs):
    pieces, (keep_out, far_out, core_out) = refs[:4], refs[19:22]
    (cosine_ref, sine_ref, owner_ref, gain_ref, q_gain_ref, k_gain_ref) = refs[4:10]
    (q_ref, k_ref, v_ref, key_ref, value_ref, o_ref, list_ref, length_ref, table_ref) = refs[10:19]
    (
        x_ref, query_ref, own_scores, scores_ref, mix_ref, mixed_ref, part_ref, slots_ref, decoded_ref,
    ) = refs[22:]
    tokens, head_dim = x_ref.shape[0], k_gain_ref.shape[1]
    tp_index = lax.axis_index("tp")
    heads = q_ref.shape[1] // head_dim
    decodes = tokens - PRE
    for step, piece in enumerate(pieces):
        width = piece.shape[1]
        start = pl.multiple_of((tp_index ^ step) * width, width)
        x_ref[:, pl.ds(start, width)] = piece[...]
    token = lax.broadcasted_iota(jnp.int32, (tokens, head_dim), 0)
    lane = lax.broadcasted_iota(jnp.int32, (tokens, head_dim), 1)

    def turned(values, gain):
        values = rms_scale(values, gain)
        return values * cosine_ref[...] + pltpu.roll(values, head_dim // 2, 1) * sine_ref[...]

    def with_ones(values):
        return jnp.concatenate([values, jnp.ones_like(values)], axis=1)

    normed = rms_scale(x_ref[...].astype(jnp.float32), gain_ref[...]).astype(jnp.bfloat16)
    contract = (((1,), (1,)), ((), ()))
    key_lin = jnp.dot(normed, k_ref[...], preferred_element_type=jnp.float32)
    values_new = jnp.dot(normed, v_ref[...], preferred_element_type=jnp.float32).astype(jnp.bfloat16)
    query_lin = jnp.dot(normed, q_ref[...], preferred_element_type=jnp.float32)
    keys_new = turned(key_lin, k_gain_ref[...]).astype(jnp.bfloat16)
    values_new = with_ones(values_new)
    to_log2 = math.log2(math.e) / math.sqrt(head_dim)
    own_mask = (lane == token) | ((lane < token) & (token < PRE))
    decode_query, decode_own = [], []
    for head in range(heads):
        span = slice(head * tokens, (head + 1) * tokens)
        query = turned(query_lin[:, head * head_dim : (head + 1) * head_dim], q_gain_ref[...]) * to_log2
        rounded = query.astype(jnp.bfloat16)
        query_ref[span, :] = rounded
        scores = lax.dot_general(rounded, keys_new, contract, preferred_element_type=jnp.float32)
        scores = jnp.where(own_mask, scores, -1e30)
        own_scores[span, :] = scores
        decode_query.append(query[PRE:])
        decode_own.append(scores[PRE:])
    decode_query = jnp.concatenate(decode_query, axis=0).astype(jnp.bfloat16)
    decode_own = jnp.concatenate(decode_own, axis=0)

    def raised(top, scores):
        for start in range(0, scores.shape[1], head_dim):
            top = jnp.maximum(top, scores[:, start : start + head_dim])
        return top

    def weigh(own, score_steps, value_steps, scores_ref):
        top = own
        for step, score_step in enumerate(score_steps):
            scores = score_step()
            scores_ref[step, :, : scores.shape[1]] = scores
            top = raised(top, scores)
        top = jnp.max(top, axis=1, keepdims=True)
        mix = jnp.dot(
            jnp.exp2(own - top).astype(jnp.bfloat16), values_new, preferred_element_type=jnp.float32
        )
        for step, value_step in enumerate(value_steps):
            values = value_step()
            weights = jnp.exp2(scores_ref[step, :, : values.shape[0]] - top).astype(jnp.bfloat16)
            mix = mix + jnp.dot(weights, with_ones(values), preferred_element_type=jnp.float32)
        return mix

    def taken(ref, names):
        return jnp.concatenate([ref[name] for name in names], axis=0)

    def against(queries, keys):
        return lax.dot_general(queries, keys, contract, preferred_element_type=jnp.float32)

    def prefill(names, live):
        def score(pages):
            scores = against(query_ref[...], taken(key_ref, pages))
            return scores if live is None else jnp.where(live, scores, -1e30)

        mix_ref[...] = weigh(
            own_scores[...],
            [functools.partial(score, pages) for pages in names],
            [functools.partial(taken, value_ref, pages) for pages in names],
            scores_ref,
        )

    def decode(steps, pages_of):
        row_request = 1 + lax.broadcasted_iota(jnp.int32, (heads * decodes, 1), 0) % decodes
        width = slots_ref.shape[2]

        def score(step):
            scores = against(decode_query, pages_of(key_ref, step))
            owner = owner_ref[:, step * width : (step + 1) * width]
            return jnp.where(owner == row_request, scores, -1e30)

        mix = weigh(
            decode_own,
            [functools.partial(score, step) for step in range(steps)],
            [functools.partial(pages_of, value_ref, step) for step in range(steps)],
            slots_ref,
        )
        decoded_ref[...] = mix[:, :head_dim] / mix[:, head_dim:]

    length = length_ref[0]
    listed = slots_ref.shape[2] // PAGE
    pages = scores_ref.shape[2] // PAGE

    @pl.when(length > SHORT_PG * PAGE)
    def _():
        names = [table_ref[0, entry] for entry in range(MAXPG)]
        prefill([names[first : first + pages] for first in range(0, MAXPG, pages)], None)
        decode(
            SHORT_LIST // listed,
            lambda ref, step: taken(ref, [list_ref[step * listed + i] for i in range(listed)]),
        )

    @pl.when(length <= SHORT_PG * PAGE)
    def _():
        column = lax.broadcasted_iota(jnp.int32, (1, SHORT_PG * PAGE), 1)
        prefill([[table_ref[0, entry] for entry in range(SHORT_PG)]], column < length)
        decode(
            POOL // listed,
            lambda ref, step: ref[step * listed : (step + 1) * listed].reshape(-1, head_dim),
        )

    for head in range(heads):
        part = mix_ref[head * tokens : (head + 1) * tokens, :]
        columns = slice(head * head_dim, (head + 1) * head_dim)
        mixed_ref[:, columns] = part[:, :head_dim] / part[:, head_dim:]
        mixed_ref[PRE:, columns] = decoded_ref[head * decodes : (head + 1) * decodes]
    part_ref[...] = jnp.dot(
        mixed_ref[...].astype(jnp.bfloat16), o_ref[...], preferred_element_type=jnp.float32
    )
    share_rows = keep_out.shape[0]

    def quarter(step):
        return pl.ds(pl.multiple_of((tp_index ^ step) * share_rows, share_rows), share_rows)

    keep_out[...] = part_ref[quarter(0), :] + x_ref[quarter(0), :].astype(jnp.float32)
    far_out[...] = part_ref[quarter(2), :]
    core_out[0] = part_ref[quarter(1), :].astype(jnp.bfloat16)
    core_out[1] = part_ref[quarter(3), :].astype(jnp.bfloat16)


def attention_shares(
    hidden_in, norm_in_gain, q_weight, k_weight, v_weight, q_gain, k_gain, o_weight,
    key_pages, value_pages, page_table, cache_len,
):
    tokens, width = hidden_in.shape[0], 4 * hidden_in.shape[1]
    head_dim = q_gain.shape[0]
    rows = q_weight.shape[1] // head_dim * tokens
    decode_rows = rows // tokens * (tokens - PRE)
    half = ROPE_BASE ** (-np.arange(head_dim // 2) / (head_dim // 2))
    frequency = jnp.asarray(np.concatenate([half, half])[None, :], jnp.float32)
    large = (
        norm_in_gain[None, :], q_gain[None, :], k_gain[None, :], q_weight, k_weight, v_weight,
        key_pages[0], value_pages[0], o_weight,
    )
    scalars = (cache_len, page_table)
    sources = [
        pltpu.with_memory_space_constraint(array, pltpu.HBM)
        for array in (*scalars, frequency, *large)
    ]
    rope = pltpu.VMEM((tokens, head_dim), jnp.float32)
    *staged, page_list, lengths, table = pl.pallas_call(
        stage_kernel,
        out_shape=[rope, rope, pltpu.VMEM((1, POOL * PAGE), jnp.int32)]
        + [pltpu.VMEM(array.shape, array.dtype) for array in large]
        + [jax.ShapeDtypeStruct((POOL,), jnp.int32)]
        + [jax.ShapeDtypeStruct(array.shape, array.dtype) for array in scalars],
        in_specs=[pl.BlockSpec(memory_space=pltpu.HBM)] * 12,
        out_specs=[VMEM] * 12 + [SMEM] * 3,
        scratch_shapes=[
            pltpu.VMEM(frequency.shape, frequency.dtype),
            pltpu.SMEM((2, POOL), jnp.int32),
            pltpu.SemaphoreType.DMA((12,)),
        ],
        compiler_params=pltpu.CompilerParams(vmem_limit_bytes=4 * 1024 * 1024),
        name="stage",
    )(*sources)
    far, *staged = ordered(flip(hidden_in, "tp", 2), *staged, page_list, lengths, table)
    pieces = (hidden_in, flip(hidden_in, "tp", 1), far, flip(far, "tp", 1))
    share = (tokens // 4, width)
    score_pages, list_pages = 4, 8
    return pl.pallas_call(
        attention_kernel,
        out_shape=[
            jax.ShapeDtypeStruct(share, jnp.float32),
            jax.ShapeDtypeStruct(share, jnp.float32),
            jax.ShapeDtypeStruct((2, *share), jnp.bfloat16),
        ],
        in_specs=[VMEM] * 16 + [SMEM] * 3,
        out_specs=[VMEM] * 3,
        scratch_shapes=[
            pltpu.VMEM((tokens, width), jnp.bfloat16),
            pltpu.VMEM((rows, head_dim), jnp.bfloat16),
            pltpu.VMEM((rows, tokens), jnp.float32),
            pltpu.VMEM((MAXPG // score_pages, rows, score_pages * PAGE), jnp.float32),
            pltpu.VMEM((rows, 2 * head_dim), jnp.float32),
            pltpu.VMEM((tokens, q_weight.shape[1]), jnp.float32),
            pltpu.VMEM((tokens, width), jnp.float32),
            pltpu.VMEM((POOL // list_pages, decode_rows, list_pages * PAGE), jnp.float32),
            pltpu.VMEM((decode_rows, head_dim), jnp.float32),
        ],
        compiler_params=pltpu.CompilerParams(vmem_limit_bytes=24 * 1024 * 1024),
        name="attention",
    )(*pieces, *staged)


def pack_kernel(
    own_ref, far_ref, gain_ref, ids_ref, routes_ref,
    rows_ref, residual_ref, spread_ref,
):
    tp_index = lax.axis_index("tp")
    share_rows, width = own_ref.shape
    mine = pl.ds(pl.multiple_of(tp_index * share_rows, share_rows), share_rows)
    residual = own_ref[...] + far_ref[...].astype(jnp.float32)
    residual_ref[...] = residual
    rows_ref[:, :width] = rms_scale(residual, gain_ref[...]).astype(jnp.bfloat16)
    expert = lax.broadcasted_iota(jnp.int32, (LANES, spread_ref.shape[0]), 0) % (LANES // 2)
    spread = jnp.zeros(expert.shape, jnp.float32)
    for k in range(ids_ref.shape[0]):
        spread = spread + jnp.where(expert == ids_ref[k : k + 1, :], routes_ref[k : k + 1, :], 0.0)
    spread_ref[...] = spread.T
    spread = spread_ref[mine, :]
    lane = lax.broadcasted_iota(jnp.int32, spread.shape, 1)
    high = spread.astype(jnp.bfloat16).astype(jnp.float32)
    rows_ref[:, width:] = jnp.where(lane < LANES // 2, high, spread - high).astype(jnp.bfloat16)


def experts_kernel(plan, residuals, *refs):
    pieces, residual_refs = refs[: len(plan)], refs[len(plan) : len(plan) + residuals]
    gate_ref, up_ref, down_ref, keep_ref, *send_refs, rows_ref, sums_ref = refs[len(plan) + residuals :]
    req_index, tp_index = lax.axis_index("req"), lax.axis_index("tp")
    columns, _, levels, group_rows, share_width = keep_ref.shape
    width = gate_ref.shape[1]
    units = gate_ref.shape[0] // 2
    for (column, step, first), piece in zip(plan, pieces):
        count = piece.shape[1]
        for level in range(levels):
            start = (column * levels + level) * group_rows + first
            start = start + (tp_index ^ step) * (group_rows // 4)
            rows_ref[pl.ds(pl.multiple_of(start, count), count), :] = piece[level]
    spread = rows_ref[:, width:].astype(jnp.float32)
    lane = lax.broadcasted_iota(jnp.int32, spread.shape, 1) % (LANES // 2)
    weights = [
        jnp.sum(jnp.where(lane == 2 * req_index + e, spread, 0.0), axis=1, keepdims=True)
        for e in range(2)
    ]
    contract = (((1,), (1,)), ((), ()))
    rows = rows_ref[:, :width]
    gate = lax.dot_general(rows, gate_ref[...], contract, preferred_element_type=jnp.float32)
    up = lax.dot_general(rows, up_ref[...], contract, preferred_element_type=jnp.float32)
    unit = lax.broadcasted_iota(jnp.int32, gate.shape, 1)
    weight = jnp.where(unit < units, weights[0], weights[1])
    acts = (gate / (1.0 + jnp.exp(-gate)) * up * weight).astype(jnp.bfloat16)
    for step in range(4):
        start = pl.multiple_of((tp_index ^ step) * share_width, share_width)
        part = jnp.dot(
            acts, down_ref[:, pl.ds(start, share_width)], preferred_element_type=jnp.float32
        )
        for residual_ref in residual_refs:
            count = residual_ref.shape[0]
            mine = pl.ds(pl.multiple_of(tp_index * count, count), count)
            sums_ref[...] = part
            sums_ref[mine, :] += residual_ref[:, pl.ds(start, share_width)]
            part = sums_ref[...]
        part = part.reshape(columns, levels, group_rows, share_width)
        if step % 2:
            send_refs[step // 2][...] = part.astype(jnp.bfloat16)
            continue
        for column in range(columns):
            keep_ref[column, step // 2] = part[column]


def run_experts(pieces, weights, group_rows, *residual):
    plan = tuple(place for place, _ in pieces)
    pieces = [piece for _, piece in pieces]
    columns, levels, packed = 1 + max(place[0] for place in plan), *pieces[0].shape[::2]
    rows, share_width = columns * levels * group_rows, weights[2].shape[1] // 4
    sums = (levels, group_rows, share_width)
    keep, *send = pl.pallas_call(
        functools.partial(experts_kernel, plan, len(residual)),
        out_shape=[jax.ShapeDtypeStruct((columns, 2, *sums), jnp.float32)]
        + [jax.ShapeDtypeStruct((columns, *sums), jnp.bfloat16)] * 2,
        in_specs=[VMEM] * (len(pieces) + len(residual) + 3),
        out_specs=[VMEM] * 3,
        scratch_shapes=[
            pltpu.VMEM((rows, packed), jnp.bfloat16),
            pltpu.VMEM((rows, share_width), jnp.float32),
        ],
        compiler_params=pltpu.CompilerParams(vmem_limit_bytes=VMEM_LIMIT),
        name="experts",
    )(*pieces, *residual, *weights)
    return keep, send


def ordered(*values):
    return lax.optimization_barrier(values)


def across_parts(line_x, line_y):
    half = line_x.shape[1] // 2
    return flip(line_x[:, :half], "tp", 2), flip(line_y[:, half:], "req", 1)


def other_core(parts):
    return tuple(flip(part, "tp", 1) for part in parts)


def with_core(pair):
    return pair[0], list(other_core(pair[1]))


def joined(pair, column, y):
    return pair[0][column, y] + pair[1][y][column].astype(jnp.float32)


def near_pieces(column, line, core):
    return [((column, 0, 0), line), ((column, 1, 0), core)]


def far_pieces(column, parts, cores):
    half = parts[0].shape[1]
    if len(parts) == 1:
        return [((column, 2, 0), parts[0]), ((column, 3, 0), cores[0])]
    return [((column, 2, i * half), part) for i, part in enumerate(parts)] + [
        ((column, 3, i * half), part) for i, part in enumerate(cores)
    ]


def relayed(side):
    part = side.astype(jnp.bfloat16)
    half = part.shape[1] // 2
    return flip(part[:, :half], "req", 1), flip(part[:, half:], "tp", 2)


def with_lower(sums, part):
    half = part.shape[1]
    sums = [sums[:, :half] + part.astype(jnp.float32), sums[:, half:]]
    return jnp.concatenate(sums, axis=1).astype(jnp.bfloat16)


def with_upper(sums, part):
    half = part.shape[1]
    sums = [sums[:, :half], sums[:, half:] + part.astype(jnp.float32)]
    return jnp.concatenate(sums, axis=1).astype(jnp.bfloat16)


def neighbours(to_x, to_y, by_x, by_y):
    return flip(with_upper(to_x, by_y), "req", 1), flip(with_lower(to_y, by_x), "tp", 2)


def moe_dense(
    kept,
    far,
    core,
    norm_post_gain,
    expert_ids,
    route_weights,
    gate_weight,
    up_weight,
    down_weight,
):
    share_rows, width = kept.shape
    token_count, share_width = 4 * share_rows, width // 4
    core = flip(core, "tp", 1)
    far, kept, core = ordered((far + core[1].astype(jnp.float32)).astype(jnp.bfloat16), kept, core)
    kept, far = ordered(kept + core[0].astype(jnp.float32), flip(far, "tp", 2))
    rows, residual = pl.pallas_call(
        pack_kernel,
        out_shape=[
            jax.ShapeDtypeStruct((share_rows, width + LANES), jnp.bfloat16),
            jax.ShapeDtypeStruct((share_rows, width), jnp.float32),
        ],
        in_specs=[VMEM] * 5,
        out_specs=[VMEM] * 2,
        scratch_shapes=[pltpu.VMEM((token_count, LANES), jnp.float32)],
        compiler_params=pltpu.CompilerParams(vmem_limit_bytes=8 * 1024 * 1024),
        name="pack_rows",
    )(kept, far, norm_post_gain[None, :], expert_ids.T, route_weights.T)
    gate_up = [w.transpose(0, 2, 1).reshape(-1, width) for w in (gate_weight, up_weight)]
    weights = (*gate_up, down_weight.reshape(-1, width))
    line_0 = rows[None]
    z_1, z_2 = flip(line_0, "req", 2), flip(line_0, "req", 4)
    y_0, x_0 = flip(line_0, "tp", 2), flip(line_0, "req", 1)
    line_12, z_2, y_0, x_0 = ordered(jnp.concatenate([z_1, z_2]), z_2, y_0, x_0)
    line_3, across_0, core_0, y_core_0 = ordered(
        jnp.concatenate([line_12, flip(z_2, "req", 2)]),
        across_parts(x_0, y_0),
        flip(line_0, "tp", 1),
        flip(y_0, "tp", 1),
    )
    y_3, x_3 = flip(line_3, "tp", 2), flip(line_3, "req", 1)
    x_core_0, across_core_0, core_3, y_3, x_3 = ordered(
        flip(x_0, "tp", 1), other_core(across_0), flip(line_3, "tp", 1), y_3, x_3
    )
    all_0 = run_experts(
        near_pieces(0, line_0, core_0)
        + far_pieces(0, (y_0,), (y_core_0,))
        + near_pieces(1, x_0, x_core_0)
        + far_pieces(1, across_0, across_core_0),
        weights,
        token_count,
        residual,
    )
    x_core_3, y_core_3, all_0, across_3 = ordered(
        *other_core((x_3, y_3)), all_0, jnp.concatenate(across_parts(x_3, y_3), axis=1)
    )
    side_3 = run_experts(
        near_pieces(0, x_3, x_core_3) + far_pieces(0, (across_3,), (flip(across_3, "tp", 1),)),
        weights,
        token_count,
    )
    y_core_3, all_0, (keep, (send, first)) = ordered(y_core_3, all_0, side_3)
    all_0, y_core_3, keep, send, first = ordered(all_0, y_core_3, keep, send, flip(first, "tp", 1))
    diagonal, keep, send = ordered(joined((keep, (send, first)), 0, 1).astype(jnp.bfloat16), keep, send)
    by_x, by_y = relayed(diagonal)
    near_keep, (near_send, near_first) = run_experts(
        near_pieces(0, line_3, core_3) + far_pieces(0, (y_3,), (y_core_3,)), weights, token_count
    )
    send = flip(send, "tp", 1)
    all_0, near_keep, near_send, near_first, by_x, to_x = ordered(
        all_0,
        near_keep,
        near_send,
        flip(near_first, "tp", 1),
        by_x.astype(jnp.float32),
        with_upper(joined((keep, (send, first)), 0, 0), by_y),
    )
    to_y = with_lower(joined((near_keep, (near_send, near_first)), 0, 1), by_x)
    sums_3 = flip(to_x, "req", 1).astype(jnp.float32) + flip(to_y, "tp", 2).astype(jnp.float32)
    all_0, near_send, sums_3 = ordered(with_core(all_0), flip(near_send, "tp", 1), sums_3)
    sent = joined((near_keep, (near_send, near_first)), 0, 0) + sums_3
    sent_3, relay_0 = ordered(
        flip(sent[2].astype(jnp.bfloat16), "req", 2), relayed(joined(all_0, 1, 1))
    )
    sent_2, relay_0 = ordered(
        (sent[1] + sent_3.astype(jnp.float32)).astype(jnp.bfloat16), relay_0
    )
    from_z = [flip(sent[0].astype(jnp.bfloat16), "req", 2), flip(sent_2, "req", 4)]
    sums_0 = neighbours(joined(all_0, 1, 0), joined(all_0, 0, 1), *relay_0)
    total = joined(all_0, 0, 0) + from_z[0].astype(jnp.float32) + from_z[1].astype(jnp.float32)
    total, from_x, from_y = ordered(total[0], *sums_0)
    return (total + from_x[0].astype(jnp.float32) + from_y[0].astype(jnp.float32)).astype(jnp.bfloat16)


def moe_routed(
    x_full,
    head_part,
    norm_post_gain,
    expert_ids,
    route_weights,
    gate_weight,
    up_weight,
    down_weight,
):
    req_count = lax.axis_size("req")
    tp_index = lax.axis_index("tp")
    x_float = x_full.astype(jnp.float32)
    token_count = x_float.shape[0]
    share_width = x_float.shape[1] // lax.axis_size("tp")
    top_count = expert_ids.shape[1]
    expert_count = gate_weight.shape[0] * req_count
    capacity = max(2, 3 * token_count * top_count // (2 * expert_count))
    flat_expert = expert_ids.reshape(token_count * top_count)
    one_hot = (flat_expert[:, None] == jnp.arange(expert_count, dtype=jnp.int32)[None, :]).astype(
        jnp.int32
    )
    slot_rank = jnp.sum((jnp.cumsum(one_hot, axis=0) - one_hot) * one_hot, axis=1)
    slot_index = flat_expert * capacity + slot_rank
    head_sum = lax.psum(head_part.astype(jnp.bfloat16), "tp").astype(jnp.float32)
    residual_full = x_float + head_sum
    normed_post = rms_scale(residual_full, norm_post_gain).astype(jnp.bfloat16)
    residual = lax.dynamic_slice_in_dim(residual_full, tp_index * share_width, share_width, 1)
    send_buffer = build_buffer(normed_post, slot_index, top_count, expert_count, capacity)
    part_sums = expert_apply(
        lax.all_to_all(send_buffer, "req", split_axis=0, concat_axis=0, tiled=True),
        gate_weight,
        up_weight,
        down_weight,
    )
    returned = lax.all_to_all(part_sums, "req", split_axis=0, concat_axis=0, tiled=True)
    moe_term = weigh_back(returned, slot_index, route_weights, token_count, top_count)
    moe_share = lax.psum_scatter(
        moe_term.astype(jnp.bfloat16), "tp", scatter_dimension=1, tiled=True
    ).astype(jnp.float32)
    return (residual + moe_share).astype(jnp.bfloat16)


def attention_part(
    x_full,
    norm_in_gain,
    q_weight,
    k_weight,
    v_weight,
    q_gain,
    k_gain,
    o_weight,
    key_pages,
    value_pages,
    page_table,
    cache_len,
):
    head_dim = q_gain.shape[0]
    kv_local = key_pages.shape[0]
    group_size = q_weight.shape[1] // head_dim // kv_local
    token_count = x_full.shape[0]
    x_float = x_full.astype(jnp.float32)
    normed_in = rms_scale(x_float, norm_in_gain).astype(jnp.bfloat16)
    query_lin = jnp.dot(normed_in, q_weight, preferred_element_type=jnp.float32).reshape(
        token_count, kv_local * group_size, head_dim
    )
    key_lin = jnp.dot(normed_in, k_weight, preferred_element_type=jnp.float32).reshape(
        token_count, kv_local, head_dim
    )
    values_new = (
        jnp.dot(normed_in, v_weight, preferred_element_type=jnp.float32)
        .astype(jnp.bfloat16)
        .reshape(token_count, kv_local, head_dim)
    )
    requests, positions = token_layout(cache_len)
    queries = (
        rotate(rms_scale(query_lin, q_gain), positions)
        .astype(jnp.bfloat16)
        .reshape(token_count, kv_local, group_size, head_dim)
    )
    keys_new = rotate(rms_scale(key_lin, k_gain), positions).astype(jnp.bfloat16)
    slot_owner = page_slots(page_table, cache_len)
    cache_slots = key_pages.shape[1] * key_pages.shape[2]
    keys_cache = key_pages.reshape(kv_local, cache_slots, head_dim)
    values_cache = value_pages.reshape(kv_local, cache_slots, head_dim)
    attended = attend(
        queries, keys_new, values_new, keys_cache, values_cache, requests, positions, slot_owner
    )
    return jnp.dot(attended, o_weight, preferred_element_type=jnp.float32)


def body(
    hidden_in,
    norm_in_gain,
    q_weight,
    k_weight,
    v_weight,
    q_gain,
    k_gain,
    o_weight,
    key_pages,
    value_pages,
    page_table,
    cache_len,
    norm_post_gain,
    expert_ids,
    route_weights,
    gate_weight,
    up_weight,
    down_weight,
):
    req_count = lax.axis_size("req")
    attention = (
        norm_in_gain,
        q_weight,
        k_weight,
        v_weight,
        q_gain,
        k_gain,
        o_weight,
        key_pages,
        value_pages,
        page_table,
        cache_len,
    )
    experts = (norm_post_gain, expert_ids, route_weights, gate_weight, up_weight, down_weight)
    expert_count = gate_weight.shape[0] * req_count
    staged = (req_count, lax.axis_size("tp"), gate_weight.shape[0]) == (8, 4, 2)
    if staged and expert_count <= LANES // 2:
        return moe_dense(*attention_shares(hidden_in, *attention), *experts)
    x_full = lax.all_gather(hidden_in, "tp", axis=1, tiled=True)
    return moe_routed(x_full, attention_part(x_full, *attention), *experts)


def solution(mesh):
    return jax.shard_map(
        body,
        mesh=mesh,
        in_specs=(
            P("req", "tp"),
            P(),
            P(None, "tp"),
            P(None, "tp"),
            P(None, "tp"),
            P(),
            P(),
            P("tp", None),
            P("tp", "req", None, None),
            P("tp", "req", None, None),
            P("req", None),
            P("req"),
            P(),
            P("req", None),
            P("req", None),
            P("req", None, "tp"),
            P("req", None, "tp"),
            P("req", "tp", None),
        ),
        out_specs=P("req", "tp"),
        check_vma=False,
    )
```

```python
import functools
import math

import jax
import jax.numpy as jnp
import numpy as np
from jax import lax
from jax.experimental import pallas as pl
from jax.experimental.pallas import tpu as pltpu
from jax.sharding import PartitionSpec as P

PAGE = 128
MAXPG = 32
PRE = 120
TOK_DEV = 128
REQS_DEV = 9
POOL = 48
SHORT_PG = 2
SHORT_LIST = (REQS_DEV - 1) * SHORT_PG


NORM_EPS = 1e-06
ROPE_BASE = 1000000.0


def rms_scale(values, gain_vec):
    mean_square = jnp.mean(values * values, axis=-1, keepdims=True)
    return values * lax.rsqrt(mean_square + NORM_EPS) * gain_vec


def rotate(values, positions):
    half_dim = values.shape[-1] // 2
    exponent = jnp.arange(half_dim, dtype=jnp.float32) * (2.0 / values.shape[-1])
    frequency = jnp.power(jnp.float32(ROPE_BASE), -exponent)
    angles = positions.astype(jnp.float32)[:, None] * frequency[None, :]
    cosine = jnp.cos(angles)[:, None, :]
    sine_val = jnp.sin(angles)[:, None, :]
    front_half = values[..., :half_dim]
    back_half = values[..., half_dim:]
    return jnp.concatenate(
        [front_half * cosine - back_half * sine_val, back_half * cosine + front_half * sine_val],
        axis=-1,
    )


def token_layout(lengths):
    local_idx = jnp.arange(TOK_DEV, dtype=jnp.int32)
    requests = jnp.where(local_idx < PRE, 0, local_idx - PRE + 1)
    offsets = jnp.where(local_idx < PRE, local_idx, 0)
    request_hot = (requests[:, None] == jnp.arange(REQS_DEV, dtype=jnp.int32)[None, :]).astype(
        jnp.int32
    )
    positions = jnp.sum(request_hot * lengths[None, :], axis=1) + offsets
    return (requests, positions)


def page_slots(table, lengths):
    pages_used = (lengths + PAGE - 1) // PAGE
    entry_live = jnp.arange(MAXPG, dtype=jnp.int32)[None, :] < pages_used[:, None]
    page_match = (
        (table[:, :, None] == jnp.arange(POOL, dtype=jnp.int32)[None, None, :])
        & entry_live[:, :, None]
    ).astype(jnp.int32)
    page_owner = jnp.sum(
        page_match * jnp.arange(REQS_DEV, dtype=jnp.int32)[:, None, None], axis=(0, 1)
    )
    page_start = jnp.sum(
        page_match * (jnp.arange(MAXPG, dtype=jnp.int32) * PAGE)[None, :, None], axis=(0, 1)
    )
    page_used = jnp.sum(page_match, axis=(0, 1)) > 0
    owner_length = jnp.sum(page_match * lengths[:, None, None], axis=(0, 1))
    slot_pos = page_start[:, None] + jnp.arange(PAGE, dtype=jnp.int32)[None, :]
    slot_live = page_used[:, None] & (slot_pos < owner_length[:, None])
    slot_owner = jnp.where(slot_live, page_owner[:, None], -1)
    return slot_owner.reshape(POOL * PAGE)


def attend(
    queries, keys_new, values_new, keys_cache, values_cache, requests, positions, slot_owner
):
    inv_root = 1.0 / math.sqrt(queries.shape[-1])
    cache_mask = slot_owner[None, :] == requests[:, None]
    new_mask = (requests[None, :] == requests[:, None]) & (positions[None, :] <= positions[:, None])
    score_cache = (
        jnp.einsum("tkgh,knh->kgtn", queries, keys_cache, preferred_element_type=jnp.float32)
        * inv_root
    )
    score_new = (
        jnp.einsum("tkgh,skh->kgts", queries, keys_new, preferred_element_type=jnp.float32)
        * inv_root
    )
    score_cache = jnp.where(cache_mask[None, None], score_cache, -1e30)
    score_new = jnp.where(new_mask[None, None], score_new, -1e30)
    row_max = jnp.maximum(
        jnp.max(score_cache, axis=-1, keepdims=True), jnp.max(score_new, axis=-1, keepdims=True)
    )
    exp_cache = jnp.where(cache_mask[None, None], jnp.exp(score_cache - row_max), 0.0)
    exp_new = jnp.where(new_mask[None, None], jnp.exp(score_new - row_max), 0.0)
    total = jnp.sum(exp_cache, axis=-1, keepdims=True) + jnp.sum(exp_new, axis=-1, keepdims=True)
    prob_cache = (exp_cache / total).astype(jnp.bfloat16)
    prob_new = (exp_new / total).astype(jnp.bfloat16)
    mixed = jnp.einsum(
        "kgtn,knh->tkgh", prob_cache, values_cache, preferred_element_type=jnp.float32
    )
    mixed = mixed + jnp.einsum(
        "kgts,skh->tkgh", prob_new, values_new, preferred_element_type=jnp.float32
    )
    return mixed.astype(jnp.bfloat16).reshape(queries.shape[0], -1)


def expert_apply(blocks, gate_weight, up_weight, down_weight):
    local_experts = gate_weight.shape[0]
    sources = blocks.shape[0] // local_experts
    slot_count = blocks.shape[1]
    grouped = blocks.reshape(sources, local_experts, slot_count, blocks.shape[2])
    gate_acts = jnp.einsum(
        "sekd,edf->sekf", grouped, gate_weight, preferred_element_type=jnp.float32
    )
    up_acts = jnp.einsum("sekd,edf->sekf", grouped, up_weight, preferred_element_type=jnp.float32)
    hidden_act = (jax.nn.silu(gate_acts) * up_acts).astype(jnp.bfloat16)
    part_sums = jnp.einsum(
        "sekf,efd->sekd", hidden_act, down_weight, preferred_element_type=jnp.float32
    ).astype(jnp.bfloat16)
    return part_sums.reshape(sources * local_experts, slot_count, part_sums.shape[3])


def build_buffer(normed, slot_index, top_count, expert_count, capacity):
    picked = jnp.repeat(normed, top_count, axis=0)
    buffer_rows = (
        jnp.zeros((expert_count * capacity, normed.shape[1]), normed.dtype)
        .at[slot_index]
        .set(picked)
    )
    return buffer_rows.reshape(expert_count, capacity, normed.shape[1])


def weigh_back(returned, slot_index, route_weights, token_count, top_count):
    row_width = returned.shape[2]
    back_rows = returned.reshape(returned.shape[0] * returned.shape[1], row_width)[slot_index]
    weighted = (
        back_rows.astype(jnp.float32) * route_weights.reshape(token_count * top_count)[:, None]
    )
    return jnp.sum(weighted.reshape(token_count, top_count, row_width), axis=1)


LANES = 128
VMEM = pl.BlockSpec(memory_space=pltpu.VMEM)
SMEM = pl.BlockSpec(memory_space=pltpu.SMEM)
VMEM_LIMIT = 24 * 1024 * 1024


def flip(value, axis, bits):
    return lax.ppermute(value, axis, [(i, i ^ bits) for i in range(lax.axis_size(axis))])


def stage_kernel(*refs):
    length_hbm, table_hbm, frequency_hbm, *large = refs[:12]
    cosine_ref, sine_ref, owner_ref, *staged = refs[12:24]
    list_ref, length_out, table_out = refs[24:27]
    frequency_ref, owners, sems = refs[27:]
    length_ref, table_ref = length_out, table_out
    sources = (length_hbm, table_hbm, frequency_hbm, *large)
    targets = (length_out, table_out, frequency_ref, *staged)
    copies = [
        pltpu.make_async_copy(source, target, sems.at[i])
        for i, (source, target) in enumerate(zip(sources, targets))
    ]
    for copy in copies:
        copy.start()
    for copy in copies[:3]:
        copy.wait()
    tokens, head_dim = cosine_ref.shape
    for entry in range(POOL):
        list_ref[entry] = 0
        owners[0, entry] = -1
        owners[1, entry] = 0
    prefill_long = length_ref[0] > SHORT_PG * PAGE
    count = jnp.int32(0)
    for request in range(1, REQS_DEV):

        def name_page(entry, count):
            page = table_ref[request, entry]
            place = jnp.where(prefill_long, count, page)
            list_ref[place] = page
            owners[0, place] = request
            owners[1, place] = jnp.minimum(length_ref[request] - entry * PAGE, PAGE)
            return count + 1

        count = lax.fori_loop(0, (length_ref[request] + PAGE - 1) // PAGE, name_page, count)
    slot = lax.broadcasted_iota(jnp.int32, (1, PAGE), 1)
    for entry in range(POOL):
        owner_ref[:, entry * PAGE : (entry + 1) * PAGE] = jnp.where(
            slot < owners[1, entry], owners[0, entry], -1
        )
    token = lax.broadcasted_iota(jnp.int32, (tokens, head_dim), 0)
    lane = lax.broadcasted_iota(jnp.int32, (tokens, head_dim), 1)
    position = length_ref[0] + token
    for i in range(tokens - PRE):
        position = jnp.where(token == PRE + i, length_ref[i + 1], position)
    angle = position.astype(jnp.float32) * frequency_ref[...]
    sine = jnp.sin(angle)
    cosine_ref[...] = jnp.cos(angle)
    sine_ref[...] = jnp.where(lane < head_dim // 2, -sine, sine)
    for copy in copies[3:]:
        copy.wait()


def attention_kernel(*refs):
    pieces, (keep_out, far_out, core_out) = refs[:4], refs[19:22]
    (cosine_ref, sine_ref, owner_ref, gain_ref, q_gain_ref, k_gain_ref) = refs[4:10]
    (q_ref, k_ref, v_ref, key_ref, value_ref, o_ref, list_ref, length_ref, table_ref) = refs[10:19]
    (
        x_ref, query_ref, own_scores, scores_ref, mix_ref, mixed_ref, part_ref, slots_ref, decoded_ref,
    ) = refs[22:]
    tokens, head_dim = x_ref.shape[0], k_gain_ref.shape[1]
    tp_index = lax.axis_index("tp")
    heads = q_ref.shape[1] // head_dim
    decodes = tokens - PRE
    for step, piece in enumerate(pieces):
        width = piece.shape[1]
        start = pl.multiple_of((tp_index ^ step) * width, width)
        x_ref[:, pl.ds(start, width)] = piece[...]
    token = lax.broadcasted_iota(jnp.int32, (tokens, head_dim), 0)
    lane = lax.broadcasted_iota(jnp.int32, (tokens, head_dim), 1)

    def turned(values, gain):
        values = rms_scale(values, gain)
        return values * cosine_ref[...] + pltpu.roll(values, head_dim // 2, 1) * sine_ref[...]

    def with_ones(values):
        return jnp.concatenate([values, jnp.ones_like(values)], axis=1)

    normed = rms_scale(x_ref[...].astype(jnp.float32), gain_ref[...]).astype(jnp.bfloat16)
    contract = (((1,), (1,)), ((), ()))
    key_lin = jnp.dot(normed, k_ref[...], preferred_element_type=jnp.float32)
    values_new = jnp.dot(normed, v_ref[...], preferred_element_type=jnp.float32).astype(jnp.bfloat16)
    query_lin = jnp.dot(normed, q_ref[...], preferred_element_type=jnp.float32)
    keys_new = turned(key_lin, k_gain_ref[...]).astype(jnp.bfloat16)
    values_new = with_ones(values_new)
    to_log2 = math.log2(math.e) / math.sqrt(head_dim)
    own_mask = (lane == token) | ((lane < token) & (token < PRE))
    decode_query, decode_own = [], []
    for head in range(heads):
        span = slice(head * tokens, (head + 1) * tokens)
        query = turned(query_lin[:, head * head_dim : (head + 1) * head_dim], q_gain_ref[...]) * to_log2
        rounded = query.astype(jnp.bfloat16)
        query_ref[span, :] = rounded
        scores = lax.dot_general(rounded, keys_new, contract, preferred_element_type=jnp.float32)
        scores = jnp.where(own_mask, scores, -1e30)
        own_scores[span, :] = scores
        decode_query.append(query[PRE:])
        decode_own.append(scores[PRE:])
    decode_query = jnp.concatenate(decode_query, axis=0).astype(jnp.bfloat16)
    decode_own = jnp.concatenate(decode_own, axis=0)

    def raised(top, scores):
        for start in range(0, scores.shape[1], head_dim):
            top = jnp.maximum(top, scores[:, start : start + head_dim])
        return top

    def weigh(own, score_steps, value_steps, scores_ref):
        top = own
        for step, score_step in enumerate(score_steps):
            scores = score_step()
            scores_ref[step, :, : scores.shape[1]] = scores
            top = raised(top, scores)
        top = jnp.max(top, axis=1, keepdims=True)
        mix = jnp.dot(
            jnp.exp2(own - top).astype(jnp.bfloat16), values_new, preferred_element_type=jnp.float32
        )
        for step, value_step in enumerate(value_steps):
            values = value_step()
            weights = jnp.exp2(scores_ref[step, :, : values.shape[0]] - top).astype(jnp.bfloat16)
            mix = mix + jnp.dot(weights, with_ones(values), preferred_element_type=jnp.float32)
        return mix

    def taken(ref, names):
        return jnp.concatenate([ref[name] for name in names], axis=0)

    def against(queries, keys):
        return lax.dot_general(queries, keys, contract, preferred_element_type=jnp.float32)

    def prefill(names, live):
        def score(pages):
            scores = against(query_ref[...], taken(key_ref, pages))
            return scores if live is None else jnp.where(live, scores, -1e30)

        mix_ref[...] = weigh(
            own_scores[...],
            [functools.partial(score, pages) for pages in names],
            [functools.partial(taken, value_ref, pages) for pages in names],
            scores_ref,
        )

    def decode(steps, pages_of):
        row_request = 1 + lax.broadcasted_iota(jnp.int32, (heads * decodes, 1), 0) % decodes
        width = slots_ref.shape[2]

        def score(step):
            scores = against(decode_query, pages_of(key_ref, step))
            owner = owner_ref[:, step * width : (step + 1) * width]
            return jnp.where(owner == row_request, scores, -1e30)

        mix = weigh(
            decode_own,
            [functools.partial(score, step) for step in range(steps)],
            [functools.partial(pages_of, value_ref, step) for step in range(steps)],
            slots_ref,
        )
        decoded_ref[...] = mix[:, :head_dim] / mix[:, head_dim:]

    length = length_ref[0]
    listed = slots_ref.shape[2] // PAGE
    pages = scores_ref.shape[2] // PAGE

    @pl.when(length > SHORT_PG * PAGE)
    def _():
        names = [table_ref[0, entry] for entry in range(MAXPG)]
        prefill([names[first : first + pages] for first in range(0, MAXPG, pages)], None)
        decode(
            SHORT_LIST // listed,
            lambda ref, step: taken(ref, [list_ref[step * listed + i] for i in range(listed)]),
        )

    @pl.when(length <= SHORT_PG * PAGE)
    def _():
        column = lax.broadcasted_iota(jnp.int32, (1, SHORT_PG * PAGE), 1)
        prefill([[table_ref[0, entry] for entry in range(SHORT_PG)]], column < length)
        decode(
            POOL // listed,
            lambda ref, step: ref[step * listed : (step + 1) * listed].reshape(-1, head_dim),
        )

    for head in range(heads):
        part = mix_ref[head * tokens : (head + 1) * tokens, :]
        columns = slice(head * head_dim, (head + 1) * head_dim)
        mixed_ref[:, columns] = part[:, :head_dim] / part[:, head_dim:]
        mixed_ref[PRE:, columns] = decoded_ref[head * decodes : (head + 1) * decodes]
    part_ref[...] = jnp.dot(
        mixed_ref[...].astype(jnp.bfloat16), o_ref[...], preferred_element_type=jnp.float32
    )
    share_rows = keep_out.shape[0]

    def quarter(step):
        return pl.ds(pl.multiple_of((tp_index ^ step) * share_rows, share_rows), share_rows)

    keep_out[...] = part_ref[quarter(0), :] + x_ref[quarter(0), :].astype(jnp.float32)
    far_out[...] = part_ref[quarter(2), :]
    core_out[0] = part_ref[quarter(1), :].astype(jnp.bfloat16)
    core_out[1] = part_ref[quarter(3), :].astype(jnp.bfloat16)


def attention_shares(
    hidden_in, norm_in_gain, q_weight, k_weight, v_weight, q_gain, k_gain, o_weight,
    key_pages, value_pages, page_table, cache_len,
):
    tokens, width = hidden_in.shape[0], 4 * hidden_in.shape[1]
    head_dim = q_gain.shape[0]
    rows = q_weight.shape[1] // head_dim * tokens
    decode_rows = rows // tokens * (tokens - PRE)
    half = ROPE_BASE ** (-np.arange(head_dim // 2) / (head_dim // 2))
    frequency = jnp.asarray(np.concatenate([half, half])[None, :], jnp.float32)
    large = (
        norm_in_gain[None, :], q_gain[None, :], k_gain[None, :], q_weight, k_weight, v_weight,
        key_pages[0], value_pages[0], o_weight,
    )
    scalars = (cache_len, page_table)
    sources = [
        pltpu.with_memory_space_constraint(array, pltpu.HBM)
        for array in (*scalars, frequency, *large)
    ]
    rope = pltpu.VMEM((tokens, head_dim), jnp.float32)
    *staged, page_list, lengths, table = pl.pallas_call(
        stage_kernel,
        out_shape=[rope, rope, pltpu.VMEM((1, POOL * PAGE), jnp.int32)]
        + [pltpu.VMEM(array.shape, array.dtype) for array in large]
        + [jax.ShapeDtypeStruct((POOL,), jnp.int32)]
        + [jax.ShapeDtypeStruct(array.shape, array.dtype) for array in scalars],
        in_specs=[pl.BlockSpec(memory_space=pltpu.HBM)] * 12,
        out_specs=[VMEM] * 12 + [SMEM] * 3,
        scratch_shapes=[
            pltpu.VMEM(frequency.shape, frequency.dtype),
            pltpu.SMEM((2, POOL), jnp.int32),
            pltpu.SemaphoreType.DMA((12,)),
        ],
        compiler_params=pltpu.CompilerParams(vmem_limit_bytes=4 * 1024 * 1024),
        name="stage",
    )(*sources)
    far, *staged = ordered(flip(hidden_in, "tp", 2), *staged, page_list, lengths, table)
    pieces = (hidden_in, flip(hidden_in, "tp", 1), far, flip(far, "tp", 1))
    share = (tokens // 4, width)
    score_pages, list_pages = 8, 8
    return pl.pallas_call(
        attention_kernel,
        out_shape=[
            jax.ShapeDtypeStruct(share, jnp.float32),
            jax.ShapeDtypeStruct(share, jnp.float32),
            jax.ShapeDtypeStruct((2, *share), jnp.bfloat16),
        ],
        in_specs=[VMEM] * 16 + [SMEM] * 3,
        out_specs=[VMEM] * 3,
        scratch_shapes=[
            pltpu.VMEM((tokens, width), jnp.bfloat16),
            pltpu.VMEM((rows, head_dim), jnp.bfloat16),
            pltpu.VMEM((rows, tokens), jnp.float32),
            pltpu.VMEM((MAXPG // score_pages, rows, score_pages * PAGE), jnp.float32),
            pltpu.VMEM((rows, 2 * head_dim), jnp.float32),
            pltpu.VMEM((tokens, q_weight.shape[1]), jnp.float32),
            pltpu.VMEM((tokens, width), jnp.float32),
            pltpu.VMEM((POOL // list_pages, decode_rows, list_pages * PAGE), jnp.float32),
            pltpu.VMEM((decode_rows, head_dim), jnp.float32),
        ],
        compiler_params=pltpu.CompilerParams(vmem_limit_bytes=24 * 1024 * 1024),
        name="attention",
    )(*pieces, *staged)


def pack_kernel(
    own_ref, far_ref, gain_ref, ids_ref, routes_ref,
    rows_ref, residual_ref, spread_ref,
):
    tp_index = lax.axis_index("tp")
    share_rows, width = own_ref.shape
    mine = pl.ds(pl.multiple_of(tp_index * share_rows, share_rows), share_rows)
    residual = own_ref[...] + far_ref[...].astype(jnp.float32)
    residual_ref[...] = residual
    rows_ref[:, :width] = rms_scale(residual, gain_ref[...]).astype(jnp.bfloat16)
    expert = lax.broadcasted_iota(jnp.int32, (LANES, spread_ref.shape[0]), 0) % (LANES // 2)
    spread = jnp.zeros(expert.shape, jnp.float32)
    for k in range(ids_ref.shape[0]):
        spread = spread + jnp.where(expert == ids_ref[k : k + 1, :], routes_ref[k : k + 1, :], 0.0)
    spread_ref[...] = spread.T
    spread = spread_ref[mine, :]
    lane = lax.broadcasted_iota(jnp.int32, spread.shape, 1)
    high = spread.astype(jnp.bfloat16).astype(jnp.float32)
    rows_ref[:, width:] = jnp.where(lane < LANES // 2, high, spread - high).astype(jnp.bfloat16)


def experts_kernel(plan, residuals, *refs):
    pieces, residual_refs = refs[: len(plan)], refs[len(plan) : len(plan) + residuals]
    gate_ref, up_ref, down_ref, keep_ref, *send_refs, rows_ref, sums_ref = refs[len(plan) + residuals :]
    req_index, tp_index = lax.axis_index("req"), lax.axis_index("tp")
    columns, _, levels, group_rows, share_width = keep_ref.shape
    width = gate_ref.shape[1]
    units = gate_ref.shape[0] // 2
    for (column, step, first), piece in zip(plan, pieces):
        count = piece.shape[1]
        for level in range(levels):
            start = (column * levels + level) * group_rows + first
            start = start + (tp_index ^ step) * (group_rows // 4)
            rows_ref[pl.ds(pl.multiple_of(start, count), count), :] = piece[level]
    spread = rows_ref[:, width:].astype(jnp.float32)
    lane = lax.broadcasted_iota(jnp.int32, spread.shape, 1) % (LANES // 2)
    weights = [
        jnp.sum(jnp.where(lane == 2 * req_index + e, spread, 0.0), axis=1, keepdims=True)
        for e in range(2)
    ]
    contract = (((1,), (1,)), ((), ()))
    rows = rows_ref[:, :width]
    gate = lax.dot_general(rows, gate_ref[...], contract, preferred_element_type=jnp.float32)
    up = lax.dot_general(rows, up_ref[...], contract, preferred_element_type=jnp.float32)
    unit = lax.broadcasted_iota(jnp.int32, gate.shape, 1)
    weight = jnp.where(unit < units, weights[0], weights[1])
    acts = (gate / (1.0 + jnp.exp(-gate)) * up * weight).astype(jnp.bfloat16)
    for step in range(4):
        start = pl.multiple_of((tp_index ^ step) * share_width, share_width)
        part = jnp.dot(
            acts, down_ref[:, pl.ds(start, share_width)], preferred_element_type=jnp.float32
        )
        for residual_ref in residual_refs:
            count = residual_ref.shape[0]
            mine = pl.ds(pl.multiple_of(tp_index * count, count), count)
            sums_ref[...] = part
            sums_ref[mine, :] += residual_ref[:, pl.ds(start, share_width)]
            part = sums_ref[...]
        part = part.reshape(columns, levels, group_rows, share_width)
        if step % 2:
            send_refs[step // 2][...] = part.astype(jnp.bfloat16)
            continue
        for column in range(columns):
            keep_ref[column, step // 2] = part[column]


def run_experts(pieces, weights, group_rows, *residual):
    plan = tuple(place for place, _ in pieces)
    pieces = [piece for _, piece in pieces]
    columns, levels, packed = 1 + max(place[0] for place in plan), *pieces[0].shape[::2]
    rows, share_width = columns * levels * group_rows, weights[2].shape[1] // 4
    sums = (levels, group_rows, share_width)
    keep, *send = pl.pallas_call(
        functools.partial(experts_kernel, plan, len(residual)),
        out_shape=[jax.ShapeDtypeStruct((columns, 2, *sums), jnp.float32)]
        + [jax.ShapeDtypeStruct((columns, *sums), jnp.bfloat16)] * 2,
        in_specs=[VMEM] * (len(pieces) + len(residual) + 3),
        out_specs=[VMEM] * 3,
        scratch_shapes=[
            pltpu.VMEM((rows, packed), jnp.bfloat16),
            pltpu.VMEM((rows, share_width), jnp.float32),
        ],
        compiler_params=pltpu.CompilerParams(vmem_limit_bytes=VMEM_LIMIT),
        name="experts",
    )(*pieces, *residual, *weights)
    return keep, send


def ordered(*values):
    return lax.optimization_barrier(values)


def across_parts(line_x, line_y):
    half = line_x.shape[1] // 2
    return flip(line_x[:, :half], "tp", 2), flip(line_y[:, half:], "req", 1)


def other_core(parts):
    return tuple(flip(part, "tp", 1) for part in parts)


def with_core(pair):
    return pair[0], list(other_core(pair[1]))


def joined(pair, column, y):
    return pair[0][column, y] + pair[1][y][column].astype(jnp.float32)


def near_pieces(column, line, core):
    return [((column, 0, 0), line), ((column, 1, 0), core)]


def far_pieces(column, parts, cores):
    half = parts[0].shape[1]
    if len(parts) == 1:
        return [((column, 2, 0), parts[0]), ((column, 3, 0), cores[0])]
    return [((column, 2, i * half), part) for i, part in enumerate(parts)] + [
        ((column, 3, i * half), part) for i, part in enumerate(cores)
    ]


def relayed(side):
    part = side.astype(jnp.bfloat16)
    half = part.shape[1] // 2
    return flip(part[:, :half], "req", 1), flip(part[:, half:], "tp", 2)


def with_lower(sums, part):
    half = part.shape[1]
    sums = [sums[:, :half] + part.astype(jnp.float32), sums[:, half:]]
    return jnp.concatenate(sums, axis=1).astype(jnp.bfloat16)


def with_upper(sums, part):
    half = part.shape[1]
    sums = [sums[:, :half], sums[:, half:] + part.astype(jnp.float32)]
    return jnp.concatenate(sums, axis=1).astype(jnp.bfloat16)


def neighbours(to_x, to_y, by_x, by_y):
    return flip(with_upper(to_x, by_y), "req", 1), flip(with_lower(to_y, by_x), "tp", 2)


def moe_dense(
    kept,
    far,
    core,
    norm_post_gain,
    expert_ids,
    route_weights,
    gate_weight,
    up_weight,
    down_weight,
):
    share_rows, width = kept.shape
    token_count, share_width = 4 * share_rows, width // 4
    core = flip(core, "tp", 1)
    far, kept, core = ordered((far + core[1].astype(jnp.float32)).astype(jnp.bfloat16), kept, core)
    kept, far = ordered(kept + core[0].astype(jnp.float32), flip(far, "tp", 2))
    rows, residual = pl.pallas_call(
        pack_kernel,
        out_shape=[
            jax.ShapeDtypeStruct((share_rows, width + LANES), jnp.bfloat16),
            jax.ShapeDtypeStruct((share_rows, width), jnp.float32),
        ],
        in_specs=[VMEM] * 5,
        out_specs=[VMEM] * 2,
        scratch_shapes=[pltpu.VMEM((token_count, LANES), jnp.float32)],
        compiler_params=pltpu.CompilerParams(vmem_limit_bytes=8 * 1024 * 1024),
        name="pack_rows",
    )(kept, far, norm_post_gain[None, :], expert_ids.T, route_weights.T)
    gate_up = [w.transpose(0, 2, 1).reshape(-1, width) for w in (gate_weight, up_weight)]
    weights = (*gate_up, down_weight.reshape(-1, width))
    line_0 = rows[None]
    z_1, z_2 = flip(line_0, "req", 2), flip(line_0, "req", 4)
    y_0, x_0 = flip(line_0, "tp", 2), flip(line_0, "req", 1)
    line_12, z_2, y_0, x_0 = ordered(jnp.concatenate([z_1, z_2]), z_2, y_0, x_0)
    line_3, across_0, core_0, y_core_0 = ordered(
        jnp.concatenate([line_12, flip(z_2, "req", 2)]),
        across_parts(x_0, y_0),
        flip(line_0, "tp", 1),
        flip(y_0, "tp", 1),
    )
    y_3, x_3 = flip(line_3, "tp", 2), flip(line_3, "req", 1)
    x_core_0, across_core_0, core_3, y_3, x_3 = ordered(
        flip(x_0, "tp", 1), other_core(across_0), flip(line_3, "tp", 1), y_3, x_3
    )
    all_0 = run_experts(
        near_pieces(0, line_0, core_0)
        + far_pieces(0, (y_0,), (y_core_0,))
        + near_pieces(1, x_0, x_core_0)
        + far_pieces(1, across_0, across_core_0),
        weights,
        token_count,
        residual,
    )
    x_core_3, y_core_3, all_0, across_3 = ordered(
        *other_core((x_3, y_3)), all_0, jnp.concatenate(across_parts(x_3, y_3), axis=1)
    )
    side_3 = run_experts(
        near_pieces(0, x_3, x_core_3) + far_pieces(0, (across_3,), (flip(across_3, "tp", 1),)),
        weights,
        token_count,
    )
    y_core_3, all_0, (keep, (send, first)) = ordered(y_core_3, all_0, side_3)
    all_0, y_core_3, keep, send, first = ordered(all_0, y_core_3, keep, send, flip(first, "tp", 1))
    diagonal, keep, send = ordered(joined((keep, (send, first)), 0, 1).astype(jnp.bfloat16), keep, send)
    by_x, by_y = relayed(diagonal)
    near_keep, (near_send, near_first) = run_experts(
        near_pieces(0, line_3, core_3) + far_pieces(0, (y_3,), (y_core_3,)), weights, token_count
    )
    send = flip(send, "tp", 1)
    all_0, near_keep, near_send, near_first, by_x, to_x = ordered(
        all_0,
        near_keep,
        near_send,
        flip(near_first, "tp", 1),
        by_x.astype(jnp.float32),
        with_upper(joined((keep, (send, first)), 0, 0), by_y),
    )
    to_y = with_lower(joined((near_keep, (near_send, near_first)), 0, 1), by_x)
    sums_3 = flip(to_x, "req", 1).astype(jnp.float32) + flip(to_y, "tp", 2).astype(jnp.float32)
    all_0, near_send, sums_3 = ordered(with_core(all_0), flip(near_send, "tp", 1), sums_3)
    sent = joined((near_keep, (near_send, near_first)), 0, 0) + sums_3
    sent_3, relay_0 = ordered(
        flip(sent[2].astype(jnp.bfloat16), "req", 2), relayed(joined(all_0, 1, 1))
    )
    sent_2, relay_0 = ordered(
        (sent[1] + sent_3.astype(jnp.float32)).astype(jnp.bfloat16), relay_0
    )
    from_z = [flip(sent[0].astype(jnp.bfloat16), "req", 2), flip(sent_2, "req", 4)]
    sums_0 = neighbours(joined(all_0, 1, 0), joined(all_0, 0, 1), *relay_0)
    total = joined(all_0, 0, 0) + from_z[0].astype(jnp.float32) + from_z[1].astype(jnp.float32)
    total, from_x, from_y = ordered(total[0], *sums_0)
    return (total + from_x[0].astype(jnp.float32) + from_y[0].astype(jnp.float32)).astype(jnp.bfloat16)


def moe_routed(
    x_full,
    head_part,
    norm_post_gain,
    expert_ids,
    route_weights,
    gate_weight,
    up_weight,
    down_weight,
):
    req_count = lax.axis_size("req")
    tp_index = lax.axis_index("tp")
    x_float = x_full.astype(jnp.float32)
    token_count = x_float.shape[0]
    share_width = x_float.shape[1] // lax.axis_size("tp")
    top_count = expert_ids.shape[1]
    expert_count = gate_weight.shape[0] * req_count
    capacity = max(2, 3 * token_count * top_count // (2 * expert_count))
    flat_expert = expert_ids.reshape(token_count * top_count)
    one_hot = (flat_expert[:, None] == jnp.arange(expert_count, dtype=jnp.int32)[None, :]).astype(
        jnp.int32
    )
    slot_rank = jnp.sum((jnp.cumsum(one_hot, axis=0) - one_hot) * one_hot, axis=1)
    slot_index = flat_expert * capacity + slot_rank
    head_sum = lax.psum(head_part.astype(jnp.bfloat16), "tp").astype(jnp.float32)
    residual_full = x_float + head_sum
    normed_post = rms_scale(residual_full, norm_post_gain).astype(jnp.bfloat16)
    residual = lax.dynamic_slice_in_dim(residual_full, tp_index * share_width, share_width, 1)
    send_buffer = build_buffer(normed_post, slot_index, top_count, expert_count, capacity)
    part_sums = expert_apply(
        lax.all_to_all(send_buffer, "req", split_axis=0, concat_axis=0, tiled=True),
        gate_weight,
        up_weight,
        down_weight,
    )
    returned = lax.all_to_all(part_sums, "req", split_axis=0, concat_axis=0, tiled=True)
    moe_term = weigh_back(returned, slot_index, route_weights, token_count, top_count)
    moe_share = lax.psum_scatter(
        moe_term.astype(jnp.bfloat16), "tp", scatter_dimension=1, tiled=True
    ).astype(jnp.float32)
    return (residual + moe_share).astype(jnp.bfloat16)


def attention_part(
    x_full,
    norm_in_gain,
    q_weight,
    k_weight,
    v_weight,
    q_gain,
    k_gain,
    o_weight,
    key_pages,
    value_pages,
    page_table,
    cache_len,
):
    head_dim = q_gain.shape[0]
    kv_local = key_pages.shape[0]
    group_size = q_weight.shape[1] // head_dim // kv_local
    token_count = x_full.shape[0]
    x_float = x_full.astype(jnp.float32)
    normed_in = rms_scale(x_float, norm_in_gain).astype(jnp.bfloat16)
    query_lin = jnp.dot(normed_in, q_weight, preferred_element_type=jnp.float32).reshape(
        token_count, kv_local * group_size, head_dim
    )
    key_lin = jnp.dot(normed_in, k_weight, preferred_element_type=jnp.float32).reshape(
        token_count, kv_local, head_dim
    )
    values_new = (
        jnp.dot(normed_in, v_weight, preferred_element_type=jnp.float32)
        .astype(jnp.bfloat16)
        .reshape(token_count, kv_local, head_dim)
    )
    requests, positions = token_layout(cache_len)
    queries = (
        rotate(rms_scale(query_lin, q_gain), positions)
        .astype(jnp.bfloat16)
        .reshape(token_count, kv_local, group_size, head_dim)
    )
    keys_new = rotate(rms_scale(key_lin, k_gain), positions).astype(jnp.bfloat16)
    slot_owner = page_slots(page_table, cache_len)
    cache_slots = key_pages.shape[1] * key_pages.shape[2]
    keys_cache = key_pages.reshape(kv_local, cache_slots, head_dim)
    values_cache = value_pages.reshape(kv_local, cache_slots, head_dim)
    attended = attend(
        queries, keys_new, values_new, keys_cache, values_cache, requests, positions, slot_owner
    )
    return jnp.dot(attended, o_weight, preferred_element_type=jnp.float32)


def body(
    hidden_in,
    norm_in_gain,
    q_weight,
    k_weight,
    v_weight,
    q_gain,
    k_gain,
    o_weight,
    key_pages,
    value_pages,
    page_table,
    cache_len,
    norm_post_gain,
    expert_ids,
    route_weights,
    gate_weight,
    up_weight,
    down_weight,
):
    req_count = lax.axis_size("req")
    attention = (
        norm_in_gain,
        q_weight,
        k_weight,
        v_weight,
        q_gain,
        k_gain,
        o_weight,
        key_pages,
        value_pages,
        page_table,
        cache_len,
    )
    experts = (norm_post_gain, expert_ids, route_weights, gate_weight, up_weight, down_weight)
    expert_count = gate_weight.shape[0] * req_count
    staged = (req_count, lax.axis_size("tp"), gate_weight.shape[0]) == (8, 4, 2)
    if staged and expert_count <= LANES // 2:
        return moe_dense(*attention_shares(hidden_in, *attention), *experts)
    x_full = lax.all_gather(hidden_in, "tp", axis=1, tiled=True)
    return moe_routed(x_full, attention_part(x_full, *attention), *experts)


def solution(mesh):
    return jax.shard_map(
        body,
        mesh=mesh,
        in_specs=(
            P("req", "tp"),
            P(),
            P(None, "tp"),
            P(None, "tp"),
            P(None, "tp"),
            P(),
            P(),
            P("tp", None),
            P("tp", "req", None, None),
            P("tp", "req", None, None),
            P("req", None),
            P("req"),
            P(),
            P("req", None),
            P("req", None),
            P("req", None, "tp"),
            P("req", None, "tp"),
            P("req", "tp", None),
        ),
        out_specs=P("req", "tp"),
        check_vma=False,
    )
```
